32 devices in a mesh: ctx: 16 (over z, y, x), head: 2 (over core).
Axes of the slice: x: 2, y: 2, z: 4, core: 2. Of those that a mesh axis runs over, the one named last changes fastest.
Arguments:
- hidden: bfloat16 [8192, 4096], P('ctx', 'head'), may hold values from -6 to 6
- w_query: bfloat16 [4096, 2048], P(None, 'head'), may hold values from -0.09375 to 0.09375
- keys: bfloat16 [8192, 2048], P('ctx', 'head'), may hold values from -6 to 6
- values: bfloat16 [8192, 2048], P('ctx', 'head'), may hold values from -6 to 6
- d_out: bfloat16 [8192, 2048], P('ctx', 'head'), may hold values from -6 to 6
- log_decay: float32 [8192, 16], P('ctx', 'head'), may hold values from -1.5 to 0, as said below
Outputs:
- d_hidden: bfloat16 [8192, 4096], P('ctx', 'head')
- d_keys: bfloat16 [8192, 2048], P('ctx', 'head')
- d_values: bfloat16 [8192, 2048], P('ctx', 'head')
The draws below stay inside these ranges and needn't reach their ends.
Inputs may be any that keep to these rules, and one draw needn't show every extreme that they name: `log_decay`: every entry is negative.
All inputs are finite; a program needn't handle non-finite values.
Results may differ from the reference program's by a relative error of at most 0.013.
Values may be sent and summed in bfloat16 or wider, within the bound.
No kernel may reach another device: no remote copies, remote signals or barrier semaphores. Data moves between devices by JAX's collectives and lax.ppermute only.
A program may use at most 128 MiB of HBM per device.

```python
import math
import jax
import jax.numpy as jnp
from jax import lax

D = 4096
HDIM = 128
HEAD_GROUP = 16
TOK_DEV = 512
TOKEN_COUNT = 8192
N_CTX = 16
N_HEAD = 2


def draw_log_decay(key, part):
    draw_keys = jax.random.split(key, 7)
    fast_share = 0.5
    picker = jax.random.uniform(draw_keys[0], (HEAD_GROUP,))
    fast_rate = jnp.exp(jax.random.uniform(draw_keys[1], (HEAD_GROUP,), minval=math.log(1.0 / 50.0), maxval=math.log(1.0 / 30.0)))
    slow_rate = jnp.exp(jax.random.uniform(draw_keys[2], (HEAD_GROUP,), minval=math.log(0.1), maxval=math.log(0.5))) / TOKEN_COUNT
    head_decay_rate = jnp.where(picker < fast_share, fast_rate, slow_rate)
    jaggedness = jnp.exp(jax.random.uniform(draw_keys[3], (TOKEN_COUNT, HEAD_GROUP), minval=-math.log(2.0), maxval=math.log(2.0)))
    block_count = TOKEN_COUNT // TOK_DEV
    block_local = jnp.exp(jax.random.uniform(draw_keys[4], (block_count, HEAD_GROUP), minval=-math.log(2.0), maxval=math.log(2.0)))
    block_local = jnp.repeat(block_local, TOK_DEV, axis=0)
    spike_positions = jax.random.randint(draw_keys[5], (3, HEAD_GROUP), 0, TOKEN_COUNT)
    spike_loss = jax.random.uniform(draw_keys[6], (3, HEAD_GROUP), minval=0.2, maxval=0.35)
    match_flags = jnp.arange(TOKEN_COUNT)[:, None, None] == spike_positions[None]
    spike_events = jnp.sum(jnp.where(match_flags, jnp.log1p(-spike_loss)[None], 0.0), axis=1)
    return (-head_decay_rate[None] * jaggedness * block_local + spike_events).astype(jnp.float32)


def steps_of(key, dims, pieces, low, largest):
    loudness, own = 1.0, jax.random.fold_in(key, 6)
    for dim, blocks in pieces:
        heights = jnp.exp(jax.random.uniform(jax.random.fold_in(own, dim), (blocks,), jnp.float32, low / len(pieces), largest / len(pieces)))
        loudness = loudness * jnp.repeat(heights, dims[dim] // blocks).reshape([-1 if axis == dim else 1 for axis in range(len(dims))])
    return loudness


def gaussian(rng, dims, scale, most, cuts=(), kind=jnp.bfloat16):
    array = scale * jax.random.normal(rng, dims, jnp.float32)
    if cuts:
        array = array * steps_of(rng, dims, cuts, -0.22, 0.18)
    return jnp.clip(array, -most, most).astype(kind)


def setup_inputs(seed: int = 0) -> dict:
    key_list = jax.random.split(jax.random.key(seed), 7)
    return {
        "hidden": gaussian(key_list[0], (TOKEN_COUNT, D), 1.0, 6.0, ((0, 16), (1, 2))),
        "w_query": gaussian(key_list[1], (D, HEAD_GROUP * HDIM), D ** -0.5, 0.09375, ((1, 2),)),
        "keys": gaussian(key_list[2], (TOKEN_COUNT, HEAD_GROUP * HDIM), 1.0, 6.0, ((0, 16), (1, 2))),
        "values": gaussian(key_list[3], (TOKEN_COUNT, HEAD_GROUP * HDIM), 1.0, 6.0, ((0, 16), (1, 2))),
        "d_out": gaussian(key_list[4], (TOKEN_COUNT, HEAD_GROUP * HDIM), 1.0, 6.0, ((0, 16), (1, 2))),
        "log_decay": draw_log_decay(jax.random.fold_in(key_list[6], 71), 0),
    }


highest = lax.Precision.HIGHEST

def rounded(value):
    return lax.optimization_barrier(value.astype(jnp.bfloat16)).astype(jnp.float32)

def summaries(query_heads, scaled_keys, value_heads, grad_heads, cumulative, block_total, scaling):
    keep_share = jnp.exp(block_total[None] - cumulative)[:, :, None]
    decayed_keys = rounded(keep_share * scaled_keys.astype(jnp.float32))
    local_state = jnp.einsum('bhe,bhf->hef', decayed_keys, value_heads.astype(jnp.float32))
    decayed_queries = rounded(scaling * jnp.exp(cumulative)[:, :, None] * query_heads.astype(jnp.float32))
    local_adjoint = jnp.einsum('bhe,bhf->hef', decayed_queries, grad_heads.astype(jnp.float32))
    return (local_state, local_adjoint)

def gradients(query_heads, scaled_keys, value_heads, grad_heads, gate_gain, cumulative, block_total, state_in, adjoint_in, scaling):
    row_count = query_heads.shape[0]
    places = jnp.arange(row_count)
    causal = (places[:, None] >= places[None, :])[None]
    cumul_heads = cumulative.T
    spread = cumul_heads[:, :, None] - cumul_heads[:, None, :]
    decays = jnp.where(causal, jnp.exp(jnp.where(causal, spread, 0.0)), 0.0) * scaling
    query_wide = query_heads.astype(jnp.float32)
    keys_wide = scaled_keys.astype(jnp.float32)
    values_wide = value_heads.astype(jnp.float32)
    grads_wide = grad_heads.astype(jnp.float32)
    weight_dv = rounded(decays * jnp.einsum('the,she->hts', grads_wide, values_wide))
    weight_kq = rounded(decays * jnp.einsum('the,she->hts', query_wide, keys_wide))
    carry_query = jnp.einsum('thf,hef->the', grads_wide, state_in, precision=highest)
    d_query = jnp.einsum('hts,she->the', weight_dv, keys_wide) + scaling * jnp.exp(cumulative)[:, :, None] * carry_query
    tail_decay = jnp.exp(block_total[None] - cumulative)[:, :, None]
    carry_keys = jnp.einsum('shf,hef->she', values_wide, adjoint_in, precision=highest)
    carry_values = jnp.einsum('she,hef->shf', keys_wide, adjoint_in, precision=highest)
    d_scaled = jnp.einsum('hts,the->she', weight_dv, query_wide) + tail_decay * carry_keys
    d_values = jnp.einsum('hts,the->she', weight_kq, grads_wide) + tail_decay * carry_values
    d_keys = gate_gain[:, :, None] * d_scaled
    return (d_query.astype(jnp.bfloat16), d_keys.astype(jnp.bfloat16), d_values.astype(jnp.bfloat16))

def reference(hidden, w_query, keys, values, d_out, log_decay):
    scaling = HDIM ** (-0.5)
    query = jnp.dot(hidden, w_query, preferred_element_type=jnp.float32).astype(jnp.bfloat16)
    gate_gain = jnp.sqrt(-jnp.expm1(2.0 * log_decay))
    head_shape = (N_CTX, TOK_DEV, HEAD_GROUP, HDIM)
    gain_blocks = gate_gain.reshape(N_CTX, TOK_DEV, HEAD_GROUP)
    query_heads = query.reshape(head_shape)
    scaled_keys = (gain_blocks[..., None] * keys.reshape(head_shape).astype(jnp.float32)).astype(jnp.bfloat16)
    value_heads = values.reshape(head_shape)
    grad_heads = d_out.reshape(head_shape)
    cumulative = jnp.cumsum(log_decay.reshape(N_CTX, TOK_DEV, HEAD_GROUP), axis=1)
    block_total = cumulative[:, -1]
    local_state, local_adjoint = lax.map(lambda items: summaries(*items, scaling), (query_heads, scaled_keys, value_heads, grad_heads, cumulative, block_total))
    zero_states = jnp.zeros((HEAD_GROUP, HDIM, HDIM), jnp.float32)

    def advance(carried, item):
        total_log, local_part = item
        return (jnp.exp(total_log)[:, None, None] * carried + local_part, carried)
    _, state_in = lax.scan(advance, zero_states, (block_total, local_state))
    _, adjoint_in = lax.scan(advance, zero_states, (block_total, local_adjoint), reverse=True)
    d_query, d_keys, d_values = lax.map(lambda items: gradients(*items, scaling), (query_heads, scaled_keys, value_heads, grad_heads, gain_blocks, cumulative, block_total, state_in, adjoint_in))
    d_flat = d_query.reshape(TOKEN_COUNT, HEAD_GROUP * HDIM)
    group_width = HEAD_GROUP // N_HEAD * HDIM
    summed = jnp.zeros((TOKEN_COUNT, D), jnp.float32)
    for group_index in range(N_HEAD):
        low_col = group_index * group_width
        group_term = jnp.dot(d_flat[:, low_col:low_col + group_width], w_query[:, low_col:low_col + group_width].T, preferred_element_type=jnp.float32)
        summed = summed + rounded(group_term)
    d_hidden = summed.astype(jnp.bfloat16)
    return (d_hidden, d_keys.reshape(TOKEN_COUNT, HEAD_GROUP * HDIM), d_values.reshape(TOKEN_COUNT, HEAD_GROUP * HDIM))
```

```python
import functools

import jax
import jax.numpy as jnp
from jax import lax
from jax.experimental import pallas as pl
from jax.experimental.pallas import tpu as pltpu
from jax.sharding import PartitionSpec as P

HDIM = 128
LANES = 128
F32, BF16 = jnp.float32, jnp.bfloat16
MIB = 1 << 20

NN = (((1,), (0,)), ((), ()))
NT = (((1,), (1,)), ((), ()))
TN = (((0,), (0,)), ((), ()))


def dot(a, b, dims):
    return lax.dot_general(a, b, dims, preferred_element_type=F32)


def params(mib, **kw):
    return pltpu.CompilerParams(vmem_limit_bytes=mib * MIB, **kw)


def cost(flops, nbytes):
    return pl.CostEstimate(flops=int(flops), bytes_accessed=int(nbytes), transcendentals=0)


def sublanes(count):
    return -(-count // 8) * 8


def expm1_negative(z):
    series = jnp.full_like(z, 1.0)
    for order in range(10, 1, -1):
        series = 1.0 + z * series * (1.0 / order)
    return jnp.where(z > -0.5, z * series, jnp.exp(z) - 1.0)


def column(table, lane, width=LANES):
    return jnp.broadcast_to(table[:, lane : lane + 1], (table.shape[0], width))


def prepare_kernel(heads, hp, scaling, ld_ref, k_ref, v_ref, ks_ref, table_ref, cumt_ref, msg_ref, state_ref, wide):
    rows = ld_ref.shape[0]
    wide[...] = jnp.zeros_like(wide)
    wide[:, :heads] = ld_ref[...]
    logs = wide[...].T[:hp]
    lane = lax.broadcasted_iota(jnp.int32, logs.shape, 1)
    cumulative = logs
    step = 1
    while step < rows:
        moved = pltpu.roll(cumulative, step, 1)
        cumulative = cumulative + jnp.where(lane >= step, moved, 0.0)
        step *= 2
    cumt_ref[...] = cumulative
    total = cumulative[:, rows - 1 :]
    gain = jnp.sqrt(-expm1_negative(2.0 * logs))
    tail = jnp.exp(total - cumulative)
    lead = scaling * jnp.exp(cumulative)
    spare = jnp.zeros((LANES - 4 * hp, rows), F32)
    table = jnp.concatenate([cumulative, gain, tail, lead, spare], axis=0).T
    table_ref[...] = table
    share = jnp.broadcast_to(jnp.exp(total), (hp, LANES))
    high = share.astype(BF16)
    low = (share - high.astype(F32)).astype(BF16)
    base = heads * HDIM
    msg_ref[base:, :] = jnp.concatenate([high.astype(F32), low.astype(F32)], axis=0).astype(BF16)
    for h in range(heads):
        cols = slice(h * HDIM, (h + 1) * HDIM)
        scaled = (column(table, hp + h) * k_ref[:, cols].astype(F32)).astype(BF16)
        ks_ref[:, cols] = scaled
        decayed = (column(table, 2 * hp + h) * scaled.astype(F32)).astype(BF16)
        local = dot(decayed, v_ref[:, cols], TN)
        state_ref[cols, :] = local
        msg_ref[cols, :] = local.astype(BF16)


def prepare(log_decay, keys, values, heads, hp, scaling):
    rows, width = keys.shape
    vm = pl.BlockSpec(memory_space=pltpu.VMEM)
    return pl.pallas_call(
        functools.partial(prepare_kernel, heads, hp, scaling),
        out_shape=(
            jax.ShapeDtypeStruct((rows, width), BF16),
            jax.ShapeDtypeStruct((rows, LANES), F32),
            jax.ShapeDtypeStruct((hp, rows), F32),
            jax.ShapeDtypeStruct((width + 2 * hp, HDIM), BF16),
            jax.ShapeDtypeStruct((width, HDIM), F32),
        ),
        in_specs=[vm] * 3,
        out_specs=(vm,) * 5,
        scratch_shapes=[pltpu.VMEM((rows, LANES), F32)],
        compiler_params=params(24),
        cost_estimate=cost(2 * rows * width * HDIM, 8 * rows * width),
        name="prepare",
    )(log_decay, keys, values)


def project_kernel(places, hp, nparts, place_ref, *refs):
    parts, (w_ref, do_ref, table_ref, q_ref, adj_ref, msg_ref) = refs[:nparts], refs[nparts:]
    step = pl.program_id(0)
    rows, feat = parts[0].shape
    total = None
    for part, ref in enumerate(parts):
        start = pl.multiple_of(place_ref[part] * feat, feat)
        term = dot(ref[...], w_ref[pl.ds(start, feat), :], NN)
        total = term if total is None else total + term
    query = total.astype(BF16)
    q_ref[...] = query
    table = pltpu.roll(table_ref[...], LANES - step * places, 1)
    for h in range(places):
        cols = slice(h * HDIM, (h + 1) * HDIM)
        decayed = (column(table, 3 * hp + h) * query[:, cols].astype(F32)).astype(BF16)
        local = dot(decayed, do_ref[:, cols], TN)
        adj_ref[cols, :] = local
        msg_ref[cols, :] = local.astype(BF16)


def project(parts, owners, w_query, d_out, table, hp):
    rows, feat = parts[0].shape
    depth, width = w_query.shape
    block = min(256, width)
    whole = lambda shape: pl.BlockSpec(shape, lambda j, s: (0, 0))
    tall = lambda r: pl.BlockSpec((r, block), lambda j, s: (0, j))
    flat = pl.BlockSpec((block, HDIM), lambda j, s: (j, 0))
    return pl.pallas_call(
        functools.partial(project_kernel, block // HDIM, hp, len(parts)),
        grid_spec=pltpu.PrefetchScalarGridSpec(
            num_scalar_prefetch=1,
            grid=(width // block,),
            in_specs=[whole((rows, feat))] * len(parts) + [tall(depth), tall(rows), whole((rows, LANES))],
            out_specs=(tall(rows), flat, flat),
        ),
        out_shape=(
            jax.ShapeDtypeStruct((rows, width), BF16),
            jax.ShapeDtypeStruct((width, HDIM), F32),
            jax.ShapeDtypeStruct((width, HDIM), BF16),
        ),
        compiler_params=params(40),
        cost_estimate=cost(2 * rows * width * depth, 2 * (depth * width + rows * depth)),
        name="project",
    )(owners, *parts, w_query, d_out, table)


def inner_kernel(hp, scaling, q_ref, ks_ref, v_ref, do_ref, table_ref, cumt_ref, dq_ref, dk_ref, dv_ref):
    head = pl.program_id(0)
    rows = q_ref.shape[0]
    size = min(256, rows)
    table = pltpu.roll(table_ref[...], LANES - head, 1)
    cum_col = column(table, 0)
    cum_row = cumt_ref[pl.ds(head, 1), :]
    dq = [None] * (rows // size)
    dk = [None] * (rows // size)
    dv = [None] * (rows // size)
    plus = lambda a, b: b if a is None else a + b
    for i in range(rows // size):
        ti = slice(i * size, (i + 1) * size)
        here = jnp.concatenate([cum_col[ti]] * (size // LANES), axis=1)
        for j in range(i + 1):
            sj = slice(j * size, (j + 1) * size)
            gap = here - cum_row[:, sj]
            if i == j:
                keep = lax.broadcasted_iota(jnp.int32, gap.shape, 0) >= lax.broadcasted_iota(
                    jnp.int32, gap.shape, 1
                )
                decays = jnp.where(keep, jnp.exp(jnp.where(keep, gap, 0.0)) * scaling, 0.0)
            else:
                decays = jnp.exp(gap) * scaling
            wdv = (decays * dot(do_ref[ti, :], v_ref[sj, :], NT)).astype(BF16)
            wkq = (decays * dot(q_ref[ti, :], ks_ref[sj, :], NT)).astype(BF16)
            dq[i] = plus(dq[i], dot(wdv, ks_ref[sj, :], NN))
            dk[j] = plus(dk[j], dot(wdv, q_ref[ti, :], TN))
            dv[j] = plus(dv[j], dot(wkq, do_ref[ti, :], TN))
    for i in range(rows // size):
        ti = slice(i * size, (i + 1) * size)
        dq_ref[ti, :] = dq[i]
        dk_ref[ti, :] = dk[i]
        dv_ref[ti, :] = dv[i]


def inner(query, scaled_keys, values, d_out, table, cumt, heads, hp, scaling):
    rows, width = query.shape
    tall = pl.BlockSpec((rows, HDIM), lambda h: (0, h))
    whole = lambda a: pl.BlockSpec(a.shape, lambda h: (0, 0))
    return pl.pallas_call(
        functools.partial(inner_kernel, hp, scaling),
        grid=(heads,),
        in_specs=[tall] * 4 + [whole(table), whole(cumt)],
        out_specs=(tall,) * 3,
        out_shape=(jax.ShapeDtypeStruct((rows, width), F32),) * 3,
        compiler_params=params(32),
        cost_estimate=cost(10 * rows * rows * width, 20 * rows * width),
        name="inner",
    )(query, scaled_keys, values, d_out, table, cumt)


def mix(coef_ref, pieces, heads, h):
    cols = slice(h * HDIM, (h + 1) * HDIM)
    total = None
    for stage, piece in enumerate(pieces):
        row = stage * heads + h
        term = coef_ref[row : row + 1, :] * piece[cols, :].astype(F32)
        total = term if total is None else total + term
    return total.astype(BF16)


def query_kernel(heads, hp, stages, place_ref, *refs):
    pieces = refs[:stages]
    coef_ref, inner_ref, do_ref, table_ref, w_ref, dq_ref, out_ref, held = refs[stages:]

    @pl.when(pl.program_id(0) == 0)
    def _():
        for h in range(heads):
            cols = slice(h * HDIM, (h + 1) * HDIM)
            state = mix(coef_ref, pieces, heads, h)
            carry = dot(do_ref[:, cols], state, NT)
            full = inner_ref[:, cols] + column(table_ref[...], 3 * hp + h) * carry
            held[:, cols] = full.astype(BF16)
        dq_ref[...] = held[...]

    out_ref[...] = dot(held[...], w_ref[...], NT).astype(BF16)


def query_term(pieces, coefs, inner_dq, d_out, table, w_query, place, feat, heads, hp):
    rows, width = d_out.shape
    block = min(512, feat)
    whole = lambda a: pl.BlockSpec(a.shape, lambda j, s: (0,) * a.ndim)
    args = (*pieces, coefs, inner_dq, d_out, table)
    return pl.pallas_call(
        functools.partial(query_kernel, heads, hp, len(pieces)),
        grid_spec=pltpu.PrefetchScalarGridSpec(
            num_scalar_prefetch=1,
            grid=(feat // block,),
            in_specs=[whole(a) for a in args]
            + [pl.BlockSpec((block, width), lambda j, s: (s[0] * (feat // block) + j, 0))],
            out_specs=(
                pl.BlockSpec((rows, width), lambda j, s: (0, 0)),
                pl.BlockSpec((rows, block), lambda j, s: (0, j)),
            ),
            scratch_shapes=[pltpu.VMEM((rows, width), BF16)],
        ),
        out_shape=(
            jax.ShapeDtypeStruct((rows, width), BF16),
            jax.ShapeDtypeStruct((rows, feat), BF16),
        ),
        compiler_params=params(40),
        cost_estimate=cost(2 * rows * width * feat, 2 * (width + rows) * feat + 10 * rows * width),
        name="query_term",
    )(place, *args, w_query)


def term_kernel(place_ref, dq_ref, w_ref, out_ref):
    out_ref[...] = dot(dq_ref[...], w_ref[...], NT).astype(BF16)


def plain_term(d_query, w_query, place, feat):
    rows, width = d_query.shape
    block = min(512, feat)
    return pl.pallas_call(
        term_kernel,
        grid_spec=pltpu.PrefetchScalarGridSpec(
            num_scalar_prefetch=1,
            grid=(feat // block,),
            in_specs=[
                pl.BlockSpec((rows, width), lambda j, s: (0, 0)),
                pl.BlockSpec((block, width), lambda j, s: (s[0] * (feat // block) + j, 0)),
            ],
            out_specs=pl.BlockSpec((rows, block), lambda j, s: (0, j)),
        ),
        out_shape=jax.ShapeDtypeStruct((rows, feat), BF16),
        compiler_params=params(24),
        cost_estimate=cost(2 * rows * width * feat, 2 * (width + rows) * feat),
        name="term",
    )(place, d_query, w_query)


def close_kernel(heads, hp, stages, *refs):
    pieces = refs[:stages]
    coef_ref, dk_ref, dv_ref, ks_ref, v_ref, table_ref, out_k, out_v = refs[stages:]
    for h in range(heads):
        cols = slice(h * HDIM, (h + 1) * HDIM)
        adjoint = mix(coef_ref, pieces, heads, h)
        table = table_ref[...]
        tail, gain = column(table, 2 * hp + h), column(table, hp + h)
        carry_k = dot(v_ref[:, cols], adjoint, NT)
        out_k[:, cols] = (gain * (dk_ref[:, cols] + tail * carry_k)).astype(BF16)
        carry_v = dot(ks_ref[:, cols], adjoint, NN)
        out_v[:, cols] = (dv_ref[:, cols] + tail * carry_v).astype(BF16)


def close(pieces, coefs, dk, dv, scaled_keys, values, table, heads, hp):
    rows, width = dk.shape
    vm = pl.BlockSpec(memory_space=pltpu.VMEM)
    return pl.pallas_call(
        functools.partial(close_kernel, heads, hp, len(pieces)),
        out_shape=(jax.ShapeDtypeStruct((rows, width), BF16),) * 2,
        in_specs=[vm] * (len(pieces) + 6),
        out_specs=(vm,) * 2,
        compiler_params=params(32),
        cost_estimate=cost(4 * rows * width * HDIM, 16 * rows * width),
        name="close",
    )(*pieces, coefs, dk, dv, scaled_keys, values, table)


def body(ctx_size, head_size, hidden, w_query, keys, values, d_out, log_decay):
    rows, feat = hidden.shape
    heads = log_decay.shape[1]
    width = w_query.shape[1]
    hp = sublanes(heads)
    scaling = HDIM ** (-0.5)
    me = lax.axis_index("ctx")
    mine = lax.axis_index("head")

    parts = [hidden]
    for shift in range(1, head_size):
        ring = [(i, (i + shift) % head_size) for i in range(head_size)]
        parts.append(lax.ppermute(hidden, "head", ring))
    owners = jnp.stack([(mine + head_size - s) % head_size for s in range(head_size)]).astype(jnp.int32)

    scaled_keys, table, cumt, state_msg, state = prepare(log_decay, keys, values, heads, hp, scaling)
    query, adjoint, adjoint_msg = project(parts, owners, w_query, d_out, table, hp)

    wide = lambda factor: factor[:heads, None, :]
    cube = lambda flat: flat.reshape(heads, HDIM, HDIM)
    msg = state_msg
    tail_rows = msg[width:]
    share = tail_rows[:hp].astype(F32) + tail_rows[hp:].astype(F32)
    before = jnp.ones_like(share)
    after = jnp.ones_like(share)
    state_pieces, state_coefs, adjoint_pieces, adjoint_coefs = [], [], [], []
    amsg = adjoint_msg
    dist = 1
    while dist < ctx_size:
        upper = (me & dist) != 0
        last = 2 * dist >= ctx_size
        state_coefs.append(jnp.where(upper, before, 0.0)[:heads])
        adjoint_coefs.append(jnp.where(upper, 0.0, after)[:heads])
        if last:
            up = [(i, i + dist) for i in range(ctx_size) if not i & dist]
            down = [(j, i) for i, j in up]
            got = lax.ppermute(msg[:width], "ctx", up)
            agot = lax.ppermute(amsg, "ctx", down)
        else:
            pairs = [(i, i ^ dist) for i in range(ctx_size)]
            got = lax.ppermute(msg, "ctx", pairs)
            agot = lax.ppermute(amsg, "ctx", pairs)
            theirs = got[width : width + hp].astype(F32) + got[width + hp :].astype(F32)
            arrived = cube(got[:width]).astype(F32)
            state = (
                wide(jnp.where(upper, 1.0, theirs)) * cube(state) + wide(jnp.where(upper, share, 1.0)) * arrived
            ).reshape(width, HDIM)
            aarrived = cube(agot).astype(F32)
            adjoint = (
                wide(jnp.where(upper, theirs, 1.0)) * cube(adjoint) + wide(jnp.where(upper, 1.0, share)) * aarrived
            ).reshape(width, HDIM)
            before = jnp.where(upper, before * theirs, before)
            after = jnp.where(upper, after, after * theirs)
            share = share * theirs
            high = share.astype(BF16)
            low = (share - high.astype(F32)).astype(BF16)
            msg = state.astype(BF16)
            if 4 * dist < ctx_size:
                msg = jnp.concatenate([msg, high, low], axis=0)
            amsg = adjoint.astype(BF16)
        state_pieces.append(got)
        adjoint_pieces.append(agot)
        dist *= 2
    state_coefs = jnp.concatenate(state_coefs, axis=0)
    adjoint_coefs = jnp.concatenate(adjoint_coefs, axis=0)

    inner_dq, inner_dk, inner_dv = inner(query, scaled_keys, values, d_out, table, cumt, heads, hp, scaling)

    place = lambda shift: ((mine + shift) % head_size).astype(jnp.int32).reshape(1)
    d_query, term = query_term(
        state_pieces, state_coefs, inner_dq, d_out, table, w_query, place(1), feat, heads, hp
    )
    arrived = []
    for shift in range(1, head_size):
        if shift > 1:
            term = plain_term(d_query, w_query, place(shift), feat)
        ring = [(i, (i + shift) % head_size) for i in range(head_size)]
        arrived.append(lax.ppermute(term, "head", ring))
    summed = plain_term(d_query, w_query, place(0), feat).astype(F32)
    d_keys, d_values = close(
        adjoint_pieces, adjoint_coefs, inner_dk, inner_dv, scaled_keys, values, table, heads, hp
    )
    for piece in arrived:
        summed = summed + piece.astype(F32)
    return (summed.astype(BF16), d_keys, d_values)


def solution(mesh):
    return jax.shard_map(
        functools.partial(body, mesh.shape["ctx"], mesh.shape["head"]),
        mesh=mesh,
        in_specs=(
            P("ctx", "head"),
            P(None, "head"),
            P("ctx", "head"),
            P("ctx", "head"),
            P("ctx", "head"),
            P("ctx", "head"),
        ),
        out_specs=(P("ctx", "head"), P("ctx", "head"), P("ctx", "head")),
        check_vma=False,
    )
```

```python
import functools
import math

import jax
import jax.numpy as jnp
from jax import lax
from jax.experimental import pallas as pl
from jax.experimental.pallas import tpu as pltpu
from jax.sharding import PartitionSpec as P

HDIM = 128
LANES = 128
F32, BF16 = jnp.float32, jnp.bfloat16
MIB = 1 << 20
VM = pl.BlockSpec(memory_space=pltpu.VMEM)

NN = (((1,), (0,)), ((), ()))
NT = (((1,), (1,)), ((), ()))
TN = (((0,), (0,)), ((), ()))


def dot(a, b, dims):
    return lax.dot_general(a, b, dims, preferred_element_type=F32)


def params(mib, **kw):
    return pltpu.CompilerParams(vmem_limit_bytes=mib * MIB, **kw)


def cost(flops, nbytes):
    return pl.CostEstimate(flops=int(flops), bytes_accessed=int(nbytes), transcendentals=0)


def sublanes(count):
    return -(-count // 8) * 8


def expm1_negative(z):
    series = jnp.full_like(z, 1.0)
    for order in range(10, 1, -1):
        series = 1.0 + z * series * (1.0 / order)
    return jnp.where(z > -0.5, z * series, jnp.exp(z) - 1.0)


def column(table, lane, width=LANES):
    return jnp.broadcast_to(table[:, lane : lane + 1], (table.shape[0], width))


def prepare_kernel(
    heads, hp, scaling, ld_hbm, k_hbm, v_hbm, ks_ref, table_ref, cumt_ref, msg_ref, state_ref, ld, kbuf, vbuf, sems
):
    rows = kbuf.shape[0]
    copies = [pltpu.make_async_copy(ld_hbm, ld, sems.at[0])]
    for h in range(heads):
        cols = pl.ds(h * HDIM, HDIM)
        copies.append(pltpu.make_async_copy(k_hbm.at[:, cols], kbuf.at[:, cols], sems.at[1 + 2 * h]))
        copies.append(pltpu.make_async_copy(v_hbm.at[:, cols], vbuf.at[:, cols], sems.at[2 + 2 * h]))
    for copy in copies:
        copy.start()
    copies[0].wait()
    logs = ld[...]
    if heads < hp:
        logs = jnp.concatenate([logs, jnp.zeros((hp - heads, rows), F32)], axis=0)
    lane = lax.broadcasted_iota(jnp.int32, logs.shape, 1)
    cumulative = logs
    step = 1
    while step < rows:
        moved = pltpu.roll(cumulative, step, 1)
        cumulative = cumulative + jnp.where(lane >= step, moved, 0.0)
        step *= 2
    cumt_ref[...] = cumulative
    total = cumulative[:, rows - 1 :]
    gain = jnp.sqrt(-expm1_negative(2.0 * logs))
    tail = jnp.exp(total - cumulative)
    lead = scaling * jnp.exp(cumulative)
    spare = jnp.zeros((LANES - 4 * hp, rows), F32)
    table = jnp.concatenate([cumulative, gain, tail, lead, spare], axis=0).T
    table_ref[...] = table
    share = jnp.broadcast_to(jnp.exp(total), (hp, LANES))
    high = share.astype(BF16)
    low = (share - high.astype(F32)).astype(BF16)
    base = heads * HDIM
    msg_ref[base:, :] = jnp.concatenate([high.astype(F32), low.astype(F32)], axis=0).astype(BF16)
    for h in range(heads):
        cols = slice(h * HDIM, (h + 1) * HDIM)
        copies[1 + 2 * h].wait()
        scaled = (column(table, hp + h) * kbuf[:, cols].astype(F32)).astype(BF16)
        ks_ref[:, cols] = scaled
        decayed = (column(table, 2 * hp + h) * scaled.astype(F32)).astype(BF16)
        copies[2 + 2 * h].wait()
        local = dot(decayed, vbuf[:, cols], TN)
        state_ref[cols, :] = local
        msg_ref[cols, :] = local.astype(BF16)


def prepare(logs, keys, values, heads, hp, scaling):
    rows, width = keys.shape
    return pl.pallas_call(
        functools.partial(prepare_kernel, heads, hp, scaling),
        out_shape=(
            jax.ShapeDtypeStruct((rows, width), BF16),
            jax.ShapeDtypeStruct((rows, LANES), F32),
            jax.ShapeDtypeStruct((hp, rows), F32),
            jax.ShapeDtypeStruct((width + 2 * hp, HDIM), BF16),
            jax.ShapeDtypeStruct((width, HDIM), F32),
        ),
        in_specs=[pl.BlockSpec(memory_space=pl.ANY)] * 3,
        out_specs=(VM,) * 5,
        scratch_shapes=[
            pltpu.VMEM((heads, rows), F32),
            pltpu.VMEM((rows, width), BF16),
            pltpu.VMEM((rows, width), BF16),
            pltpu.SemaphoreType.DMA((1 + 2 * heads,)),
        ],
        compiler_params=params(8),
        cost_estimate=cost(2 * rows * width * HDIM, 8 * rows * width),
        name="prepare",
    )(logs, keys, values)


def project_kernel(hp, nparts, place_ref, *refs):
    parts, (w_ref, do_ref, table_ref, q_ref, adj_ref, msg_ref) = refs[:nparts], refs[nparts:]
    rows, feat = parts[0].shape
    width = w_ref.shape[1]
    block = min(256, width)
    starts = [pl.multiple_of(place_ref[part] * feat, feat) for part in range(nparts)]
    for first in range(0, width, block):
        wide = slice(first, first + block)
        total = None
        for start, ref in zip(starts, parts):
            term = dot(ref[...], w_ref[pl.ds(start, feat), wide], NN)
            total = term if total is None else total + term
        query = total.astype(BF16)
        q_ref[:, wide] = query
        for h in range(first // HDIM, (first + block) // HDIM):
            cols = slice(h * HDIM, (h + 1) * HDIM)
            lead = column(table_ref[...], 3 * hp + h)
            decayed = (lead * query[:, h * HDIM - first : (h + 1) * HDIM - first].astype(F32)).astype(BF16)
            local = dot(decayed, do_ref[:, cols], TN)
            adj_ref[cols, :] = local
            msg_ref[cols, :] = local.astype(BF16)


def project(parts, owners, w_query, d_out, table, hp):
    rows, feat = parts[0].shape
    depth, width = w_query.shape
    return pl.pallas_call(
        functools.partial(project_kernel, hp, len(parts)),
        in_specs=[pl.BlockSpec(memory_space=pltpu.SMEM)] + [VM] * (len(parts) + 3),
        out_specs=(VM,) * 3,
        out_shape=(
            jax.ShapeDtypeStruct((rows, width), BF16),
            jax.ShapeDtypeStruct((width, HDIM), F32),
            jax.ShapeDtypeStruct((width, HDIM), BF16),
        ),
        compiler_params=params(10),
        cost_estimate=cost(2 * rows * width * depth, 2 * (depth * width + rows * depth)),
        name="project",
    )(owners, *parts, w_query, d_out, table)


def inner_kernel(first, last, q_ref, ks_ref, v_ref, do_ref, table_ref, cumt_ref, dq_ref, dk_ref, dv_ref):
    rows = q_ref.shape[0]
    row = lax.broadcasted_iota(jnp.int32, (rows, rows), 0)
    keep = row >= lax.broadcasted_iota(jnp.int32, (rows, rows), 1)
    shift = -0.5 * math.log2(HDIM)
    turn = math.log2(math.e)
    for h in range(first, last):
        cols = slice(h * HDIM, (h + 1) * HDIM)
        outs = slice((h - first) * HDIM, (h - first + 1) * HDIM)
        later = column(table_ref[...], h) * turn + shift
        sooner = cumt_ref[h : h + 1, :] * turn
        gap = jnp.concatenate([later] * (rows // LANES), axis=1) - sooner
        decays = jnp.exp2(jnp.where(keep, gap, -1e30))
        query, scaled, grad = q_ref[:, cols], ks_ref[:, cols], do_ref[:, cols]
        wdv = (decays * dot(grad, v_ref[:, cols], NT)).astype(BF16)
        wkq = (decays * dot(query, scaled, NT)).astype(BF16)
        dq_ref[:, outs] = dot(wdv, scaled, NN)
        dk_ref[:, outs] = dot(query, wdv, TN).T
        dv_ref[:, outs] = dot(grad, wkq, TN).T


def inner(first, last, query, scaled_keys, values, d_out, table, cumt):
    rows = query.shape[0]
    width = (last - first) * HDIM
    return pl.pallas_call(
        functools.partial(inner_kernel, first, last),
        in_specs=[VM] * 6,
        out_specs=(VM,) * 3,
        out_shape=(jax.ShapeDtypeStruct((rows, width), F32),) * 3,
        compiler_params=params(16),
        cost_estimate=cost(10 * rows * rows * width, 20 * rows * width),
        name="inner",
    )(query, scaled_keys, values, d_out, table, cumt)


def mix(coef_ref, pieces, heads, h):
    cols = slice(h * HDIM, (h + 1) * HDIM)
    total = None
    for stage, piece in enumerate(pieces):
        row = stage * heads + h
        term = coef_ref[row : row + 1, :] * piece[cols, :].astype(F32)
        total = term if total is None else total + term
    return total.astype(BF16)


def query_kernel(heads, hp, stages, place_ref, *refs):
    pieces = refs[:stages]
    coef_ref, do_ref, table_ref, w_ref = refs[stages : stages + 4]
    inner_refs, (dq_ref, out_ref) = refs[stages + 4 : -2], refs[-2:]
    each = heads // len(inner_refs)
    for h in range(heads):
        cols = slice(h * HDIM, (h + 1) * HDIM)
        state = mix(coef_ref, pieces, heads, h)
        carry = dot(do_ref[:, cols], state, NT)
        local = inner_refs[h // each][:, (h % each) * HDIM : (h % each + 1) * HDIM]
        dq_ref[:, cols] = (local + column(table_ref[...], 3 * hp + h) * carry).astype(BF16)
    term_kernel(place_ref, dq_ref, w_ref, out_ref)


def query_term(pieces, coefs, inner_dq, d_out, table, w_query, place, feat, heads, hp):
    rows, width = d_out.shape
    args = (*pieces, coefs, d_out, table, w_query, *inner_dq)
    return pl.pallas_call(
        functools.partial(query_kernel, heads, hp, len(pieces)),
        in_specs=[pl.BlockSpec(memory_space=pltpu.SMEM)] + [VM] * len(args),
        out_specs=(VM,) * 2,
        out_shape=(
            jax.ShapeDtypeStruct((rows, width), BF16),
            jax.ShapeDtypeStruct((rows, feat), BF16),
        ),
        compiler_params=params(10),
        cost_estimate=cost(2 * rows * width * feat, 2 * (width + rows) * feat + 10 * rows * width),
        name="query_term",
    )(place, *args)


def term_kernel(place_ref, dq_ref, w_ref, out_ref):
    feat = out_ref.shape[1]
    block = min(512, feat)
    for first in range(0, feat, block):
        start = pl.multiple_of(place_ref[0] * feat + first, block)
        out_ref[:, first : first + block] = dot(dq_ref[...], w_ref[pl.ds(start, block), :], NT).astype(BF16)


def plain_term(d_query, w_query, place, feat):
    rows, width = d_query.shape
    return pl.pallas_call(
        term_kernel,
        in_specs=[pl.BlockSpec(memory_space=pltpu.SMEM), VM, VM],
        out_specs=VM,
        out_shape=jax.ShapeDtypeStruct((rows, feat), BF16),
        compiler_params=params(10),
        cost_estimate=cost(2 * rows * width * feat, 2 * (width + rows) * feat),
        name="term",
    )(place, d_query, w_query)


def close_kernel(heads, hp, stages, *refs):
    pieces = refs[:stages]
    coef_ref, ks_ref, v_ref, table_ref = refs[stages : stages + 4]
    rest, (out_k, out_v) = refs[stages + 4 : -2], refs[-2:]
    dks, dvs = rest[: len(rest) // 2], rest[len(rest) // 2 :]
    each = heads // len(dks)
    for h in range(heads):
        cols = slice(h * HDIM, (h + 1) * HDIM)
        part = slice((h % each) * HDIM, (h % each + 1) * HDIM)
        adjoint = mix(coef_ref, pieces, heads, h)
        table = table_ref[...]
        tail, gain = column(table, 2 * hp + h), column(table, hp + h)
        carry_k = dot(v_ref[:, cols], adjoint, NT)
        out_k[:, cols] = (gain * (dks[h // each][:, part] + tail * carry_k)).astype(BF16)
        carry_v = dot(ks_ref[:, cols], adjoint, NN)
        out_v[:, cols] = (dvs[h // each][:, part] + tail * carry_v).astype(BF16)


def close(pieces, coefs, dks, dvs, scaled_keys, values, table, heads, hp):
    rows, width = values.shape
    args = (*pieces, coefs, scaled_keys, values, table, *dks, *dvs)
    return pl.pallas_call(
        functools.partial(close_kernel, heads, hp, len(pieces)),
        out_shape=(jax.ShapeDtypeStruct((rows, width), BF16),) * 2,
        in_specs=[VM] * len(args),
        out_specs=(VM,) * 2,
        compiler_params=params(8),
        cost_estimate=cost(4 * rows * width * HDIM, 16 * rows * width),
        name="close",
    )(*args)


def body(ctx_size, head_size, hidden, w_query, keys, values, d_out, log_decay):
    rows, feat = hidden.shape
    heads = log_decay.shape[1]
    width = w_query.shape[1]
    hp = sublanes(heads)
    scaling = HDIM ** (-0.5)
    me = lax.axis_index("ctx")
    mine = lax.axis_index("head")

    parts = [hidden]
    for shift in range(1, head_size):
        ring = [(i, (i + shift) % head_size) for i in range(head_size)]
        parts.append(lax.ppermute(hidden, "head", ring))
    owners = jnp.stack([(mine + head_size - s) % head_size for s in range(head_size)]).astype(jnp.int32)

    scaled_keys, table, cumt, msg, state = prepare(log_decay.T, keys, values, heads, hp, scaling)
    query, adjoint, amsg = project(parts, owners, w_query, d_out, table, hp)

    wide = lambda factor: factor[:heads, None, :]
    cube = lambda flat: flat.reshape(heads, HDIM, HDIM)
    split = lambda f: (f.astype(BF16), (f - f.astype(BF16).astype(F32)).astype(BF16))
    joined = lambda pair: pair[:hp].astype(F32) + pair[hp:].astype(F32)
    stages = (ctx_size - 1).bit_length()

    def send(array, stage, up):
        dist = 1 << stage
        if stage < stages - 1:
            pairs = [(i, i ^ dist) for i in range(ctx_size)]
        else:
            pairs = [(i, i + dist) if up else (i + dist, i) for i in range(ctx_size) if not i & dist]
        return lax.ppermute(array, "ctx", pairs)

    uppers = [(me & (1 << stage)) != 0 for stage in range(stages)]
    shares, others = [joined(msg[width:])], []
    got, agot = [], []
    before, after = [jnp.ones_like(shares[0])], [jnp.ones_like(shares[0])]

    def fold_state(stage, state):
        upper, arrived = uppers[stage], cube(got[stage][:width]).astype(F32)
        theirs = joined(got[stage][width:])
        others.append(theirs)
        own, other = jnp.where(upper, 1.0, theirs), jnp.where(upper, shares[stage], 1.0)
        state = (wide(own) * cube(state) + wide(other) * arrived).reshape(width, HDIM)
        shares.append(shares[stage] * theirs)
        before.append(jnp.where(upper, before[stage] * theirs, before[stage]))
        after.append(jnp.where(upper, after[stage], after[stage] * theirs))
        msg = state.astype(BF16)
        if stage + 2 < stages:
            msg = jnp.concatenate([msg, *split(shares[-1])], axis=0)
        return msg, state

    def fold_adjoint(stage, adjoint):
        upper, arrived = uppers[stage], cube(agot[stage]).astype(F32)
        own, other = jnp.where(upper, others[stage], 1.0), jnp.where(upper, 1.0, shares[stage])
        adjoint = (wide(own) * cube(adjoint) + wide(other) * arrived).reshape(width, HDIM)
        return adjoint.astype(BF16), adjoint

    half = max(1, heads // 2)
    pending = [(first, first + half) for first in range(0, heads, half)]
    inner_parts = []

    def next_inner():
        return inner(*pending.pop(0), query, scaled_keys, values, d_out, table, cumt)

    barrier = lax.optimization_barrier
    for stage in range(stages):
        arrived = send(msg if stage < stages - 1 else msg[:width], stage, True)
        if stage == 0:
            arrived, query, adjoint, amsg = barrier((arrived, query, adjoint, amsg))
        else:
            agot.append(send(amsg, stage - 1, False))
            if pending and (stage == 1 or stage == stages - 1):
                part = next_inner()
                arrived, *part = barrier((arrived, *part))
                inner_parts.append(part)
        got.append(arrived)
        if stage < stages - 1:
            msg, state = fold_state(stage, state)
        if stage >= 1:
            amsg, adjoint = fold_adjoint(stage - 1, adjoint)
    while pending:
        inner_parts.append(next_inner())
    agot.append(send(amsg, stages - 1, False))
    got[-1], _ = barrier((got[-1], amsg))

    state_coefs = [jnp.where(u, f, 0.0)[:heads] for u, f in zip(uppers, before)]
    adjoint_coefs = [jnp.where(u, 0.0, f)[:heads] for u, f in zip(uppers, after)]
    state_coefs = jnp.concatenate(state_coefs, axis=0)
    adjoint_coefs = jnp.concatenate(adjoint_coefs, axis=0)
    dqs, dks, dvs = zip(*inner_parts)

    place = lambda shift: ((mine + shift) % head_size).astype(jnp.int32).reshape(1)
    d_query, term = query_term(got, state_coefs, dqs, d_out, table, w_query, place(1), feat, heads, hp)
    arrived = []
    for shift in range(1, head_size):
        if shift > 1:
            term = plain_term(d_query, w_query, place(shift), feat)
        ring = [(i, (i + shift) % head_size) for i in range(head_size)]
        arrived.append(lax.ppermute(term, "head", ring))
    summed = plain_term(d_query, w_query, place(0), feat).astype(F32)
    d_keys, d_values = close(agot, adjoint_coefs, dks, dvs, scaled_keys, values, table, heads, hp)
    for piece in arrived:
        summed = summed + piece.astype(F32)
    return (summed.astype(BF16), d_keys, d_values)


def solution(mesh):
    return jax.shard_map(
        functools.partial(body, mesh.shape["ctx"], mesh.shape["head"]),
        mesh=mesh,
        in_specs=(
            P("ctx", "head"),
            P(None, "head"),
            P("ctx", "head"),
            P("ctx", "head"),
            P("ctx", "head"),
            P("ctx", "head"),
        ),
        out_specs=(P("ctx", "head"), P("ctx", "head"), P("ctx", "head")),
        check_vma=False,
    )
```

```python
import functools
import math

import jax
import jax.numpy as jnp
from jax import lax
from jax.experimental import pallas as pl
from jax.experimental.pallas import tpu as pltpu
from jax.sharding import PartitionSpec as P

HDIM = 128
LANES = 128
F32, BF16 = jnp.float32, jnp.bfloat16
MIB = 1 << 20
VM = pl.BlockSpec(memory_space=pltpu.VMEM)
SM = pl.BlockSpec(memory_space=pltpu.SMEM)
HB = pl.BlockSpec(memory_space=pltpu.HBM)

NN = (((1,), (0,)), ((), ()))
NT = (((1,), (1,)), ((), ()))
TN = (((0,), (0,)), ((), ()))


def dot(a, b, dims):
    return lax.dot_general(a, b, dims, preferred_element_type=F32)


def params(mib, **kw):
    return pltpu.CompilerParams(vmem_limit_bytes=mib * MIB, **kw)


def pinned(array):
    return pltpu.with_memory_space_constraint(array, pltpu.HBM)


def cost(flops, nbytes):
    return pl.CostEstimate(flops=int(flops), bytes_accessed=int(nbytes), transcendentals=0)


def sublanes(count):
    return -(-count // 8) * 8


def expm1_negative(z):
    series = jnp.full_like(z, 1.0)
    for order in range(10, 1, -1):
        series = 1.0 + z * series * (1.0 / order)
    return jnp.where(z > -0.5, z * series, jnp.exp(z) - 1.0)


def column(table, lane, width=LANES):
    return jnp.broadcast_to(table[:, lane : lane + 1], (table.shape[0], width))


class Copies:
    def __init__(self, sems):
        self.sems, self.count, self.out = sems, 0, []

    def start(self, src, dst):
        copy = pltpu.make_async_copy(src, dst, self.sems.at[self.count])
        self.count += 1
        copy.start()
        return copy

    def store(self, src, dst):
        self.out.append(self.start(src, dst))

    def finish(self):
        for copy in self.out:
            copy.wait()


def groups(heads):
    size = min(4, heads)
    return [(f, f + size, slice(f * HDIM, (f + size) * HDIM)) for f in range(0, heads, size)]


def turned(facts):
    spare = jnp.zeros((LANES - facts.shape[0], facts.shape[1]), F32)
    return jnp.concatenate([facts, spare], axis=0).T


def prepare_kernel(
    heads, hp, scaling, ld_hbm, k_hbm, v_hbm, ks_hbm, facts_hbm, msg_ref, state_ref, ld, facts_ref, kbuf, vbuf, ksbuf, sems
):
    rows = kbuf.shape[0]
    copies = Copies(sems)
    ld_in = copies.start(ld_hbm, ld)
    parts = [pl.ds(f, rows // 2) for f in (0, rows // 2)]
    k_in = [copies.start(k_hbm.at[p, :], kbuf.at[p, :]) for p in parts]
    v_in = [copies.start(v_hbm.at[p, :], vbuf.at[p, :]) for p in parts]
    ld_in.wait()
    logs = ld[...]
    if heads < hp:
        logs = jnp.concatenate([logs, jnp.zeros((hp - heads, rows), F32)], axis=0)
    lane = lax.broadcasted_iota(jnp.int32, logs.shape, 1)
    cumulative = logs
    step = 1
    while step < rows:
        moved = pltpu.roll(cumulative, step, 1)
        cumulative = cumulative + jnp.where(lane >= step, moved, 0.0)
        step *= 2
    total = cumulative[:, rows - 1 :]
    gain = jnp.sqrt(-expm1_negative(2.0 * logs))
    tail = jnp.exp(total - cumulative)
    lead = scaling * jnp.exp(cumulative)
    facts = jnp.concatenate([cumulative, gain, tail, lead], axis=0)
    facts_ref[...] = facts
    copies.store(facts_ref, facts_hbm)
    table = turned(facts)
    share = jnp.broadcast_to(jnp.exp(total), (hp, LANES))
    high = share.astype(BF16)
    low = (share - high.astype(F32)).astype(BF16)
    base = heads * HDIM
    msg_ref[base:, :] = jnp.concatenate([high.astype(F32), low.astype(F32)], axis=0).astype(BF16)
    for copy in k_in + v_in:
        copy.wait()
    for first, last, wide in groups(heads):
        for h in range(first, last):
            cols = slice(h * HDIM, (h + 1) * HDIM)
            scaled = (column(table, hp + h) * kbuf[:, cols].astype(F32)).astype(BF16)
            ksbuf[:, cols] = scaled
            decayed = (column(table, 2 * hp + h) * scaled.astype(F32)).astype(BF16)
            local = dot(decayed, vbuf[:, cols], TN)
            state_ref[cols, :] = local
            msg_ref[cols, :] = local.astype(BF16)
        copies.store(ksbuf.at[:, wide], ks_hbm.at[:, wide])
    copies.finish()


def prepare(logs, keys, values, heads, hp, scaling):
    rows, width = keys.shape
    buf = pltpu.VMEM((rows, width), BF16)
    return pl.pallas_call(
        functools.partial(prepare_kernel, heads, hp, scaling),
        out_shape=(
            jax.ShapeDtypeStruct((rows, width), BF16),
            jax.ShapeDtypeStruct((4 * hp, rows), F32),
            jax.ShapeDtypeStruct((width + 2 * hp, HDIM), BF16),
            jax.ShapeDtypeStruct((width, HDIM), F32),
        ),
        in_specs=[HB] * 3,
        out_specs=(HB, HB, VM, VM),
        scratch_shapes=[
            pltpu.VMEM((heads, rows), F32),
            pltpu.VMEM((4 * hp, rows), F32),
            buf,
            buf,
            buf,
            pltpu.SemaphoreType.DMA((6 + len(groups(heads)),)),
        ],
        compiler_params=params(12),
        cost_estimate=cost(2 * rows * width * HDIM, 8 * rows * width),
        name="prepare",
    )(pinned(logs), pinned(keys), pinned(values))


def project_kernel(hp, nparts, chunk, place_ref, *refs):
    parts, (w_hbm, do_hbm, facts_hbm, q_hbm, adj_ref, msg_ref) = refs[:nparts], refs[nparts : nparts + 6]
    hbuf, wbuf, dobuf, facts_ref, qbuf, total, sems = refs[nparts + 6 :]
    rows, feat = parts[0].shape
    width = wbuf.shape[1]
    heads = width // HDIM
    copies = Copies(sems)
    loads = []
    for part, ref in enumerate(parts):
        for first in range(0, feat, chunk):
            here = pl.ds(part * feat + first, chunk)
            start = pl.multiple_of(place_ref[part] * feat + first, chunk)
            loads.append(
                (
                    slice(part * feat + first, part * feat + first + chunk),
                    copies.start(ref.at[:, pl.ds(first, chunk)], hbuf.at[:, here]),
                    copies.start(w_hbm.at[pl.ds(start, chunk), :], wbuf.at[here, :]),
                )
            )
    late = [copies.start(facts_hbm, facts_ref), copies.start(do_hbm, dobuf)]
    block = min(256, width)
    for order, (here, h_in, w_in) in enumerate(loads):
        h_in.wait()
        w_in.wait()
        for first in range(0, width, block):
            wide = slice(first, first + block)
            term = dot(hbuf[:, here], wbuf[here, wide], NN)
            if order == 0:
                total[:, wide] = term
            elif order < len(loads) - 1:
                total[:, wide] += term
            else:
                qbuf[:, wide] = (total[:, wide] + term).astype(BF16)
    for copy in late:
        copy.wait()
    copies.store(qbuf, q_hbm)
    table = turned(facts_ref[...])
    for h in range(heads):
        cols = slice(h * HDIM, (h + 1) * HDIM)
        decayed = (column(table, 3 * hp + h) * qbuf[:, cols].astype(F32)).astype(BF16)
        local = dot(decayed, dobuf[:, cols], TN)
        adj_ref[cols, :] = local
        msg_ref[cols, :] = local.astype(BF16)
    copies.finish()


def project(parts, owners, w_query, d_out, facts, hp):
    rows, feat = parts[0].shape
    depth, width = w_query.shape
    chunk = min(512, feat)
    return pl.pallas_call(
        functools.partial(project_kernel, hp, len(parts), chunk),
        in_specs=[SM] + [HB] * (len(parts) + 3),
        out_specs=(HB, VM, VM),
        out_shape=(
            jax.ShapeDtypeStruct((rows, width), BF16),
            jax.ShapeDtypeStruct((width, HDIM), F32),
            jax.ShapeDtypeStruct((width, HDIM), BF16),
        ),
        scratch_shapes=[
            pltpu.VMEM((rows, depth), BF16),
            pltpu.VMEM((depth, width), BF16),
            pltpu.VMEM((rows, width), BF16),
            pltpu.VMEM(facts.shape, F32),
            pltpu.VMEM((rows, width), BF16),
            pltpu.VMEM((rows, width), F32),
            pltpu.SemaphoreType.DMA((2 * len(parts) * (feat // chunk) + 3,)),
        ],
        compiler_params=params(28),
        cost_estimate=cost(2 * rows * width * depth, 2 * (depth * width + rows * depth)),
        name="project",
    )(owners, pinned(parts[0]), *parts[1:], pinned(w_query), d_out, facts)


def inner_kernel(first, last, hp, *refs):
    ins, facts_hbm, outs = refs[:4], refs[4], refs[5:8]
    bufs, facts_ref, sides, sems = refs[8:12], refs[12], refs[13:16], refs[16]
    rows = ins[0].shape[0]
    wide = pl.ds(first * HDIM, (last - first) * HDIM)
    copies = Copies(sems)
    facts_in = copies.start(facts_hbm, facts_ref)
    loads = [copies.start(src.at[:, wide], dst) for src, dst in zip(ins, bufs)]
    facts_in.wait()
    table = turned(facts_ref[...])
    row = lax.broadcasted_iota(jnp.int32, (rows, rows), 0)
    keep = row >= lax.broadcasted_iota(jnp.int32, (rows, rows), 1)
    shift = -0.5 * math.log2(HDIM)
    turn = math.log2(math.e)
    for copy in loads:
        copy.wait()
    q_ref, ks_ref, v_ref, do_ref = bufs
    for h in range(first, last):
        cols = slice((h - first) * HDIM, (h - first + 1) * HDIM)
        later = column(table, h) * turn + shift
        sooner = facts_ref[h : h + 1, :] * turn
        gap = jnp.concatenate([later] * (rows // LANES), axis=1) - sooner
        decays = jnp.exp2(jnp.where(keep, gap, -1e30))
        query, scaled, grad = q_ref[:, cols], ks_ref[:, cols], do_ref[:, cols]
        wdv = (decays * dot(grad, v_ref[:, cols], NT)).astype(BF16)
        wkq = (decays * dot(query, scaled, NT)).astype(BF16)
        sides[0][:, cols] = dot(wdv, scaled, NN)
        sides[1][:, cols] = dot(query, wdv, TN).T
        sides[2][:, cols] = dot(grad, wkq, TN).T
    for side, out in zip(sides, outs):
        copies.store(side, out)
    copies.finish()


def inner(first, last, query, scaled_keys, values, d_out, facts, hp):
    rows = query.shape[0]
    width = (last - first) * HDIM
    return pl.pallas_call(
        functools.partial(inner_kernel, first, last, hp),
        in_specs=[HB] * 5,
        out_specs=(HB,) * 3,
        out_shape=(jax.ShapeDtypeStruct((rows, width), F32),) * 3,
        scratch_shapes=[
            *[pltpu.VMEM((rows, width), BF16)] * 4,
            pltpu.VMEM(facts.shape, F32),
            *[pltpu.VMEM((rows, width), F32)] * 3,
            pltpu.SemaphoreType.DMA((8,)),
        ],
        compiler_params=params(24),
        cost_estimate=cost(10 * rows * rows * width, 20 * rows * width),
        name="inner",
    )(query, scaled_keys, values, d_out, facts)


def mix(coef_ref, pieces, heads, h):
    cols = slice(h * HDIM, (h + 1) * HDIM)
    total = None
    for stage, piece in enumerate(pieces):
        row = stage * heads + h
        term = coef_ref[row : row + 1, :] * piece[cols, :].astype(F32)
        total = term if total is None else total + term
    return total.astype(BF16)


def load_weight(copies, place_ref, first, w_hbm, wbuf, feat, block):
    loads = []
    for at in range(0, wbuf.shape[0], block):
        start = pl.multiple_of(place_ref[0] * feat + first + at, block)
        loads.append((at, copies.start(w_hbm.at[pl.ds(start, block), :], wbuf.at[pl.ds(at, block), :])))
    return loads


def query_kernel(heads, hp, stages, feat, block, place_ref, *refs):
    pieces = refs[:stages]
    coef_ref, do_hbm, facts_hbm, w_hbm = refs[stages : stages + 4]
    inner_hbm = refs[stages + 4 : -9]
    dq_hbm, out_hbm, dobuf, facts_ref, wbuf, local, held, sent, sems = refs[-9:]
    copies = Copies(sems)
    each = heads // len(inner_hbm)
    facts_in = copies.start(facts_hbm, facts_ref)
    loads = []
    for part, src in enumerate(inner_hbm):
        wide = pl.ds(part * each * HDIM, each * HDIM)
        loads.append(
            (copies.start(do_hbm.at[:, wide], dobuf.at[:, wide]), copies.start(src, local.at[:, wide]))
        )
    w_in = load_weight(copies, place_ref, 0, w_hbm, wbuf, feat, block)
    facts_in.wait()
    table = turned(facts_ref[...])
    for h in range(heads):
        if h % each == 0:
            for copy in loads[h // each]:
                copy.wait()
        cols = slice(h * HDIM, (h + 1) * HDIM)
        state = mix(coef_ref, pieces, heads, h)
        carry = dot(dobuf[:, cols], state, NT)
        held[:, cols] = (local[:, cols] + column(table, 3 * hp + h) * carry).astype(BF16)
    copies.store(held, dq_hbm)
    send_terms(copies, w_in, held, wbuf, sent, out_hbm, block)
    copies.finish()


def send_terms(copies, w_in, dq_ref, wbuf, sent, out_hbm, block):
    for at, copy in w_in:
        copy.wait()
        wide = slice(at, at + block)
        sent[:, wide] = dot(dq_ref[...], wbuf[wide, :], NT).astype(BF16)
        copies.store(sent.at[:, wide], out_hbm.at[:, wide])


def query_term(pieces, coefs, inner_dq, d_out, facts, w_query, place, feat, count, heads, hp):
    rows, width = d_out.shape
    block = min(512, count)
    args = (coefs, d_out, facts, w_query, *inner_dq)
    return pl.pallas_call(
        functools.partial(query_kernel, heads, hp, len(pieces), feat, block),
        in_specs=[SM] + [VM] * (len(pieces) + 1) + [HB] * (len(args) - 1),
        out_specs=(HB, HB),
        out_shape=(
            jax.ShapeDtypeStruct((rows, width), BF16),
            jax.ShapeDtypeStruct((rows, count), BF16),
        ),
        scratch_shapes=[
            pltpu.VMEM((rows, width), BF16),
            pltpu.VMEM(facts.shape, F32),
            pltpu.VMEM((count, width), BF16),
            pltpu.VMEM((rows, width), F32),
            pltpu.VMEM((rows, width), BF16),
            pltpu.VMEM((rows, count), BF16),
            pltpu.SemaphoreType.DMA((2 + 2 * len(inner_dq) + 2 * (count // block),)),
        ],
        compiler_params=params(20),
        cost_estimate=cost(2 * rows * width * count, 2 * (width + rows) * count + 10 * rows * width),
        name="query_term",
    )(place, *pieces, *args)


def term_kernel(feat, first, block, place_ref, dq_hbm, w_hbm, out_hbm, held, wbuf, sent, sems):
    copies = Copies(sems)
    dq_in = copies.start(dq_hbm, held)
    w_in = load_weight(copies, place_ref, first, w_hbm, wbuf, feat, block)
    dq_in.wait()
    send_terms(copies, w_in, held, wbuf, sent, out_hbm, block)
    copies.finish()


def plain_term(d_query, w_query, place, feat, first, count):
    rows, width = d_query.shape
    block = min(512, count)
    return pl.pallas_call(
        functools.partial(term_kernel, feat, first, block),
        in_specs=[SM, HB, HB],
        out_specs=HB,
        out_shape=jax.ShapeDtypeStruct((rows, count), BF16),
        scratch_shapes=[
            pltpu.VMEM((rows, width), BF16),
            pltpu.VMEM((count, width), BF16),
            pltpu.VMEM((rows, count), BF16),
            pltpu.SemaphoreType.DMA((1 + 2 * (count // block),)),
        ],
        compiler_params=params(16),
        cost_estimate=cost(2 * rows * width * count, 2 * (width + rows) * count),
        name="term",
    )(place, d_query, w_query)


def finish_kernel(count, block, place_ref, *refs):
    dq_hbm, w_hbm = refs[:2]
    arrived, (out_hbm, held, wbuf, extra, sent, sems) = refs[2:-6], refs[-6:]
    feat = sent.shape[1]
    copies = Copies(sems)
    dq_in = copies.start(dq_hbm, held)
    w_in = load_weight(copies, place_ref, 0, w_hbm, wbuf, feat, block)
    per = feat // count
    others = []
    for index, src in enumerate(arrived):
        shift, first = divmod(index, per)
        others.append(copies.start(src, extra.at[shift, :, pl.ds(first * count, count)]))
    dq_in.wait()
    for at, copy in w_in:
        copy.wait()
        wide = slice(at, at + block)
        total = dot(held[...], wbuf[wide, :], NT).astype(BF16).astype(F32)
        for index, other in enumerate(others):
            if at == index % per * count:
                other.wait()
        for shift in range(extra.shape[0]):
            total = total + extra[shift, :, wide].astype(F32)
        sent[:, wide] = total.astype(BF16)
        copies.store(sent.at[:, wide], out_hbm.at[:, wide])
    copies.finish()


def finish(d_query, w_query, place, arrived, feat):
    rows, width = d_query.shape
    count = arrived[0].shape[1]
    block = min(512, count)
    return pl.pallas_call(
        functools.partial(finish_kernel, count, block),
        in_specs=[SM] + [HB] * (2 + len(arrived)),
        out_specs=HB,
        out_shape=jax.ShapeDtypeStruct((rows, feat), BF16),
        scratch_shapes=[
            pltpu.VMEM((rows, width), BF16),
            pltpu.VMEM((feat, width), BF16),
            pltpu.VMEM((len(arrived) * count // feat, rows, feat), BF16),
            pltpu.VMEM((rows, feat), BF16),
            pltpu.SemaphoreType.DMA((1 + 2 * (feat // block) + len(arrived),)),
        ],
        compiler_params=params(24),
        cost_estimate=cost(2 * rows * width * feat, 2 * (width + 3 * rows) * feat),
        name="finish",
    )(place, d_query, w_query, *arrived)


def close_kernel(heads, hp, stages, *refs):
    pieces = refs[:stages]
    coef_ref, ks_hbm, v_hbm, facts_hbm = refs[stages : stages + 4]
    rest = refs[stages + 4 : -10]
    k_hbm, dv_hbm, ksbuf, vbuf, facts_ref, dkbuf, dvbuf, kside, vside, sems = refs[-10:]
    dks, dvs = rest[: len(rest) // 2], rest[len(rest) // 2 :]
    each = heads // len(dks)
    copies = Copies(sems)
    facts_in = copies.start(facts_hbm, facts_ref)
    loads = []
    for part, (dk, dv) in enumerate(zip(dks, dvs)):
        wide = pl.ds(part * each * HDIM, each * HDIM)
        loads.append(
            (
                copies.start(v_hbm.at[:, wide], vbuf.at[:, wide]),
                copies.start(dk, dkbuf.at[:, wide]),
                copies.start(ks_hbm.at[:, wide], ksbuf.at[:, wide]),
                copies.start(dv, dvbuf.at[:, wide]),
            )
        )
    facts_in.wait()
    table = turned(facts_ref[...])
    for h in range(heads):
        if h % each == 0:
            for copy in loads[h // each]:
                copy.wait()
        cols = slice(h * HDIM, (h + 1) * HDIM)
        adjoint = mix(coef_ref, pieces, heads, h)
        tail, gain = column(table, 2 * hp + h), column(table, hp + h)
        carry_k = dot(vbuf[:, cols], adjoint, NT)
        kside[:, cols] = (gain * (dkbuf[:, cols] + tail * carry_k)).astype(BF16)
        carry_v = dot(ksbuf[:, cols], adjoint, NN)
        vside[:, cols] = (dvbuf[:, cols] + tail * carry_v).astype(BF16)
        if (h + 1) % each == 0:
            wide = slice((h + 1 - each) * HDIM, (h + 1) * HDIM)
            copies.store(kside.at[:, wide], k_hbm.at[:, wide])
            copies.store(vside.at[:, wide], dv_hbm.at[:, wide])
    copies.finish()


def close(pieces, coefs, dks, dvs, scaled_keys, values, facts, heads, hp):
    rows, width = values.shape
    args = (coefs, scaled_keys, values, facts, *dks, *dvs)
    buf, wide = pltpu.VMEM((rows, width), BF16), pltpu.VMEM((rows, width), F32)
    return pl.pallas_call(
        functools.partial(close_kernel, heads, hp, len(pieces)),
        out_shape=(jax.ShapeDtypeStruct((rows, width), BF16),) * 2,
        in_specs=[VM] * (len(pieces) + 1) + [HB] * (len(args) - 1),
        out_specs=(HB,) * 2,
        scratch_shapes=[
            buf,
            buf,
            pltpu.VMEM(facts.shape, F32),
            wide,
            wide,
            buf,
            buf,
            pltpu.SemaphoreType.DMA((1 + 6 * len(dks),)),
        ],
        compiler_params=params(20),
        cost_estimate=cost(4 * rows * width * HDIM, 16 * rows * width),
        name="close",
    )(*pieces, *args)


def body(ctx_size, head_size, hidden, w_query, keys, values, d_out, log_decay):
    rows, feat = hidden.shape
    heads = log_decay.shape[1]
    width = w_query.shape[1]
    hp = sublanes(heads)
    scaling = HDIM ** (-0.5)
    me = lax.axis_index("ctx")
    mine = lax.axis_index("head")

    parts = [hidden]
    for shift in range(1, head_size):
        ring = [(i, (i + shift) % head_size) for i in range(head_size)]
        parts.append(lax.ppermute(hidden, "head", ring))
    owners = jnp.stack([(mine + head_size - s) % head_size for s in range(head_size)]).astype(jnp.int32)

    scaled_keys, facts, msg, state = prepare(log_decay.T, keys, values, heads, hp, scaling)
    query, adjoint, amsg = project(parts, owners, w_query, d_out, facts, hp)

    wide = lambda factor: factor[:heads, None, :]
    cube = lambda flat: flat.reshape(heads, HDIM, HDIM)
    split = lambda f: (f.astype(BF16), (f - f.astype(BF16).astype(F32)).astype(BF16))
    joined = lambda pair: pair[:hp].astype(F32) + pair[hp:].astype(F32)
    stages = (ctx_size - 1).bit_length()

    def send(array, stage, up):
        dist = 1 << stage
        if stage < stages - 1:
            pairs = [(i, i ^ dist) for i in range(ctx_size)]
        else:
            pairs = [(i, i + dist) if up else (i + dist, i) for i in range(ctx_size) if not i & dist]
        return lax.ppermute(array, "ctx", pairs)

    uppers = [(me & (1 << stage)) != 0 for stage in range(stages)]
    shares, others = [joined(msg[width:])], []
    got, agot = [], []
    before, after = [jnp.ones_like(shares[0])], [jnp.ones_like(shares[0])]

    def fold_state(stage, state):
        upper, arrived = uppers[stage], cube(got[stage][:width]).astype(F32)
        theirs = joined(got[stage][width:])
        others.append(theirs)
        own, other = jnp.where(upper, 1.0, theirs), jnp.where(upper, shares[stage], 1.0)
        state = (wide(own) * cube(state) + wide(other) * arrived).reshape(width, HDIM)
        shares.append(shares[stage] * theirs)
        before.append(jnp.where(upper, before[stage] * theirs, before[stage]))
        after.append(jnp.where(upper, after[stage], after[stage] * theirs))
        msg = state.astype(BF16)
        if stage + 2 < stages:
            msg = jnp.concatenate([msg, *split(shares[-1])], axis=0)
        return msg, state

    def fold_adjoint(stage, adjoint):
        upper, arrived = uppers[stage], cube(agot[stage]).astype(F32)
        own, other = jnp.where(upper, others[stage], 1.0), jnp.where(upper, 1.0, shares[stage])
        adjoint = (wide(own) * cube(adjoint) + wide(other) * arrived).reshape(width, HDIM)
        return adjoint.astype(BF16), adjoint

    half = max(1, heads // 2)
    pending = [(first, first + half) for first in range(0, heads, half)]
    inner_parts = []

    def next_inner():
        return inner(*pending.pop(0), query, scaled_keys, values, d_out, facts, hp)

    barrier = lax.optimization_barrier
    for stage in range(stages):
        arrived = send(msg if stage < stages - 1 else msg[:width], stage, True)
        if stage == 0:
            arrived, query, adjoint, amsg = barrier((arrived, query, adjoint, amsg))
        else:
            agot.append(send(amsg, stage - 1, False))
            if pending and (stage == 1 or stage == stages - 1):
                part = next_inner()
                arrived, *part = barrier((arrived, *part))
                inner_parts.append(part)
        got.append(arrived)
        if stage < stages - 1:
            msg, state = fold_state(stage, state)
        if stage >= 1:
            amsg, adjoint = fold_adjoint(stage - 1, adjoint)
    while pending:
        inner_parts.append(next_inner())
    agot.append(send(amsg, stages - 1, False))
    got[-1], _ = barrier((got[-1], amsg))

    state_coefs = [jnp.where(u, f, 0.0)[:heads] for u, f in zip(uppers, before)]
    adjoint_coefs = [jnp.where(u, 0.0, f)[:heads] for u, f in zip(uppers, after)]
    state_coefs = jnp.concatenate(state_coefs, axis=0)
    adjoint_coefs = jnp.concatenate(adjoint_coefs, axis=0)
    dqs, dks, dvs = zip(*inner_parts)

    place = lambda shift: ((mine + shift) % head_size).astype(jnp.int32).reshape(1)
    count = feat // 2 if feat >= 1024 else feat
    arrived = []
    for shift in range(1, head_size):
        ring = [(i, (i + shift) % head_size) for i in range(head_size)]
        for first in range(0, feat, count):
            if shift == 1 and first == 0:
                d_query, term = query_term(
                    got, state_coefs, dqs, d_out, facts, w_query, place(1), feat, count, heads, hp
                )
            else:
                term = plain_term(d_query, w_query, place(shift), feat, first, count)
            arrived.append(lax.ppermute(term, "head", ring))
    d_keys, d_values = close(agot, adjoint_coefs, dks, dvs, scaled_keys, values, facts, heads, hp)
    d_hidden = finish(d_query, w_query, place(0), arrived, feat)
    return (d_hidden, d_keys, d_values)


def solution(mesh):
    return jax.shard_map(
        functools.partial(body, mesh.shape["ctx"], mesh.shape["head"]),
        mesh=mesh,
        in_specs=(
            P("ctx", "head"),
            P(None, "head"),
            P("ctx", "head"),
            P("ctx", "head"),
            P("ctx", "head"),
            P("ctx", "head"),
        ),
        out_specs=(P("ctx", "head"), P("ctx", "head"), P("ctx", "head")),
        check_vma=False,
    )
```

```python
import functools
import math

import jax
import jax.numpy as jnp
from jax import lax
from jax.experimental import pallas as pl
from jax.experimental.pallas import tpu as pltpu
from jax.sharding import PartitionSpec as P

HDIM = 128
LANES = 128
F32, BF16 = jnp.float32, jnp.bfloat16
MIB = 1 << 20
VM = pl.BlockSpec(memory_space=pltpu.VMEM)
SM = pl.BlockSpec(memory_space=pltpu.SMEM)
HB = pl.BlockSpec(memory_space=pltpu.HBM)
AN = pl.BlockSpec(memory_space=pl.ANY)

NN = (((1,), (0,)), ((), ()))
NT = (((1,), (1,)), ((), ()))
TN = (((0,), (0,)), ((), ()))


def dot(a, b, dims):
    return lax.dot_general(a, b, dims, preferred_element_type=F32)


def kernel_call(kernel, args, specs, outs, out_specs, scratch, mib, name):
    pinned = [pltpu.with_memory_space_constraint(a, pltpu.HBM) if s is HB else a for a, s in zip(args, specs)]
    placed = tuple(
        (pltpu.HBM if s is HB else jax.ShapeDtypeStruct)(shape, dtype) for (shape, dtype), s in zip(outs, out_specs)
    )
    return pl.pallas_call(
        kernel,
        in_specs=specs,
        out_specs=tuple(out_specs),
        out_shape=placed,
        scratch_shapes=scratch,
        compiler_params=pltpu.CompilerParams(vmem_limit_bytes=mib * MIB),
        cost_estimate=pl.CostEstimate(flops=1, bytes_accessed=1, transcendentals=0),
        name=name,
    )(*pinned)


def sublanes(count):
    return -(-count // 8) * 8


def expm1_negative(z):
    series = jnp.full_like(z, 1.0)
    for order in range(10, 1, -1):
        series = 1.0 + z * series * (1.0 / order)
    return jnp.where(z > -0.5, z * series, jnp.exp(z) - 1.0)


def column(table, lane, width=LANES):
    return jnp.broadcast_to(table[:, lane : lane + 1], (table.shape[0], width))


class Copies:
    def __init__(self, sems):
        self.sems, self.count, self.out = sems, 0, []

    def start(self, src, dst):
        copy = pltpu.make_async_copy(src, dst, self.sems.at[self.count])
        self.count += 1
        copy.start()
        return copy

    def store(self, src, dst):
        self.out.append(self.start(src, dst))

    def finish(self):
        for copy in self.out:
            copy.wait()


def groups(heads):
    size = min(4, heads)
    return [(f, f + size, slice(f * HDIM, (f + size) * HDIM)) for f in range(0, heads, size)]


def turned(facts):
    spare = jnp.zeros((LANES - facts.shape[0], facts.shape[1]), F32)
    return jnp.concatenate([facts, spare], axis=0).T


def prepare_kernel(
    heads, hp, scaling, ld_hbm, k_hbm, v_hbm, ks_hbm, facts_hbm, msg_ref, state_ref, ld, facts_ref, kbuf, vbuf, ksbuf, sems
):
    rows = kbuf.shape[0]
    copies = Copies(sems)
    ld_in = copies.start(ld_hbm, ld)
    parts = [pl.ds(f, rows // 2) for f in (0, rows // 2)]
    k_in = [copies.start(k_hbm.at[p, :], kbuf.at[p, :]) for p in parts]
    v_in = [copies.start(v_hbm.at[p, :], vbuf.at[p, :]) for p in parts]
    ld_in.wait()
    logs = ld[...]
    if heads < hp:
        logs = jnp.concatenate([logs, jnp.zeros((hp - heads, rows), F32)], axis=0)
    lane = lax.broadcasted_iota(jnp.int32, logs.shape, 1)
    cumulative = logs
    step = 1
    while step < rows:
        moved = pltpu.roll(cumulative, step, 1)
        cumulative = cumulative + jnp.where(lane >= step, moved, 0.0)
        step *= 2
    total = cumulative[:, rows - 1 :]
    gain = jnp.sqrt(-expm1_negative(2.0 * logs))
    tail = jnp.exp(total - cumulative)
    lead = scaling * jnp.exp(cumulative)
    facts = jnp.concatenate([cumulative, gain, tail, lead], axis=0)
    facts_ref[...] = facts
    copies.store(facts_ref, facts_hbm)
    table = turned(facts)
    share = jnp.broadcast_to(jnp.exp(total), (hp, LANES))
    high = share.astype(BF16)
    low = (share - high.astype(F32)).astype(BF16)
    base = heads * HDIM
    msg_ref[base:, :] = jnp.concatenate([high.astype(F32), low.astype(F32)], axis=0).astype(BF16)
    for copy in k_in + v_in:
        copy.wait()
    for first, last, wide in groups(heads):
        for h in range(first, last):
            cols = slice(h * HDIM, (h + 1) * HDIM)
            scaled = (column(table, hp + h) * kbuf[:, cols].astype(F32)).astype(BF16)
            ksbuf[:, cols] = scaled
            decayed = (column(table, 2 * hp + h) * scaled.astype(F32)).astype(BF16)
            local = dot(decayed, vbuf[:, cols], TN)
            state_ref[cols, :] = local
            msg_ref[cols, :] = local.astype(BF16)
        copies.store(ksbuf.at[:, wide], ks_hbm.at[:, wide])
    copies.finish()


def prepare(logs, keys, values, heads, hp, scaling):
    rows, width = keys.shape
    buf = pltpu.VMEM((rows, width), BF16)
    return kernel_call(
        functools.partial(prepare_kernel, heads, hp, scaling),
        (logs, keys, values),
        [HB] * 3,
        [((rows, width), BF16), ((4 * hp, rows), F32), ((width + 2 * hp, HDIM), BF16), ((width, HDIM), F32)],
        (HB, HB, VM, VM),
        [
            pltpu.VMEM((heads, rows), F32),
            pltpu.VMEM((4 * hp, rows), F32),
            buf,
            buf,
            buf,
            pltpu.SemaphoreType.DMA((6 + len(groups(heads)),)),
        ],
        12,
        "prepare",
    )


def project_kernel(hp, nparts, chunk, place_ref, *refs):
    parts, (w_hbm, do_hbm, facts_hbm, q_hbm, adj_ref, msg_ref) = refs[:nparts], refs[nparts : nparts + 6]
    hbuf, wbuf, dobuf, facts_ref, qbuf, total, sems = refs[nparts + 6 :]
    rows, feat = parts[0].shape
    width = wbuf.shape[1]
    heads = width // HDIM
    copies = Copies(sems)
    loads = []
    for part, ref in enumerate(parts):
        for first in range(0, feat, chunk):
            here = pl.ds(part * feat + first, chunk)
            start = pl.multiple_of(place_ref[part] * feat + first, chunk)
            loads.append(
                (
                    slice(part * feat + first, part * feat + first + chunk),
                    copies.start(ref.at[:, pl.ds(first, chunk)], hbuf.at[:, here]),
                    copies.start(w_hbm.at[pl.ds(start, chunk), :], wbuf.at[here, :]),
                )
            )
    late = [copies.start(facts_hbm, facts_ref), copies.start(do_hbm, dobuf)]
    block = min(256, width)
    for order, (here, h_in, w_in) in enumerate(loads):
        h_in.wait()
        w_in.wait()
        for first in range(0, width, block):
            wide = slice(first, first + block)
            term = dot(hbuf[:, here], wbuf[here, wide], NN)
            if order == 0:
                total[:, wide] = term
            elif order < len(loads) - 1:
                total[:, wide] += term
            else:
                qbuf[:, wide] = (total[:, wide] + term).astype(BF16)
    for copy in late:
        copy.wait()
    copies.store(qbuf, q_hbm)
    table = turned(facts_ref[...])
    for h in range(heads):
        cols = slice(h * HDIM, (h + 1) * HDIM)
        decayed = (column(table, 3 * hp + h) * qbuf[:, cols].astype(F32)).astype(BF16)
        local = dot(decayed, dobuf[:, cols], TN)
        adj_ref[cols, :] = local
        msg_ref[cols, :] = local.astype(BF16)
    copies.finish()


def project(parts, owners, w_query, d_out, facts, hp):
    rows, feat = parts[0].shape
    depth, width = w_query.shape
    chunk = min(512, feat)
    return kernel_call(
        functools.partial(project_kernel, hp, len(parts), chunk),
        (owners, *parts, w_query, d_out, facts),
        [SM, HB] + [AN] * (len(parts) - 1) + [HB] * 3,
        [((rows, width), BF16), ((width, HDIM), F32), ((width, HDIM), BF16)],
        (HB, VM, VM),
        [
            pltpu.VMEM((rows, depth), BF16),
            pltpu.VMEM((depth, width), BF16),
            pltpu.VMEM((rows, width), BF16),
            pltpu.VMEM(facts.shape, F32),
            pltpu.VMEM((rows, width), BF16),
            pltpu.VMEM((rows, width), F32),
            pltpu.SemaphoreType.DMA((2 * len(parts) * (feat // chunk) + 3,)),
        ],
        28,
        "project",
    )


def inner_kernel(first, last, hp, *refs):
    ins, facts_hbm, outs = refs[:4], refs[4], refs[5:8]
    bufs, facts_ref, sides, sems = refs[8:12], refs[12], refs[13:16], refs[16]
    rows = ins[0].shape[0]
    wide = pl.ds(first * HDIM, (last - first) * HDIM)
    copies = Copies(sems)
    facts_in = copies.start(facts_hbm, facts_ref)
    loads = [copies.start(src.at[:, wide], dst) for src, dst in zip(ins, bufs)]
    facts_in.wait()
    table = turned(facts_ref[...])
    row = lax.broadcasted_iota(jnp.int32, (rows, rows), 0)
    keep = row >= lax.broadcasted_iota(jnp.int32, (rows, rows), 1)
    shift = -0.5 * math.log2(HDIM)
    turn = math.log2(math.e)
    for copy in loads:
        copy.wait()
    q_ref, ks_ref, v_ref, do_ref = bufs
    for h in range(first, last):
        cols = slice((h - first) * HDIM, (h - first + 1) * HDIM)
        later = column(table, h) * turn + shift
        sooner = facts_ref[h : h + 1, :] * turn
        gap = jnp.concatenate([later] * (rows // LANES), axis=1) - sooner
        decays = jnp.exp2(jnp.where(keep, gap, -1e30))
        query, scaled, grad = q_ref[:, cols], ks_ref[:, cols], do_ref[:, cols]
        wdv = (decays * dot(grad, v_ref[:, cols], NT)).astype(BF16)
        wkq = (decays * dot(query, scaled, NT)).astype(BF16)
        sides[0][:, cols] = dot(wdv, scaled, NN)
        sides[1][:, cols] = dot(query, wdv, TN).T
        sides[2][:, cols] = dot(grad, wkq, TN).T
    for side, out in zip(sides, outs):
        copies.store(side, out)
    copies.finish()


def inner(first, last, query, scaled_keys, values, d_out, facts, hp):
    rows = query.shape[0]
    width = (last - first) * HDIM
    return kernel_call(
        functools.partial(inner_kernel, first, last, hp),
        (query, scaled_keys, values, d_out, facts),
        [HB] * 5,
        [((rows, width), F32)] * 3,
        (HB,) * 3,
        [
            *[pltpu.VMEM((rows, width), BF16)] * 4,
            pltpu.VMEM(facts.shape, F32),
            *[pltpu.VMEM((rows, width), F32)] * 3,
            pltpu.SemaphoreType.DMA((8,)),
        ],
        24,
        "inner",
    )


def mix(coef_ref, pieces, heads, h):
    cols = slice(h * HDIM, (h + 1) * HDIM)
    total = None
    for stage, piece in enumerate(pieces):
        row = stage * heads + h
        term = coef_ref[row : row + 1, :] * piece[cols, :].astype(F32)
        total = term if total is None else total + term
    return total.astype(BF16)


def load_weight(copies, place_ref, first, w_hbm, wbuf, feat, block):
    loads = []
    for at in range(0, wbuf.shape[0], block):
        start = pl.multiple_of(place_ref[0] * feat + first + at, block)
        loads.append((at, copies.start(w_hbm.at[pl.ds(start, block), :], wbuf.at[pl.ds(at, block), :])))
    return loads


def query_kernel(heads, hp, stages, feat, block, place_ref, *refs):
    pieces = refs[:stages]
    coef_ref, do_hbm, facts_hbm, w_hbm = refs[stages : stages + 4]
    inner_hbm = refs[stages + 4 : -9]
    dq_hbm, out_hbm, dobuf, facts_ref, wbuf, local, held, sent, sems = refs[-9:]
    copies = Copies(sems)
    each = heads // len(inner_hbm)
    facts_in = copies.start(facts_hbm, facts_ref)
    loads = []
    for part, src in enumerate(inner_hbm):
        wide = pl.ds(part * each * HDIM, each * HDIM)
        loads.append(
            (copies.start(do_hbm.at[:, wide], dobuf.at[:, wide]), copies.start(src, local.at[:, wide]))
        )
    w_in = load_weight(copies, place_ref, 0, w_hbm, wbuf, feat, block)
    facts_in.wait()
    table = turned(facts_ref[...])
    for h in range(heads):
        if h % each == 0:
            for copy in loads[h // each]:
                copy.wait()
        cols = slice(h * HDIM, (h + 1) * HDIM)
        state = mix(coef_ref, pieces, heads, h)
        carry = dot(dobuf[:, cols], state, NT)
        held[:, cols] = (local[:, cols] + column(table, 3 * hp + h) * carry).astype(BF16)
    copies.store(held, dq_hbm)
    send_terms(copies, w_in, held, wbuf, sent, out_hbm, block)
    copies.finish()


def send_terms(copies, w_in, dq_ref, wbuf, sent, out_hbm, block):
    for at, copy in w_in:
        copy.wait()
        wide = slice(at, at + block)
        sent[:, wide] = dot(dq_ref[...], wbuf[wide, :], NT).astype(BF16)
        copies.store(sent.at[:, wide], out_hbm.at[:, wide])


def query_term(pieces, coefs, inner_dq, d_out, facts, w_query, place, feat, count, heads, hp):
    rows, width = d_out.shape
    block = min(512, count)
    args = (coefs, d_out, facts, w_query, *inner_dq)
    return kernel_call(
        functools.partial(query_kernel, heads, hp, len(pieces), feat, block),
        (place, *pieces, *args),
        [SM] + [VM] * (len(pieces) + 1) + [HB] * (len(args) - 1),
        [((rows, width), BF16), ((rows, count), BF16)],
        (HB, HB),
        [
            pltpu.VMEM((rows, width), BF16),
            pltpu.VMEM(facts.shape, F32),
            pltpu.VMEM((count, width), BF16),
            pltpu.VMEM((rows, width), F32),
            pltpu.VMEM((rows, width), BF16),
            pltpu.VMEM((rows, count), BF16),
            pltpu.SemaphoreType.DMA((2 + 2 * len(inner_dq) + 2 * (count // block),)),
        ],
        20,
        "query_term",
    )


def term_kernel(feat, first, block, place_ref, dq_hbm, w_hbm, out_hbm, held, wbuf, sent, sems):
    copies = Copies(sems)
    dq_in = copies.start(dq_hbm, held)
    w_in = load_weight(copies, place_ref, first, w_hbm, wbuf, feat, block)
    dq_in.wait()
    send_terms(copies, w_in, held, wbuf, sent, out_hbm, block)
    copies.finish()


def plain_term(d_query, w_query, place, feat, first, count):
    rows, width = d_query.shape
    block = min(512, count)
    return kernel_call(
        functools.partial(term_kernel, feat, first, block),
        (place, d_query, w_query),
        [SM, HB, HB],
        [((rows, count), BF16)],
        (HB,),
        [
            pltpu.VMEM((rows, width), BF16),
            pltpu.VMEM((count, width), BF16),
            pltpu.VMEM((rows, count), BF16),
            pltpu.SemaphoreType.DMA((1 + 2 * (count // block),)),
        ],
        16,
        "term",
    )[0]


def finish_kernel(count, block, place_ref, *refs):
    dq_hbm, w_hbm = refs[:2]
    arrived, (out_hbm, held, wbuf, extra, sent, sems) = refs[2:-6], refs[-6:]
    feat = sent.shape[1]
    copies = Copies(sems)
    dq_in = copies.start(dq_hbm, held)
    w_in = load_weight(copies, place_ref, 0, w_hbm, wbuf, feat, block)
    per = feat // count
    others = []
    for index, src in enumerate(arrived):
        shift, first = divmod(index, per)
        others.append(copies.start(src, extra.at[shift, :, pl.ds(first * count, count)]))
    dq_in.wait()
    for at, copy in w_in:
        copy.wait()
        wide = slice(at, at + block)
        total = dot(held[...], wbuf[wide, :], NT).astype(BF16).astype(F32)
        for index, other in enumerate(others):
            if at == index % per * count:
                other.wait()
        for shift in range(extra.shape[0]):
            total = total + extra[shift, :, wide].astype(F32)
        sent[:, wide] = total.astype(BF16)
        copies.store(sent.at[:, wide], out_hbm.at[:, wide])
    copies.finish()


def finish(d_query, w_query, place, arrived, feat):
    rows, width = d_query.shape
    count = arrived[0].shape[1]
    block = min(512, count)
    return kernel_call(
        functools.partial(finish_kernel, count, block),
        (place, d_query, w_query, *arrived),
        [SM, HB, HB] + [AN] * len(arrived),
        [((rows, feat), BF16)],
        (HB,),
        [
            pltpu.VMEM((rows, width), BF16),
            pltpu.VMEM((feat, width), BF16),
            pltpu.VMEM((len(arrived) * count // feat, rows, feat), BF16),
            pltpu.VMEM((rows, feat), BF16),
            pltpu.SemaphoreType.DMA((1 + 2 * (feat // block) + len(arrived),)),
        ],
        24,
        "finish",
    )[0]


def close_kernel(heads, hp, stages, *refs):
    pieces = refs[:stages]
    coef_ref, ks_hbm, v_hbm, facts_hbm = refs[stages : stages + 4]
    rest = refs[stages + 4 : -10]
    k_hbm, dv_hbm, ksbuf, vbuf, facts_ref, dkbuf, dvbuf, kside, vside, sems = refs[-10:]
    dks, dvs = rest[: len(rest) // 2], rest[len(rest) // 2 :]
    each = heads // len(dks)
    copies = Copies(sems)
    facts_in = copies.start(facts_hbm, facts_ref)
    loads = []
    for part, (dk, dv) in enumerate(zip(dks, dvs)):
        wide = pl.ds(part * each * HDIM, each * HDIM)
        loads.append(
            (
                copies.start(v_hbm.at[:, wide], vbuf.at[:, wide]),
                copies.start(dk, dkbuf.at[:, wide]),
                copies.start(ks_hbm.at[:, wide], ksbuf.at[:, wide]),
                copies.start(dv, dvbuf.at[:, wide]),
            )
        )
    facts_in.wait()
    table = turned(facts_ref[...])
    for h in range(heads):
        if h % each == 0:
            for copy in loads[h // each]:
                copy.wait()
        cols = slice(h * HDIM, (h + 1) * HDIM)
        adjoint = mix(coef_ref, pieces, heads, h)
        tail, gain = column(table, 2 * hp + h), column(table, hp + h)
        carry_k = dot(vbuf[:, cols], adjoint, NT)
        kside[:, cols] = (gain * (dkbuf[:, cols] + tail * carry_k)).astype(BF16)
        carry_v = dot(ksbuf[:, cols], adjoint, NN)
        vside[:, cols] = (dvbuf[:, cols] + tail * carry_v).astype(BF16)
        if (h + 1) % each == 0:
            wide = slice((h + 1 - each) * HDIM, (h + 1) * HDIM)
            copies.store(kside.at[:, wide], k_hbm.at[:, wide])
            copies.store(vside.at[:, wide], dv_hbm.at[:, wide])
    copies.finish()


def close(pieces, coefs, dks, dvs, scaled_keys, values, facts, heads, hp):
    rows, width = values.shape
    args = (coefs, scaled_keys, values, facts, *dks, *dvs)
    buf, wide = pltpu.VMEM((rows, width), BF16), pltpu.VMEM((rows, width), F32)
    return kernel_call(
        functools.partial(close_kernel, heads, hp, len(pieces)),
        (*pieces, *args),
        [VM] * (len(pieces) + 1) + [HB] * (len(args) - 1),
        [((rows, width), BF16)] * 2,
        (HB,) * 2,
        [
            buf,
            buf,
            pltpu.VMEM(facts.shape, F32),
            wide,
            wide,
            buf,
            buf,
            pltpu.SemaphoreType.DMA((1 + 6 * len(dks),)),
        ],
        20,
        "close",
    )


def body(ctx_size, head_size, hidden, w_query, keys, values, d_out, log_decay):
    rows, feat = hidden.shape
    heads = log_decay.shape[1]
    width = w_query.shape[1]
    hp = sublanes(heads)
    scaling = HDIM ** (-0.5)
    me = lax.axis_index("ctx")
    mine = lax.axis_index("head")

    parts = [hidden]
    for shift in range(1, head_size):
        ring = [(i, (i + shift) % head_size) for i in range(head_size)]
        parts.append(lax.ppermute(hidden, "head", ring))
    owners = jnp.stack([(mine + head_size - s) % head_size for s in range(head_size)]).astype(jnp.int32)

    scaled_keys, facts, msg, state = prepare(log_decay.T, keys, values, heads, hp, scaling)
    query, adjoint, amsg = project(parts, owners, w_query, d_out, facts, hp)

    wide = lambda factor: factor[:heads, None, :]
    cube = lambda flat: flat.reshape(heads, HDIM, HDIM)
    split = lambda f: (f.astype(BF16), (f - f.astype(BF16).astype(F32)).astype(BF16))
    joined = lambda pair: pair[:hp].astype(F32) + pair[hp:].astype(F32)
    stages = (ctx_size - 1).bit_length()

    def send(array, stage, up):
        dist = 1 << stage
        if stage < stages - 1:
            pairs = [(i, i ^ dist) for i in range(ctx_size)]
        else:
            pairs = [(i, i + dist) if up else (i + dist, i) for i in range(ctx_size) if not i & dist]
        return lax.ppermute(array, "ctx", pairs)

    uppers = [(me & (1 << stage)) != 0 for stage in range(stages)]
    shares, others = [joined(msg[width:])], []
    got, agot = [], []
    before, after = [jnp.ones_like(shares[0])], [jnp.ones_like(shares[0])]

    def fold_state(stage, state):
        upper, arrived = uppers[stage], cube(got[stage][:width]).astype(F32)
        theirs = joined(got[stage][width:])
        others.append(theirs)
        own, other = jnp.where(upper, 1.0, theirs), jnp.where(upper, shares[stage], 1.0)
        state = (wide(own) * cube(state) + wide(other) * arrived).reshape(width, HDIM)
        shares.append(shares[stage] * theirs)
        before.append(jnp.where(upper, before[stage] * theirs, before[stage]))
        after.append(jnp.where(upper, after[stage], after[stage] * theirs))
        msg = state.astype(BF16)
        if stage + 2 < stages:
            msg = jnp.concatenate([msg, *split(shares[-1])], axis=0)
        return msg, state

    def fold_adjoint(stage, adjoint):
        upper, arrived = uppers[stage], cube(agot[stage]).astype(F32)
        own, other = jnp.where(upper, others[stage], 1.0), jnp.where(upper, 1.0, shares[stage])
        adjoint = (wide(own) * cube(adjoint) + wide(other) * arrived).reshape(width, HDIM)
        return adjoint.astype(BF16), adjoint

    half = max(1, heads // 2)
    pending = [(first, first + half) for first in range(0, heads, half)]
    inner_parts = []

    def next_inner():
        return inner(*pending.pop(0), query, scaled_keys, values, d_out, facts, hp)

    barrier = lax.optimization_barrier
    for stage in range(stages):
        arrived = send(msg if stage < stages - 1 else msg[:width], stage, True)
        if stage == 0:
            arrived, query, adjoint, amsg = barrier((arrived, query, adjoint, amsg))
        else:
            agot.append(send(amsg, stage - 1, False))
            if pending and (stage == 1 or stage == stages - 1):
                part = next_inner()
                arrived, *part = barrier((arrived, *part))
                inner_parts.append(part)
        got.append(arrived)
        if stage < stages - 1:
            msg, state = fold_state(stage, state)
        if stage >= 1:
            amsg, adjoint = fold_adjoint(stage - 1, adjoint)
    while pending:
        inner_parts.append(next_inner())
    agot.append(send(amsg, stages - 1, False))
    got[-1], _ = barrier((got[-1], amsg))

    state_coefs = [jnp.where(u, f, 0.0)[:heads] for u, f in zip(uppers, before)]
    adjoint_coefs = [jnp.where(u, 0.0, f)[:heads] for u, f in zip(uppers, after)]
    state_coefs = jnp.concatenate(state_coefs, axis=0)
    adjoint_coefs = jnp.concatenate(adjoint_coefs, axis=0)
    dqs, dks, dvs = zip(*inner_parts)

    place = lambda shift: ((mine + shift) % head_size).astype(jnp.int32).reshape(1)
    count = feat // 2 if feat >= 1024 else feat
    arrived = []
    for shift in range(1, head_size):
        ring = [(i, (i + shift) % head_size) for i in range(head_size)]
        for first in range(0, feat, count):
            if shift == 1 and first == 0:
                d_query, term = query_term(
                    got, state_coefs, dqs, d_out, facts, w_query, place(1), feat, count, heads, hp
                )
            else:
                term = plain_term(d_query, w_query, place(shift), feat, first, count)
            arrived.append(lax.ppermute(term, "head", ring))
    d_keys, d_values = close(agot, adjoint_coefs, dks, dvs, scaled_keys, values, facts, heads, hp)
    d_hidden = finish(d_query, w_query, place(0), arrived, feat)
    return (d_hidden, d_keys, d_values)


def solution(mesh):
    return jax.shard_map(
        functools.partial(body, mesh.shape["ctx"], mesh.shape["head"]),
        mesh=mesh,
        in_specs=(
            P("ctx", "head"),
            P(None, "head"),
            P("ctx", "head"),
            P("ctx", "head"),
            P("ctx", "head"),
            P("ctx", "head"),
        ),
        out_specs=(P("ctx", "head"), P("ctx", "head"), P("ctx", "head")),
        check_vma=False,
    )
```

```python
import functools
import math

import jax
import jax.numpy as jnp
from jax import lax
from jax.experimental import pallas as pl
from jax.experimental.pallas import tpu as pltpu
from jax.sharding import PartitionSpec as P

HDIM = 128
LANES = 128
F32, BF16 = jnp.float32, jnp.bfloat16
MIB = 1 << 20
VM = pl.BlockSpec(memory_space=pltpu.VMEM)
SM = pl.BlockSpec(memory_space=pltpu.SMEM)
HB = pl.BlockSpec(memory_space=pltpu.HBM)
AN = pl.BlockSpec(memory_space=pl.ANY)

NN = (((1,), (0,)), ((), ()))
NT = (((1,), (1,)), ((), ()))
TN = (((0,), (0,)), ((), ()))


def dot(a, b, dims):
    return lax.dot_general(a, b, dims, preferred_element_type=F32)


def kernel_call(kernel, args, specs, outs, out_specs, scratch, mib, name, flops=1):
    pinned = [pltpu.with_memory_space_constraint(a, pltpu.HBM) if s is HB else a for a, s in zip(args, specs)]
    placed = tuple(
        (pltpu.HBM if s is HB else jax.ShapeDtypeStruct)(shape, dtype) for (shape, dtype), s in zip(outs, out_specs)
    )
    return pl.pallas_call(
        kernel,
        in_specs=specs,
        out_specs=tuple(out_specs),
        out_shape=placed,
        scratch_shapes=scratch,
        compiler_params=pltpu.CompilerParams(vmem_limit_bytes=mib * MIB),
        cost_estimate=pl.CostEstimate(flops=flops, bytes_accessed=1, transcendentals=0),
        name=name,
    )(*pinned)


def sublanes(count):
    return -(-count // 8) * 8


def expm1_negative(z):
    series = jnp.full_like(z, 1.0)
    for order in range(10, 1, -1):
        series = 1.0 + z * series * (1.0 / order)
    return jnp.where(z > -0.5, z * series, jnp.exp(z) - 1.0)


def column(table, lane, width=LANES):
    return jnp.broadcast_to(table[:, lane : lane + 1], (table.shape[0], width))


class Copies:
    def __init__(self, sems):
        self.sems, self.count, self.out = sems, 0, []

    def start(self, src, dst):
        copy = pltpu.make_async_copy(src, dst, self.sems.at[self.count])
        self.count += 1
        copy.start()
        return copy

    def store(self, src, dst):
        self.out.append(self.start(src, dst))

    def finish(self):
        for copy in self.out:
            copy.wait()


def groups(heads):
    size = min(4, heads)
    return [(f, f + size, slice(f * HDIM, (f + size) * HDIM)) for f in range(0, heads, size)]


def turned(facts):
    spare = jnp.zeros((LANES - facts.shape[0], facts.shape[1]), F32)
    return jnp.concatenate([facts, spare], axis=0).T


def prepare_kernel(
    heads, hp, scaling, ld_hbm, k_hbm, v_hbm, ks_hbm, facts_hbm, msg_ref, state_ref, ld, facts_ref, kbuf, vbuf, ksbuf, sems
):
    rows = kbuf.shape[0]
    copies = Copies(sems)
    ld_in = copies.start(ld_hbm, ld)
    parts = [pl.ds(f, rows // 2) for f in (0, rows // 2)]
    k_in = [copies.start(k_hbm.at[p, :], kbuf.at[p, :]) for p in parts]
    v_in = [copies.start(v_hbm.at[p, :], vbuf.at[p, :]) for p in parts]
    ld_in.wait()
    logs = ld[...]
    if heads < hp:
        logs = jnp.concatenate([logs, jnp.zeros((hp - heads, rows), F32)], axis=0)
    lane = lax.broadcasted_iota(jnp.int32, logs.shape, 1)
    cumulative = logs
    step = 1
    while step < rows:
        moved = pltpu.roll(cumulative, step, 1)
        cumulative = cumulative + jnp.where(lane >= step, moved, 0.0)
        step *= 2
    total = cumulative[:, rows - 1 :]
    gain = jnp.sqrt(-expm1_negative(2.0 * logs))
    tail = jnp.exp(total - cumulative)
    lead = scaling * jnp.exp(cumulative)
    facts = jnp.concatenate([cumulative, gain, tail, lead], axis=0)
    facts_ref[...] = facts
    copies.store(facts_ref, facts_hbm)
    table = turned(facts)
    share = jnp.broadcast_to(jnp.exp(total), (hp, LANES))
    high = share.astype(BF16)
    low = (share - high.astype(F32)).astype(BF16)
    base = heads * HDIM
    msg_ref[base:, :] = jnp.concatenate([high.astype(F32), low.astype(F32)], axis=0).astype(BF16)
    for copy in k_in + v_in:
        copy.wait()
    for first, last, wide in groups(heads):
        for h in range(first, last):
            cols = slice(h * HDIM, (h + 1) * HDIM)
            scaled = (column(table, hp + h) * kbuf[:, cols].astype(F32)).astype(BF16)
            ksbuf[:, cols] = scaled
            decayed = (column(table, 2 * hp + h) * scaled.astype(F32)).astype(BF16)
            local = dot(decayed, vbuf[:, cols], TN)
            state_ref[cols, :] = local
            msg_ref[cols, :] = local.astype(BF16)
        copies.store(ksbuf.at[:, wide], ks_hbm.at[:, wide])
    copies.finish()


def prepare(logs, keys, values, heads, hp, scaling):
    rows, width = keys.shape
    buf = pltpu.VMEM((rows, width), BF16)
    return kernel_call(
        functools.partial(prepare_kernel, heads, hp, scaling),
        (logs, keys, values),
        [HB] * 3,
        [((rows, width), BF16), ((4 * hp, rows), F32), ((width + 2 * hp, HDIM), BF16), ((width, HDIM), F32)],
        (HB, HB, VM, VM),
        [
            pltpu.VMEM((heads, rows), F32),
            pltpu.VMEM((4 * hp, rows), F32),
            buf,
            buf,
            buf,
            pltpu.SemaphoreType.DMA((6 + len(groups(heads)),)),
        ],
        12,
        "prepare",
    )


def project_kernel(hp, nparts, chunk, place_ref, *refs):
    parts, (w_hbm, do_hbm, facts_hbm, q_hbm, adj_ref, msg_ref) = refs[:nparts], refs[nparts : nparts + 6]
    hbuf, wbuf, dobuf, facts_ref, qbuf, total, sems = refs[nparts + 6 :]
    rows, feat = parts[0].shape
    width = wbuf.shape[1]
    heads = width // HDIM
    copies = Copies(sems)
    loads = []
    for part, ref in enumerate(parts):
        for first in range(0, feat, chunk):
            here = pl.ds(part * feat + first, chunk)
            start = pl.multiple_of(place_ref[part] * feat + first, chunk)
            loads.append(
                (
                    slice(part * feat + first, part * feat + first + chunk),
                    copies.start(ref.at[:, pl.ds(first, chunk)], hbuf.at[:, here]),
                    copies.start(w_hbm.at[pl.ds(start, chunk), :], wbuf.at[here, :]),
                )
            )
    late = [copies.start(facts_hbm, facts_ref), copies.start(do_hbm, dobuf)]
    block = min(256, width)
    for order, (here, h_in, w_in) in enumerate(loads):
        h_in.wait()
        w_in.wait()
        for first in range(0, width, block):
            wide = slice(first, first + block)
            term = dot(hbuf[:, here], wbuf[here, wide], NN)
            if order == 0:
                total[:, wide] = term
            elif order < len(loads) - 1:
                total[:, wide] += term
            else:
                qbuf[:, wide] = (total[:, wide] + term).astype(BF16)
    for copy in late:
        copy.wait()
    copies.store(qbuf, q_hbm)
    table = turned(facts_ref[...])
    for h in range(heads):
        cols = slice(h * HDIM, (h + 1) * HDIM)
        decayed = (column(table, 3 * hp + h) * qbuf[:, cols].astype(F32)).astype(BF16)
        local = dot(decayed, dobuf[:, cols], TN)
        adj_ref[cols, :] = local
        msg_ref[cols, :] = local.astype(BF16)
    copies.finish()


def project(parts, owners, w_query, d_out, facts, hp):
    rows, feat = parts[0].shape
    depth, width = w_query.shape
    chunk = min(512, feat)
    return kernel_call(
        functools.partial(project_kernel, hp, len(parts), chunk),
        (owners, *parts, w_query, d_out, facts),
        [SM, HB] + [AN] * (len(parts) - 1) + [HB] * 3,
        [((rows, width), BF16), ((width, HDIM), F32), ((width, HDIM), BF16)],
        (HB, VM, VM),
        [
            pltpu.VMEM((rows, depth), BF16),
            pltpu.VMEM((depth, width), BF16),
            pltpu.VMEM((rows, width), BF16),
            pltpu.VMEM(facts.shape, F32),
            pltpu.VMEM((rows, width), BF16),
            pltpu.VMEM((rows, width), F32),
            pltpu.SemaphoreType.DMA((2 * len(parts) * (feat // chunk) + 3,)),
        ],
        28,
        "project",
    )


def inner_kernel(first, last, hp, *refs):
    ins, facts_hbm, outs = refs[:4], refs[4], refs[5:8]
    bufs, facts_ref, sides, sems = refs[8:12], refs[12], refs[13:16], refs[16]
    rows = ins[0].shape[0]
    wide = pl.ds(first * HDIM, (last - first) * HDIM)
    copies = Copies(sems)
    facts_in = copies.start(facts_hbm, facts_ref)
    loads = [copies.start(src.at[:, wide], dst) for src, dst in zip(ins, bufs)]
    facts_in.wait()
    table = turned(facts_ref[...])
    row = lax.broadcasted_iota(jnp.int32, (rows, rows), 0)
    keep = row >= lax.broadcasted_iota(jnp.int32, (rows, rows), 1)
    shift = -0.5 * math.log2(HDIM)
    turn = math.log2(math.e)
    for copy in loads:
        copy.wait()
    q_ref, ks_ref, v_ref, do_ref = bufs
    for h in range(first, last):
        cols = slice((h - first) * HDIM, (h - first + 1) * HDIM)
        later = column(table, h) * turn + shift
        sooner = facts_ref[h : h + 1, :] * turn
        gap = jnp.concatenate([later] * (rows // LANES), axis=1) - sooner
        decays = jnp.exp2(jnp.where(keep, gap, -1e30))
        query, scaled, grad = q_ref[:, cols], ks_ref[:, cols], do_ref[:, cols]
        wdv = (decays * dot(grad, v_ref[:, cols], NT)).astype(BF16)
        wkq = (decays * dot(query, scaled, NT)).astype(BF16)
        sides[0][:, cols] = dot(wdv, scaled, NN)
        sides[1][:, cols] = dot(query, wdv, TN).T
        sides[2][:, cols] = dot(grad, wkq, TN).T
    for side, out in zip(sides, outs):
        copies.store(side, out)
    copies.finish()


def inner(first, last, query, scaled_keys, values, d_out, facts, hp):
    rows = query.shape[0]
    width = (last - first) * HDIM
    return kernel_call(
        functools.partial(inner_kernel, first, last, hp),
        (query, scaled_keys, values, d_out, facts),
        [HB] * 5,
        [((rows, width), F32)] * 3,
        (HB,) * 3,
        [
            *[pltpu.VMEM((rows, width), BF16)] * 4,
            pltpu.VMEM(facts.shape, F32),
            *[pltpu.VMEM((rows, width), F32)] * 3,
            pltpu.SemaphoreType.DMA((8,)),
        ],
        24,
        "inner",
    )


def mix(coef_ref, pieces, heads, h):
    cols = slice(h * HDIM, (h + 1) * HDIM)
    total = None
    for stage, piece in enumerate(pieces):
        row = stage * heads + h
        term = coef_ref[row : row + 1, :] * piece[cols, :].astype(F32)
        total = term if total is None else total + term
    return total.astype(BF16)


def load_weight(copies, place_ref, first, w_hbm, wbuf, feat, block):
    loads = []
    for at in range(0, wbuf.shape[0], block):
        start = pl.multiple_of(place_ref[0] * feat + first + at, block)
        loads.append((at, copies.start(w_hbm.at[pl.ds(start, block), :], wbuf.at[pl.ds(at, block), :])))
    return loads


def query_kernel(heads, hp, stages, feat, block, place_ref, *refs):
    pieces = refs[:stages]
    coef_ref, do_hbm, facts_hbm, w_hbm = refs[stages : stages + 4]
    inner_hbm = refs[stages + 4 : -9]
    dq_hbm, out_hbm, dobuf, facts_ref, wbuf, local, held, sent, sems = refs[-9:]
    copies = Copies(sems)
    each = heads // len(inner_hbm)
    facts_in = copies.start(facts_hbm, facts_ref)
    loads = []
    for part, src in enumerate(inner_hbm):
        wide = pl.ds(part * each * HDIM, each * HDIM)
        loads.append(
            (copies.start(do_hbm.at[:, wide], dobuf.at[:, wide]), copies.start(src, local.at[:, wide]))
        )
    w_in = load_weight(copies, place_ref, 0, w_hbm, wbuf, feat, block)
    facts_in.wait()
    table = turned(facts_ref[...])
    for h in range(heads):
        if h % each == 0:
            for copy in loads[h // each]:
                copy.wait()
        cols = slice(h * HDIM, (h + 1) * HDIM)
        state = mix(coef_ref, pieces, heads, h)
        carry = dot(dobuf[:, cols], state, NT)
        held[:, cols] = (local[:, cols] + column(table, 3 * hp + h) * carry).astype(BF16)
    copies.store(held, dq_hbm)
    send_terms(copies, w_in, held, wbuf, sent, out_hbm, block)
    copies.finish()


def send_terms(copies, w_in, dq_ref, wbuf, sent, out_hbm, block):
    for at, copy in w_in:
        copy.wait()
        wide = slice(at, at + block)
        sent[:, wide] = dot(dq_ref[...], wbuf[wide, :], NT).astype(BF16)
        copies.store(sent.at[:, wide], out_hbm.at[:, wide])


def query_term(pieces, coefs, inner_dq, d_out, facts, w_query, place, feat, count, heads, hp):
    rows, width = d_out.shape
    block = min(512, count)
    args = (coefs, d_out, facts, w_query, *inner_dq)
    return kernel_call(
        functools.partial(query_kernel, heads, hp, len(pieces), feat, block),
        (place, *pieces, *args),
        [SM] + [VM] * (len(pieces) + 1) + [HB] * (len(args) - 1),
        [((rows, width), BF16), ((rows, count), BF16)],
        (HB, HB),
        [
            pltpu.VMEM((rows, width), BF16),
            pltpu.VMEM(facts.shape, F32),
            pltpu.VMEM((count, width), BF16),
            pltpu.VMEM((rows, width), F32),
            pltpu.VMEM((rows, width), BF16),
            pltpu.VMEM((rows, count), BF16),
            pltpu.SemaphoreType.DMA((2 + 2 * len(inner_dq) + 2 * (count // block),)),
        ],
        20,
        "query_term",
    )


def term_kernel(feat, first, block, place_ref, dq_hbm, w_hbm, out_hbm, held, wbuf, sent, sems):
    copies = Copies(sems)
    dq_in = copies.start(dq_hbm, held)
    w_in = load_weight(copies, place_ref, first, w_hbm, wbuf, feat, block)
    dq_in.wait()
    send_terms(copies, w_in, held, wbuf, sent, out_hbm, block)
    copies.finish()


def plain_term(d_query, w_query, place, feat, first, count):
    rows, width = d_query.shape
    block = min(512, count)
    return kernel_call(
        functools.partial(term_kernel, feat, first, block),
        (place, d_query, w_query),
        [SM, HB, HB],
        [((rows, count), BF16)],
        (HB,),
        [
            pltpu.VMEM((rows, width), BF16),
            pltpu.VMEM((count, width), BF16),
            pltpu.VMEM((rows, count), BF16),
            pltpu.SemaphoreType.DMA((1 + 2 * (count // block),)),
        ],
        16,
        "term",
    )[0]


def finish_kernel(count, block, place_ref, *refs):
    dq_hbm, w_hbm = refs[:2]
    arrived, (out_hbm, held, wbuf, extra, sent, sems) = refs[2:-6], refs[-6:]
    feat = sent.shape[1]
    copies = Copies(sems)
    dq_in = copies.start(dq_hbm, held)
    w_in = load_weight(copies, place_ref, 0, w_hbm, wbuf, feat, block)
    per = feat // count
    others = []
    for index, src in enumerate(arrived):
        shift, first = divmod(index, per)
        others.append(copies.start(src, extra.at[shift, :, pl.ds(first * count, count)]))
    dq_in.wait()
    for at, copy in w_in:
        copy.wait()
        wide = slice(at, at + block)
        total = dot(held[...], wbuf[wide, :], NT).astype(BF16).astype(F32)
        for index, other in enumerate(others):
            if at == index % per * count:
                other.wait()
        for shift in range(extra.shape[0]):
            total = total + extra[shift, :, wide].astype(F32)
        sent[:, wide] = total.astype(BF16)
        copies.store(sent.at[:, wide], out_hbm.at[:, wide])
    copies.finish()


def finish(d_query, w_query, place, arrived, feat):
    rows, width = d_query.shape
    count = arrived[0].shape[1]
    block = min(512, count)
    return kernel_call(
        functools.partial(finish_kernel, count, block),
        (place, d_query, w_query, *arrived),
        [SM, HB, HB] + [AN] * len(arrived),
        [((rows, feat), BF16)],
        (HB,),
        [
            pltpu.VMEM((rows, width), BF16),
            pltpu.VMEM((feat, width), BF16),
            pltpu.VMEM((len(arrived) * count // feat, rows, feat), BF16),
            pltpu.VMEM((rows, feat), BF16),
            pltpu.SemaphoreType.DMA((1 + 2 * (feat // block) + len(arrived),)),
        ],
        24,
        "finish",
    )[0]


def close_kernel(heads, hp, stages, *refs):
    pieces = refs[:stages]
    coef_ref, ks_hbm, v_hbm, facts_hbm = refs[stages : stages + 4]
    rest = refs[stages + 4 : -10]
    k_hbm, dv_hbm, ksbuf, vbuf, facts_ref, dkbuf, dvbuf, kside, vside, sems = refs[-10:]
    dks, dvs = rest[: len(rest) // 2], rest[len(rest) // 2 :]
    each = heads // len(dks)
    copies = Copies(sems)
    facts_in = copies.start(facts_hbm, facts_ref)
    loads = []
    for part, (dk, dv) in enumerate(zip(dks, dvs)):
        wide = pl.ds(part * each * HDIM, each * HDIM)
        loads.append(
            (
                copies.start(v_hbm.at[:, wide], vbuf.at[:, wide]),
                copies.start(dk, dkbuf.at[:, wide]),
                copies.start(ks_hbm.at[:, wide], ksbuf.at[:, wide]),
                copies.start(dv, dvbuf.at[:, wide]),
            )
        )
    facts_in.wait()
    table = turned(facts_ref[...])
    for h in range(heads):
        if h % each == 0:
            for copy in loads[h // each]:
                copy.wait()
        cols = slice(h * HDIM, (h + 1) * HDIM)
        adjoint = mix(coef_ref, pieces, heads, h)
        tail, gain = column(table, 2 * hp + h), column(table, hp + h)
        carry_k = dot(vbuf[:, cols], adjoint, NT)
        kside[:, cols] = (gain * (dkbuf[:, cols] + tail * carry_k)).astype(BF16)
        carry_v = dot(ksbuf[:, cols], adjoint, NN)
        vside[:, cols] = (dvbuf[:, cols] + tail * carry_v).astype(BF16)
        if (h + 1) % each == 0:
            wide = slice((h + 1 - each) * HDIM, (h + 1) * HDIM)
            copies.store(kside.at[:, wide], k_hbm.at[:, wide])
            copies.store(vside.at[:, wide], dv_hbm.at[:, wide])
    copies.finish()


def close(pieces, coefs, dks, dvs, scaled_keys, values, facts, heads, hp):
    rows, width = values.shape
    args = (coefs, scaled_keys, values, facts, *dks, *dvs)
    buf, wide = pltpu.VMEM((rows, width), BF16), pltpu.VMEM((rows, width), F32)
    return kernel_call(
        functools.partial(close_kernel, heads, hp, len(pieces)),
        (*pieces, *args),
        [VM] * (len(pieces) + 1) + [HB] * (len(args) - 1),
        [((rows, width), BF16)] * 2,
        (HB,) * 2,
        [
            buf,
            buf,
            pltpu.VMEM(facts.shape, F32),
            wide,
            wide,
            buf,
            buf,
            pltpu.SemaphoreType.DMA((1 + 6 * len(dks),)),
        ],
        20,
        "close",
        flops=10**11,
    )


def body(ctx_size, head_size, hidden, w_query, keys, values, d_out, log_decay):
    rows, feat = hidden.shape
    heads = log_decay.shape[1]
    width = w_query.shape[1]
    hp = sublanes(heads)
    scaling = HDIM ** (-0.5)
    me = lax.axis_index("ctx")
    mine = lax.axis_index("head")

    parts = [hidden]
    for shift in range(1, head_size):
        ring = [(i, (i + shift) % head_size) for i in range(head_size)]
        parts.append(lax.ppermute(hidden, "head", ring))
    owners = jnp.stack([(mine + head_size - s) % head_size for s in range(head_size)]).astype(jnp.int32)

    scaled_keys, facts, msg, state = prepare(log_decay.T, keys, values, heads, hp, scaling)
    query, adjoint, amsg = project(parts, owners, w_query, d_out, facts, hp)

    wide = lambda factor: factor[:heads, None, :]
    cube = lambda flat: flat.reshape(heads, HDIM, HDIM)
    split = lambda f: (f.astype(BF16), (f - f.astype(BF16).astype(F32)).astype(BF16))
    joined = lambda pair: pair[:hp].astype(F32) + pair[hp:].astype(F32)
    stages = (ctx_size - 1).bit_length()

    def send(array, stage, up):
        dist = 1 << stage
        if stage < stages - 1:
            pairs = [(i, i ^ dist) for i in range(ctx_size)]
        else:
            pairs = [(i, i + dist) if up else (i + dist, i) for i in range(ctx_size) if not i & dist]
        return lax.ppermute(array, "ctx", pairs)

    uppers = [(me & (1 << stage)) != 0 for stage in range(stages)]
    shares, others = [joined(msg[width:])], []
    got, agot = [], []
    before, after = [jnp.ones_like(shares[0])], [jnp.ones_like(shares[0])]

    def fold_state(stage, state):
        upper, arrived = uppers[stage], cube(got[stage][:width]).astype(F32)
        theirs = joined(got[stage][width:])
        others.append(theirs)
        own, other = jnp.where(upper, 1.0, theirs), jnp.where(upper, shares[stage], 1.0)
        state = (wide(own) * cube(state) + wide(other) * arrived).reshape(width, HDIM)
        shares.append(shares[stage] * theirs)
        before.append(jnp.where(upper, before[stage] * theirs, before[stage]))
        after.append(jnp.where(upper, after[stage], after[stage] * theirs))
        msg = state.astype(BF16)
        if stage + 2 < stages:
            msg = jnp.concatenate([msg, *split(shares[-1])], axis=0)
        return msg, state

    def fold_adjoint(stage, adjoint):
        upper, arrived = uppers[stage], cube(agot[stage]).astype(F32)
        own, other = jnp.where(upper, others[stage], 1.0), jnp.where(upper, 1.0, shares[stage])
        adjoint = (wide(own) * cube(adjoint) + wide(other) * arrived).reshape(width, HDIM)
        return adjoint.astype(BF16), adjoint

    half = max(1, heads // 2)
    pending = [(first, first + half) for first in range(0, heads, half)]
    inner_parts = []

    def next_inner():
        return inner(*pending.pop(0), query, scaled_keys, values, d_out, facts, hp)

    barrier = lax.optimization_barrier
    for stage in range(stages):
        arrived = send(msg if stage < stages - 1 else msg[:width], stage, True)
        if stage == 0:
            arrived, query, adjoint, amsg = barrier((arrived, query, adjoint, amsg))
        else:
            agot.append(send(amsg, stage - 1, False))
            if pending and (stage == 1 or stage == stages - 1):
                part = next_inner()
                arrived, *part = barrier((arrived, *part))
                inner_parts.append(part)
        got.append(arrived)
        if stage < stages - 1:
            msg, state = fold_state(stage, state)
        if stage >= 1:
            amsg, adjoint = fold_adjoint(stage - 1, adjoint)
    while pending:
        inner_parts.append(next_inner())
    agot.append(send(amsg, stages - 1, False))
    got[-1], _ = barrier((got[-1], amsg))

    state_coefs = [jnp.where(u, f, 0.0)[:heads] for u, f in zip(uppers, before)]
    adjoint_coefs = [jnp.where(u, 0.0, f)[:heads] for u, f in zip(uppers, after)]
    state_coefs = jnp.concatenate(state_coefs, axis=0)
    adjoint_coefs = jnp.concatenate(adjoint_coefs, axis=0)
    dqs, dks, dvs = zip(*inner_parts)

    place = lambda shift: ((mine + shift) % head_size).astype(jnp.int32).reshape(1)
    count = feat // 2 if feat >= 1024 else feat
    arrived = []
    for shift in range(1, head_size):
        ring = [(i, (i + shift) % head_size) for i in range(head_size)]
        for first in range(0, feat, count):
            if shift == 1 and first == 0:
                d_query, term = query_term(
                    got, state_coefs, dqs, d_out, facts, w_query, place(1), feat, count, heads, hp
                )
            else:
                term = plain_term(d_query, w_query, place(shift), feat, first, count)
            arrived.append(lax.ppermute(term, "head", ring))
    d_keys, d_values = close(agot, adjoint_coefs, dks, dvs, scaled_keys, values, facts, heads, hp)
    d_hidden = finish(d_query, w_query, place(0), arrived, feat)
    return (d_hidden, d_keys, d_values)


def solution(mesh):
    return jax.shard_map(
        functools.partial(body, mesh.shape["ctx"], mesh.shape["head"]),
        mesh=mesh,
        in_specs=(
            P("ctx", "head"),
            P(None, "head"),
            P("ctx", "head"),
            P("ctx", "head"),
            P("ctx", "head"),
            P("ctx", "head"),
        ),
        out_specs=(P("ctx", "head"), P("ctx", "head"), P("ctx", "head")),
        check_vma=False,
    )
```

```python
import functools
import math

import jax
import jax.numpy as jnp
from jax import lax
from jax.experimental import pallas as pl
from jax.experimental.pallas import tpu as pltpu
from jax.sharding import PartitionSpec as P

HDIM = 128
LANES = 128
F32, BF16 = jnp.float32, jnp.bfloat16
MIB = 1 << 20
VM = pl.BlockSpec(memory_space=pltpu.VMEM)
SM = pl.BlockSpec(memory_space=pltpu.SMEM)
HB = pl.BlockSpec(memory_space=pltpu.HBM)
AN = pl.BlockSpec(memory_space=pl.ANY)

NN = (((1,), (0,)), ((), ()))
NT = (((1,), (1,)), ((), ()))
TN = (((0,), (0,)), ((), ()))


def dot(a, b, dims):
    return lax.dot_general(a, b, dims, preferred_element_type=F32)


def kernel_call(kernel, args, specs, outs, out_specs, scratch, mib, name, flops=1):
    pinned = [pltpu.with_memory_space_constraint(a, pltpu.HBM) if s is HB else a for a, s in zip(args, specs)]
    placed = tuple(
        (pltpu.HBM if s is HB else jax.ShapeDtypeStruct)(shape, dtype) for (shape, dtype), s in zip(outs, out_specs)
    )
    return pl.pallas_call(
        kernel,
        in_specs=specs,
        out_specs=tuple(out_specs),
        out_shape=placed,
        scratch_shapes=scratch,
        compiler_params=pltpu.CompilerParams(vmem_limit_bytes=mib * MIB),
        cost_estimate=pl.CostEstimate(flops=flops, bytes_accessed=1, transcendentals=0),
        name=name,
    )(*pinned)


def sublanes(count):
    return -(-count // 8) * 8


def expm1_negative(z):
    series = jnp.full_like(z, 1.0)
    for order in range(10, 1, -1):
        series = 1.0 + z * series * (1.0 / order)
    return jnp.where(z > -0.5, z * series, jnp.exp(z) - 1.0)


def column(table, lane, width=LANES):
    return jnp.broadcast_to(table[:, lane : lane + 1], (table.shape[0], width))


class Copies:
    def __init__(self, sems):
        self.sems, self.count, self.out = sems, 0, []

    def start(self, src, dst):
        copy = pltpu.make_async_copy(src, dst, self.sems.at[self.count])
        self.count += 1
        copy.start()
        return copy

    def store(self, src, dst):
        self.out.append(self.start(src, dst))

    def finish(self):
        for copy in self.out:
            copy.wait()


def groups(heads):
    size = min(4, heads)
    return [(f, f + size, slice(f * HDIM, (f + size) * HDIM)) for f in range(0, heads, size)]


def turned(facts):
    spare = jnp.zeros((LANES - facts.shape[0], facts.shape[1]), F32)
    return jnp.concatenate([facts, spare], axis=0).T


def prepare_kernel(heads, hp, scaling, ld_hbm, k_hbm, v_hbm, facts_hbm, msg_ref, state_ref, ld, facts_ref, kbuf, vbuf, sems):
    rows = kbuf.shape[0]
    copies = Copies(sems)
    ld_in = copies.start(ld_hbm, ld)
    loads = []
    for _, _, wide in groups(heads):
        loads.append([copies.start(src.at[:, wide], dst.at[:, wide]) for src, dst in ((k_hbm, kbuf), (v_hbm, vbuf))])
    ld_in.wait()
    logs = ld[...]
    if heads < hp:
        logs = jnp.concatenate([logs, jnp.zeros((hp - heads, rows), F32)], axis=0)
    lane = lax.broadcasted_iota(jnp.int32, logs.shape, 1)
    cumulative = logs
    step = 1
    while step < rows:
        moved = pltpu.roll(cumulative, step, 1)
        cumulative = cumulative + jnp.where(lane >= step, moved, 0.0)
        step *= 2
    total = cumulative[:, rows - 1 :]
    gain = jnp.sqrt(-expm1_negative(2.0 * logs))
    tail = jnp.exp(total - cumulative)
    lead = scaling * jnp.exp(cumulative)
    facts = jnp.concatenate([cumulative, gain, tail, lead], axis=0)
    facts_ref[...] = facts
    copies.store(facts_ref, facts_hbm)
    table = turned(facts)
    share = jnp.broadcast_to(jnp.exp(total), (hp, LANES))
    high = share.astype(BF16)
    low = (share - high.astype(F32)).astype(BF16)
    base = heads * HDIM
    msg_ref[base:, :] = jnp.concatenate([high.astype(F32), low.astype(F32)], axis=0).astype(BF16)
    for (first, last, _), load in zip(groups(heads), loads):
        for copy in load:
            copy.wait()
        for h in range(first, last):
            cols = slice(h * HDIM, (h + 1) * HDIM)
            scaled = scaled_keys(table, hp, h, kbuf[:, cols])
            decayed = (column(table, 2 * hp + h) * scaled.astype(F32)).astype(BF16)
            local = dot(decayed, vbuf[:, cols], TN)
            state_ref[cols, :] = local
            msg_ref[cols, :] = local.astype(BF16)
    copies.finish()


def scaled_keys(table, hp, h, keys):
    return (column(table, hp + h) * keys.astype(F32)).astype(BF16)


def prepare(logs, keys, values, heads, hp, scaling):
    rows, width = keys.shape
    buf = pltpu.VMEM((rows, width), BF16)
    return kernel_call(
        functools.partial(prepare_kernel, heads, hp, scaling),
        (logs, keys, values),
        [HB] * 3,
        [((4 * hp, rows), F32), ((width + 2 * hp, HDIM), BF16), ((width, HDIM), F32)],
        (HB, VM, VM),
        [
            pltpu.VMEM((heads, rows), F32),
            pltpu.VMEM((4 * hp, rows), F32),
            buf,
            buf,
            pltpu.SemaphoreType.DMA((2 + 2 * len(groups(heads)),)),
        ],
        12,
        "prepare",
    )


def project_kernel(hp, nparts, chunk, place_ref, *refs):
    parts, (w_hbm, do_hbm, facts_hbm, q_hbm, adj_ref, msg_ref) = refs[:nparts], refs[nparts : nparts + 6]
    hbuf, wbuf, dobuf, facts_ref, qbuf, total, sems = refs[nparts + 6 :]
    rows, feat = parts[0].shape
    width = wbuf.shape[1]
    heads = width // HDIM
    copies = Copies(sems)
    loads = []
    for part, ref in enumerate(parts):
        for first in range(0, feat, chunk):
            here = pl.ds(part * feat + first, chunk)
            start = pl.multiple_of(place_ref[part] * feat + first, chunk)
            loads.append(
                (
                    slice(part * feat + first, part * feat + first + chunk),
                    copies.start(ref.at[:, pl.ds(first, chunk)], hbuf.at[:, here]),
                    copies.start(w_hbm.at[pl.ds(start, chunk), :], wbuf.at[here, :]),
                )
            )
    late = [copies.start(facts_hbm, facts_ref), copies.start(do_hbm, dobuf)]
    block = min(256, width)
    for order, (here, h_in, w_in) in enumerate(loads):
        h_in.wait()
        w_in.wait()
        for first in range(0, width, block):
            wide = slice(first, first + block)
            term = dot(hbuf[:, here], wbuf[here, wide], NN)
            if order == 0:
                total[:, wide] = term
            elif order < len(loads) - 1:
                total[:, wide] += term
            else:
                qbuf[:, wide] = (total[:, wide] + term).astype(BF16)
    for copy in late:
        copy.wait()
    copies.store(qbuf, q_hbm)
    table = turned(facts_ref[...])
    for h in range(heads):
        cols = slice(h * HDIM, (h + 1) * HDIM)
        decayed = (column(table, 3 * hp + h) * qbuf[:, cols].astype(F32)).astype(BF16)
        local = dot(decayed, dobuf[:, cols], TN)
        adj_ref[cols, :] = local
        msg_ref[cols, :] = local.astype(BF16)
    copies.finish()


def project(parts, owners, w_query, d_out, facts, hp):
    rows, feat = parts[0].shape
    depth, width = w_query.shape
    chunk = min(512, feat)
    return kernel_call(
        functools.partial(project_kernel, hp, len(parts), chunk),
        (owners, *parts, w_query, d_out, facts),
        [SM, HB] + [AN] * (len(parts) - 1) + [HB] * 3,
        [((rows, width), BF16), ((width, HDIM), F32), ((width, HDIM), BF16)],
        (HB, VM, VM),
        [
            pltpu.VMEM((rows, depth), BF16),
            pltpu.VMEM((depth, width), BF16),
            pltpu.VMEM((rows, width), BF16),
            pltpu.VMEM(facts.shape, F32),
            pltpu.VMEM((rows, width), BF16),
            pltpu.VMEM((rows, width), F32),
            pltpu.SemaphoreType.DMA((2 * len(parts) * (feat // chunk) + 3,)),
        ],
        28,
        "project",
    )


def inner_kernel(first, last, hp, *refs):
    ins, facts_hbm, outs = refs[:4], refs[4], refs[5:8]
    bufs, facts_ref, sides, sems = refs[8:12], refs[12], refs[13:16], refs[16]
    rows = ins[0].shape[0]
    copies = Copies(sems)
    facts_in = copies.start(facts_hbm, facts_ref)
    loads = {}
    for h in range(first, last, 2):
        count = min(2, last - h)
        src, dst = pl.ds(h * HDIM, count * HDIM), pl.ds((h - first) * HDIM, count * HDIM)
        loads[h] = [copies.start(ref.at[:, src], buf.at[:, dst]) for ref, buf in zip(ins, bufs)]
    facts_in.wait()
    table = turned(facts_ref[...])
    row = lax.broadcasted_iota(jnp.int32, (rows, rows), 0)
    keep = row >= lax.broadcasted_iota(jnp.int32, (rows, rows), 1)
    shift = -0.5 * math.log2(HDIM)
    turn = math.log2(math.e)
    q_ref, k_ref, v_ref, do_ref = bufs
    for h in range(first, last):
        for copy in loads.get(h, ()):
            copy.wait()
        cols = slice((h - first) * HDIM, (h - first + 1) * HDIM)
        later = column(table, h) * turn + shift
        sooner = facts_ref[h : h + 1, :] * turn
        gap = jnp.concatenate([later] * (rows // LANES), axis=1) - sooner
        decays = jnp.exp2(jnp.where(keep, gap, -1e30))
        query, grad = q_ref[:, cols], do_ref[:, cols]
        scaled = scaled_keys(table, hp, h, k_ref[:, cols])
        wdv = (decays * dot(grad, v_ref[:, cols], NT)).astype(BF16)
        wkq = (decays * dot(query, scaled, NT)).astype(BF16)
        sides[0][:, cols] = dot(wdv, scaled, NN).astype(BF16)
        sides[1][:, cols] = dot(query, wdv, TN).T.astype(BF16)
        sides[2][:, cols] = dot(grad, wkq, TN).T.astype(BF16)
        if h + 1 == last or h + 1 in loads:
            from_head = h if h in loads else h - 1
            done = slice((from_head - first) * HDIM, (h + 1 - first) * HDIM)
            for side, out in zip(sides, outs):
                copies.store(side.at[:, done], out.at[:, done])
    copies.finish()


def inner(first, last, query, keys, values, d_out, facts, hp):
    rows = query.shape[0]
    width = (last - first) * HDIM
    pairs = -(-(last - first) // 2)
    return kernel_call(
        functools.partial(inner_kernel, first, last, hp),
        (query, keys, values, d_out, facts),
        [HB] * 5,
        [((rows, width), BF16)] * 3,
        (HB,) * 3,
        [
            *[pltpu.VMEM((rows, width), BF16)] * 4,
            pltpu.VMEM(facts.shape, F32),
            *[pltpu.VMEM((rows, width), BF16)] * 3,
            pltpu.SemaphoreType.DMA((1 + 7 * pairs,)),
        ],
        24,
        "inner",
    )


def mix(coef_ref, pieces, heads, h):
    cols = slice(h * HDIM, (h + 1) * HDIM)
    total = None
    for stage, piece in enumerate(pieces):
        row = stage * heads + h
        term = coef_ref[row : row + 1, :] * piece[cols, :].astype(F32)
        total = term if total is None else total + term
    return total.astype(BF16)


def load_weight(copies, place_ref, first, w_hbm, wbuf, feat, block):
    loads = []
    for at in range(0, wbuf.shape[0], block):
        start = pl.multiple_of(place_ref[0] * feat + first + at, block)
        loads.append((at, copies.start(w_hbm.at[pl.ds(start, block), :], wbuf.at[pl.ds(at, block), :])))
    return loads


def query_kernel(heads, hp, stages, feat, block, place_ref, *refs):
    pieces = refs[:stages]
    coef_ref, do_hbm, facts_hbm, w_hbm = refs[stages : stages + 4]
    inner_hbm = refs[stages + 4 : -9]
    dq_hbm, out_hbm, dobuf, facts_ref, wbuf, local, held, sent, sems = refs[-9:]
    copies = Copies(sems)
    each = heads // len(inner_hbm)
    facts_in = copies.start(facts_hbm, facts_ref)
    loads = []
    for part, src in enumerate(inner_hbm):
        wide = pl.ds(part * each * HDIM, each * HDIM)
        loads.append(
            (copies.start(do_hbm.at[:, wide], dobuf.at[:, wide]), copies.start(src, local.at[:, wide]))
        )
    w_in = load_weight(copies, place_ref, 0, w_hbm, wbuf, feat, block)
    facts_in.wait()
    table = turned(facts_ref[...])
    for h in range(heads):
        if h % each == 0:
            for copy in loads[h // each]:
                copy.wait()
        cols = slice(h * HDIM, (h + 1) * HDIM)
        state = mix(coef_ref, pieces, heads, h)
        carry = dot(dobuf[:, cols], state, NT)
        held[:, cols] = (local[:, cols].astype(F32) + column(table, 3 * hp + h) * carry).astype(BF16)
    copies.store(held, dq_hbm)
    send_terms(copies, w_in, held, wbuf, sent, out_hbm, block)
    copies.finish()


def send_terms(copies, w_in, dq_ref, wbuf, sent, out_hbm, block):
    for at, copy in w_in:
        copy.wait()
        wide = slice(at, at + block)
        sent[:, wide] = dot(dq_ref[...], wbuf[wide, :], NT).astype(BF16)
        copies.store(sent.at[:, wide], out_hbm.at[:, wide])


def query_term(pieces, coefs, inner_dq, d_out, facts, w_query, place, feat, count, heads, hp):
    rows, width = d_out.shape
    block = min(512, count)
    args = (coefs, d_out, facts, w_query, *inner_dq)
    return kernel_call(
        functools.partial(query_kernel, heads, hp, len(pieces), feat, block),
        (place, *pieces, *args),
        [SM] + [VM] * (len(pieces) + 1) + [HB] * (len(args) - 1),
        [((rows, width), BF16), ((rows, count), BF16)],
        (HB, HB),
        [
            pltpu.VMEM((rows, width), BF16),
            pltpu.VMEM(facts.shape, F32),
            pltpu.VMEM((count, width), BF16),
            pltpu.VMEM((rows, width), BF16),
            pltpu.VMEM((rows, width), BF16),
            pltpu.VMEM((rows, count), BF16),
            pltpu.SemaphoreType.DMA((2 + 2 * len(inner_dq) + 2 * (count // block),)),
        ],
        20,
        "query_term",
    )


def term_kernel(feat, first, block, place_ref, dq_hbm, w_hbm, out_hbm, held, wbuf, sent, sems):
    copies = Copies(sems)
    dq_in = copies.start(dq_hbm, held)
    w_in = load_weight(copies, place_ref, first, w_hbm, wbuf, feat, block)
    dq_in.wait()
    send_terms(copies, w_in, held, wbuf, sent, out_hbm, block)
    copies.finish()


def plain_term(d_query, w_query, place, feat, first, count):
    rows, width = d_query.shape
    block = min(512, count)
    return kernel_call(
        functools.partial(term_kernel, feat, first, block),
        (place, d_query, w_query),
        [SM, HB, HB],
        [((rows, count), BF16)],
        (HB,),
        [
            pltpu.VMEM((rows, width), BF16),
            pltpu.VMEM((count, width), BF16),
            pltpu.VMEM((rows, count), BF16),
            pltpu.SemaphoreType.DMA((1 + 2 * (count // block),)),
        ],
        16,
        "term",
    )[0]


def finish_kernel(count, block, place_ref, *refs):
    dq_hbm, w_hbm = refs[:2]
    arrived, (out_hbm, held, wbuf, extra, sent, sems) = refs[2:-6], refs[-6:]
    feat = sent.shape[1]
    copies = Copies(sems)
    dq_in = copies.start(dq_hbm, held)
    w_in = load_weight(copies, place_ref, 0, w_hbm, wbuf, feat, block)
    per = feat // count
    others = []
    for index, src in enumerate(arrived):
        shift, first = divmod(index, per)
        others.append(copies.start(src, extra.at[shift, :, pl.ds(first * count, count)]))
    dq_in.wait()
    for at, copy in w_in:
        copy.wait()
        wide = slice(at, at + block)
        total = dot(held[...], wbuf[wide, :], NT).astype(BF16).astype(F32)
        for index, other in enumerate(others):
            if at == index % per * count:
                other.wait()
        for shift in range(extra.shape[0]):
            total = total + extra[shift, :, wide].astype(F32)
        sent[:, wide] = total.astype(BF16)
        copies.store(sent.at[:, wide], out_hbm.at[:, wide])
    copies.finish()


def finish(d_query, w_query, place, arrived, feat):
    rows, width = d_query.shape
    count = arrived[0].shape[1]
    block = min(512, count)
    return kernel_call(
        functools.partial(finish_kernel, count, block),
        (place, d_query, w_query, *arrived),
        [SM, HB, HB] + [AN] * len(arrived),
        [((rows, feat), BF16)],
        (HB,),
        [
            pltpu.VMEM((rows, width), BF16),
            pltpu.VMEM((feat, width), BF16),
            pltpu.VMEM((len(arrived) * count // feat, rows, feat), BF16),
            pltpu.VMEM((rows, feat), BF16),
            pltpu.SemaphoreType.DMA((1 + 2 * (feat // block) + len(arrived),)),
        ],
        24,
        "finish",
    )[0]


def close_kernel(heads, hp, stages, *refs):
    pieces = refs[:stages]
    coef_ref, in_hbm, v_hbm, facts_hbm = refs[stages : stages + 4]
    rest = refs[stages + 4 : -10]
    dk_hbm, dv_hbm, kbuf, vbuf, facts_ref, dkbuf, dvbuf, kside, vside, sems = refs[-10:]
    dks, dvs = rest[: len(rest) // 2], rest[len(rest) // 2 :]
    each = heads // len(dks)
    copies = Copies(sems)
    facts_in = copies.start(facts_hbm, facts_ref)
    loads = []
    for part, (dk, dv) in enumerate(zip(dks, dvs)):
        wide = pl.ds(part * each * HDIM, each * HDIM)
        loads.append(
            (
                copies.start(v_hbm.at[:, wide], vbuf.at[:, wide]),
                copies.start(dk, dkbuf.at[:, wide]),
                copies.start(in_hbm.at[:, wide], kbuf.at[:, wide]),
                copies.start(dv, dvbuf.at[:, wide]),
            )
        )
    facts_in.wait()
    table = turned(facts_ref[...])
    for h in range(heads):
        if h % each == 0:
            for copy in loads[h // each]:
                copy.wait()
        cols = slice(h * HDIM, (h + 1) * HDIM)
        adjoint = mix(coef_ref, pieces, heads, h)
        tail, gain = column(table, 2 * hp + h), column(table, hp + h)
        carry_k = dot(vbuf[:, cols], adjoint, NT)
        kside[:, cols] = (gain * (dkbuf[:, cols].astype(F32) + tail * carry_k)).astype(BF16)
        carry_v = dot(scaled_keys(table, hp, h, kbuf[:, cols]), adjoint, NN)
        vside[:, cols] = (dvbuf[:, cols].astype(F32) + tail * carry_v).astype(BF16)
        if (h + 1) % each == 0:
            wide = slice((h + 1 - each) * HDIM, (h + 1) * HDIM)
            copies.store(kside.at[:, wide], dk_hbm.at[:, wide])
            copies.store(vside.at[:, wide], dv_hbm.at[:, wide])
    copies.finish()


def close(pieces, coefs, dks, dvs, keys, values, facts, heads, hp):
    rows, width = values.shape
    args = (coefs, keys, values, facts, *dks, *dvs)
    buf = pltpu.VMEM((rows, width), BF16)
    return kernel_call(
        functools.partial(close_kernel, heads, hp, len(pieces)),
        (*pieces, *args),
        [VM] * (len(pieces) + 1) + [HB] * (len(args) - 1),
        [((rows, width), BF16)] * 2,
        (HB,) * 2,
        [
            buf,
            buf,
            pltpu.VMEM(facts.shape, F32),
            buf,
            buf,
            buf,
            buf,
            pltpu.SemaphoreType.DMA((1 + 6 * len(dks),)),
        ],
        20,
        "close",
        flops=10**11,
    )


def body(ctx_size, head_size, hidden, w_query, keys, values, d_out, log_decay):
    rows, feat = hidden.shape
    heads = log_decay.shape[1]
    width = w_query.shape[1]
    hp = sublanes(heads)
    scaling = HDIM ** (-0.5)
    me = lax.axis_index("ctx")
    mine = lax.axis_index("head")

    parts = [hidden]
    for shift in range(1, head_size):
        ring = [(i, (i + shift) % head_size) for i in range(head_size)]
        parts.append(lax.ppermute(hidden, "head", ring))
    owners = jnp.stack([(mine + head_size - s) % head_size for s in range(head_size)]).astype(jnp.int32)

    facts, msg, state = prepare(log_decay.T, keys, values, heads, hp, scaling)
    query, adjoint, amsg = project(parts, owners, w_query, d_out, facts, hp)

    wide = lambda factor: factor[:heads, None, :]
    cube = lambda flat: flat.reshape(heads, HDIM, HDIM)
    split = lambda f: (f.astype(BF16), (f - f.astype(BF16).astype(F32)).astype(BF16))
    joined = lambda pair: pair[:hp].astype(F32) + pair[hp:].astype(F32)
    stages = (ctx_size - 1).bit_length()

    def send(array, stage, up):
        dist = 1 << stage
        if stage < stages - 1:
            pairs = [(i, i ^ dist) for i in range(ctx_size)]
        else:
            pairs = [(i, i + dist) if up else (i + dist, i) for i in range(ctx_size) if not i & dist]
        return lax.ppermute(array, "ctx", pairs)

    uppers = [(me & (1 << stage)) != 0 for stage in range(stages)]
    shares, others = [joined(msg[width:])], []
    got, agot = [], []
    before, after = [jnp.ones_like(shares[0])], [jnp.ones_like(shares[0])]

    def fold_state(stage, state):
        upper, arrived = uppers[stage], cube(got[stage][:width]).astype(F32)
        theirs = joined(got[stage][width:])
        others.append(theirs)
        own, other = jnp.where(upper, 1.0, theirs), jnp.where(upper, shares[stage], 1.0)
        state = (wide(own) * cube(state) + wide(other) * arrived).reshape(width, HDIM)
        shares.append(shares[stage] * theirs)
        before.append(jnp.where(upper, before[stage] * theirs, before[stage]))
        after.append(jnp.where(upper, after[stage], after[stage] * theirs))
        msg = state.astype(BF16)
        if stage + 2 < stages:
            msg = jnp.concatenate([msg, *split(shares[-1])], axis=0)
        return msg, state

    def fold_adjoint(stage, adjoint):
        upper, arrived = uppers[stage], cube(agot[stage]).astype(F32)
        own, other = jnp.where(upper, others[stage], 1.0), jnp.where(upper, 1.0, shares[stage])
        adjoint = (wide(own) * cube(adjoint) + wide(other) * arrived).reshape(width, HDIM)
        return adjoint.astype(BF16), adjoint

    half = max(1, heads // 2)
    pending = [(first, first + half) for first in range(0, heads, half)]
    inner_parts = []

    def next_inner():
        return inner(*pending.pop(0), query, keys, values, d_out, facts, hp)

    barrier = lax.optimization_barrier
    for stage in range(stages):
        if stage == stages - 1:
            msg, query = barrier((msg, query))
        arrived = send(msg if stage < stages - 1 else msg[:width], stage, True)
        if stage == 0:
            arrived, query, adjoint, amsg = barrier((arrived, query, adjoint, amsg))
        else:
            agot.append(send(amsg, stage - 1, False))
            if pending and (stage == 1 or stage == stages - 1):
                part = next_inner()
                arrived, *part = barrier((arrived, *part))
                inner_parts.append(part)
        got.append(arrived)
        if stage < stages - 1:
            msg, state = fold_state(stage, state)
        if stage >= 1:
            amsg, adjoint = fold_adjoint(stage - 1, adjoint)
    while pending:
        inner_parts.append(next_inner())
    agot.append(send(amsg, stages - 1, False))
    got[-1], _ = barrier((got[-1], amsg))

    state_coefs = [jnp.where(u, f, 0.0)[:heads] for u, f in zip(uppers, before)]
    adjoint_coefs = [jnp.where(u, 0.0, f)[:heads] for u, f in zip(uppers, after)]
    state_coefs = jnp.concatenate(state_coefs, axis=0)
    adjoint_coefs = jnp.concatenate(adjoint_coefs, axis=0)
    dqs, dks, dvs = zip(*inner_parts)

    place = lambda shift: ((mine + shift) % head_size).astype(jnp.int32).reshape(1)
    count = feat
    arrived = []
    for shift in range(1, head_size):
        ring = [(i, (i + shift) % head_size) for i in range(head_size)]
        for first in range(0, feat, count):
            if shift == 1 and first == 0:
                d_query, term = query_term(
                    got, state_coefs, dqs, d_out, facts, w_query, place(1), feat, count, heads, hp
                )
            else:
                term = plain_term(d_query, w_query, place(shift), feat, first, count)
            arrived.append(lax.ppermute(term, "head", ring))
    d_keys, d_values = close(agot, adjoint_coefs, dks, dvs, keys, values, facts, heads, hp)
    d_hidden = finish(d_query, w_query, place(0), arrived, feat)
    return (d_hidden, d_keys, d_values)


def solution(mesh):
    return jax.shard_map(
        functools.partial(body, mesh.shape["ctx"], mesh.shape["head"]),
        mesh=mesh,
        in_specs=(
            P("ctx", "head"),
            P(None, "head"),
            P("ctx", "head"),
            P("ctx", "head"),
            P("ctx", "head"),
            P("ctx", "head"),
        ),
        out_specs=(P("ctx", "head"), P("ctx", "head"), P("ctx", "head")),
        check_vma=False,
    )
```

```python
import functools
import math

import jax
import jax.numpy as jnp
from jax import lax
from jax.experimental import pallas as pl
from jax.experimental.pallas import tpu as pltpu
from jax.sharding import PartitionSpec as P

HDIM = 128
LANES = 128
F32, BF16 = jnp.float32, jnp.bfloat16
MIB = 1 << 20
VM = pl.BlockSpec(memory_space=pltpu.VMEM)
SM = pl.BlockSpec(memory_space=pltpu.SMEM)
HB = pl.BlockSpec(memory_space=pltpu.HBM)
AN = pl.BlockSpec(memory_space=pl.ANY)

NN = (((1,), (0,)), ((), ()))
NT = (((1,), (1,)), ((), ()))
TN = (((0,), (0,)), ((), ()))


def dot(a, b, dims):
    return lax.dot_general(a, b, dims, preferred_element_type=F32)


def kernel_call(kernel, args, specs, outs, out_specs, scratch, mib, name, micros):
    pinned = [pltpu.with_memory_space_constraint(a, pltpu.HBM) if s is HB else a for a, s in zip(args, specs)]
    placed = tuple(
        (pltpu.HBM if s is HB else jax.ShapeDtypeStruct)(shape, dtype) for (shape, dtype), s in zip(outs, out_specs)
    )
    return pl.pallas_call(
        kernel,
        in_specs=specs,
        out_specs=tuple(out_specs),
        out_shape=placed,
        scratch_shapes=scratch,
        compiler_params=pltpu.CompilerParams(vmem_limit_bytes=mib * MIB),
        cost_estimate=pl.CostEstimate(flops=int(micros * 1e9), bytes_accessed=1, transcendentals=0),
        name=name,
    )(*pinned)


def sublanes(count):
    return -(-count // 8) * 8


def expm1_negative(z):
    series = jnp.full_like(z, 1.0)
    for order in range(10, 1, -1):
        series = 1.0 + z * series * (1.0 / order)
    return jnp.where(z > -0.5, z * series, jnp.exp(z) - 1.0)


def column(table, lane, width=LANES):
    return jnp.broadcast_to(table[:, lane : lane + 1], (table.shape[0], width))


class Copies:
    def __init__(self, sems):
        self.sems, self.count, self.out = sems, 0, []

    def start(self, src, dst):
        copy = pltpu.make_async_copy(src, dst, self.sems.at[self.count])
        self.count += 1
        copy.start()
        return copy

    def store(self, src, dst):
        self.out.append(self.start(src, dst))

    def finish(self):
        for copy in self.out:
            copy.wait()


def groups(heads):
    size = min(4, heads)
    return [(f, f + size, slice(f * HDIM, (f + size) * HDIM)) for f in range(0, heads, size)]


def turned(facts):
    spare = jnp.zeros((LANES - facts.shape[0], facts.shape[1]), F32)
    return jnp.concatenate([facts, spare], axis=0).T


def prepare_kernel(heads, hp, scaling, ld_hbm, k_hbm, v_hbm, facts_hbm, msg_ref, state_ref, ld, facts_ref, kbuf, vbuf, sems):
    rows = kbuf.shape[0]
    copies = Copies(sems)
    ld_in = copies.start(ld_hbm, ld)
    loads = []
    for _, _, wide in groups(heads):
        loads.append([copies.start(src.at[:, wide], dst.at[:, wide]) for src, dst in ((k_hbm, kbuf), (v_hbm, vbuf))])
    ld_in.wait()
    logs = ld[...]
    if heads < hp:
        logs = jnp.concatenate([logs, jnp.zeros((hp - heads, rows), F32)], axis=0)
    lane = lax.broadcasted_iota(jnp.int32, logs.shape, 1)
    cumulative = logs
    step = 1
    while step < rows:
        moved = pltpu.roll(cumulative, step, 1)
        cumulative = cumulative + jnp.where(lane >= step, moved, 0.0)
        step *= 2
    total = cumulative[:, rows - 1 :]
    gain = jnp.sqrt(-expm1_negative(2.0 * logs))
    tail = jnp.exp(total - cumulative)
    lead = scaling * jnp.exp(cumulative)
    facts = jnp.concatenate([cumulative, gain, tail, lead], axis=0)
    facts_ref[...] = facts
    copies.store(facts_ref, facts_hbm)
    table = turned(facts)
    share = jnp.broadcast_to(jnp.exp(total), (hp, LANES))
    high = share.astype(BF16)
    low = (share - high.astype(F32)).astype(BF16)
    base = heads * HDIM
    msg_ref[base:, :] = jnp.concatenate([high.astype(F32), low.astype(F32)], axis=0).astype(BF16)
    for (first, last, _), load in zip(groups(heads), loads):
        for copy in load:
            copy.wait()
        for h in range(first, last):
            cols = slice(h * HDIM, (h + 1) * HDIM)
            scaled = scaled_keys(table, hp, h, kbuf[:, cols])
            decayed = (column(table, 2 * hp + h) * scaled.astype(F32)).astype(BF16)
            local = dot(decayed, vbuf[:, cols], TN)
            state_ref[cols, :] = local
            msg_ref[cols, :] = local.astype(BF16)
    copies.finish()


def scaled_keys(table, hp, h, keys):
    return (column(table, hp + h) * keys.astype(F32)).astype(BF16)


def prepare(logs, keys, values, heads, hp, scaling):
    rows, width = keys.shape
    buf = pltpu.VMEM((rows, width), BF16)
    return kernel_call(
        functools.partial(prepare_kernel, heads, hp, scaling),
        (logs, keys, values),
        [HB] * 3,
        [((4 * hp, rows), F32), ((width + 2 * hp, HDIM), BF16), ((width, HDIM), F32)],
        (HB, VM, VM),
        [
            pltpu.VMEM((heads, rows), F32),
            pltpu.VMEM((4 * hp, rows), F32),
            buf,
            buf,
            pltpu.SemaphoreType.DMA((2 + 2 * len(groups(heads)),)),
        ],
        12,
        "prepare",
        4,
    )


def project_kernel(hp, nparts, chunk, place_ref, *refs):
    parts, (w_hbm, do_hbm, facts_hbm, q_hbm, adj_ref, msg_ref) = refs[:nparts], refs[nparts : nparts + 6]
    hbuf, wbuf, dobuf, facts_ref, qbuf, total, sems = refs[nparts + 6 :]
    rows, feat = parts[0].shape
    width = wbuf.shape[1]
    heads = width // HDIM
    copies = Copies(sems)
    loads = []
    for part, ref in enumerate(parts):
        for first in range(0, feat, chunk):
            here = pl.ds(part * feat + first, chunk)
            start = pl.multiple_of(place_ref[part] * feat + first, chunk)
            loads.append(
                (
                    slice(part * feat + first, part * feat + first + chunk),
                    copies.start(ref.at[:, pl.ds(first, chunk)], hbuf.at[:, here]),
                    copies.start(w_hbm.at[pl.ds(start, chunk), :], wbuf.at[here, :]),
                )
            )
    late = [copies.start(facts_hbm, facts_ref), copies.start(do_hbm, dobuf)]
    block = min(256, width)
    for order, (here, h_in, w_in) in enumerate(loads):
        h_in.wait()
        w_in.wait()
        for first in range(0, width, block):
            wide = slice(first, first + block)
            term = dot(hbuf[:, here], wbuf[here, wide], NN)
            if order == 0:
                total[:, wide] = term
            elif order < len(loads) - 1:
                total[:, wide] += term
            else:
                qbuf[:, wide] = (total[:, wide] + term).astype(BF16)
    for copy in late:
        copy.wait()
    copies.store(qbuf, q_hbm)
    table = turned(facts_ref[...])
    for h in range(heads):
        cols = slice(h * HDIM, (h + 1) * HDIM)
        decayed = (column(table, 3 * hp + h) * qbuf[:, cols].astype(F32)).astype(BF16)
        local = dot(decayed, dobuf[:, cols], TN)
        adj_ref[cols, :] = local
        msg_ref[cols, :] = local.astype(BF16)
    copies.finish()


def project(parts, owners, w_query, d_out, facts, hp):
    rows, feat = parts[0].shape
    depth, width = w_query.shape
    chunk = min(512, feat)
    return kernel_call(
        functools.partial(project_kernel, hp, len(parts), chunk),
        (owners, *parts, w_query, d_out, facts),
        [SM, HB] + [AN] * (len(parts) - 1) + [HB] * 3,
        [((rows, width), BF16), ((width, HDIM), F32), ((width, HDIM), BF16)],
        (HB, VM, VM),
        [
            pltpu.VMEM((rows, depth), BF16),
            pltpu.VMEM((depth, width), BF16),
            pltpu.VMEM((rows, width), BF16),
            pltpu.VMEM(facts.shape, F32),
            pltpu.VMEM((rows, width), BF16),
            pltpu.VMEM((rows, width), F32),
            pltpu.SemaphoreType.DMA((2 * len(parts) * (feat // chunk) + 3,)),
        ],
        28,
        "project",
        8,
    )


def inner_kernel(first, last, hp, *refs):
    ins, facts_hbm, outs = refs[:4], refs[4], refs[5:8]
    bufs, facts_ref, sides, sems = refs[8:12], refs[12], refs[13:16], refs[16]
    rows = ins[0].shape[0]
    copies = Copies(sems)
    facts_in = copies.start(facts_hbm, facts_ref)
    loads = {}
    for h in range(first, last, 2):
        count = min(2, last - h)
        src, dst = pl.ds(h * HDIM, count * HDIM), pl.ds((h - first) * HDIM, count * HDIM)
        loads[h] = [copies.start(ref.at[:, src], buf.at[:, dst]) for ref, buf in zip(ins, bufs)]
    facts_in.wait()
    table = turned(facts_ref[...])
    row = lax.broadcasted_iota(jnp.int32, (rows, rows), 0)
    keep = row >= lax.broadcasted_iota(jnp.int32, (rows, rows), 1)
    shift = -0.5 * math.log2(HDIM)
    turn = math.log2(math.e)
    q_ref, k_ref, v_ref, do_ref = bufs
    for h in range(first, last):
        for copy in loads.get(h, ()):
            copy.wait()
        cols = slice((h - first) * HDIM, (h - first + 1) * HDIM)
        later = column(table, h) * turn + shift
        sooner = facts_ref[h : h + 1, :] * turn
        gap = jnp.concatenate([later] * (rows // LANES), axis=1) - sooner
        decays = jnp.exp2(jnp.where(keep, gap, -1e30))
        query, grad = q_ref[:, cols], do_ref[:, cols]
        scaled = scaled_keys(table, hp, h, k_ref[:, cols])
        wdv = (decays * dot(grad, v_ref[:, cols], NT)).astype(BF16)
        wkq = (decays * dot(query, scaled, NT)).astype(BF16)
        sides[0][:, cols] = dot(wdv, scaled, NN).astype(BF16)
        sides[1][:, cols] = dot(query, wdv, TN).T.astype(BF16)
        sides[2][:, cols] = dot(grad, wkq, TN).T.astype(BF16)
        if h + 1 == last or h + 1 in loads:
            from_head = h if h in loads else h - 1
            done = slice((from_head - first) * HDIM, (h + 1 - first) * HDIM)
            for side, out in zip(sides, outs):
                copies.store(side.at[:, done], out.at[:, done])
    copies.finish()


def inner(first, last, query, keys, values, d_out, facts, hp):
    rows = query.shape[0]
    width = (last - first) * HDIM
    pairs = -(-(last - first) // 2)
    return kernel_call(
        functools.partial(inner_kernel, first, last, hp),
        (query, keys, values, d_out, facts),
        [HB] * 5,
        [((rows, width), BF16)] * 3,
        (HB,) * 3,
        [
            *[pltpu.VMEM((rows, width), BF16)] * 4,
            pltpu.VMEM(facts.shape, F32),
            *[pltpu.VMEM((rows, width), BF16)] * 3,
            pltpu.SemaphoreType.DMA((1 + 7 * pairs,)),
        ],
        24,
        "inner",
        2,
    )


def mix(coef_ref, pieces, heads, h):
    cols = slice(h * HDIM, (h + 1) * HDIM)
    total = None
    for stage, piece in enumerate(pieces):
        row = stage * heads + h
        term = coef_ref[row : row + 1, :] * piece[cols, :].astype(F32)
        total = term if total is None else total + term
    return total.astype(BF16)


def load_weight(copies, place_ref, first, w_hbm, wbuf, feat, block):
    loads = []
    for at in range(0, wbuf.shape[0], block):
        start = pl.multiple_of(place_ref[0] * feat + first + at, block)
        loads.append((at, copies.start(w_hbm.at[pl.ds(start, block), :], wbuf.at[pl.ds(at, block), :])))
    return loads


def query_kernel(heads, hp, stages, feat, block, place_ref, *refs):
    pieces = refs[:stages]
    coef_ref, do_hbm, facts_hbm, w_hbm = refs[stages : stages + 4]
    inner_hbm = refs[stages + 4 : -9]
    dq_hbm, out_hbm, dobuf, facts_ref, wbuf, local, held, sent, sems = refs[-9:]
    copies = Copies(sems)
    each = heads // len(inner_hbm)
    facts_in = copies.start(facts_hbm, facts_ref)
    loads = []
    for part, src in enumerate(inner_hbm):
        wide = pl.ds(part * each * HDIM, each * HDIM)
        loads.append(
            (copies.start(do_hbm.at[:, wide], dobuf.at[:, wide]), copies.start(src, local.at[:, wide]))
        )
    w_in = load_weight(copies, place_ref, 0, w_hbm, wbuf, feat, block)
    facts_in.wait()
    table = turned(facts_ref[...])
    for h in range(heads):
        if h % each == 0:
            for copy in loads[h // each]:
                copy.wait()
        cols = slice(h * HDIM, (h + 1) * HDIM)
        state = mix(coef_ref, pieces, heads, h)
        carry = dot(dobuf[:, cols], state, NT)
        held[:, cols] = (local[:, cols].astype(F32) + column(table, 3 * hp + h) * carry).astype(BF16)
    copies.store(held, dq_hbm)
    send_terms(copies, w_in, held, wbuf, sent, out_hbm, block)
    copies.finish()


def send_terms(copies, w_in, dq_ref, wbuf, sent, out_hbm, block):
    for at, copy in w_in:
        copy.wait()
        wide = slice(at, at + block)
        sent[:, wide] = dot(dq_ref[...], wbuf[wide, :], NT).astype(BF16)
        copies.store(sent.at[:, wide], out_hbm.at[:, wide])


def query_term(pieces, coefs, inner_dq, d_out, facts, w_query, place, feat, count, heads, hp):
    rows, width = d_out.shape
    block = min(512, count)
    args = (coefs, d_out, facts, w_query, *inner_dq)
    return kernel_call(
        functools.partial(query_kernel, heads, hp, len(pieces), feat, block),
        (place, *pieces, *args),
        [SM] + [VM] * (len(pieces) + 1) + [HB] * (len(args) - 1),
        [((rows, width), BF16), ((rows, count), BF16)],
        (HB, HB),
        [
            pltpu.VMEM((rows, width), BF16),
            pltpu.VMEM(facts.shape, F32),
            pltpu.VMEM((count, width), BF16),
            pltpu.VMEM((rows, width), BF16),
            pltpu.VMEM((rows, width), BF16),
            pltpu.VMEM((rows, count), BF16),
            pltpu.SemaphoreType.DMA((2 + 2 * len(inner_dq) + 2 * (count // block),)),
        ],
        20,
        "query_term",
        6,
    )


def term_kernel(feat, first, block, place_ref, dq_hbm, w_hbm, out_hbm, held, wbuf, sent, sems):
    copies = Copies(sems)
    dq_in = copies.start(dq_hbm, held)
    w_in = load_weight(copies, place_ref, first, w_hbm, wbuf, feat, block)
    dq_in.wait()
    send_terms(copies, w_in, held, wbuf, sent, out_hbm, block)
    copies.finish()


def plain_term(d_query, w_query, place, feat, first, count):
    rows, width = d_query.shape
    block = min(512, count)
    return kernel_call(
        functools.partial(term_kernel, feat, first, block),
        (place, d_query, w_query),
        [SM, HB, HB],
        [((rows, count), BF16)],
        (HB,),
        [
            pltpu.VMEM((rows, width), BF16),
            pltpu.VMEM((count, width), BF16),
            pltpu.VMEM((rows, count), BF16),
            pltpu.SemaphoreType.DMA((1 + 2 * (count // block),)),
        ],
        16,
        "term",
        4,
    )[0]


def finish_kernel(count, block, place_ref, *refs):
    dq_hbm, w_hbm = refs[:2]
    arrived, (out_hbm, held, wbuf, extra, sent, sems) = refs[2:-6], refs[-6:]
    feat = sent.shape[1]
    copies = Copies(sems)
    dq_in = copies.start(dq_hbm, held)
    w_in = load_weight(copies, place_ref, 0, w_hbm, wbuf, feat, block)
    per = feat // count
    others = []
    for index, src in enumerate(arrived):
        shift, first = divmod(index, per)
        others.append(copies.start(src, extra.at[shift, :, pl.ds(first * count, count)]))
    dq_in.wait()
    for at, copy in w_in:
        copy.wait()
        wide = slice(at, at + block)
        total = dot(held[...], wbuf[wide, :], NT).astype(BF16).astype(F32)
        for index, other in enumerate(others):
            if at == index % per * count:
                other.wait()
        for shift in range(extra.shape[0]):
            total = total + extra[shift, :, wide].astype(F32)
        sent[:, wide] = total.astype(BF16)
        copies.store(sent.at[:, wide], out_hbm.at[:, wide])
    copies.finish()


def finish(d_query, w_query, place, arrived, feat):
    rows, width = d_query.shape
    count = arrived[0].shape[1]
    block = min(512, count)
    return kernel_call(
        functools.partial(finish_kernel, count, block),
        (place, d_query, w_query, *arrived),
        [SM, HB, HB] + [AN] * len(arrived),
        [((rows, feat), BF16)],
        (HB,),
        [
            pltpu.VMEM((rows, width), BF16),
            pltpu.VMEM((feat, width), BF16),
            pltpu.VMEM((len(arrived) * count // feat, rows, feat), BF16),
            pltpu.VMEM((rows, feat), BF16),
            pltpu.SemaphoreType.DMA((1 + 2 * (feat // block) + len(arrived),)),
        ],
        24,
        "finish",
        6,
    )[0]


def close_kernel(heads, hp, stages, *refs):
    pieces = refs[:stages]
    coef_ref, in_hbm, v_hbm, facts_hbm = refs[stages : stages + 4]
    rest = refs[stages + 4 : -10]
    dk_hbm, dv_hbm, kbuf, vbuf, facts_ref, dkbuf, dvbuf, kside, vside, sems = refs[-10:]
    dks, dvs = rest[: len(rest) // 2], rest[len(rest) // 2 :]
    each = heads // len(dks)
    copies = Copies(sems)
    facts_in = copies.start(facts_hbm, facts_ref)
    loads = []
    for part, (dk, dv) in enumerate(zip(dks, dvs)):
        wide = pl.ds(part * each * HDIM, each * HDIM)
        loads.append(
            (
                copies.start(v_hbm.at[:, wide], vbuf.at[:, wide]),
                copies.start(dk, dkbuf.at[:, wide]),
                copies.start(in_hbm.at[:, wide], kbuf.at[:, wide]),
                copies.start(dv, dvbuf.at[:, wide]),
            )
        )
    facts_in.wait()
    table = turned(facts_ref[...])
    for h in range(heads):
        if h % each == 0:
            for copy in loads[h // each]:
                copy.wait()
        cols = slice(h * HDIM, (h + 1) * HDIM)
        adjoint = mix(coef_ref, pieces, heads, h)
        tail, gain = column(table, 2 * hp + h), column(table, hp + h)
        carry_k = dot(vbuf[:, cols], adjoint, NT)
        kside[:, cols] = (gain * (dkbuf[:, cols].astype(F32) + tail * carry_k)).astype(BF16)
        carry_v = dot(scaled_keys(table, hp, h, kbuf[:, cols]), adjoint, NN)
        vside[:, cols] = (dvbuf[:, cols].astype(F32) + tail * carry_v).astype(BF16)
        if (h + 1) % each == 0:
            wide = slice((h + 1 - each) * HDIM, (h + 1) * HDIM)
            copies.store(kside.at[:, wide], dk_hbm.at[:, wide])
            copies.store(vside.at[:, wide], dv_hbm.at[:, wide])
    copies.finish()


def close(pieces, coefs, dks, dvs, keys, values, facts, heads, hp):
    rows, width = values.shape
    args = (coefs, keys, values, facts, *dks, *dvs)
    buf = pltpu.VMEM((rows, width), BF16)
    return kernel_call(
        functools.partial(close_kernel, heads, hp, len(pieces)),
        (*pieces, *args),
        [VM] * (len(pieces) + 1) + [HB] * (len(args) - 1),
        [((rows, width), BF16)] * 2,
        (HB,) * 2,
        [
            buf,
            buf,
            pltpu.VMEM(facts.shape, F32),
            buf,
            buf,
            buf,
            buf,
            pltpu.SemaphoreType.DMA((1 + 6 * len(dks),)),
        ],
        20,
        "close",
        100,
    )


def body(ctx_size, head_size, hidden, w_query, keys, values, d_out, log_decay):
    rows, feat = hidden.shape
    heads = log_decay.shape[1]
    width = w_query.shape[1]
    hp = sublanes(heads)
    scaling = HDIM ** (-0.5)
    me = lax.axis_index("ctx")
    mine = lax.axis_index("head")

    parts = [hidden]
    for shift in range(1, head_size):
        ring = [(i, (i + shift) % head_size) for i in range(head_size)]
        parts.append(lax.ppermute(hidden, "head", ring))
    owners = jnp.stack([(mine + head_size - s) % head_size for s in range(head_size)]).astype(jnp.int32)

    facts, msg, state = prepare(log_decay.T, keys, values, heads, hp, scaling)
    query, adjoint, amsg = project(parts, owners, w_query, d_out, facts, hp)

    wide = lambda factor: factor[:heads, None, :]
    cube = lambda flat: flat.reshape(heads, HDIM, HDIM)
    split = lambda f: (f.astype(BF16), (f - f.astype(BF16).astype(F32)).astype(BF16))
    joined = lambda pair: pair[:hp].astype(F32) + pair[hp:].astype(F32)
    stages = (ctx_size - 1).bit_length()

    def send(array, stage, up):
        dist = 1 << stage
        if stage < stages - 1:
            pairs = [(i, i ^ dist) for i in range(ctx_size)]
        else:
            pairs = [(i, i + dist) if up else (i + dist, i) for i in range(ctx_size) if not i & dist]
        return lax.ppermute(array, "ctx", pairs)

    uppers = [(me & (1 << stage)) != 0 for stage in range(stages)]
    shares, others = [joined(msg[width:])], []
    got, agot = [], []
    before, after = [jnp.ones_like(shares[0])], [jnp.ones_like(shares[0])]

    def fold_state(stage, state):
        upper, arrived = uppers[stage], cube(got[stage][:width]).astype(F32)
        theirs = joined(got[stage][width:])
        others.append(theirs)
        own, other = jnp.where(upper, 1.0, theirs), jnp.where(upper, shares[stage], 1.0)
        state = (wide(own) * cube(state) + wide(other) * arrived).reshape(width, HDIM)
        shares.append(shares[stage] * theirs)
        before.append(jnp.where(upper, before[stage] * theirs, before[stage]))
        after.append(jnp.where(upper, after[stage], after[stage] * theirs))
        msg = state.astype(BF16)
        if stage + 2 < stages:
            msg = jnp.concatenate([msg, *split(shares[-1])], axis=0)
        return msg, state

    def fold_adjoint(stage, adjoint):
        upper, arrived = uppers[stage], cube(agot[stage]).astype(F32)
        own, other = jnp.where(upper, others[stage], 1.0), jnp.where(upper, 1.0, shares[stage])
        adjoint = (wide(own) * cube(adjoint) + wide(other) * arrived).reshape(width, HDIM)
        return adjoint.astype(BF16), adjoint

    half = max(1, heads // 2)
    pending = [(first, first + half) for first in range(0, heads, half)]
    inner_parts = []

    def next_inner():
        return inner(*pending.pop(0), query, keys, values, d_out, facts, hp)

    barrier = lax.optimization_barrier
    for stage in range(stages):
        arrived = send(msg if stage < stages - 1 else msg[:width], stage, True)
        if stage == 0:
            arrived, query, adjoint, amsg = barrier((arrived, query, adjoint, amsg))
        else:
            agot.append(send(amsg, stage - 1, False))
            if pending and (stage == 1 or stage == stages - 1):
                part = next_inner()
                arrived, *part = barrier((arrived, *part))
                inner_parts.append(part)
        got.append(arrived)
        if stage < stages - 1:
            msg, state = fold_state(stage, state)
        if stage >= 1:
            agot[-1], _ = barrier((agot[-1], msg))
            amsg, adjoint = fold_adjoint(stage - 1, adjoint)
    while pending:
        inner_parts.append(next_inner())
    agot.append(send(amsg, stages - 1, False))
    got[-1], _ = barrier((got[-1], amsg))

    state_coefs = [jnp.where(u, f, 0.0)[:heads] for u, f in zip(uppers, before)]
    adjoint_coefs = [jnp.where(u, 0.0, f)[:heads] for u, f in zip(uppers, after)]
    state_coefs = jnp.concatenate(state_coefs, axis=0)
    adjoint_coefs = jnp.concatenate(adjoint_coefs, axis=0)
    dqs, dks, dvs = zip(*inner_parts)

    place = lambda shift: ((mine + shift) % head_size).astype(jnp.int32).reshape(1)
    count = feat
    arrived = []
    for shift in range(1, head_size):
        ring = [(i, (i + shift) % head_size) for i in range(head_size)]
        for first in range(0, feat, count):
            if shift == 1 and first == 0:
                d_query, term = query_term(
                    got, state_coefs, dqs, d_out, facts, w_query, place(1), feat, count, heads, hp
                )
            else:
                term = plain_term(d_query, w_query, place(shift), feat, first, count)
            arrived.append(lax.ppermute(term, "head", ring))
    d_keys, d_values = close(agot, adjoint_coefs, dks, dvs, keys, values, facts, heads, hp)
    d_hidden = finish(d_query, w_query, place(0), arrived, feat)
    return (d_hidden, d_keys, d_values)


def solution(mesh):
    return jax.shard_map(
        functools.partial(body, mesh.shape["ctx"], mesh.shape["head"]),
        mesh=mesh,
        in_specs=(
            P("ctx", "head"),
            P(None, "head"),
            P("ctx", "head"),
            P("ctx", "head"),
            P("ctx", "head"),
            P("ctx", "head"),
        ),
        out_specs=(P("ctx", "head"), P("ctx", "head"), P("ctx", "head")),
        check_vma=False,
    )
```

```python
import functools
import math

import jax
import jax.numpy as jnp
from jax import lax
from jax.experimental import pallas as pl
from jax.experimental.pallas import tpu as pltpu
from jax.sharding import PartitionSpec as P

HDIM = 128
LANES = 128
F32, BF16 = jnp.float32, jnp.bfloat16
MIB = 1 << 20
VM = pl.BlockSpec(memory_space=pltpu.VMEM)
SM = pl.BlockSpec(memory_space=pltpu.SMEM)
HB = pl.BlockSpec(memory_space=pltpu.HBM)
AN = pl.BlockSpec(memory_space=pl.ANY)

NN = (((1,), (0,)), ((), ()))
NT = (((1,), (1,)), ((), ()))
TN = (((0,), (0,)), ((), ()))


def dot(a, b, dims):
    return lax.dot_general(a, b, dims, preferred_element_type=F32)


def kernel_call(kernel, args, specs, outs, out_specs, scratch, mib, name, micros):
    pinned = [pltpu.with_memory_space_constraint(a, pltpu.HBM) if s is HB else a for a, s in zip(args, specs)]
    placed = tuple(
        (pltpu.HBM if s is HB else jax.ShapeDtypeStruct)(shape, dtype) for (shape, dtype), s in zip(outs, out_specs)
    )
    return pl.pallas_call(
        kernel,
        in_specs=specs,
        out_specs=tuple(out_specs),
        out_shape=placed,
        scratch_shapes=scratch,
        compiler_params=pltpu.CompilerParams(vmem_limit_bytes=mib * MIB),
        cost_estimate=pl.CostEstimate(flops=int(micros * 1e9), bytes_accessed=1, transcendentals=0),
        name=name,
    )(*pinned)


def sublanes(count):
    return -(-count // 8) * 8


def expm1_negative(z):
    series = jnp.full_like(z, 1.0)
    for order in range(10, 1, -1):
        series = 1.0 + z * series * (1.0 / order)
    return jnp.where(z > -0.5, z * series, jnp.exp(z) - 1.0)


def column(table, lane, width=LANES):
    return jnp.broadcast_to(table[:, lane : lane + 1], (table.shape[0], width))


class Copies:
    def __init__(self, sems):
        self.sems, self.count, self.out = sems, 0, []

    def start(self, src, dst):
        copy = pltpu.make_async_copy(src, dst, self.sems.at[self.count])
        self.count += 1
        copy.start()
        return copy

    def store(self, src, dst):
        self.out.append(self.start(src, dst))

    def finish(self):
        for copy in self.out:
            copy.wait()


def groups(heads):
    size = min(4, heads)
    return [(f, f + size, slice(f * HDIM, (f + size) * HDIM)) for f in range(0, heads, size)]


def turned(facts):
    spare = jnp.zeros((LANES - facts.shape[0], facts.shape[1]), F32)
    return jnp.concatenate([facts, spare], axis=0).T


def put_halves(upper, h, local, kept_ref, sent_ref):
    half = HDIM // 2
    at = slice(h * half, (h + 1) * half)
    kept_ref[at, :] = jnp.where(upper, local[half:], local[:half]).astype(BF16)
    sent_ref[at, :] = jnp.where(upper, local[:half], local[half:]).astype(BF16)


def prepare_kernel(
    heads, hp, scaling, ld_hbm, k_hbm, v_hbm, facts_hbm, kept_ref, sent_ref, share_ref, ld, facts_ref, kbuf, vbuf, sems
):
    upper = lax.axis_index("ctx") % 2 == 1
    rows = kbuf.shape[0]
    copies = Copies(sems)
    ld_in = copies.start(ld_hbm, ld)
    loads = []
    for _, _, wide in groups(heads):
        loads.append([copies.start(src.at[:, wide], dst.at[:, wide]) for src, dst in ((k_hbm, kbuf), (v_hbm, vbuf))])
    ld_in.wait()
    logs = ld[...]
    if heads < hp:
        logs = jnp.concatenate([logs, jnp.zeros((hp - heads, rows), F32)], axis=0)
    lane = lax.broadcasted_iota(jnp.int32, logs.shape, 1)
    cumulative = logs
    step = 1
    while step < rows:
        moved = pltpu.roll(cumulative, step, 1)
        cumulative = cumulative + jnp.where(lane >= step, moved, 0.0)
        step *= 2
    total = cumulative[:, rows - 1 :]
    gain = jnp.sqrt(-expm1_negative(2.0 * logs))
    tail = jnp.exp(total - cumulative)
    lead = scaling * jnp.exp(cumulative)
    facts = jnp.concatenate([cumulative, gain, tail, lead], axis=0)
    facts_ref[...] = facts
    copies.store(facts_ref, facts_hbm)
    table = turned(facts)
    share = jnp.broadcast_to(jnp.exp(total), (hp, LANES))
    high = share.astype(BF16)
    low = (share - high.astype(F32)).astype(BF16)
    share_ref[...] = share
    base = heads * HDIM // 2
    sent_ref[base:, :] = jnp.concatenate([high.astype(F32), low.astype(F32)], axis=0).astype(BF16)
    for (first, last, _), load in zip(groups(heads), loads):
        for copy in load:
            copy.wait()
        for h in range(first, last):
            cols = slice(h * HDIM, (h + 1) * HDIM)
            scaled = scaled_keys(table, hp, h, kbuf[:, cols])
            decayed = (column(table, 2 * hp + h) * scaled.astype(F32)).astype(BF16)
            put_halves(upper, h, dot(decayed, vbuf[:, cols], TN), kept_ref, sent_ref)
    copies.finish()


def scaled_keys(table, hp, h, keys):
    return (column(table, hp + h) * keys.astype(F32)).astype(BF16)


def prepare(logs, keys, values, heads, hp, scaling):
    rows, width = keys.shape
    buf = pltpu.VMEM((rows, width), BF16)
    return kernel_call(
        functools.partial(prepare_kernel, heads, hp, scaling),
        (logs, keys, values),
        [HB] * 3,
        [((4 * hp, rows), F32), ((width // 2, HDIM), BF16), ((width // 2 + 2 * hp, HDIM), BF16), ((hp, LANES), F32)],
        (HB, VM, VM, VM),
        [
            pltpu.VMEM((heads, rows), F32),
            pltpu.VMEM((4 * hp, rows), F32),
            buf,
            buf,
            pltpu.SemaphoreType.DMA((2 + 2 * len(groups(heads)),)),
        ],
        12,
        "prepare",
        4,
    )


def project_kernel(hp, nparts, chunk, place_ref, *refs):
    parts, (w_hbm, do_hbm, facts_hbm, q_hbm, kept_ref, sent_ref) = refs[:nparts], refs[nparts : nparts + 6]
    hbuf, wbuf, dobuf, facts_ref, qbuf, total, sems = refs[nparts + 6 :]
    rows, feat = parts[0].shape
    width = wbuf.shape[1]
    heads = width // HDIM
    upper = lax.axis_index("ctx") % 2 == 1
    copies = Copies(sems)
    loads = []
    for part, ref in enumerate(parts):
        for first in range(0, feat, chunk):
            here = pl.ds(part * feat + first, chunk)
            start = pl.multiple_of(place_ref[part] * feat + first, chunk)
            loads.append(
                (
                    slice(part * feat + first, part * feat + first + chunk),
                    copies.start(ref.at[:, pl.ds(first, chunk)], hbuf.at[:, here]),
                    copies.start(w_hbm.at[pl.ds(start, chunk), :], wbuf.at[here, :]),
                )
            )
    late = [copies.start(facts_hbm, facts_ref), copies.start(do_hbm, dobuf)]
    block = min(256, width)
    for order, (here, h_in, w_in) in enumerate(loads):
        h_in.wait()
        w_in.wait()
        for first in range(0, width, block):
            wide = slice(first, first + block)
            term = dot(hbuf[:, here], wbuf[here, wide], NN)
            if order == 0:
                total[:, wide] = term
            elif order < len(loads) - 1:
                total[:, wide] += term
            else:
                qbuf[:, wide] = (total[:, wide] + term).astype(BF16)
    for copy in late:
        copy.wait()
    copies.store(qbuf, q_hbm)
    table = turned(facts_ref[...])
    for h in range(heads):
        cols = slice(h * HDIM, (h + 1) * HDIM)
        decayed = (column(table, 3 * hp + h) * qbuf[:, cols].astype(F32)).astype(BF16)
        put_halves(upper, h, dot(decayed, dobuf[:, cols], TN), kept_ref, sent_ref)
    copies.finish()


def project(parts, owners, w_query, d_out, facts, hp):
    rows, feat = parts[0].shape
    depth, width = w_query.shape
    chunk = min(512, feat)
    return kernel_call(
        functools.partial(project_kernel, hp, len(parts), chunk),
        (owners, *parts, w_query, d_out, facts),
        [SM, HB] + [AN] * (len(parts) - 1) + [HB] * 3,
        [((rows, width), BF16), ((width // 2, HDIM), BF16), ((width // 2, HDIM), BF16)],
        (HB, VM, VM),
        [
            pltpu.VMEM((rows, depth), BF16),
            pltpu.VMEM((depth, width), BF16),
            pltpu.VMEM((rows, width), BF16),
            pltpu.VMEM(facts.shape, F32),
            pltpu.VMEM((rows, width), BF16),
            pltpu.VMEM((rows, width), F32),
            pltpu.SemaphoreType.DMA((2 * len(parts) * (feat // chunk) + 3,)),
        ],
        28,
        "project",
        8,
    )


def inner_kernel(first, last, hp, *refs):
    ins, facts_hbm, outs = refs[:4], refs[4], refs[5:8]
    bufs, facts_ref, sides, sems = refs[8:12], refs[12], refs[13:16], refs[16]
    rows = ins[0].shape[0]
    copies = Copies(sems)
    facts_in = copies.start(facts_hbm, facts_ref)
    loads = {}
    for h in range(first, last, 2):
        count = min(2, last - h)
        src, dst = pl.ds(h * HDIM, count * HDIM), pl.ds((h - first) * HDIM, count * HDIM)
        loads[h] = [copies.start(ref.at[:, src], buf.at[:, dst]) for ref, buf in zip(ins, bufs)]
    facts_in.wait()
    table = turned(facts_ref[...])
    row = lax.broadcasted_iota(jnp.int32, (rows, rows), 0)
    keep = row >= lax.broadcasted_iota(jnp.int32, (rows, rows), 1)
    shift = -0.5 * math.log2(HDIM)
    turn = math.log2(math.e)
    q_ref, k_ref, v_ref, do_ref = bufs
    for h in range(first, last):
        for copy in loads.get(h, ()):
            copy.wait()
        cols = slice((h - first) * HDIM, (h - first + 1) * HDIM)
        later = column(table, h) * turn + shift
        sooner = facts_ref[h : h + 1, :] * turn
        gap = jnp.concatenate([later] * (rows // LANES), axis=1) - sooner
        decays = jnp.exp2(jnp.where(keep, gap, -1e30))
        query, grad = q_ref[:, cols], do_ref[:, cols]
        scaled = scaled_keys(table, hp, h, k_ref[:, cols])
        wdv = (decays * dot(grad, v_ref[:, cols], NT)).astype(BF16)
        wkq = (decays * dot(query, scaled, NT)).astype(BF16)
        sides[0][:, cols] = dot(wdv, scaled, NN).astype(BF16)
        sides[1][:, cols] = dot(query, wdv, TN).T.astype(BF16)
        sides[2][:, cols] = dot(grad, wkq, TN).T.astype(BF16)
        if h + 1 == last or h + 1 in loads:
            from_head = h if h in loads else h - 1
            done = slice((from_head - first) * HDIM, (h + 1 - first) * HDIM)
            for side, out in zip(sides, outs):
                copies.store(side.at[:, done], out.at[:, done])
    copies.finish()


def inner(first, last, query, keys, values, d_out, facts, hp):
    rows = query.shape[0]
    width = (last - first) * HDIM
    pairs = -(-(last - first) // 2)
    return kernel_call(
        functools.partial(inner_kernel, first, last, hp),
        (query, keys, values, d_out, facts),
        [HB] * 5,
        [((rows, width), BF16)] * 3,
        (HB,) * 3,
        [
            *[pltpu.VMEM((rows, width), BF16)] * 4,
            pltpu.VMEM(facts.shape, F32),
            *[pltpu.VMEM((rows, width), BF16)] * 3,
            pltpu.SemaphoreType.DMA((1 + 7 * pairs,)),
        ],
        24,
        "inner",
        3,
    )


def whole_head(upper, h, mine_ref, theirs_ref):
    half = HDIM // 2
    at = slice(h * half, (h + 1) * half)
    mine, theirs = mine_ref[at, :], theirs_ref[at, :]
    return jnp.concatenate([jnp.where(upper, theirs, mine), jnp.where(upper, mine, theirs)], axis=0)


def load_weight(copies, place_ref, first, w_hbm, wbuf, feat, block):
    loads = []
    for at in range(0, wbuf.shape[0], block):
        start = pl.multiple_of(place_ref[0] * feat + first + at, block)
        loads.append((at, copies.start(w_hbm.at[pl.ds(start, block), :], wbuf.at[pl.ds(at, block), :])))
    return loads


def query_kernel(heads, hp, feat, block, place_ref, *refs):
    mine_ref, theirs_ref, do_hbm, facts_hbm, w_hbm = refs[:5]
    inner_hbm = refs[5:-9]
    dq_hbm, out_hbm, dobuf, facts_ref, wbuf, local, held, sent, sems = refs[-9:]
    upper = lax.axis_index("ctx") % 2 == 1
    copies = Copies(sems)
    each = heads // len(inner_hbm)
    facts_in = copies.start(facts_hbm, facts_ref)
    loads = []
    for part, src in enumerate(inner_hbm):
        wide = pl.ds(part * each * HDIM, each * HDIM)
        loads.append(
            (copies.start(do_hbm.at[:, wide], dobuf.at[:, wide]), copies.start(src, local.at[:, wide]))
        )
    w_in = load_weight(copies, place_ref, 0, w_hbm, wbuf, feat, block)
    facts_in.wait()
    table = turned(facts_ref[...])
    for h in range(heads):
        if h % each == 0:
            for copy in loads[h // each]:
                copy.wait()
        cols = slice(h * HDIM, (h + 1) * HDIM)
        state = whole_head(upper, h, mine_ref, theirs_ref)
        carry = dot(dobuf[:, cols], state, NT)
        held[:, cols] = (local[:, cols].astype(F32) + column(table, 3 * hp + h) * carry).astype(BF16)
    copies.store(held, dq_hbm)
    send_terms(copies, w_in, held, wbuf, sent, out_hbm, block)
    copies.finish()


def send_terms(copies, w_in, dq_ref, wbuf, sent, out_hbm, block):
    for at, copy in w_in:
        copy.wait()
        wide = slice(at, at + block)
        sent[:, wide] = dot(dq_ref[...], wbuf[wide, :], NT).astype(BF16)
        copies.store(sent.at[:, wide], out_hbm.at[:, wide])


def query_term(halves, inner_dq, d_out, facts, w_query, place, feat, count, heads, hp):
    rows, width = d_out.shape
    block = min(512, count)
    args = (d_out, facts, w_query, *inner_dq)
    return kernel_call(
        functools.partial(query_kernel, heads, hp, feat, block),
        (place, *halves, *args),
        [SM, VM, VM] + [HB] * len(args),
        [((rows, width), BF16), ((rows, count), BF16)],
        (HB, HB),
        [
            pltpu.VMEM((rows, width), BF16),
            pltpu.VMEM(facts.shape, F32),
            pltpu.VMEM((count, width), BF16),
            pltpu.VMEM((rows, width), BF16),
            pltpu.VMEM((rows, width), BF16),
            pltpu.VMEM((rows, count), BF16),
            pltpu.SemaphoreType.DMA((2 + 2 * len(inner_dq) + 2 * (count // block),)),
        ],
        20,
        "query_term",
        6,
    )


def term_kernel(feat, first, block, place_ref, dq_hbm, w_hbm, out_hbm, held, wbuf, sent, sems):
    copies = Copies(sems)
    dq_in = copies.start(dq_hbm, held)
    w_in = load_weight(copies, place_ref, first, w_hbm, wbuf, feat, block)
    dq_in.wait()
    send_terms(copies, w_in, held, wbuf, sent, out_hbm, block)
    copies.finish()


def plain_term(d_query, w_query, place, feat, first, count):
    rows, width = d_query.shape
    block = min(512, count)
    return kernel_call(
        functools.partial(term_kernel, feat, first, block),
        (place, d_query, w_query),
        [SM, HB, HB],
        [((rows, count), BF16)],
        (HB,),
        [
            pltpu.VMEM((rows, width), BF16),
            pltpu.VMEM((count, width), BF16),
            pltpu.VMEM((rows, count), BF16),
            pltpu.SemaphoreType.DMA((1 + 2 * (count // block),)),
        ],
        16,
        "term",
        4,
    )[0]


def finish_kernel(count, block, place_ref, *refs):
    dq_hbm, w_hbm = refs[:2]
    arrived, (out_hbm, held, wbuf, extra, sent, sems) = refs[2:-6], refs[-6:]
    feat = sent.shape[1]
    copies = Copies(sems)
    dq_in = copies.start(dq_hbm, held)
    w_in = load_weight(copies, place_ref, 0, w_hbm, wbuf, feat, block)
    per = feat // count
    others = []
    for index, src in enumerate(arrived):
        shift, first = divmod(index, per)
        others.append(copies.start(src, extra.at[shift, :, pl.ds(first * count, count)]))
    dq_in.wait()
    for at, copy in w_in:
        copy.wait()
        wide = slice(at, at + block)
        total = dot(held[...], wbuf[wide, :], NT).astype(BF16).astype(F32)
        for index, other in enumerate(others):
            if at == index % per * count:
                other.wait()
        for shift in range(extra.shape[0]):
            total = total + extra[shift, :, wide].astype(F32)
        sent[:, wide] = total.astype(BF16)
        copies.store(sent.at[:, wide], out_hbm.at[:, wide])
    copies.finish()


def finish(d_query, w_query, place, arrived, feat):
    rows, width = d_query.shape
    count = arrived[0].shape[1]
    block = min(512, count)
    return kernel_call(
        functools.partial(finish_kernel, count, block),
        (place, d_query, w_query, *arrived),
        [SM, HB, HB] + [AN] * len(arrived),
        [((rows, feat), BF16)],
        (HB,),
        [
            pltpu.VMEM((rows, width), BF16),
            pltpu.VMEM((feat, width), BF16),
            pltpu.VMEM((len(arrived) * count // feat, rows, feat), BF16),
            pltpu.VMEM((rows, feat), BF16),
            pltpu.SemaphoreType.DMA((1 + 2 * (feat // block) + len(arrived),)),
        ],
        24,
        "finish",
        6,
    )[0]


def close_kernel(heads, hp, *refs):
    mine_ref, theirs_ref, in_hbm, v_hbm, facts_hbm = refs[:5]
    rest = refs[5:-10]
    upper = lax.axis_index("ctx") % 2 == 1
    dk_hbm, dv_hbm, kbuf, vbuf, facts_ref, dkbuf, dvbuf, kside, vside, sems = refs[-10:]
    dks, dvs = rest[: len(rest) // 2], rest[len(rest) // 2 :]
    each = heads // len(dks)
    copies = Copies(sems)
    facts_in = copies.start(facts_hbm, facts_ref)
    loads = []
    for part, (dk, dv) in enumerate(zip(dks, dvs)):
        wide = pl.ds(part * each * HDIM, each * HDIM)
        loads.append(
            (
                copies.start(v_hbm.at[:, wide], vbuf.at[:, wide]),
                copies.start(dk, dkbuf.at[:, wide]),
                copies.start(in_hbm.at[:, wide], kbuf.at[:, wide]),
                copies.start(dv, dvbuf.at[:, wide]),
            )
        )
    facts_in.wait()
    table = turned(facts_ref[...])
    for h in range(heads):
        if h % each == 0:
            for copy in loads[h // each]:
                copy.wait()
        cols = slice(h * HDIM, (h + 1) * HDIM)
        adjoint = whole_head(upper, h, mine_ref, theirs_ref)
        tail, gain = column(table, 2 * hp + h), column(table, hp + h)
        carry_k = dot(vbuf[:, cols], adjoint, NT)
        kside[:, cols] = (gain * (dkbuf[:, cols].astype(F32) + tail * carry_k)).astype(BF16)
        carry_v = dot(scaled_keys(table, hp, h, kbuf[:, cols]), adjoint, NN)
        vside[:, cols] = (dvbuf[:, cols].astype(F32) + tail * carry_v).astype(BF16)
        if (h + 1) % each == 0:
            wide = slice((h + 1 - each) * HDIM, (h + 1) * HDIM)
            copies.store(kside.at[:, wide], dk_hbm.at[:, wide])
            copies.store(vside.at[:, wide], dv_hbm.at[:, wide])
    copies.finish()


def close(halves, dks, dvs, keys, values, facts, heads, hp):
    rows, width = values.shape
    args = (keys, values, facts, *dks, *dvs)
    buf = pltpu.VMEM((rows, width), BF16)
    return kernel_call(
        functools.partial(close_kernel, heads, hp),
        (*halves, *args),
        [VM, VM] + [HB] * len(args),
        [((rows, width), BF16)] * 2,
        (HB,) * 2,
        [
            buf,
            buf,
            pltpu.VMEM(facts.shape, F32),
            buf,
            buf,
            buf,
            buf,
            pltpu.SemaphoreType.DMA((1 + 6 * len(dks),)),
        ],
        20,
        "close",
        100,
    )


def body(ctx_size, head_size, hidden, w_query, keys, values, d_out, log_decay):
    rows, feat = hidden.shape
    heads = log_decay.shape[1]
    width = w_query.shape[1]
    hp = sublanes(heads)
    scaling = HDIM ** (-0.5)
    me = lax.axis_index("ctx")
    mine = lax.axis_index("head")

    parts = [hidden]
    for shift in range(1, head_size):
        ring = [(i, (i + shift) % head_size) for i in range(head_size)]
        parts.append(lax.ppermute(hidden, "head", ring))
    owners = jnp.stack([(mine + head_size - s) % head_size for s in range(head_size)]).astype(jnp.int32)

    facts, kept, sent, share = prepare(log_decay.T, keys, values, heads, hp, scaling)
    query, akept, asent = project(parts, owners, w_query, d_out, facts, hp)

    size = width // 2
    wide = lambda factor: factor[:heads, None, :]
    cube = lambda flat: flat[:size].reshape(heads, HDIM // 2, HDIM).astype(F32)
    flat = lambda cubes: cubes.astype(BF16).reshape(size, HDIM)
    split = lambda f: (f.astype(BF16), (f - f.astype(BF16).astype(F32)).astype(BF16))
    joined = lambda rows: rows[size : size + hp].astype(F32) + rows[size + hp :].astype(F32)
    stages = (ctx_size - 1).bit_length()
    uppers = [(me & (1 << stage)) != 0 for stage in range(stages)]

    def send(array, stage, up):
        dist = 1 << (stage % stages)
        if stage != stages - 1:
            pairs = [(i, i ^ dist) for i in range(ctx_size)]
        else:
            pairs = [(i, i + dist) if up else (i + dist, i) for i in range(ctx_size) if not i & dist]
        return lax.ppermute(array, "ctx", pairs)

    shares, others = [share], []
    before, after = [jnp.ones_like(share)], [jnp.ones_like(share)]

    def fold(stage, total, carried, arrived, up):
        upper = uppers[stage]
        first = upper if up else ~upper
        arrived = cube(arrived)
        if stage > 0:
            weight = jnp.where(first, before[stage] if up else after[stage], 0.0)
            carried = carried + wide(weight) * arrived
        if stage == stages - 1:
            lead = uppers[0] if up else ~uppers[0]
            block, other = total
            mine = jnp.where(lead, cube(other) + wide(others[0]) * carried, carried)
            theirs = jnp.where(lead, carried, cube(block) + wide(shares[0]) * carried)
            return flat(theirs), flat(mine), None
        own, other = jnp.where(first, 1.0, others[stage]), jnp.where(first, shares[stage], 1.0)
        total = wide(own) * total + wide(other) * arrived
        return flat(total), total, carried

    def fold_factors(stage, arrived):
        theirs = joined(arrived)
        others.append(theirs)
        shares.append(shares[stage] * theirs)
        upper = uppers[stage]
        pair = stage == 0
        before.append(before[stage] if pair else jnp.where(upper, before[stage] * theirs, before[stage]))
        after.append(after[stage] if pair else jnp.where(upper, after[stage], after[stage] * theirs))

    class Chain:
        def __init__(self, kept, sent, up):
            self.kept, self.sent, self.up = kept, sent, up
            self.total, self.carried, self.stage, self.arrived = cube(kept), jnp.zeros_like(cube(kept)), 0, None

        def go(self):
            self.arrived = send(self.sent, self.stage, self.up)

        def take(self):
            stage, self.stage = self.stage, self.stage + 1
            if stage == 0:
                self.first = self.arrived
            total = self.total if stage < stages - 1 else (self.kept, self.first)
            if self.up and stage < stages - 1:
                fold_factors(stage, self.arrived)
            self.sent, self.total, self.carried = fold(stage, total, self.carried, self.arrived, self.up)
            if self.up and stage + 2 < stages:
                self.sent = jnp.concatenate([self.sent, *split(shares[-1])], axis=0)

    states, adjoints = Chain(kept, sent, True), Chain(akept, asent, False)
    half = max(1, heads // 2)
    pending = [(first, first + half) for first in range(0, heads, half)]
    inner_parts = []
    barrier = lax.optimization_barrier
    for stage in range(stages + 1):
        states.go()
        if stage == 0:
            states.arrived, query, adjoints.kept, adjoints.sent = barrier(
                (states.arrived, query, adjoints.kept, adjoints.sent)
            )
            adjoints.total = cube(adjoints.kept)
        else:
            adjoints.go()
            if pending:
                query, _ = barrier((query, adjoints.sent))
                part = inner(*pending.pop(0), query, keys, values, d_out, facts, hp)
                states.arrived, *part = barrier((states.arrived, *part))
                inner_parts.append(part)
        if stage < stages:
            states.take()
        if stage >= 1:
            adjoints.arrived, _ = barrier((adjoints.arrived, states.sent if stage < stages else states.total))
            adjoints.take()
    while pending:
        inner_parts.append(inner(*pending.pop(0), query, keys, values, d_out, facts, hp))
    adjoints.go()
    states.arrived, _ = barrier((states.arrived, adjoints.sent))
    state_halves = (states.total, states.arrived)
    adjoint_halves = (adjoints.total, adjoints.arrived)
    dqs, dks, dvs = zip(*inner_parts)

    place = lambda shift: ((mine + shift) % head_size).astype(jnp.int32).reshape(1)
    count = feat
    arrived = []
    for shift in range(1, head_size):
        ring = [(i, (i + shift) % head_size) for i in range(head_size)]
        for first in range(0, feat, count):
            if shift == 1 and first == 0:
                d_query, term = query_term(
                    state_halves, dqs, d_out, facts, w_query, place(1), feat, count, heads, hp
                )
            else:
                term = plain_term(d_query, w_query, place(shift), feat, first, count)
            arrived.append(lax.ppermute(term, "head", ring))
    d_keys, d_values = close(adjoint_halves, dks, dvs, keys, values, facts, heads, hp)
    d_hidden = finish(d_query, w_query, place(0), arrived, feat)
    return (d_hidden, d_keys, d_values)


def solution(mesh):
    return jax.shard_map(
        functools.partial(body, mesh.shape["ctx"], mesh.shape["head"]),
        mesh=mesh,
        in_specs=(
            P("ctx", "head"),
            P(None, "head"),
            P("ctx", "head"),
            P("ctx", "head"),
            P("ctx", "head"),
            P("ctx", "head"),
        ),
        out_specs=(P("ctx", "head"), P("ctx", "head"), P("ctx", "head")),
        check_vma=False,
    )
```

```python
import functools
import math

import jax
import jax.numpy as jnp
from jax import lax
from jax.experimental import pallas as pl
from jax.experimental.pallas import tpu as pltpu
from jax.sharding import PartitionSpec as P

HDIM = 128
LANES = 128
F32, BF16 = jnp.float32, jnp.bfloat16
MIB = 1 << 20
VM = pl.BlockSpec(memory_space=pltpu.VMEM)
SM = pl.BlockSpec(memory_space=pltpu.SMEM)
HB = pl.BlockSpec(memory_space=pltpu.HBM)
AN = pl.BlockSpec(memory_space=pl.ANY)

NN = (((1,), (0,)), ((), ()))
NT = (((1,), (1,)), ((), ()))
TN = (((0,), (0,)), ((), ()))


def dot(a, b, dims):
    return lax.dot_general(a, b, dims, preferred_element_type=F32)


def kernel_call(kernel, args, specs, outs, out_specs, scratch, mib, name, micros):
    pinned = [pltpu.with_memory_space_constraint(a, pltpu.HBM) if s is HB else a for a, s in zip(args, specs)]
    placed = tuple(
        (pltpu.HBM if s is HB else jax.ShapeDtypeStruct)(shape, dtype) for (shape, dtype), s in zip(outs, out_specs)
    )
    return pl.pallas_call(
        kernel,
        in_specs=specs,
        out_specs=tuple(out_specs),
        out_shape=placed,
        scratch_shapes=scratch,
        compiler_params=pltpu.CompilerParams(vmem_limit_bytes=mib * MIB),
        cost_estimate=pl.CostEstimate(flops=int(micros * 1e9), bytes_accessed=1, transcendentals=0),
        name=name,
    )(*pinned)


def sublanes(count):
    return -(-count // 8) * 8


def expm1_negative(z):
    series = jnp.full_like(z, 1.0)
    for order in range(10, 1, -1):
        series = 1.0 + z * series * (1.0 / order)
    return jnp.where(z > -0.5, z * series, jnp.exp(z) - 1.0)


def column(table, lane, width=LANES):
    return jnp.broadcast_to(table[:, lane : lane + 1], (table.shape[0], width))


class Copies:
    def __init__(self, sems):
        self.sems, self.count, self.out = sems, 0, []

    def start(self, src, dst):
        copy = pltpu.make_async_copy(src, dst, self.sems.at[self.count])
        self.count += 1
        copy.start()
        return copy

    def store(self, src, dst):
        self.out.append(self.start(src, dst))

    def finish(self):
        for copy in self.out:
            copy.wait()


def spans_of(heads):
    half, quarter = heads // 2, heads // 4
    edges = sorted({0, half, half + quarter, heads})
    return list(zip(edges, edges[1:]))


def groups(heads):
    size = min(4, heads)
    return [(f, f + size, slice(f * HDIM, (f + size) * HDIM)) for f in range(0, heads, size)]


def turned(facts):
    spare = jnp.zeros((LANES - facts.shape[0], facts.shape[1]), F32)
    return jnp.concatenate([facts, spare], axis=0).T


def put_halves(upper, h, local, kept_ref, sent_ref):
    half = HDIM // 2
    at = slice(h * half, (h + 1) * half)
    kept_ref[at, :] = jnp.where(upper, local[half:], local[:half]).astype(BF16)
    sent_ref[at, :] = jnp.where(upper, local[:half], local[half:]).astype(BF16)


def prepare_kernel(
    heads, hp, scaling, ld_hbm, k_hbm, v_hbm, facts_hbm, kept_ref, sent_ref, share_ref, ld, facts_ref, kbuf, vbuf, sems
):
    upper = lax.axis_index("ctx") % 2 == 1
    rows = kbuf.shape[0]
    copies = Copies(sems)
    ld_in = copies.start(ld_hbm, ld)
    loads = []
    for _, _, wide in groups(heads):
        loads.append([copies.start(src.at[:, wide], dst.at[:, wide]) for src, dst in ((k_hbm, kbuf), (v_hbm, vbuf))])
    ld_in.wait()
    logs = ld[...]
    if heads < hp:
        logs = jnp.concatenate([logs, jnp.zeros((hp - heads, rows), F32)], axis=0)
    lane = lax.broadcasted_iota(jnp.int32, logs.shape, 1)
    cumulative = logs
    step = 1
    while step < rows:
        moved = pltpu.roll(cumulative, step, 1)
        cumulative = cumulative + jnp.where(lane >= step, moved, 0.0)
        step *= 2
    total = cumulative[:, rows - 1 :]
    gain = jnp.sqrt(-expm1_negative(2.0 * logs))
    tail = jnp.exp(total - cumulative)
    lead = scaling * jnp.exp(cumulative)
    facts = jnp.concatenate([cumulative, gain, tail, lead], axis=0)
    facts_ref[...] = facts
    copies.store(facts_ref, facts_hbm)
    table = turned(facts)
    share = jnp.broadcast_to(jnp.exp(total), (hp, LANES))
    high = share.astype(BF16)
    low = (share - high.astype(F32)).astype(BF16)
    share_ref[...] = share
    base = heads * HDIM // 2
    sent_ref[base:, :] = jnp.concatenate([high.astype(F32), low.astype(F32)], axis=0).astype(BF16)
    for (first, last, _), load in zip(groups(heads), loads):
        for copy in load:
            copy.wait()
        for h in range(first, last):
            cols = slice(h * HDIM, (h + 1) * HDIM)
            scaled = scaled_keys(table, hp, h, kbuf[:, cols])
            decayed = (column(table, 2 * hp + h) * scaled.astype(F32)).astype(BF16)
            put_halves(upper, h, dot(decayed, vbuf[:, cols], TN), kept_ref, sent_ref)
    copies.finish()


def scaled_keys(table, hp, h, keys):
    return (column(table, hp + h) * keys.astype(F32)).astype(BF16)


def prepare(logs, keys, values, heads, hp, scaling):
    rows, width = keys.shape
    buf = pltpu.VMEM((rows, width), BF16)
    return kernel_call(
        functools.partial(prepare_kernel, heads, hp, scaling),
        (logs, keys, values),
        [HB] * 3,
        [((4 * hp, rows), F32), ((width // 2, HDIM), BF16), ((width // 2 + 2 * hp, HDIM), BF16), ((hp, LANES), F32)],
        (HB, VM, VM, VM),
        [
            pltpu.VMEM((heads, rows), F32),
            pltpu.VMEM((4 * hp, rows), F32),
            buf,
            buf,
            pltpu.SemaphoreType.DMA((2 + 2 * len(groups(heads)),)),
        ],
        12,
        "prepare",
        4,
    )


def project_kernel(hp, nparts, chunks, place_ref, *refs):
    parts, (w_hbm, do_hbm, facts_hbm, q_hbm, kept_ref, sent_ref) = refs[:nparts], refs[nparts : nparts + 6]
    hbuf, wbuf, dobuf, facts_ref, qbuf, total, sems = refs[nparts + 6 :]
    rows, feat = parts[0].shape
    width = wbuf.shape[1]
    upper = lax.axis_index("ctx") % 2 == 1
    copies = Copies(sems)
    loads = []
    for part, first, size in chunks:
        at = part * feat + first
        start = pl.multiple_of(place_ref[part] * feat + first, math.gcd(feat, first) if first else feat)
        loads.append(
            (
                slice(at, at + size),
                copies.start(parts[part].at[:, pl.ds(first, size)], hbuf.at[:, pl.ds(at, size)]),
                copies.start(w_hbm.at[pl.ds(start, size), :], wbuf.at[pl.ds(at, size), :]),
            )
        )
        if len(loads) == min(4, len(chunks)):
            late = [copies.start(facts_hbm, facts_ref), copies.start(do_hbm, dobuf)]
    block = min(256, width)
    for order, (here, h_in, w_in) in enumerate(loads):
        h_in.wait()
        w_in.wait()
        if order == len(loads) - 1:
            for copy in late:
                copy.wait()
            table = turned(facts_ref[...])
        for first in range(0, width, block):
            wide = slice(first, first + block)
            term = dot(hbuf[:, here], wbuf[here, wide], NN)
            if order > 0:
                term = total[:, wide] + term
            if order < len(loads) - 1:
                total[:, wide] = term
                continue
            qbuf[:, wide] = term.astype(BF16)
            copies.store(qbuf.at[:, wide], q_hbm.at[:, wide])
            for h in range(first // HDIM, (first + block) // HDIM):
                cols = slice(h * HDIM, (h + 1) * HDIM)
                decayed = (column(table, 3 * hp + h) * qbuf[:, cols].astype(F32)).astype(BF16)
                put_halves(upper, h, dot(decayed, dobuf[:, cols], TN), kept_ref, sent_ref)
    copies.finish()


def project(parts, owners, w_query, d_out, facts, hp):
    rows, feat = parts[0].shape
    depth, width = w_query.shape
    chunks = []
    for part in range(len(parts)):
        sizes = [feat] if feat % 1024 else ([256, 256, 512] + [1024] * (feat // 1024 - 1) if part == 0 else [1024] * (feat // 1024))
        for order, size in enumerate(sizes):
            chunks.append((part, sum(sizes[:order]), size))
    return kernel_call(
        functools.partial(project_kernel, hp, len(parts), chunks),
        (owners, *parts, w_query, d_out, facts),
        [SM, HB] + [AN] * (len(parts) - 1) + [HB] * 3,
        [((rows, width), BF16), ((width // 2, HDIM), BF16), ((width // 2, HDIM), BF16)],
        (HB, VM, VM),
        [
            pltpu.VMEM((rows, depth), BF16),
            pltpu.VMEM((depth, width), BF16),
            pltpu.VMEM((rows, width), BF16),
            pltpu.VMEM(facts.shape, F32),
            pltpu.VMEM((rows, width), BF16),
            pltpu.VMEM((rows, width), F32),
            pltpu.SemaphoreType.DMA((2 * len(chunks) + 2 + width // min(256, width),)),
        ],
        28,
        "project",
        8,
    )


def inner_kernel(first, last, hp, *refs):
    ins, facts_hbm, outs = refs[:4], refs[4], refs[5:8]
    bufs, facts_ref, sides, sems = refs[8:12], refs[12], refs[13:16], refs[16]
    rows = ins[0].shape[0]
    copies = Copies(sems)
    facts_in = copies.start(facts_hbm, facts_ref)
    loads = {}
    for h in range(first, last, 2):
        count = min(2, last - h)
        src, dst = pl.ds(h * HDIM, count * HDIM), pl.ds((h - first) * HDIM, count * HDIM)
        loads[h] = [copies.start(ref.at[:, src], buf.at[:, dst]) for ref, buf in zip(ins, bufs)]
    facts_in.wait()
    table = turned(facts_ref[...])
    row = lax.broadcasted_iota(jnp.int32, (rows, rows), 0)
    keep = row >= lax.broadcasted_iota(jnp.int32, (rows, rows), 1)
    shift = -0.5 * math.log2(HDIM)
    turn = math.log2(math.e)
    q_ref, k_ref, v_ref, do_ref = bufs
    for h in range(first, last):
        for copy in loads.get(h, ()):
            copy.wait()
        cols = slice((h - first) * HDIM, (h - first + 1) * HDIM)
        later = column(table, h) * turn + shift
        sooner = facts_ref[h : h + 1, :] * turn
        gap = jnp.concatenate([later] * (rows // LANES), axis=1) - sooner
        decays = jnp.exp2(jnp.where(keep, gap, -1e30))
        query, grad = q_ref[:, cols], do_ref[:, cols]
        scaled = scaled_keys(table, hp, h, k_ref[:, cols])
        wdv = (decays * dot(grad, v_ref[:, cols], NT)).astype(BF16)
        wkq = (decays * dot(query, scaled, NT)).astype(BF16)
        sides[0][:, cols] = dot(wdv, scaled, NN).astype(BF16)
        sides[1][:, cols] = dot(query, wdv, TN).T.astype(BF16)
        sides[2][:, cols] = dot(grad, wkq, TN).T.astype(BF16)
        if h + 1 == last or h + 1 in loads:
            from_head = h if h in loads else h - 1
            done = slice((from_head - first) * HDIM, (h + 1 - first) * HDIM)
            for side, out in zip(sides, outs):
                copies.store(side.at[:, done], out.at[:, done])
    copies.finish()


def inner(first, last, query, keys, values, d_out, facts, hp):
    rows = query.shape[0]
    width = (last - first) * HDIM
    pairs = -(-(last - first) // 2)
    return kernel_call(
        functools.partial(inner_kernel, first, last, hp),
        (query, keys, values, d_out, facts),
        [HB] * 5,
        [((rows, width), BF16)] * 3,
        (HB,) * 3,
        [
            *[pltpu.VMEM((rows, width), BF16)] * 4,
            pltpu.VMEM(facts.shape, F32),
            *[pltpu.VMEM((rows, width), BF16)] * 3,
            pltpu.SemaphoreType.DMA((1 + 7 * pairs,)),
        ],
        24,
        "inner",
        1,
    )


def whole_head(upper, h, mine_ref, theirs_ref):
    half = HDIM // 2
    at = slice(h * half, (h + 1) * half)
    mine, theirs = mine_ref[at, :], theirs_ref[at, :]
    return jnp.concatenate([jnp.where(upper, theirs, mine), jnp.where(upper, mine, theirs)], axis=0)


def load_weight(copies, place_ref, first, w_hbm, wbuf, feat, blocks):
    loads, at = [], 0
    for block in blocks:
        start = pl.multiple_of(place_ref[0] * feat + first + at, block)
        loads.append((at, block, copies.start(w_hbm.at[pl.ds(start, block), :], wbuf.at[pl.ds(at, block), :])))
        at += block
    return loads


def query_kernel(heads, hp, feat, blocks, place_ref, *refs):
    mine_ref, theirs_ref, do_hbm, facts_hbm, w_hbm = refs[:5]
    inner_hbm = refs[5:-7]
    held, out_ref, dobuf, facts_ref, wbuf, local, sems = refs[-7:]
    upper = lax.axis_index("ctx") % 2 == 1
    copies = Copies(sems)
    facts_in = copies.start(facts_hbm, facts_ref)
    loads = {}
    for (first, last), src in zip(spans_of(heads), inner_hbm):
        wide = pl.ds(first * HDIM, (last - first) * HDIM)
        loads[first] = (copies.start(do_hbm.at[:, wide], dobuf.at[:, wide]), copies.start(src, local.at[:, wide]))
    w_in = load_weight(copies, place_ref, 0, w_hbm, wbuf, feat, blocks)
    facts_in.wait()
    table = turned(facts_ref[...])
    for h in range(heads):
        for copy in loads.get(h, ()):
            copy.wait()
        cols = slice(h * HDIM, (h + 1) * HDIM)
        state = whole_head(upper, h, mine_ref, theirs_ref)
        carry = dot(dobuf[:, cols], state, NT)
        held[:, cols] = (local[:, cols].astype(F32) + column(table, 3 * hp + h) * carry).astype(BF16)
    put_terms(w_in, held, wbuf, out_ref)


def put_terms(w_in, dq_ref, wbuf, out_ref):
    for at, block, copy in w_in:
        copy.wait()
        wide = slice(at, at + block)
        out_ref[:, wide] = dot(dq_ref[...], wbuf[wide, :], NT).astype(BF16)


def query_term(halves, inner_dq, d_out, facts, w_query, place, feat, count, heads, hp):
    rows, width = d_out.shape
    blocks = blocks_of(count)
    args = (d_out, facts, w_query, *inner_dq)
    return kernel_call(
        functools.partial(query_kernel, heads, hp, feat, blocks),
        (place, *halves, *args),
        [SM, VM, VM] + [HB] * len(args),
        [((rows, width), BF16), ((rows, count), BF16)],
        (VM, VM),
        [
            pltpu.VMEM((rows, width), BF16),
            pltpu.VMEM(facts.shape, F32),
            pltpu.VMEM((count, width), BF16),
            pltpu.VMEM((rows, width), BF16),
            pltpu.SemaphoreType.DMA((1 + 2 * len(inner_dq) + len(blocks),)),
        ],
        16,
        "query_term",
        6,
    )


def term_kernel(feat, first, blocks, place_ref, dq_ref, w_hbm, out_ref, wbuf, sems):
    copies = Copies(sems)
    put_terms(load_weight(copies, place_ref, first, w_hbm, wbuf, feat, blocks), dq_ref, wbuf, out_ref)


def plain_term(d_query, w_query, place, feat, first, count):
    rows, width = d_query.shape
    blocks = blocks_of(count)
    return kernel_call(
        functools.partial(term_kernel, feat, first, blocks),
        (place, d_query, w_query),
        [SM, VM, HB],
        [((rows, count), BF16)],
        (VM,),
        [
            pltpu.VMEM((count, width), BF16),
            pltpu.SemaphoreType.DMA((len(blocks),)),
        ],
        16,
        "term",
        4,
    )[0]


def finish_kernel(count, blocks, place_ref, dq_ref, w_hbm, *refs):
    arrived, (out_hbm, wbuf, sent, sems) = refs[:-4], refs[-4:]
    feat = sent.shape[1]
    per = feat // count
    copies = Copies(sems)
    w_in = load_weight(copies, place_ref, 0, w_hbm, wbuf, feat, blocks)
    for at, block, copy in w_in:
        copy.wait()
        wide = slice(at, at + block)
        total = dot(dq_ref[...], wbuf[wide, :], NT).astype(BF16).astype(F32)
        part, here = at // count, slice(at % count, at % count + block)
        for shift in range(len(arrived) // per):
            total = total + arrived[shift * per + part][:, here].astype(F32)
        sent[:, wide] = total.astype(BF16)
        copies.store(sent.at[:, wide], out_hbm.at[:, wide])
    copies.finish()


def blocks_of(count):
    if count % 512 or count < 1024:
        return [count]
    return [256, 256] + [512] * (count // 512 - 2) + [256, 256]


def finish(d_query, w_query, place, arrived, feat):
    rows, width = d_query.shape
    count = arrived[0].shape[1]
    blocks = blocks_of(feat) if count == feat else [count] * (feat // count)
    return kernel_call(
        functools.partial(finish_kernel, count, blocks),
        (place, d_query, w_query, *arrived),
        [SM, VM, HB] + [VM] * len(arrived),
        [((rows, feat), BF16)],
        (HB,),
        [
            pltpu.VMEM((feat, width), BF16),
            pltpu.VMEM((rows, feat), BF16),
            pltpu.SemaphoreType.DMA((2 * len(blocks),)),
        ],
        16,
        "finish",
        6,
    )[0]


def close_kernel(heads, hp, *refs):
    mine_ref, theirs_ref, in_hbm, v_hbm, facts_hbm = refs[:5]
    rest = refs[5:-10]
    upper = lax.axis_index("ctx") % 2 == 1
    dk_hbm, dv_hbm, kbuf, vbuf, facts_ref, dkbuf, dvbuf, kside, vside, sems = refs[-10:]
    dks, dvs = rest[: len(rest) // 2], rest[len(rest) // 2 :]
    pair = 2 if all(edge % 2 == 0 for span in spans_of(heads) for edge in span) else 1
    copies = Copies(sems)
    facts_in = copies.start(facts_hbm, facts_ref)
    loads = []
    for (start, last), dk, dv in zip(spans_of(heads), dks, dvs):
        for h in range(start, last, pair):
            wide = pl.ds(h * HDIM, pair * HDIM)
            part = pl.ds((h - start) * HDIM, pair * HDIM)
            loads.append(
                (
                    copies.start(v_hbm.at[:, wide], vbuf.at[:, wide]),
                    copies.start(dk.at[:, part], dkbuf.at[:, wide]),
                    copies.start(in_hbm.at[:, wide], kbuf.at[:, wide]),
                    copies.start(dv.at[:, part], dvbuf.at[:, wide]),
                )
            )
    facts_in.wait()
    table = turned(facts_ref[...])
    for h in range(heads):
        if h % pair == 0:
            for copy in loads[h // pair]:
                copy.wait()
        cols = slice(h * HDIM, (h + 1) * HDIM)
        adjoint = whole_head(upper, h, mine_ref, theirs_ref)
        tail, gain = column(table, 2 * hp + h), column(table, hp + h)
        carry_k = dot(vbuf[:, cols], adjoint, NT)
        kside[:, cols] = (gain * (dkbuf[:, cols].astype(F32) + tail * carry_k)).astype(BF16)
        carry_v = dot(scaled_keys(table, hp, h, kbuf[:, cols]), adjoint, NN)
        vside[:, cols] = (dvbuf[:, cols].astype(F32) + tail * carry_v).astype(BF16)
        if (h + 1) % pair == 0:
            wide = slice((h + 1 - pair) * HDIM, (h + 1) * HDIM)
            copies.store(kside.at[:, wide], dk_hbm.at[:, wide])
            copies.store(vside.at[:, wide], dv_hbm.at[:, wide])
    copies.finish()


def close(halves, dks, dvs, keys, values, facts, heads, hp):
    rows, width = values.shape
    args = (keys, values, facts, *dks, *dvs)
    buf = pltpu.VMEM((rows, width), BF16)
    return kernel_call(
        functools.partial(close_kernel, heads, hp),
        (*halves, *args),
        [VM, VM] + [HB] * len(args),
        [((rows, width), BF16)] * 2,
        (HB,) * 2,
        [
            buf,
            buf,
            pltpu.VMEM(facts.shape, F32),
            buf,
            buf,
            buf,
            buf,
            pltpu.SemaphoreType.DMA((1 + 6 * heads,)),
        ],
        20,
        "close",
        100,
    )


def body(ctx_size, head_size, hidden, w_query, keys, values, d_out, log_decay):
    rows, feat = hidden.shape
    heads = log_decay.shape[1]
    width = w_query.shape[1]
    hp = sublanes(heads)
    scaling = HDIM ** (-0.5)
    me = lax.axis_index("ctx")
    mine = lax.axis_index("head")

    parts = [hidden]
    for shift in range(1, head_size):
        ring = [(i, (i + shift) % head_size) for i in range(head_size)]
        parts.append(lax.ppermute(hidden, "head", ring))
    owners = jnp.stack([(mine + head_size - s) % head_size for s in range(head_size)]).astype(jnp.int32)

    facts, kept, sent, share = prepare(log_decay.T, keys, values, heads, hp, scaling)
    query, akept, asent = project(parts, owners, w_query, d_out, facts, hp)

    size = width // 2
    wide = lambda factor: factor[:heads, None, :]
    cube = lambda flat: flat[:size].reshape(heads, HDIM // 2, HDIM).astype(F32)
    flat = lambda cubes: cubes.astype(BF16).reshape(size, HDIM)
    split = lambda f: (f.astype(BF16), (f - f.astype(BF16).astype(F32)).astype(BF16))
    joined = lambda rows: rows[size : size + hp].astype(F32) + rows[size + hp :].astype(F32)
    stages = (ctx_size - 1).bit_length()
    uppers = [(me & (1 << stage)) != 0 for stage in range(stages)]

    def send(array, stage):
        dist = 1 << (stage % stages)
        return lax.ppermute(array, "ctx", [(i, i ^ dist) for i in range(ctx_size)])

    shares, others = [share], []
    before, after = [jnp.ones_like(share)], [jnp.ones_like(share)]

    def fold(stage, total, carried, arrived, up):
        upper = uppers[stage]
        first = upper if up else ~upper
        arrived = cube(arrived)
        if stage > 0:
            weight = jnp.where(first, before[stage] if up else after[stage], 0.0)
            carried = carried + wide(weight) * arrived
        if stage == stages - 1:
            lead = uppers[0] if up else ~uppers[0]
            block, other = total
            mine = jnp.where(lead, cube(other) + wide(others[0]) * carried, carried)
            theirs = jnp.where(lead, carried, cube(block) + wide(shares[0]) * carried)
            return flat(theirs), flat(mine), None
        own, other = jnp.where(first, 1.0, others[stage]), jnp.where(first, shares[stage], 1.0)
        total = wide(own) * total + wide(other) * arrived
        return flat(total), total, carried

    def fold_factors(stage, arrived):
        theirs = joined(arrived)
        others.append(theirs)
        shares.append(shares[stage] * theirs)
        upper = uppers[stage]
        pair = stage == 0
        before.append(before[stage] if pair else jnp.where(upper, before[stage] * theirs, before[stage]))
        after.append(after[stage] if pair else jnp.where(upper, after[stage], after[stage] * theirs))

    class Chain:
        def __init__(self, kept, sent, up):
            self.kept, self.sent, self.up = kept, sent, up
            self.total, self.carried, self.stage, self.arrived = cube(kept), jnp.zeros_like(cube(kept)), 0, None

        def go(self):
            self.arrived = send(self.sent, self.stage)

        def take(self):
            stage, self.stage = self.stage, self.stage + 1
            if stage == 0:
                self.first = self.arrived
            total = self.total if stage < stages - 1 else (self.kept, self.first)
            if self.up and stage < stages - 1:
                fold_factors(stage, self.arrived)
            self.sent, self.total, self.carried = fold(stage, total, self.carried, self.arrived, self.up)
            if self.up and stage + 2 < stages:
                self.sent = jnp.concatenate([self.sent, *split(shares[-1])], axis=0)

    states, adjoints = Chain(kept, sent, True), Chain(akept, asent, False)
    spans = spans_of(heads)
    pending = list(spans)
    inner_parts = []
    barrier = lax.optimization_barrier
    for stage in range(stages + 1):
        states.go()
        if stage == 0:
            states.arrived, query, adjoints.kept, adjoints.sent = barrier(
                (states.arrived, query, adjoints.kept, adjoints.sent)
            )
            adjoints.total = cube(adjoints.kept)
        else:
            adjoints.go()
            if pending and stage <= len(spans):
                query, _ = barrier((query, adjoints.sent))
                part = inner(*pending.pop(0), query, keys, values, d_out, facts, hp)
                states.arrived, *part = barrier((states.arrived, *part))
                inner_parts.append(part)
        if stage < stages:
            states.take()
        if stage >= 1:
            adjoints.arrived, _ = barrier((adjoints.arrived, states.sent if stage < stages else states.total))
            adjoints.take()
    while pending:
        inner_parts.append(inner(*pending.pop(0), query, keys, values, d_out, facts, hp))
    adjoints.go()
    states.arrived, _ = barrier((states.arrived, adjoints.sent))
    state_halves = (states.total, states.arrived)
    adjoint_halves = (adjoints.total, adjoints.arrived)
    dqs, dks, dvs = zip(*inner_parts)

    place = lambda shift: ((mine + shift) % head_size).astype(jnp.int32).reshape(1)
    count = feat
    arrived = []
    for shift in range(1, head_size):
        ring = [(i, (i + shift) % head_size) for i in range(head_size)]
        for first in range(0, feat, count):
            if shift == 1 and first == 0:
                d_query, term = query_term(
                    state_halves, dqs, d_out, facts, w_query, place(1), feat, count, heads, hp
                )
            else:
                term = plain_term(d_query, w_query, place(shift), feat, first, count)
            arrived.append(lax.ppermute(term, "head", ring))
    d_keys, d_values = close(adjoint_halves, dks, dvs, keys, values, facts, heads, hp)
    d_hidden = finish(d_query, w_query, place(0), arrived, feat)
    return (d_hidden, d_keys, d_values)


def solution(mesh):
    return jax.shard_map(
        functools.partial(body, mesh.shape["ctx"], mesh.shape["head"]),
        mesh=mesh,
        in_specs=(
            P("ctx", "head"),
            P(None, "head"),
            P("ctx", "head"),
            P("ctx", "head"),
            P("ctx", "head"),
            P("ctx", "head"),
        ),
        out_specs=(P("ctx", "head"), P("ctx", "head"), P("ctx", "head")),
        check_vma=False,
    )
```

```python
import functools
import math

import jax
import jax.numpy as jnp
from jax import lax
from jax.experimental import pallas as pl
from jax.experimental.pallas import tpu as pltpu
from jax.sharding import PartitionSpec as P

HDIM = 128
LANES = 128
F32, BF16 = jnp.float32, jnp.bfloat16
MIB = 1 << 20
VM = pl.BlockSpec(memory_space=pltpu.VMEM)
SM = pl.BlockSpec(memory_space=pltpu.SMEM)
HB = pl.BlockSpec(memory_space=pltpu.HBM)
AN = pl.BlockSpec(memory_space=pl.ANY)

NN = (((1,), (0,)), ((), ()))
NT = (((1,), (1,)), ((), ()))
TN = (((0,), (0,)), ((), ()))


def dot(a, b, dims):
    return lax.dot_general(a, b, dims, preferred_element_type=F32)


def kernel_call(kernel, args, specs, outs, out_specs, scratch, mib, name, micros):
    pinned = [pltpu.with_memory_space_constraint(a, pltpu.HBM) if s is HB else a for a, s in zip(args, specs)]
    placed = tuple(
        (pltpu.HBM if s is HB else jax.ShapeDtypeStruct)(shape, dtype) for (shape, dtype), s in zip(outs, out_specs)
    )
    return pl.pallas_call(
        kernel,
        in_specs=specs,
        out_specs=tuple(out_specs),
        out_shape=placed,
        scratch_shapes=scratch,
        compiler_params=pltpu.CompilerParams(vmem_limit_bytes=mib * MIB),
        cost_estimate=pl.CostEstimate(flops=int(micros * 1e9), bytes_accessed=1, transcendentals=0),
        name=name,
    )(*pinned)


def sublanes(count):
    return -(-count // 8) * 8


def expm1_negative(z):
    series = jnp.full_like(z, 1.0)
    for order in range(10, 1, -1):
        series = 1.0 + z * series * (1.0 / order)
    return jnp.where(z > -0.5, z * series, jnp.exp(z) - 1.0)


def column(table, lane, width=LANES):
    return jnp.broadcast_to(table[:, lane : lane + 1], (table.shape[0], width))


class Copies:
    def __init__(self, sems):
        self.sems, self.count, self.out = sems, 0, []

    def start(self, src, dst):
        copy = pltpu.make_async_copy(src, dst, self.sems.at[self.count])
        self.count += 1
        copy.start()
        return copy

    def store(self, src, dst):
        self.out.append(self.start(src, dst))

    def finish(self):
        for copy in self.out:
            copy.wait()


def spans_of(heads):
    half, quarter = heads // 2, heads // 4
    edges = sorted({0, half, half + quarter, heads})
    return list(zip(edges, edges[1:]))


def groups(heads):
    size = min(4, heads)
    return [(f, f + size, slice(f * HDIM, (f + size) * HDIM)) for f in range(0, heads, size)]


def turned(facts):
    spare = jnp.zeros((LANES - facts.shape[0], facts.shape[1]), F32)
    return jnp.concatenate([facts, spare], axis=0).T


def put_halves(upper, h, local, kept_ref, sent_ref):
    half = HDIM // 2
    at = slice(h * half, (h + 1) * half)
    kept_ref[at, :] = jnp.where(upper, local[half:], local[:half]).astype(BF16)
    sent_ref[at, :] = jnp.where(upper, local[:half], local[half:]).astype(BF16)


def prepare_kernel(
    heads, hp, scaling, ld_hbm, k_hbm, v_hbm, facts_hbm, kept_ref, sent_ref, share_ref, *scratch
):
    ld, facts_ref, kbuf, vbuf, sems = scratch
    upper = lax.axis_index("ctx") % 2 == 1
    rows = kbuf.shape[0]
    copies = Copies(sems)
    ld_in = copies.start(ld_hbm, ld)
    loads = []
    for _, _, wide in groups(heads):
        loads.append([copies.start(src.at[:, wide], dst.at[:, wide]) for src, dst in ((k_hbm, kbuf), (v_hbm, vbuf))])
    ld_in.wait()
    logs = ld[...]
    if heads < hp:
        logs = jnp.concatenate([logs, jnp.zeros((hp - heads, rows), F32)], axis=0)
    lane = lax.broadcasted_iota(jnp.int32, logs.shape, 1)
    cumulative = logs
    step = 1
    while step < rows:
        moved = pltpu.roll(cumulative, step, 1)
        cumulative = cumulative + jnp.where(lane >= step, moved, 0.0)
        step *= 2
    total = cumulative[:, rows - 1 :]
    gain = jnp.sqrt(-expm1_negative(2.0 * logs))
    tail = jnp.exp(total - cumulative)
    lead = scaling * jnp.exp(cumulative)
    facts = jnp.concatenate([cumulative, gain, tail, lead], axis=0)
    facts_ref[...] = facts
    copies.store(facts_ref, facts_hbm)
    table = turned(facts)
    share = jnp.broadcast_to(jnp.exp(total), (hp, LANES))
    high = share.astype(BF16)
    low = (share - high.astype(F32)).astype(BF16)
    share_ref[...] = share
    base = heads * HDIM // 2
    sent_ref[base:, :] = jnp.concatenate([high.astype(F32), low.astype(F32)], axis=0).astype(BF16)
    for (first, last, _), load in zip(groups(heads), loads):
        for copy in load:
            copy.wait()
        for h in range(first, last):
            cols = slice(h * HDIM, (h + 1) * HDIM)
            scaled = scaled_keys(table, hp, h, kbuf[:, cols])
            decayed = (column(table, 2 * hp + h) * scaled.astype(F32)).astype(BF16)
            put_halves(upper, h, dot(decayed, vbuf[:, cols], TN), kept_ref, sent_ref)
    copies.finish()


def scaled_keys(table, hp, h, keys):
    return (column(table, hp + h) * keys.astype(F32)).astype(BF16)


def prepare(logs, keys, values, heads, hp, scaling):
    rows, width = keys.shape
    buf = pltpu.VMEM((rows, width), BF16)
    return kernel_call(
        functools.partial(prepare_kernel, heads, hp, scaling),
        (logs, keys, values),
        [HB] * 3,
        [
            ((4 * hp, rows), F32),
            ((width // 2, HDIM), BF16),
            ((width // 2 + 2 * hp, HDIM), BF16),
            ((hp, LANES), F32),
        ],
        (HB, VM, VM, VM),
        [
            pltpu.VMEM((heads, rows), F32),
            pltpu.VMEM((4 * hp, rows), F32),
            buf,
            buf,
            pltpu.SemaphoreType.DMA((2 + 2 * len(groups(heads)),)),
        ],
        12,
        "prepare",
        4,
    )


def project_kernel(hp, nparts, chunk, place_ref, *refs):
    parts, (w_hbm, do_hbm, facts_hbm, q_hbm, kept_ref, sent_ref) = refs[:nparts], refs[nparts : nparts + 6]
    hbuf, wbuf, dobuf, facts_ref, qbuf, total, sems = refs[nparts + 6 :]
    rows, feat = parts[0].shape
    width = wbuf.shape[1]
    heads = width // HDIM
    upper = lax.axis_index("ctx") % 2 == 1
    copies = Copies(sems)
    loads = []
    for part, ref in enumerate(parts):
        for first in range(0, feat, chunk):
            here = pl.ds(part * feat + first, chunk)
            start = pl.multiple_of(place_ref[part] * feat + first, chunk)
            loads.append(
                (
                    slice(part * feat + first, part * feat + first + chunk),
                    copies.start(ref.at[:, pl.ds(first, chunk)], hbuf.at[:, here]),
                    copies.start(w_hbm.at[pl.ds(start, chunk), :], wbuf.at[here, :]),
                )
            )
    late = [copies.start(facts_hbm, facts_ref), copies.start(do_hbm, dobuf)]
    block = min(256, width)
    for order, (here, h_in, w_in) in enumerate(loads):
        h_in.wait()
        w_in.wait()
        for first in range(0, width, block):
            wide = slice(first, first + block)
            term = dot(hbuf[:, here], wbuf[here, wide], NN)
            if order == 0:
                total[:, wide] = term
            elif order < len(loads) - 1:
                total[:, wide] += term
            else:
                qbuf[:, wide] = (total[:, wide] + term).astype(BF16)
    for copy in late:
        copy.wait()
    copies.store(qbuf, q_hbm)
    table = turned(facts_ref[...])
    for h in range(heads):
        cols = slice(h * HDIM, (h + 1) * HDIM)
        decayed = (column(table, 3 * hp + h) * qbuf[:, cols].astype(F32)).astype(BF16)
        put_halves(upper, h, dot(decayed, dobuf[:, cols], TN), kept_ref, sent_ref)
    copies.finish()


def project(parts, owners, w_query, d_out, facts, hp):
    rows, feat = parts[0].shape
    depth, width = w_query.shape
    chunk = min(512, feat)
    return kernel_call(
        functools.partial(project_kernel, hp, len(parts), chunk),
        (owners, *parts, w_query, d_out, facts),
        [SM, HB] + [AN] * (len(parts) - 1) + [HB] * 3,
        [((rows, width), BF16), ((width // 2, HDIM), BF16), ((width // 2, HDIM), BF16)],
        (HB, VM, VM),
        [
            pltpu.VMEM((rows, depth), BF16),
            pltpu.VMEM((depth, width), BF16),
            pltpu.VMEM((rows, width), BF16),
            pltpu.VMEM(facts.shape, F32),
            pltpu.VMEM((rows, width), BF16),
            pltpu.VMEM((rows, width), F32),
            pltpu.SemaphoreType.DMA((2 * len(parts) * (feat // chunk) + 3,)),
        ],
        28,
        "project",
        8,
    )


def inner_kernel(first, last, hp, *refs):
    ins, facts_hbm, outs = refs[:4], refs[4], refs[5:8]
    bufs, facts_ref, sides, sems = refs[8:12], refs[12], refs[13:16], refs[16]
    rows = ins[0].shape[0]
    copies = Copies(sems)
    facts_in = copies.start(facts_hbm, facts_ref)
    loads = {}
    for h in range(first, last, 2):
        count = min(2, last - h)
        src, dst = pl.ds(h * HDIM, count * HDIM), pl.ds((h - first) * HDIM, count * HDIM)
        loads[h] = [copies.start(ref.at[:, src], buf.at[:, dst]) for ref, buf in zip(ins, bufs)]
    facts_in.wait()
    table = turned(facts_ref[...])
    row = lax.broadcasted_iota(jnp.int32, (rows, rows), 0)
    keep = row >= lax.broadcasted_iota(jnp.int32, (rows, rows), 1)
    shift = -0.5 * math.log2(HDIM)
    turn = math.log2(math.e)
    q_ref, k_ref, v_ref, do_ref = bufs
    for h in range(first, last):
        for copy in loads.get(h, ()):
            copy.wait()
        cols = slice((h - first) * HDIM, (h - first + 1) * HDIM)
        later = column(table, h) * turn + shift
        sooner = facts_ref[h : h + 1, :] * turn
        gap = jnp.concatenate([later] * (rows // LANES), axis=1) - sooner
        decays = jnp.exp2(jnp.where(keep, gap, -1e30))
        query, grad = q_ref[:, cols], do_ref[:, cols]
        scaled = scaled_keys(table, hp, h, k_ref[:, cols])
        wdv = (decays * dot(grad, v_ref[:, cols], NT)).astype(BF16)
        wkq = (decays * dot(query, scaled, NT)).astype(BF16)
        sides[0][:, cols] = dot(wdv, scaled, NN).astype(BF16)
        sides[1][:, cols] = dot(query, wdv, TN).T.astype(BF16)
        sides[2][:, cols] = dot(grad, wkq, TN).T.astype(BF16)
        if h + 1 == last or h + 1 in loads:
            from_head = h if h in loads else h - 1
            done = slice((from_head - first) * HDIM, (h + 1 - first) * HDIM)
            for side, out in zip(sides, outs):
                copies.store(side.at[:, done], out.at[:, done])
    copies.finish()


def inner(first, last, query, keys, values, d_out, facts, hp):
    rows = query.shape[0]
    width = (last - first) * HDIM
    pairs = -(-(last - first) // 2)
    return kernel_call(
        functools.partial(inner_kernel, first, last, hp),
        (query, keys, values, d_out, facts),
        [HB] * 5,
        [((rows, width), BF16)] * 3,
        (HB,) * 3,
        [
            *[pltpu.VMEM((rows, width), BF16)] * 4,
            pltpu.VMEM(facts.shape, F32),
            *[pltpu.VMEM((rows, width), BF16)] * 3,
            pltpu.SemaphoreType.DMA((1 + 7 * pairs,)),
        ],
        24,
        "inner",
        1,
    )


def whole_head(upper, h, mine_ref, theirs_ref):
    half = HDIM // 2
    at = slice(h * half, (h + 1) * half)
    mine, theirs = mine_ref[at, :], theirs_ref[at, :]
    return jnp.concatenate([jnp.where(upper, theirs, mine), jnp.where(upper, mine, theirs)], axis=0)


def fetch_kernel(place_ref, w_hbm, *refs):
    outs, sems = refs[:-1], refs[-1]
    copies = Copies(sems)
    for index, out in enumerate(outs):
        feat = out.shape[0]
        start = pl.multiple_of(place_ref[index] * feat, feat)
        copies.store(w_hbm.at[pl.ds(start, feat), :], out)
    copies.finish()


def fetch(places, w_query, feat):
    count = places.shape[0]
    return kernel_call(
        fetch_kernel,
        (places, w_query),
        [SM, HB],
        [((feat, w_query.shape[1]), BF16)] * count,
        (VM,) * count,
        [pltpu.SemaphoreType.DMA((count,))],
        2,
        "fetch",
        4,
    )


def query_kernel(heads, hp, *refs):
    mine_ref, theirs_ref, w_ref, do_hbm, facts_hbm = refs[:5]
    inner_hbm = refs[5:-6]
    held, out_ref, dobuf, facts_ref, local, sems = refs[-6:]
    upper = lax.axis_index("ctx") % 2 == 1
    copies = Copies(sems)
    facts_in = copies.start(facts_hbm, facts_ref)
    loads = {}
    for (first, last), src in zip(spans_of(heads), inner_hbm):
        wide = pl.ds(first * HDIM, (last - first) * HDIM)
        loads[first] = (copies.start(do_hbm.at[:, wide], dobuf.at[:, wide]), copies.start(src, local.at[:, wide]))
    facts_in.wait()
    table = turned(facts_ref[...])
    for h in range(heads):
        for copy in loads.get(h, ()):
            copy.wait()
        cols = slice(h * HDIM, (h + 1) * HDIM)
        state = whole_head(upper, h, mine_ref, theirs_ref)
        carry = dot(dobuf[:, cols], state, NT)
        held[:, cols] = (local[:, cols].astype(F32) + column(table, 3 * hp + h) * carry).astype(BF16)
    put_terms(held, w_ref, out_ref)


def put_terms(dq_ref, w_ref, out_ref):
    block = min(512, out_ref.shape[1])
    for at in range(0, out_ref.shape[1], block):
        out_ref[:, at : at + block] = dot(dq_ref[...], w_ref[at : at + block, :], NT).astype(BF16)


def query_term(halves, inner_dq, d_out, facts, weight, heads, hp):
    rows, width = d_out.shape
    args = (d_out, facts, *inner_dq)
    return kernel_call(
        functools.partial(query_kernel, heads, hp),
        (*halves, weight, *args),
        [VM, VM, VM] + [HB] * len(args),
        [((rows, width), BF16), ((rows, weight.shape[0]), BF16)],
        (VM, VM),
        [
            pltpu.VMEM((rows, width), BF16),
            pltpu.VMEM(facts.shape, F32),
            pltpu.VMEM((rows, width), BF16),
            pltpu.SemaphoreType.DMA((1 + 2 * len(inner_dq),)),
        ],
        12,
        "query_term",
        6,
    )


def plain_term(d_query, weight):
    return kernel_call(
        put_terms,
        (d_query, weight),
        [VM, VM],
        [((d_query.shape[0], weight.shape[0]), BF16)],
        (VM,),
        [],
        12,
        "term",
        4,
    )[0]


def finish_kernel(dq_ref, w_ref, *refs):
    arrived, (out_hbm, sent, sems) = refs[:-3], refs[-3:]
    feat = sent.shape[1]
    copies = Copies(sems)
    block = min(512, feat)
    for at in range(0, feat, block):
        wide = slice(at, at + block)
        total = dot(dq_ref[...], w_ref[wide, :], NT).astype(BF16).astype(F32)
        for other in arrived:
            total = total + other[:, wide].astype(F32)
        sent[:, wide] = total.astype(BF16)
        copies.store(sent.at[:, wide], out_hbm.at[:, wide])
    copies.finish()


def finish(d_query, weight, arrived):
    rows, feat = d_query.shape[0], weight.shape[0]
    return kernel_call(
        finish_kernel,
        (d_query, weight, *arrived),
        [VM, VM] + [VM] * len(arrived),
        [((rows, feat), BF16)],
        (HB,),
        [
            pltpu.VMEM((rows, feat), BF16),
            pltpu.SemaphoreType.DMA((feat // min(512, feat),)),
        ],
        12,
        "finish",
        6,
    )[0]


def close_kernel(heads, hp, *refs):
    mine_ref, theirs_ref, in_hbm, v_hbm, facts_hbm = refs[:5]
    rest = refs[5:-10]
    upper = lax.axis_index("ctx") % 2 == 1
    dk_hbm, dv_hbm, kbuf, vbuf, facts_ref, dkbuf, dvbuf, kside, vside, sems = refs[-10:]
    dks, dvs = rest[: len(rest) // 2], rest[len(rest) // 2 :]
    pair = 2 if all(edge % 2 == 0 for span in spans_of(heads) for edge in span) else 1
    copies = Copies(sems)
    facts_in = copies.start(facts_hbm, facts_ref)
    loads = []
    for (start, last), dk, dv in zip(spans_of(heads), dks, dvs):
        for h in range(start, last, pair):
            wide = pl.ds(h * HDIM, pair * HDIM)
            part = pl.ds((h - start) * HDIM, pair * HDIM)
            loads.append(
                (
                    copies.start(v_hbm.at[:, wide], vbuf.at[:, wide]),
                    copies.start(dk.at[:, part], dkbuf.at[:, wide]),
                    copies.start(in_hbm.at[:, wide], kbuf.at[:, wide]),
                    copies.start(dv.at[:, part], dvbuf.at[:, wide]),
                )
            )
    facts_in.wait()
    table = turned(facts_ref[...])
    for h in range(heads):
        if h % pair == 0:
            for copy in loads[h // pair]:
                copy.wait()
        cols = slice(h * HDIM, (h + 1) * HDIM)
        adjoint = whole_head(upper, h, mine_ref, theirs_ref)
        tail, gain = column(table, 2 * hp + h), column(table, hp + h)
        carry_k = dot(vbuf[:, cols], adjoint, NT)
        kside[:, cols] = (gain * (dkbuf[:, cols].astype(F32) + tail * carry_k)).astype(BF16)
        carry_v = dot(scaled_keys(table, hp, h, kbuf[:, cols]), adjoint, NN)
        vside[:, cols] = (dvbuf[:, cols].astype(F32) + tail * carry_v).astype(BF16)
        if (h + 1) % pair == 0:
            wide = slice((h + 1 - pair) * HDIM, (h + 1) * HDIM)
            copies.store(kside.at[:, wide], dk_hbm.at[:, wide])
            copies.store(vside.at[:, wide], dv_hbm.at[:, wide])
    copies.finish()


def close(halves, dks, dvs, keys, values, facts, heads, hp):
    rows, width = values.shape
    args = (keys, values, facts, *dks, *dvs)
    buf = pltpu.VMEM((rows, width), BF16)
    return kernel_call(
        functools.partial(close_kernel, heads, hp),
        (*halves, *args),
        [VM, VM] + [HB] * len(args),
        [((rows, width), BF16)] * 2,
        (HB,) * 2,
        [
            buf,
            buf,
            pltpu.VMEM(facts.shape, F32),
            buf,
            buf,
            buf,
            buf,
            pltpu.SemaphoreType.DMA((1 + 6 * heads,)),
        ],
        20,
        "close",
        100,
    )


def body(ctx_size, head_size, hidden, w_query, keys, values, d_out, log_decay):
    rows, feat = hidden.shape
    heads = log_decay.shape[1]
    width = w_query.shape[1]
    hp = sublanes(heads)
    scaling = HDIM ** (-0.5)
    me = lax.axis_index("ctx")
    mine = lax.axis_index("head")

    parts = [hidden]
    for shift in range(1, head_size):
        ring = [(i, (i + shift) % head_size) for i in range(head_size)]
        parts.append(lax.ppermute(hidden, "head", ring))
    owners = jnp.stack([(mine + head_size - s) % head_size for s in range(head_size)]).astype(jnp.int32)

    facts, kept, sent, share = prepare(log_decay.T, keys, values, heads, hp, scaling)
    query, akept, asent = project(parts, owners, w_query, d_out, facts, hp)

    size = width // 2
    wide = lambda factor: factor[:heads, None, :]
    cube = lambda flat: flat[:size].reshape(heads, HDIM // 2, HDIM).astype(F32)
    flat = lambda cubes: cubes.astype(BF16).reshape(size, HDIM)
    split = lambda f: (f.astype(BF16), (f - f.astype(BF16).astype(F32)).astype(BF16))
    joined = lambda rows: rows[size : size + hp].astype(F32) + rows[size + hp :].astype(F32)
    stages = (ctx_size - 1).bit_length()
    uppers = [(me & (1 << stage)) != 0 for stage in range(stages)]

    def send(array, stage):
        dist = 1 << (stage % stages)
        return lax.ppermute(array, "ctx", [(i, i ^ dist) for i in range(ctx_size)])

    shares, others = [share], []
    before, after = [jnp.ones_like(share)], [jnp.ones_like(share)]

    def fold(stage, total, carried, arrived, up):
        upper = uppers[stage]
        first = upper if up else ~upper
        arrived = cube(arrived)
        if stage > 0:
            weight = jnp.where(first, before[stage] if up else after[stage], 0.0)
            carried = carried + wide(weight) * arrived
        if stage == stages - 1:
            lead = uppers[0] if up else ~uppers[0]
            block, other = total
            mine = jnp.where(lead, cube(other) + wide(others[0]) * carried, carried)
            theirs = jnp.where(lead, carried, cube(block) + wide(shares[0]) * carried)
            return flat(theirs), flat(mine), None
        own, other = jnp.where(first, 1.0, others[stage]), jnp.where(first, shares[stage], 1.0)
        total = wide(own) * total + wide(other) * arrived
        return flat(total), total, carried

    def fold_factors(stage, arrived):
        theirs = joined(arrived)
        others.append(theirs)
        shares.append(shares[stage] * theirs)
        upper = uppers[stage]
        pair = stage == 0
        before.append(before[stage] if pair else jnp.where(upper, before[stage] * theirs, before[stage]))
        after.append(after[stage] if pair else jnp.where(upper, after[stage], after[stage] * theirs))

    class Chain:
        def __init__(self, kept, sent, up):
            self.kept, self.sent, self.up = kept, sent, up
            self.total, self.carried, self.stage, self.arrived = cube(kept), jnp.zeros_like(cube(kept)), 0, None

        def go(self):
            self.arrived = send(self.sent, self.stage)

        def take(self):
            stage, self.stage = self.stage, self.stage + 1
            if stage == 0:
                self.first = self.arrived
            total = self.total if stage < stages - 1 else (self.kept, self.first)
            if self.up and stage < stages - 1:
                fold_factors(stage, self.arrived)
            self.sent, self.total, self.carried = fold(stage, total, self.carried, self.arrived, self.up)
            if self.up and stage + 2 < stages:
                self.sent = jnp.concatenate([self.sent, *split(shares[-1])], axis=0)

    states, adjoints = Chain(kept, sent, True), Chain(akept, asent, False)
    spans = spans_of(heads)
    pending = list(spans)
    inner_parts = []
    barrier = lax.optimization_barrier
    places = jnp.stack([(mine + shift) % head_size for shift in range(head_size)]).astype(jnp.int32)
    for stage in range(stages + 1):
        if stage == stages:
            places, _ = barrier((places, adjoints.sent))
            weights = fetch(places, w_query, feat)
        states.go()
        if stage == 0:
            states.arrived, query, adjoints.kept, adjoints.sent = barrier(
                (states.arrived, query, adjoints.kept, adjoints.sent)
            )
            adjoints.total = cube(adjoints.kept)
        else:
            adjoints.go()
            if pending and stage <= len(spans):
                query, _ = barrier((query, adjoints.sent))
                part = inner(*pending.pop(0), query, keys, values, d_out, facts, hp)
                states.arrived, *part = barrier((states.arrived, *part))
                inner_parts.append(part)
        if stage < stages:
            states.take()
        if stage >= 1:
            adjoints.arrived, _ = barrier((adjoints.arrived, states.sent if stage < stages else states.total))
            adjoints.take()
    while pending:
        inner_parts.append(inner(*pending.pop(0), query, keys, values, d_out, facts, hp))
    adjoints.go()
    states.arrived, _ = barrier((states.arrived, adjoints.sent))
    state_halves = (states.total, states.arrived)
    adjoint_halves = (adjoints.total, adjoints.arrived)
    dqs, dks, dvs = zip(*inner_parts)

    arrived = []
    for shift in range(1, head_size):
        ring = [(i, (i + shift) % head_size) for i in range(head_size)]
        if shift == 1:
            d_query, term = query_term(state_halves, dqs, d_out, facts, weights[shift], heads, hp)
        else:
            term = plain_term(d_query, weights[shift])
        arrived.append(lax.ppermute(term, "head", ring))
    d_keys, d_values = close(adjoint_halves, dks, dvs, keys, values, facts, heads, hp)
    d_hidden = finish(d_query, weights[0], arrived)
    return (d_hidden, d_keys, d_values)


def solution(mesh):
    return jax.shard_map(
        functools.partial(body, mesh.shape["ctx"], mesh.shape["head"]),
        mesh=mesh,
        in_specs=(
            P("ctx", "head"),
            P(None, "head"),
            P("ctx", "head"),
            P("ctx", "head"),
            P("ctx", "head"),
            P("ctx", "head"),
        ),
        out_specs=(P("ctx", "head"), P("ctx", "head"), P("ctx", "head")),
        check_vma=False,
    )
```

```python
import functools
import math

import jax
import jax.numpy as jnp
from jax import lax
from jax.experimental import pallas as pl
from jax.experimental.pallas import tpu as pltpu
from jax.sharding import PartitionSpec as P

HDIM = 128
LANES = 128
F32, BF16 = jnp.float32, jnp.bfloat16
MIB = 1 << 20
VM = pl.BlockSpec(memory_space=pltpu.VMEM)
SM = pl.BlockSpec(memory_space=pltpu.SMEM)
HB = pl.BlockSpec(memory_space=pltpu.HBM)
AN = pl.BlockSpec(memory_space=pl.ANY)

NN = (((1,), (0,)), ((), ()))
NT = (((1,), (1,)), ((), ()))
TN = (((0,), (0,)), ((), ()))


def dot(a, b, dims):
    return lax.dot_general(a, b, dims, preferred_element_type=F32)


def kernel_call(kernel, args, specs, outs, out_specs, scratch, mib, name, micros):
    pinned = [pltpu.with_memory_space_constraint(a, pltpu.HBM) if s is HB else a for a, s in zip(args, specs)]
    placed = tuple(
        (pltpu.HBM if s is HB else jax.ShapeDtypeStruct)(shape, dtype) for (shape, dtype), s in zip(outs, out_specs)
    )
    return pl.pallas_call(
        kernel,
        in_specs=specs,
        out_specs=tuple(out_specs),
        out_shape=placed,
        scratch_shapes=scratch,
        compiler_params=pltpu.CompilerParams(vmem_limit_bytes=mib * MIB),
        cost_estimate=pl.CostEstimate(flops=int(micros * 1e9), bytes_accessed=1, transcendentals=0),
        name=name,
    )(*pinned)


def sublanes(count):
    return -(-count // 8) * 8


def expm1_negative(z):
    series = jnp.full_like(z, 1.0)
    for order in range(10, 1, -1):
        series = 1.0 + z * series * (1.0 / order)
    return jnp.where(z > -0.5, z * series, jnp.exp(z) - 1.0)


def column(table, lane, width=LANES):
    return jnp.broadcast_to(table[:, lane : lane + 1], (table.shape[0], width))


class Copies:
    def __init__(self, sems):
        self.sems, self.count, self.out = sems, 0, []

    def start(self, src, dst):
        copy = pltpu.make_async_copy(src, dst, self.sems.at[self.count])
        self.count += 1
        copy.start()
        return copy

    def store(self, src, dst):
        self.out.append(self.start(src, dst))

    def finish(self):
        for copy in self.out:
            copy.wait()


def spans_of(heads):
    edges = sorted({0, heads // 4, heads // 2, heads})
    return list(zip(edges, edges[1:]))


def groups(heads):
    size = min(4, heads)
    return [(f, f + size, slice(f * HDIM, (f + size) * HDIM)) for f in range(0, heads, size)]


def turned(facts):
    spare = jnp.zeros((LANES - facts.shape[0], facts.shape[1]), F32)
    return jnp.concatenate([facts, spare], axis=0).T


def put_halves(upper, h, local, kept_ref, sent_ref):
    half = HDIM // 2
    at = slice(h * half, (h + 1) * half)
    kept_ref[at, :] = jnp.where(upper, local[half:], local[:half]).astype(BF16)
    sent_ref[at, :] = jnp.where(upper, local[:half], local[half:]).astype(BF16)


def prepare_kernel(
    heads, hp, scaling, ld_hbm, k_hbm, v_hbm, facts_hbm, kept_ref, sent_ref, share_ref, *scratch
):
    ld, facts_ref, kbuf, vbuf, sems = scratch
    upper = lax.axis_index("ctx") % 2 == 1
    rows = kbuf.shape[0]
    copies = Copies(sems)
    ld_in = copies.start(ld_hbm, ld)
    loads = []
    for _, _, wide in groups(heads):
        loads.append([copies.start(src.at[:, wide], dst.at[:, wide]) for src, dst in ((k_hbm, kbuf), (v_hbm, vbuf))])
    ld_in.wait()
    logs = ld[...]
    if heads < hp:
        logs = jnp.concatenate([logs, jnp.zeros((hp - heads, rows), F32)], axis=0)
    lane = lax.broadcasted_iota(jnp.int32, logs.shape, 1)
    cumulative = logs
    step = 1
    while step < rows:
        moved = pltpu.roll(cumulative, step, 1)
        cumulative = cumulative + jnp.where(lane >= step, moved, 0.0)
        step *= 2
    total = cumulative[:, rows - 1 :]
    gain = jnp.sqrt(-expm1_negative(2.0 * logs))
    tail = jnp.exp(total - cumulative)
    lead = scaling * jnp.exp(cumulative)
    facts = jnp.concatenate([cumulative, gain, tail, lead], axis=0)
    facts_ref[...] = facts
    copies.store(facts_ref, facts_hbm)
    table = turned(facts)
    share = jnp.broadcast_to(jnp.exp(total), (hp, LANES))
    high = share.astype(BF16)
    low = (share - high.astype(F32)).astype(BF16)
    share_ref[...] = share
    base = heads * HDIM // 2
    sent_ref[base:, :] = jnp.concatenate([high.astype(F32), low.astype(F32)], axis=0).astype(BF16)
    for (first, last, _), load in zip(groups(heads), loads):
        for copy in load:
            copy.wait()
        for h in range(first, last):
            cols = slice(h * HDIM, (h + 1) * HDIM)
            scaled = scaled_keys(table, hp, h, kbuf[:, cols])
            decayed = (column(table, 2 * hp + h) * scaled.astype(F32)).astype(BF16)
            put_halves(upper, h, dot(decayed, vbuf[:, cols], TN), kept_ref, sent_ref)
    copies.finish()


def scaled_keys(table, hp, h, keys):
    return (column(table, hp + h) * keys.astype(F32)).astype(BF16)


def prepare(logs, keys, values, heads, hp, scaling):
    rows, width = keys.shape
    buf = pltpu.VMEM((rows, width), BF16)
    return kernel_call(
        functools.partial(prepare_kernel, heads, hp, scaling),
        (logs, keys, values),
        [HB] * 3,
        [
            ((4 * hp, rows), F32),
            ((width // 2, HDIM), BF16),
            ((width // 2 + 2 * hp, HDIM), BF16),
            ((hp, LANES), F32),
        ],
        (HB, VM, VM, VM),
        [
            pltpu.VMEM((heads, rows), F32),
            pltpu.VMEM((4 * hp, rows), F32),
            buf,
            buf,
            pltpu.SemaphoreType.DMA((2 + 2 * len(groups(heads)),)),
        ],
        12,
        "prepare",
        4,
    )


def project_kernel(hp, nparts, chunk, *refs):
    parts, (w_hbm, do_hbm, facts_hbm, q_hbm, kept_ref, sent_ref) = refs[:nparts], refs[nparts : nparts + 6]
    hbuf, wbuf, dobuf, facts_ref, qbuf, total, sems = refs[nparts + 6 :]
    rows, feat = parts[0].shape
    width = wbuf.shape[1]
    heads = width // HDIM
    upper = lax.axis_index("ctx") % 2 == 1
    copies = Copies(sems)
    loads = []
    for part, ref in enumerate(parts):
        for first in range(0, feat, chunk):
            here = pl.ds(part * feat + first, chunk)
            owner = lax.rem(lax.axis_index("head") + nparts - part, nparts)
            start = pl.multiple_of(owner * feat + first, chunk)
            loads.append(
                (
                    slice(part * feat + first, part * feat + first + chunk),
                    copies.start(ref.at[:, pl.ds(first, chunk)], hbuf.at[:, here]),
                    copies.start(w_hbm.at[pl.ds(start, chunk), :], wbuf.at[here, :]),
                )
            )
    late = [copies.start(facts_hbm, facts_ref), copies.start(do_hbm, dobuf)]
    block = min(256, width)
    for order, (here, h_in, w_in) in enumerate(loads):
        h_in.wait()
        w_in.wait()
        for first in range(0, width, block):
            wide = slice(first, first + block)
            term = dot(hbuf[:, here], wbuf[here, wide], NN)
            if order == 0:
                total[:, wide] = term
            elif order < len(loads) - 1:
                total[:, wide] += term
            else:
                qbuf[:, wide] = (total[:, wide] + term).astype(BF16)
    for copy in late:
        copy.wait()
    copies.store(qbuf, q_hbm)
    table = turned(facts_ref[...])
    for h in range(heads):
        cols = slice(h * HDIM, (h + 1) * HDIM)
        decayed = (column(table, 3 * hp + h) * qbuf[:, cols].astype(F32)).astype(BF16)
        put_halves(upper, h, dot(decayed, dobuf[:, cols], TN), kept_ref, sent_ref)
    copies.finish()


def project(parts, w_query, d_out, facts, hp):
    rows, feat = parts[0].shape
    depth, width = w_query.shape
    chunk = min(512, feat)
    return kernel_call(
        functools.partial(project_kernel, hp, len(parts), chunk),
        (*parts, w_query, d_out, facts),
        [HB] + [AN] * (len(parts) - 1) + [HB] * 3,
        [((rows, width), BF16), ((width // 2, HDIM), BF16), ((width // 2, HDIM), BF16)],
        (HB, VM, VM),
        [
            pltpu.VMEM((rows, depth), BF16),
            pltpu.VMEM((depth, width), BF16),
            pltpu.VMEM((rows, width), BF16),
            pltpu.VMEM(facts.shape, F32),
            pltpu.VMEM((rows, width), BF16),
            pltpu.VMEM((rows, width), F32),
            pltpu.SemaphoreType.DMA((2 * len(parts) * (feat // chunk) + 3,)),
        ],
        28,
        "project",
        8,
    )


def inner_kernel(first, last, hp, *refs):
    ins, facts_hbm, outs = refs[:4], refs[4], refs[5:8]
    bufs, facts_ref, sides, sems = refs[8:12], refs[12], refs[13:16], refs[16]
    rows = ins[0].shape[0]
    copies = Copies(sems)
    facts_in = copies.start(facts_hbm, facts_ref)
    loads = {}
    for h in range(first, last, 2):
        count = min(2, last - h)
        src, dst = pl.ds(h * HDIM, count * HDIM), pl.ds((h - first) * HDIM, count * HDIM)
        loads[h] = [copies.start(ref.at[:, src], buf.at[:, dst]) for ref, buf in zip(ins, bufs)]
    facts_in.wait()
    table = turned(facts_ref[...])
    row = lax.broadcasted_iota(jnp.int32, (rows, rows), 0)
    keep = row >= lax.broadcasted_iota(jnp.int32, (rows, rows), 1)
    shift = -0.5 * math.log2(HDIM)
    turn = math.log2(math.e)
    q_ref, k_ref, v_ref, do_ref = bufs
    for h in range(first, last):
        for copy in loads.get(h, ()):
            copy.wait()
        cols = slice((h - first) * HDIM, (h - first + 1) * HDIM)
        later = column(table, h) * turn + shift
        sooner = facts_ref[h : h + 1, :] * turn
        gap = jnp.concatenate([later] * (rows // LANES), axis=1) - sooner
        decays = jnp.exp2(jnp.where(keep, gap, -1e30))
        query, grad = q_ref[:, cols], do_ref[:, cols]
        scaled = scaled_keys(table, hp, h, k_ref[:, cols])
        wdv = (decays * dot(grad, v_ref[:, cols], NT)).astype(BF16)
        wkq = (decays * dot(query, scaled, NT)).astype(BF16)
        sides[0][:, cols] = dot(wdv, scaled, NN).astype(BF16)
        sides[1][:, cols] = dot(query, wdv, TN).T.astype(BF16)
        sides[2][:, cols] = dot(grad, wkq, TN).T.astype(BF16)
        if h + 1 == last or h + 1 in loads:
            from_head = h if h in loads else h - 1
            done = slice((from_head - first) * HDIM, (h + 1 - first) * HDIM)
            for side, out in zip(sides, outs):
                copies.store(side.at[:, done], out.at[:, done])
    copies.finish()


def inner(first, last, query, keys, values, d_out, facts, hp):
    rows = query.shape[0]
    width = (last - first) * HDIM
    pairs = -(-(last - first) // 2)
    return kernel_call(
        functools.partial(inner_kernel, first, last, hp),
        (query, keys, values, d_out, facts),
        [HB] * 5,
        [((rows, width), BF16)] * 3,
        (HB,) * 3,
        [
            *[pltpu.VMEM((rows, width), BF16)] * 4,
            pltpu.VMEM(facts.shape, F32),
            *[pltpu.VMEM((rows, width), BF16)] * 3,
            pltpu.SemaphoreType.DMA((1 + 7 * pairs,)),
        ],
        24,
        "inner",
        1,
    )


def whole_head(upper, h, mine_ref, theirs_ref):
    half = HDIM // 2
    at = slice(h * half, (h + 1) * half)
    mine, theirs = mine_ref[at, :], theirs_ref[at, :]
    return jnp.concatenate([jnp.where(upper, theirs, mine), jnp.where(upper, mine, theirs)], axis=0)


def rows_of(w_hbm, shift, count, feat):
    owner = lax.rem(lax.axis_index("head") + shift, count)
    return w_hbm.at[pl.ds(pl.multiple_of(owner * feat, feat), feat), :]


def fetch_kernel(count, w_hbm, *refs):
    outs, sems = refs[:-1], refs[-1]
    copies = Copies(sems)
    for index, out in enumerate(outs):
        copies.store(rows_of(w_hbm, index + 1, count, out.shape[0]), out)
    copies.finish()


def fetch(count, w_query, feat):
    return kernel_call(
        functools.partial(fetch_kernel, count),
        (w_query,),
        [HB],
        [((feat, w_query.shape[1]), BF16)] * (count - 1),
        (VM,) * (count - 1),
        [pltpu.SemaphoreType.DMA((count - 1,))],
        2,
        "fetch",
        4,
    )


def query_kernel(heads, hp, *refs):
    mine_ref, theirs_ref, w_ref, do_hbm, facts_hbm = refs[:5]
    inner_hbm = refs[5:-6]
    held, out_ref, dobuf, facts_ref, local, sems = refs[-6:]
    upper = lax.axis_index("ctx") % 2 == 1
    copies = Copies(sems)
    facts_in = copies.start(facts_hbm, facts_ref)
    loads = {}
    for (first, last), src in zip(spans_of(heads), inner_hbm):
        wide = pl.ds(first * HDIM, (last - first) * HDIM)
        loads[first] = (copies.start(do_hbm.at[:, wide], dobuf.at[:, wide]), copies.start(src, local.at[:, wide]))
    facts_in.wait()
    table = turned(facts_ref[...])
    for h in range(heads):
        for copy in loads.get(h, ()):
            copy.wait()
        cols = slice(h * HDIM, (h + 1) * HDIM)
        state = whole_head(upper, h, mine_ref, theirs_ref)
        carry = dot(dobuf[:, cols], state, NT)
        held[:, cols] = (local[:, cols].astype(F32) + column(table, 3 * hp + h) * carry).astype(BF16)
    put_terms(held, w_ref, out_ref)


def put_terms(dq_ref, w_ref, out_ref):
    block = min(512, out_ref.shape[1])
    for at in range(0, out_ref.shape[1], block):
        out_ref[:, at : at + block] = dot(dq_ref[...], w_ref[at : at + block, :], NT).astype(BF16)


def query_term(halves, inner_dq, d_out, facts, weight, heads, hp):
    rows, width = d_out.shape
    args = (d_out, facts, *inner_dq)
    return kernel_call(
        functools.partial(query_kernel, heads, hp),
        (*halves, weight, *args),
        [VM, VM, VM] + [HB] * len(args),
        [((rows, width), BF16), ((rows, weight.shape[0]), BF16)],
        (VM, VM),
        [
            pltpu.VMEM((rows, width), BF16),
            pltpu.VMEM(facts.shape, F32),
            pltpu.VMEM((rows, width), BF16),
            pltpu.SemaphoreType.DMA((1 + 2 * len(inner_dq),)),
        ],
        12,
        "query_term",
        6,
    )


def plain_term(d_query, weight):
    return kernel_call(
        put_terms,
        (d_query, weight),
        [VM, VM],
        [((d_query.shape[0], weight.shape[0]), BF16)],
        (VM,),
        [],
        12,
        "term",
        4,
    )[0]


def finish_kernel(dq_ref, w_ref, *refs):
    arrived, (out_hbm, sent, sems) = refs[:-3], refs[-3:]
    feat = sent.shape[1]
    copies = Copies(sems)
    block = min(512, feat)
    for at in range(0, feat, block):
        wide = slice(at, at + block)
        total = dot(dq_ref[...], w_ref[wide, :], NT).astype(BF16).astype(F32)
        for other in arrived:
            total = total + other[:, wide].astype(F32)
        sent[:, wide] = total.astype(BF16)
        copies.store(sent.at[:, wide], out_hbm.at[:, wide])
    copies.finish()


def finish(d_query, weight, arrived):
    rows, feat = d_query.shape[0], weight.shape[0]
    return kernel_call(
        finish_kernel,
        (d_query, weight, *arrived),
        [VM, VM] + [VM] * len(arrived),
        [((rows, feat), BF16)],
        (HB,),
        [
            pltpu.VMEM((rows, feat), BF16),
            pltpu.SemaphoreType.DMA((feat // min(512, feat),)),
        ],
        12,
        "finish",
        6,
    )[0]


def close_kernel(heads, hp, count, *refs):
    mine_ref, theirs_ref, in_hbm, v_hbm, facts_hbm, w_hbm = refs[:6]
    rest = refs[6:-11]
    upper = lax.axis_index("ctx") % 2 == 1
    dk_hbm, dv_hbm, own_ref, kbuf, vbuf, facts_ref, dkbuf, dvbuf, kside, vside, sems = refs[-11:]
    dks, dvs = rest[: len(rest) // 2], rest[len(rest) // 2 :]
    pair = 2 if all(edge % 2 == 0 for span in spans_of(heads) for edge in span) else 1
    copies = Copies(sems)
    facts_in = copies.start(facts_hbm, facts_ref)
    loads = []
    for (start, last), dk, dv in zip(spans_of(heads), dks, dvs):
        for h in range(start, last, pair):
            wide = pl.ds(h * HDIM, pair * HDIM)
            part = pl.ds((h - start) * HDIM, pair * HDIM)
            loads.append(
                (
                    copies.start(v_hbm.at[:, wide], vbuf.at[:, wide]),
                    copies.start(dk.at[:, part], dkbuf.at[:, wide]),
                    copies.start(in_hbm.at[:, wide], kbuf.at[:, wide]),
                    copies.start(dv.at[:, part], dvbuf.at[:, wide]),
                )
            )
    copies.store(rows_of(w_hbm, 0, count, own_ref.shape[0]), own_ref)
    facts_in.wait()
    table = turned(facts_ref[...])
    for h in range(heads):
        if h % pair == 0:
            for copy in loads[h // pair]:
                copy.wait()
        cols = slice(h * HDIM, (h + 1) * HDIM)
        adjoint = whole_head(upper, h, mine_ref, theirs_ref)
        tail, gain = column(table, 2 * hp + h), column(table, hp + h)
        carry_k = dot(vbuf[:, cols], adjoint, NT)
        kside[:, cols] = (gain * (dkbuf[:, cols].astype(F32) + tail * carry_k)).astype(BF16)
        carry_v = dot(scaled_keys(table, hp, h, kbuf[:, cols]), adjoint, NN)
        vside[:, cols] = (dvbuf[:, cols].astype(F32) + tail * carry_v).astype(BF16)
        if (h + 1) % pair == 0:
            wide = slice((h + 1 - pair) * HDIM, (h + 1) * HDIM)
            copies.store(kside.at[:, wide], dk_hbm.at[:, wide])
            copies.store(vside.at[:, wide], dv_hbm.at[:, wide])
    copies.finish()


def close(halves, dks, dvs, keys, values, facts, w_query, feat, count, heads, hp):
    rows, width = values.shape
    args = (keys, values, facts, w_query, *dks, *dvs)
    buf = pltpu.VMEM((rows, width), BF16)
    return kernel_call(
        functools.partial(close_kernel, heads, hp, count),
        (*halves, *args),
        [VM, VM] + [HB] * len(args),
        [((rows, width), BF16)] * 2 + [((feat, width), BF16)],
        (HB, HB, VM),
        [
            buf,
            buf,
            pltpu.VMEM(facts.shape, F32),
            buf,
            buf,
            buf,
            buf,
            pltpu.SemaphoreType.DMA((2 + 6 * heads,)),
        ],
        20,
        "close",
        100,
    )


def body(ctx_size, head_size, hidden, w_query, keys, values, d_out, log_decay):
    rows, feat = hidden.shape
    heads = log_decay.shape[1]
    width = w_query.shape[1]
    hp = sublanes(heads)
    scaling = HDIM ** (-0.5)
    me = lax.axis_index("ctx")

    parts = [hidden]
    for shift in range(1, head_size):
        ring = [(i, (i + shift) % head_size) for i in range(head_size)]
        parts.append(lax.ppermute(hidden, "head", ring))

    facts, kept, sent, share = prepare(log_decay.T, keys, values, heads, hp, scaling)
    query, akept, asent = project(parts, w_query, d_out, facts, hp)

    size = width // 2
    wide = lambda factor: factor[:heads, None, :]
    cube = lambda flat: flat[:size].reshape(heads, HDIM // 2, HDIM).astype(F32)
    flat = lambda cubes: cubes.astype(BF16).reshape(size, HDIM)
    split = lambda f: (f.astype(BF16), (f - f.astype(BF16).astype(F32)).astype(BF16))
    joined = lambda rows: rows[size : size + hp].astype(F32) + rows[size + hp :].astype(F32)
    stages = (ctx_size - 1).bit_length()
    uppers = [(me & (1 << stage)) != 0 for stage in range(stages)]

    def send(array, stage):
        dist = 1 << (stage % stages)
        return lax.ppermute(array, "ctx", [(i, i ^ dist) for i in range(ctx_size)])

    shares, others = [share], []
    before, after = [jnp.ones_like(share)], [jnp.ones_like(share)]

    def fold(stage, total, carried, arrived, up):
        upper = uppers[stage]
        first = upper if up else ~upper
        arrived = cube(arrived)
        if stage > 0:
            weight = jnp.where(first, before[stage] if up else after[stage], 0.0)
            carried = carried + wide(weight) * arrived
        if stage == stages - 1:
            lead = uppers[0] if up else ~uppers[0]
            block, other = total
            mine = jnp.where(lead, cube(other) + wide(others[0]) * carried, carried)
            theirs = jnp.where(lead, carried, cube(block) + wide(shares[0]) * carried)
            return flat(theirs), flat(mine), None
        own, other = jnp.where(first, 1.0, others[stage]), jnp.where(first, shares[stage], 1.0)
        total = wide(own) * total + wide(other) * arrived
        return flat(total), total, carried

    def fold_factors(stage, arrived):
        theirs = joined(arrived)
        others.append(theirs)
        shares.append(shares[stage] * theirs)
        upper = uppers[stage]
        pair = stage == 0
        before.append(before[stage] if pair else jnp.where(upper, before[stage] * theirs, before[stage]))
        after.append(after[stage] if pair else jnp.where(upper, after[stage], after[stage] * theirs))

    class Chain:
        def __init__(self, kept, sent, up):
            self.kept, self.sent, self.up = kept, sent, up
            self.total, self.carried, self.stage, self.arrived = cube(kept), jnp.zeros_like(cube(kept)), 0, None

        def go(self):
            self.arrived = send(self.sent, self.stage)

        def take(self):
            stage, self.stage = self.stage, self.stage + 1
            if stage == 0:
                self.first = self.arrived
            total = self.total if stage < stages - 1 else (self.kept, self.first)
            if self.up and stage < stages - 1:
                fold_factors(stage, self.arrived)
            self.sent, self.total, self.carried = fold(stage, total, self.carried, self.arrived, self.up)
            if self.up and stage + 2 < stages:
                self.sent = jnp.concatenate([self.sent, *split(shares[-1])], axis=0)

    states, adjoints = Chain(kept, sent, True), Chain(akept, asent, False)
    spans = spans_of(heads)
    pending = list(spans)
    inner_parts = []
    barrier = lax.optimization_barrier
    for stage in range(stages + 1):
        if stage == stages:
            weight, _ = barrier((w_query, adjoints.sent))
            weights = fetch(head_size, weight, feat)
        states.go()
        if stage == 0:
            states.arrived, query, adjoints.kept, adjoints.sent = barrier(
                (states.arrived, query, adjoints.kept, adjoints.sent)
            )
            adjoints.total = cube(adjoints.kept)
        else:
            adjoints.go()
            if pending and stage <= len(spans):
                query, _ = barrier((query, adjoints.sent))
                part = inner(*pending.pop(0), query, keys, values, d_out, facts, hp)
                states.arrived, *part = barrier((states.arrived, *part))
                inner_parts.append(part)
        if stage == stages - 1:
            adjoints.take()
            states.arrived, _ = barrier((states.arrived, adjoints.sent))
            states.take()
            continue
        if stage < stages:
            states.take()
        if stage >= 1:
            adjoints.arrived, _ = barrier((adjoints.arrived, states.sent if stage < stages else states.total))
            adjoints.take()
    while pending:
        inner_parts.append(inner(*pending.pop(0), query, keys, values, d_out, facts, hp))
    adjoints.go()
    states.arrived, _ = barrier((states.arrived, adjoints.sent))
    state_halves = (states.total, states.arrived)
    adjoint_halves = (adjoints.total, adjoints.arrived)
    dqs, dks, dvs = zip(*inner_parts)

    arrived = []
    for shift in range(1, head_size):
        ring = [(i, (i + shift) % head_size) for i in range(head_size)]
        if shift == 1:
            d_query, term = query_term(state_halves, dqs, d_out, facts, weights[0], heads, hp)
        else:
            term = plain_term(d_query, weights[shift - 1])
        arrived.append(lax.ppermute(term, "head", ring))
    d_keys, d_values, own = close(
        adjoint_halves, dks, dvs, keys, values, facts, w_query, feat, head_size, heads, hp
    )
    d_hidden = finish(d_query, own, arrived)
    return (d_hidden, d_keys, d_values)


def solution(mesh):
    return jax.shard_map(
        functools.partial(body, mesh.shape["ctx"], mesh.shape["head"]),
        mesh=mesh,
        in_specs=(
            P("ctx", "head"),
            P(None, "head"),
            P("ctx", "head"),
            P("ctx", "head"),
            P("ctx", "head"),
            P("ctx", "head"),
        ),
        out_specs=(P("ctx", "head"), P("ctx", "head"), P("ctx", "head")),
        check_vma=False,
    )
```

```python
import functools
import math

import jax
import jax.numpy as jnp
from jax import lax
from jax.experimental import pallas as pl
from jax.experimental.pallas import tpu as pltpu
from jax.sharding import PartitionSpec as P

HDIM = 128
LANES = 128
F32, BF16 = jnp.float32, jnp.bfloat16
MIB = 1 << 20
VM = pl.BlockSpec(memory_space=pltpu.VMEM)
SM = pl.BlockSpec(memory_space=pltpu.SMEM)
HB = pl.BlockSpec(memory_space=pltpu.HBM)
AN = pl.BlockSpec(memory_space=pl.ANY)

NN = (((1,), (0,)), ((), ()))
NT = (((1,), (1,)), ((), ()))
TN = (((0,), (0,)), ((), ()))


def dot(a, b, dims):
    return lax.dot_general(a, b, dims, preferred_element_type=F32)


def kernel_call(kernel, args, specs, outs, out_specs, scratch, mib, name, micros):
    pinned = [pltpu.with_memory_space_constraint(a, pltpu.HBM) if s is HB else a for a, s in zip(args, specs)]
    placed = tuple(
        (pltpu.HBM if s is HB else jax.ShapeDtypeStruct)(shape, dtype) for (shape, dtype), s in zip(outs, out_specs)
    )
    return pl.pallas_call(
        kernel,
        in_specs=specs,
        out_specs=tuple(out_specs),
        out_shape=placed,
        scratch_shapes=scratch,
        compiler_params=pltpu.CompilerParams(vmem_limit_bytes=mib * MIB),
        cost_estimate=pl.CostEstimate(flops=int(micros * 1e9), bytes_accessed=1, transcendentals=0),
        name=name,
    )(*pinned)


def sublanes(count):
    return -(-count // 8) * 8


def expm1_negative(z):
    series = jnp.full_like(z, 1.0)
    for order in range(10, 1, -1):
        series = 1.0 + z * series * (1.0 / order)
    return jnp.where(z > -0.5, z * series, jnp.exp(z) - 1.0)


def column(table, lane, width=LANES):
    return jnp.broadcast_to(table[:, lane : lane + 1], (table.shape[0], width))


class Copies:
    def __init__(self, sems):
        self.sems, self.count, self.out = sems, 0, []

    def start(self, src, dst):
        copy = pltpu.make_async_copy(src, dst, self.sems.at[self.count])
        self.count += 1
        copy.start()
        return copy

    def store(self, src, dst):
        self.out.append(self.start(src, dst))

    def finish(self):
        for copy in self.out:
            copy.wait()


def spans_of(heads):
    edges = sorted({0, heads // 4, heads // 2, heads})
    return list(zip(edges, edges[1:]))


def groups(heads):
    size = min(4, heads)
    return [(f, f + size, slice(f * HDIM, (f + size) * HDIM)) for f in range(0, heads, size)]


def turned(facts):
    spare = jnp.zeros((LANES - facts.shape[0], facts.shape[1]), F32)
    return jnp.concatenate([facts, spare], axis=0).T


def put_halves(upper, h, local, kept_ref, sent_ref):
    half = HDIM // 2
    at = slice(h * half, (h + 1) * half)
    kept_ref[at, :] = jnp.where(upper, local[half:], local[:half]).astype(BF16)
    sent_ref[at, :] = jnp.where(upper, local[:half], local[half:]).astype(BF16)


def prepare_kernel(
    heads, hp, scaling, ld_hbm, k_hbm, v_hbm, facts_hbm, kept_ref, sent_ref, share_ref, *scratch
):
    ld, facts_ref, kbuf, vbuf, sems = scratch
    upper = lax.axis_index("ctx") % 2 == 1
    rows = kbuf.shape[0]
    copies = Copies(sems)
    ld_in = copies.start(ld_hbm, ld)
    loads = []
    for _, _, wide in groups(heads):
        loads.append([copies.start(src.at[:, wide], dst.at[:, wide]) for src, dst in ((k_hbm, kbuf), (v_hbm, vbuf))])
    ld_in.wait()
    logs = ld[...]
    if heads < hp:
        logs = jnp.concatenate([logs, jnp.zeros((hp - heads, rows), F32)], axis=0)
    lane = lax.broadcasted_iota(jnp.int32, logs.shape, 1)
    cumulative = logs
    step = 1
    while step < rows:
        moved = pltpu.roll(cumulative, step, 1)
        cumulative = cumulative + jnp.where(lane >= step, moved, 0.0)
        step *= 2
    total = cumulative[:, rows - 1 :]
    gain = jnp.sqrt(-expm1_negative(2.0 * logs))
    tail = jnp.exp(total - cumulative)
    lead = scaling * jnp.exp(cumulative)
    facts = jnp.concatenate([cumulative, gain, tail, lead], axis=0)
    facts_ref[...] = facts
    copies.store(facts_ref, facts_hbm)
    table = turned(facts)
    share = jnp.broadcast_to(jnp.exp(total), (hp, LANES))
    high = share.astype(BF16)
    low = (share - high.astype(F32)).astype(BF16)
    share_ref[...] = share
    base = heads * HDIM // 2
    sent_ref[base:, :] = jnp.concatenate([high.astype(F32), low.astype(F32)], axis=0).astype(BF16)
    for (first, last, _), load in zip(groups(heads), loads):
        for copy in load:
            copy.wait()
        for h in range(first, last):
            cols = slice(h * HDIM, (h + 1) * HDIM)
            scaled = scaled_keys(table, hp, h, kbuf[:, cols])
            decayed = (column(table, 2 * hp + h) * scaled.astype(F32)).astype(BF16)
            put_halves(upper, h, dot(decayed, vbuf[:, cols], TN), kept_ref, sent_ref)
    copies.finish()


def scaled_keys(table, hp, h, keys):
    return (column(table, hp + h) * keys.astype(F32)).astype(BF16)


def prepare(logs, keys, values, heads, hp, scaling):
    rows, width = keys.shape
    buf = pltpu.VMEM((rows, width), BF16)
    return kernel_call(
        functools.partial(prepare_kernel, heads, hp, scaling),
        (logs, keys, values),
        [HB] * 3,
        [
            ((4 * hp, rows), F32),
            ((width // 2, HDIM), BF16),
            ((width // 2 + 2 * hp, HDIM), BF16),
            ((hp, LANES), F32),
        ],
        (HB, VM, VM, VM),
        [
            pltpu.VMEM((heads, rows), F32),
            pltpu.VMEM((4 * hp, rows), F32),
            buf,
            buf,
            pltpu.SemaphoreType.DMA((2 + 2 * len(groups(heads)),)),
        ],
        12,
        "prepare",
        4,
    )


def project_kernel(hp, nparts, chunk, *refs):
    parts, (w_hbm, do_hbm, facts_hbm, q_hbm, kept_ref, sent_ref) = refs[:nparts], refs[nparts : nparts + 6]
    hbuf, wbuf, dobuf, facts_ref, qbuf, total, sems = refs[nparts + 6 :]
    rows, feat = parts[0].shape
    width = wbuf.shape[1]
    heads = width // HDIM
    upper = lax.axis_index("ctx") % 2 == 1
    copies = Copies(sems)
    loads = []
    for part, ref in enumerate(parts):
        for first in range(0, feat, chunk):
            here = pl.ds(part * feat + first, chunk)
            owner = lax.rem(lax.axis_index("head") + nparts - part, nparts)
            start = pl.multiple_of(owner * feat + first, chunk)
            loads.append(
                (
                    slice(part * feat + first, part * feat + first + chunk),
                    copies.start(ref.at[:, pl.ds(first, chunk)], hbuf.at[:, here]),
                    copies.start(w_hbm.at[pl.ds(start, chunk), :], wbuf.at[here, :]),
                )
            )
    late = [copies.start(facts_hbm, facts_ref), copies.start(do_hbm, dobuf)]
    block = min(256, width)
    for order, (here, h_in, w_in) in enumerate(loads):
        h_in.wait()
        w_in.wait()
        for first in range(0, width, block):
            wide = slice(first, first + block)
            term = dot(hbuf[:, here], wbuf[here, wide], NN)
            if order == 0:
                total[:, wide] = term
            elif order < len(loads) - 1:
                total[:, wide] += term
            else:
                qbuf[:, wide] = (total[:, wide] + term).astype(BF16)
    for copy in late:
        copy.wait()
    copies.store(qbuf, q_hbm)
    table = turned(facts_ref[...])
    for h in range(heads):
        cols = slice(h * HDIM, (h + 1) * HDIM)
        decayed = (column(table, 3 * hp + h) * qbuf[:, cols].astype(F32)).astype(BF16)
        put_halves(upper, h, dot(decayed, dobuf[:, cols], TN), kept_ref, sent_ref)
    copies.finish()


def project(parts, w_query, d_out, facts, hp):
    rows, feat = parts[0].shape
    depth, width = w_query.shape
    chunk = min(512, feat)
    return kernel_call(
        functools.partial(project_kernel, hp, len(parts), chunk),
        (*parts, w_query, d_out, facts),
        [HB] + [AN] * (len(parts) - 1) + [HB] * 3,
        [((rows, width), BF16), ((width // 2, HDIM), BF16), ((width // 2, HDIM), BF16)],
        (HB, VM, VM),
        [
            pltpu.VMEM((rows, depth), BF16),
            pltpu.VMEM((depth, width), BF16),
            pltpu.VMEM((rows, width), BF16),
            pltpu.VMEM(facts.shape, F32),
            pltpu.VMEM((rows, width), BF16),
            pltpu.VMEM((rows, width), F32),
            pltpu.SemaphoreType.DMA((2 * len(parts) * (feat // chunk) + 3,)),
        ],
        28,
        "project",
        8,
    )


def inner_kernel(first, last, hp, *refs):
    ins, facts_hbm, outs = refs[:4], refs[4], refs[5:8]
    bufs, facts_ref, sides, sems = refs[8:12], refs[12], refs[13:16], refs[16]
    rows = ins[0].shape[0]
    copies = Copies(sems)
    facts_in = copies.start(facts_hbm, facts_ref)
    loads = {}
    for h in range(first, last, 2):
        count = min(2, last - h)
        src, dst = pl.ds(h * HDIM, count * HDIM), pl.ds((h - first) * HDIM, count * HDIM)
        loads[h] = [copies.start(ref.at[:, src], buf.at[:, dst]) for ref, buf in zip(ins, bufs)]
    facts_in.wait()
    table = turned(facts_ref[...])
    row = lax.broadcasted_iota(jnp.int32, (rows, rows), 0)
    keep = row >= lax.broadcasted_iota(jnp.int32, (rows, rows), 1)
    shift = -0.5 * math.log2(HDIM)
    turn = math.log2(math.e)
    q_ref, k_ref, v_ref, do_ref = bufs
    for h in range(first, last):
        for copy in loads.get(h, ()):
            copy.wait()
        cols = slice((h - first) * HDIM, (h - first + 1) * HDIM)
        later = column(table, h) * turn + shift
        sooner = facts_ref[h : h + 1, :] * turn
        gap = jnp.concatenate([later] * (rows // LANES), axis=1) - sooner
        decays = jnp.exp2(jnp.where(keep, gap, -1e30))
        query, grad = q_ref[:, cols], do_ref[:, cols]
        scaled = scaled_keys(table, hp, h, k_ref[:, cols])
        wdv = (decays * dot(grad, v_ref[:, cols], NT)).astype(BF16)
        wkq = (decays * dot(query, scaled, NT)).astype(BF16)
        sides[0][:, cols] = dot(wdv, scaled, NN).astype(BF16)
        sides[1][:, cols] = dot(query, wdv, TN).T.astype(BF16)
        sides[2][:, cols] = dot(grad, wkq, TN).T.astype(BF16)
        if h + 1 == last or h + 1 in loads:
            from_head = h if h in loads else h - 1
            done = slice((from_head - first) * HDIM, (h + 1 - first) * HDIM)
            for side, out in zip(sides, outs):
                copies.store(side.at[:, done], out.at[:, done])
    copies.finish()


def inner(first, last, query, keys, values, d_out, facts, hp):
    rows = query.shape[0]
    width = (last - first) * HDIM
    pairs = -(-(last - first) // 2)
    return kernel_call(
        functools.partial(inner_kernel, first, last, hp),
        (query, keys, values, d_out, facts),
        [HB] * 5,
        [((rows, width), BF16)] * 3,
        (HB,) * 3,
        [
            *[pltpu.VMEM((rows, width), BF16)] * 4,
            pltpu.VMEM(facts.shape, F32),
            *[pltpu.VMEM((rows, width), BF16)] * 3,
            pltpu.SemaphoreType.DMA((1 + 7 * pairs,)),
        ],
        24,
        "inner",
        1,
    )


def whole_head(upper, h, mine_ref, theirs_ref):
    half = HDIM // 2
    at = slice(h * half, (h + 1) * half)
    mine, theirs = mine_ref[at, :], theirs_ref[at, :]
    return jnp.concatenate([jnp.where(upper, theirs, mine), jnp.where(upper, mine, theirs)], axis=0)


def rows_of(w_hbm, shift, count, feat):
    owner = lax.rem(lax.axis_index("head") + shift, count)
    return w_hbm.at[pl.ds(pl.multiple_of(owner * feat, feat), feat), :]


def fetch_kernel(heads, count, w_hbm, do_hbm, facts_hbm, *refs):
    inner_hbm, refs = refs[: len(spans_of(heads))], refs[len(spans_of(heads)) :]
    do_ref, local_ref, table_ref, outs, (facts_ref, sems) = refs[0], refs[1], refs[2], refs[3:-2], refs[-2:]
    copies = Copies(sems)
    facts_in = copies.start(facts_hbm, facts_ref)
    for index, out in enumerate(outs):
        copies.store(rows_of(w_hbm, index + 1, count, out.shape[0]), out)
    copies.store(do_hbm, do_ref)
    for (first, last), src in zip(spans_of(heads), inner_hbm):
        copies.store(src, local_ref.at[:, pl.ds(first * HDIM, (last - first) * HDIM)])
    facts_in.wait()
    table_ref[...] = turned(facts_ref[...])
    copies.finish()


def fetch(count, w_query, d_out, facts, inner_dq, feat, heads):
    rows, width = d_out.shape
    return kernel_call(
        functools.partial(fetch_kernel, heads, count),
        (w_query, d_out, facts, *inner_dq),
        [HB] * (3 + len(inner_dq)),
        [((rows, width), BF16)] * 2 + [((rows, LANES), F32)] + [((feat, width), BF16)] * (count - 1),
        (VM,) * (count + 2),
        [pltpu.VMEM(facts.shape, F32), pltpu.SemaphoreType.DMA((count + 1 + len(inner_dq),))],
        4,
        "fetch",
        4,
    )


def query_kernel(heads, hp, count, *refs):
    mine_ref, theirs_ref, w_ref, do_ref, local_ref, table_ref, k_hbm, v_hbm, w_hbm = refs[:9]
    parts = len(spans_of(heads))
    dks, dvs, refs = refs[9 : 9 + parts], refs[9 + parts : 9 + 2 * parts], refs[9 + 2 * parts :]
    held, out_ref, k_ref, v_ref, dk_ref, dv_ref, next_table, own_first, own_second, sems = refs
    upper = lax.axis_index("ctx") % 2 == 1
    copies = Copies(sems)
    copies.store(k_hbm, k_ref)
    copies.store(v_hbm, v_ref)
    for (first, last), dk, dv in zip(spans_of(heads), dks, dvs):
        wide = pl.ds(first * HDIM, (last - first) * HDIM)
        copies.store(dk, dk_ref.at[:, wide])
        copies.store(dv, dv_ref.at[:, wide])
    half = own_first.shape[0]
    rows = rows_of(w_hbm, 0, count, 2 * half)
    copies.store(rows.at[pl.ds(0, half), :], own_first)
    copies.store(rows.at[pl.ds(half, half), :], own_second)
    table = table_ref[...]
    next_table[...] = table
    for h in range(heads):
        cols = slice(h * HDIM, (h + 1) * HDIM)
        state = whole_head(upper, h, mine_ref, theirs_ref)
        carry = dot(do_ref[:, cols], state, NT)
        held[:, cols] = (local_ref[:, cols].astype(F32) + column(table, 3 * hp + h) * carry).astype(BF16)
    put_terms(held, w_ref, out_ref)
    copies.finish()


def put_terms(dq_ref, w_ref, out_ref):
    block = min(512, out_ref.shape[1])
    for at in range(0, out_ref.shape[1], block):
        out_ref[:, at : at + block] = dot(dq_ref[...], w_ref[at : at + block, :], NT).astype(BF16)


def query_term(halves, weight, fetched, keys, values, w_query, dks, dvs, count, heads, hp):
    rows, width = keys.shape
    feat = weight.shape[0]
    vm_args, hbm_args = (*halves, weight, *fetched), (keys, values, w_query, *dks, *dvs)
    return kernel_call(
        functools.partial(query_kernel, heads, hp, count),
        (*vm_args, *hbm_args),
        [VM] * len(vm_args) + [HB] * len(hbm_args),
        [((rows, width), BF16), ((rows, feat), BF16)]
        + [((rows, width), BF16)] * 4
        + [((rows, LANES), F32)]
        + [((feat // 2, width), BF16)] * 2,
        (VM,) * 9,
        [pltpu.SemaphoreType.DMA((4 + 2 * len(dks),))],
        8,
        "query_term",
        6,
    )


def plain_term(d_query, weight):
    return kernel_call(
        put_terms,
        (d_query, weight),
        [VM, VM],
        [((d_query.shape[0], weight.shape[0]), BF16)],
        (VM,),
        [],
        12,
        "term",
        4,
    )[0]


def finish_kernel(dq_ref, w_ref, early_ref, *refs):
    arrived, (out_hbm, sent, sems) = refs[:-3], refs[-3:]
    half = w_ref.shape[0]
    copies = Copies(sems)
    block = min(512, half)
    for at in range(0, 2 * half, block):
        wide = slice(at, at + block)
        if at < half:
            total = early_ref[:, wide].astype(F32)
        else:
            total = dot(dq_ref[...], w_ref[at - half : at - half + block, :], NT).astype(BF16).astype(F32)
        for other in arrived:
            total = total + other[:, wide].astype(F32)
        sent[:, wide] = total.astype(BF16)
        copies.store(sent.at[:, wide], out_hbm.at[:, wide])
    copies.finish()


def finish(d_query, weight, early, arrived):
    rows, feat = arrived[0].shape
    return kernel_call(
        finish_kernel,
        (d_query, weight, early, *arrived),
        [VM] * (3 + len(arrived)),
        [((rows, feat), BF16)],
        (HB,),
        [
            pltpu.VMEM((rows, feat), BF16),
            pltpu.SemaphoreType.DMA((feat // min(512, feat // 2),)),
        ],
        12,
        "finish",
        6,
    )[0]


def close_kernel(
    heads, hp, mine_ref, theirs_ref, k_ref, v_ref, dk_ref, dv_ref, table_ref, dq_ref, own_ref, dk_hbm, dv_hbm, early_ref, kside, vside, sems
):
    upper = lax.axis_index("ctx") % 2 == 1
    pair = min(2, heads)
    copies = Copies(sems)
    table = table_ref[...]
    for h in range(heads):
        cols = slice(h * HDIM, (h + 1) * HDIM)
        adjoint = whole_head(upper, h, mine_ref, theirs_ref)
        tail, gain = column(table, 2 * hp + h), column(table, hp + h)
        carry_k = dot(v_ref[:, cols], adjoint, NT)
        kside[:, cols] = (gain * (dk_ref[:, cols].astype(F32) + tail * carry_k)).astype(BF16)
        carry_v = dot(scaled_keys(table, hp, h, k_ref[:, cols]), adjoint, NN)
        vside[:, cols] = (dv_ref[:, cols].astype(F32) + tail * carry_v).astype(BF16)
        if (h + 1) % pair == 0:
            wide = slice((h + 1 - pair) * HDIM, (h + 1) * HDIM)
            copies.store(kside.at[:, wide], dk_hbm.at[:, wide])
            copies.store(vside.at[:, wide], dv_hbm.at[:, wide])
    put_terms(dq_ref, own_ref, early_ref)
    copies.finish()


def close(halves, held, d_query, own, heads, hp):
    rows, width = d_query.shape
    args = (*halves, *held, d_query, own)
    buf = pltpu.VMEM((rows, width), BF16)
    return kernel_call(
        functools.partial(close_kernel, heads, hp),
        args,
        [VM] * len(args),
        [((rows, width), BF16)] * 2 + [((rows, own.shape[0]), BF16)],
        (HB, HB, VM),
        [buf, buf, pltpu.SemaphoreType.DMA((2 * (heads // min(2, heads)),))],
        12,
        "close",
        100,
    )


def body(ctx_size, head_size, hidden, w_query, keys, values, d_out, log_decay):
    rows, feat = hidden.shape
    heads = log_decay.shape[1]
    width = w_query.shape[1]
    hp = sublanes(heads)
    scaling = HDIM ** (-0.5)
    me = lax.axis_index("ctx")

    parts = [hidden]
    for shift in range(1, head_size):
        ring = [(i, (i + shift) % head_size) for i in range(head_size)]
        parts.append(lax.ppermute(hidden, "head", ring))

    facts, kept, sent, share = prepare(log_decay.T, keys, values, heads, hp, scaling)
    query, akept, asent = project(parts, w_query, d_out, facts, hp)

    size = width // 2
    wide = lambda factor: factor[:heads, None, :]
    cube = lambda flat: flat[:size].reshape(heads, HDIM // 2, HDIM).astype(F32)
    flat = lambda cubes: cubes.astype(BF16).reshape(size, HDIM)
    split = lambda f: (f.astype(BF16), (f - f.astype(BF16).astype(F32)).astype(BF16))
    joined = lambda rows: rows[size : size + hp].astype(F32) + rows[size + hp :].astype(F32)
    stages = (ctx_size - 1).bit_length()
    uppers = [(me & (1 << stage)) != 0 for stage in range(stages)]

    def send(array, stage):
        dist = 1 << (stage % stages)
        return lax.ppermute(array, "ctx", [(i, i ^ dist) for i in range(ctx_size)])

    shares, others = [share], []
    before, after = [jnp.ones_like(share)], [jnp.ones_like(share)]

    def fold(stage, total, carried, arrived, up):
        upper = uppers[stage]
        first = upper if up else ~upper
        arrived = cube(arrived)
        if stage > 0:
            weight = jnp.where(first, before[stage] if up else after[stage], 0.0)
            carried = carried + wide(weight) * arrived
        if stage == stages - 1:
            lead = uppers[0] if up else ~uppers[0]
            block, other = total
            mine = jnp.where(lead, cube(other) + wide(others[0]) * carried, carried)
            theirs = jnp.where(lead, carried, cube(block) + wide(shares[0]) * carried)
            return flat(theirs), flat(mine), None
        own, other = jnp.where(first, 1.0, others[stage]), jnp.where(first, shares[stage], 1.0)
        total = wide(own) * total + wide(other) * arrived
        return flat(total), total, carried

    def fold_factors(stage, arrived):
        theirs = joined(arrived)
        others.append(theirs)
        shares.append(shares[stage] * theirs)
        upper = uppers[stage]
        pair = stage == 0
        before.append(before[stage] if pair else jnp.where(upper, before[stage] * theirs, before[stage]))
        after.append(after[stage] if pair else jnp.where(upper, after[stage], after[stage] * theirs))

    class Chain:
        def __init__(self, kept, sent, up):
            self.kept, self.sent, self.up = kept, sent, up
            self.total, self.carried, self.stage, self.arrived = cube(kept), jnp.zeros_like(cube(kept)), 0, None

        def go(self):
            self.arrived = send(self.sent, self.stage)

        def take(self):
            stage, self.stage = self.stage, self.stage + 1
            if stage == 0:
                self.first = self.arrived
            total = self.total if stage < stages - 1 else (self.kept, self.first)
            if self.up and stage < stages - 1:
                fold_factors(stage, self.arrived)
            self.sent, self.total, self.carried = fold(stage, total, self.carried, self.arrived, self.up)
            if self.up and stage + 2 < stages:
                self.sent = jnp.concatenate([self.sent, *split(shares[-1])], axis=0)

    states, adjoints = Chain(kept, sent, True), Chain(akept, asent, False)
    spans = spans_of(heads)
    pending = list(spans)
    inner_parts = []
    barrier = lax.optimization_barrier
    for stage in range(stages + 1):
        if stage == stages:
            weight, _ = barrier((w_query, adjoints.sent))
            dqs, dks, dvs = zip(*inner_parts)
            *fetched, = fetch(head_size, weight, d_out, facts, dqs, feat, heads)
            fetched, weights = fetched[:3], fetched[3:]
        states.go()
        if stage == 0:
            states.arrived, query, adjoints.kept, adjoints.sent = barrier(
                (states.arrived, query, adjoints.kept, adjoints.sent)
            )
            adjoints.total = cube(adjoints.kept)
        else:
            adjoints.go()
            if pending and stage <= len(spans):
                query, _ = barrier((query, adjoints.sent))
                part = inner(*pending.pop(0), query, keys, values, d_out, facts, hp)
                states.arrived, *part = barrier((states.arrived, *part))
                inner_parts.append(part)
        if stage == stages - 1:
            adjoints.take()
            states.arrived, _ = barrier((states.arrived, adjoints.sent))
            states.take()
            continue
        if stage < stages:
            states.take()
        if stage >= 1:
            adjoints.arrived, _ = barrier((adjoints.arrived, states.sent if stage < stages else states.total))
            adjoints.take()
    adjoints.go()
    states.arrived, _ = barrier((states.arrived, adjoints.sent))
    state_halves = (states.total, states.arrived)
    adjoint_halves = (adjoints.total, adjoints.arrived)
    arrived = []
    for shift in range(1, head_size):
        ring = [(i, (i + shift) % head_size) for i in range(head_size)]
        if shift == 1:
            d_query, term, *held, own_first, own_second = query_term(
                state_halves, weights[0], fetched, keys, values, w_query, dks, dvs, head_size, heads, hp
            )
        else:
            term = plain_term(d_query, weights[shift - 1])
        arrived.append(lax.ppermute(term, "head", ring))
    d_keys, d_values, early = close(adjoint_halves, held, d_query, own_first, heads, hp)
    d_hidden = finish(d_query, own_second, early, arrived)
    return (d_hidden, d_keys, d_values)


def solution(mesh):
    return jax.shard_map(
        functools.partial(body, mesh.shape["ctx"], mesh.shape["head"]),
        mesh=mesh,
        in_specs=(
            P("ctx", "head"),
            P(None, "head"),
            P("ctx", "head"),
            P("ctx", "head"),
            P("ctx", "head"),
            P("ctx", "head"),
        ),
        out_specs=(P("ctx", "head"), P("ctx", "head"), P("ctx", "head")),
        check_vma=False,
    )
```

```python
import functools
import math

import jax
import jax.numpy as jnp
from jax import lax
from jax.experimental import pallas as pl
from jax.experimental.pallas import tpu as pltpu
from jax.sharding import PartitionSpec as P

HDIM = 128
LANES = 128
F32, BF16 = jnp.float32, jnp.bfloat16
MIB = 1 << 20
VM = pl.BlockSpec(memory_space=pltpu.VMEM)
SM = pl.BlockSpec(memory_space=pltpu.SMEM)
HB = pl.BlockSpec(memory_space=pltpu.HBM)
AN = pl.BlockSpec(memory_space=pl.ANY)

NN = (((1,), (0,)), ((), ()))
NT = (((1,), (1,)), ((), ()))
TN = (((0,), (0,)), ((), ()))


def dot(a, b, dims):
    return lax.dot_general(a, b, dims, preferred_element_type=F32)


def kernel_call(kernel, args, specs, outs, out_specs, scratch, mib, name, micros):
    pinned = [pltpu.with_memory_space_constraint(a, pltpu.HBM) if s is HB else a for a, s in zip(args, specs)]
    placed = tuple(
        (pltpu.HBM if s is HB else jax.ShapeDtypeStruct)(shape, dtype) for (shape, dtype), s in zip(outs, out_specs)
    )
    return pl.pallas_call(
        kernel,
        in_specs=specs,
        out_specs=tuple(out_specs),
        out_shape=placed,
        scratch_shapes=scratch,
        compiler_params=pltpu.CompilerParams(vmem_limit_bytes=mib * MIB),
        cost_estimate=pl.CostEstimate(flops=int(micros * 1e9), bytes_accessed=1, transcendentals=0),
        name=name,
    )(*pinned)


def sublanes(count):
    return -(-count // 8) * 8


def expm1_negative(z):
    series = jnp.full_like(z, 1.0)
    for order in range(10, 1, -1):
        series = 1.0 + z * series * (1.0 / order)
    return jnp.where(z > -0.5, z * series, jnp.exp(z) - 1.0)


def column(table, lane, width=LANES):
    return jnp.broadcast_to(table[:, lane : lane + 1], (table.shape[0], width))


class Copies:
    def __init__(self, sems):
        self.sems, self.count, self.out = sems, 0, []

    def start(self, src, dst):
        copy = pltpu.make_async_copy(src, dst, self.sems.at[self.count])
        self.count += 1
        copy.start()
        return copy

    def store(self, src, dst):
        self.out.append(self.start(src, dst))

    def finish(self):
        for copy in self.out:
            copy.wait()


def spans_of(heads):
    edges = sorted({0, heads // 4, heads // 2, heads})
    return list(zip(edges, edges[1:]))


def groups(heads):
    size = min(4, heads)
    return [(f, f + size, slice(f * HDIM, (f + size) * HDIM)) for f in range(0, heads, size)]


def turned(facts):
    spare = jnp.zeros((LANES - facts.shape[0], facts.shape[1]), F32)
    return jnp.concatenate([facts, spare], axis=0).T


def put_halves(upper, h, local, kept_ref, sent_ref):
    half = HDIM // 2
    at = slice(h * half, (h + 1) * half)
    kept_ref[at, :] = jnp.where(upper, local[half:], local[:half]).astype(BF16)
    sent_ref[at, :] = jnp.where(upper, local[:half], local[half:]).astype(BF16)


def prepare_kernel(
    heads, hp, scaling, ld_hbm, k_hbm, v_hbm, facts_hbm, kept_ref, sent_ref, share_ref, *scratch
):
    ld, facts_ref, kbuf, vbuf, sems = scratch
    upper = lax.axis_index("ctx") % 2 == 1
    rows = kbuf.shape[0]
    copies = Copies(sems)
    ld_in = copies.start(ld_hbm, ld)
    loads = []
    for _, _, wide in groups(heads):
        loads.append([copies.start(src.at[:, wide], dst.at[:, wide]) for src, dst in ((k_hbm, kbuf), (v_hbm, vbuf))])
    ld_in.wait()
    logs = ld[...]
    if heads < hp:
        logs = jnp.concatenate([logs, jnp.zeros((hp - heads, rows), F32)], axis=0)
    lane = lax.broadcasted_iota(jnp.int32, logs.shape, 1)
    cumulative = logs
    step = 1
    while step < rows:
        moved = pltpu.roll(cumulative, step, 1)
        cumulative = cumulative + jnp.where(lane >= step, moved, 0.0)
        step *= 2
    total = cumulative[:, rows - 1 :]
    gain = jnp.sqrt(-expm1_negative(2.0 * logs))
    tail = jnp.exp(total - cumulative)
    lead = scaling * jnp.exp(cumulative)
    facts = jnp.concatenate([cumulative, gain, tail, lead], axis=0)
    facts_ref[...] = facts
    copies.store(facts_ref, facts_hbm)
    table = turned(facts)
    share = jnp.broadcast_to(jnp.exp(total), (hp, LANES))
    high = share.astype(BF16)
    low = (share - high.astype(F32)).astype(BF16)
    share_ref[...] = share
    base = heads * HDIM // 2
    sent_ref[base:, :] = jnp.concatenate([high.astype(F32), low.astype(F32)], axis=0).astype(BF16)
    for (first, last, _), load in zip(groups(heads), loads):
        for copy in load:
            copy.wait()
        for h in range(first, last):
            cols = slice(h * HDIM, (h + 1) * HDIM)
            scaled = scaled_keys(table, hp, h, kbuf[:, cols])
            decayed = (column(table, 2 * hp + h) * scaled.astype(F32)).astype(BF16)
            put_halves(upper, h, dot(decayed, vbuf[:, cols], TN), kept_ref, sent_ref)
    copies.finish()


def scaled_keys(table, hp, h, keys):
    return (column(table, hp + h) * keys.astype(F32)).astype(BF16)


def prepare(logs, keys, values, heads, hp, scaling):
    rows, width = keys.shape
    buf = pltpu.VMEM((rows, width), BF16)
    return kernel_call(
        functools.partial(prepare_kernel, heads, hp, scaling),
        (logs, keys, values),
        [HB] * 3,
        [
            ((4 * hp, rows), F32),
            ((width // 2, HDIM), BF16),
            ((width // 2 + 2 * hp, HDIM), BF16),
            ((hp, LANES), F32),
        ],
        (HB, VM, VM, VM),
        [
            pltpu.VMEM((heads, rows), F32),
            pltpu.VMEM((4 * hp, rows), F32),
            buf,
            buf,
            pltpu.SemaphoreType.DMA((2 + 2 * len(groups(heads)),)),
        ],
        12,
        "prepare",
        4,
    )


def project_kernel(hp, nparts, chunk, *refs):
    parts, (w_hbm, do_hbm, facts_hbm, q_hbm, kept_ref, sent_ref) = refs[:nparts], refs[nparts : nparts + 6]
    hbuf, wbuf, dobuf, facts_ref, qbuf, total, sems = refs[nparts + 6 :]
    rows, feat = parts[0].shape
    width = wbuf.shape[1]
    heads = width // HDIM
    upper = lax.axis_index("ctx") % 2 == 1
    copies = Copies(sems)
    loads = []
    for part, ref in enumerate(parts):
        for first in range(0, feat, chunk):
            here = pl.ds(part * feat + first, chunk)
            owner = lax.rem(lax.axis_index("head") + nparts - part, nparts)
            start = pl.multiple_of(owner * feat + first, chunk)
            loads.append(
                (
                    slice(part * feat + first, part * feat + first + chunk),
                    copies.start(ref.at[:, pl.ds(first, chunk)], hbuf.at[:, here]),
                    copies.start(w_hbm.at[pl.ds(start, chunk), :], wbuf.at[here, :]),
                )
            )
    late = [copies.start(facts_hbm, facts_ref), copies.start(do_hbm, dobuf)]
    block = min(256, width)
    for order, (here, h_in, w_in) in enumerate(loads):
        h_in.wait()
        w_in.wait()
        for first in range(0, width, block):
            wide = slice(first, first + block)
            term = dot(hbuf[:, here], wbuf[here, wide], NN)
            if order == 0:
                total[:, wide] = term
            elif order < len(loads) - 1:
                total[:, wide] += term
            else:
                qbuf[:, wide] = (total[:, wide] + term).astype(BF16)
    for copy in late:
        copy.wait()
    copies.store(qbuf, q_hbm)
    table = turned(facts_ref[...])
    for h in range(heads):
        cols = slice(h * HDIM, (h + 1) * HDIM)
        decayed = (column(table, 3 * hp + h) * qbuf[:, cols].astype(F32)).astype(BF16)
        put_halves(upper, h, dot(decayed, dobuf[:, cols], TN), kept_ref, sent_ref)
    copies.finish()


def project(parts, w_query, d_out, facts, hp):
    rows, feat = parts[0].shape
    depth, width = w_query.shape
    chunk = min(512, feat)
    return kernel_call(
        functools.partial(project_kernel, hp, len(parts), chunk),
        (*parts, w_query, d_out, facts),
        [HB] + [AN] * (len(parts) - 1) + [HB] * 3,
        [((rows, width), BF16), ((width // 2, HDIM), BF16), ((width // 2, HDIM), BF16)],
        (HB, VM, VM),
        [
            pltpu.VMEM((rows, depth), BF16),
            pltpu.VMEM((depth, width), BF16),
            pltpu.VMEM((rows, width), BF16),
            pltpu.VMEM(facts.shape, F32),
            pltpu.VMEM((rows, width), BF16),
            pltpu.VMEM((rows, width), F32),
            pltpu.SemaphoreType.DMA((2 * len(parts) * (feat // chunk) + 3,)),
        ],
        28,
        "project",
        8,
    )


def inner_kernel(first, last, hp, *refs):
    ins, facts_hbm, outs = refs[:4], refs[4], refs[5:8]
    bufs, facts_ref, sides, sems = refs[8:12], refs[12], refs[13:16], refs[16]
    rows = ins[0].shape[0]
    copies = Copies(sems)
    facts_in = copies.start(facts_hbm, facts_ref)
    loads = {}
    for h in range(first, last, 2):
        count = min(2, last - h)
        src, dst = pl.ds(h * HDIM, count * HDIM), pl.ds((h - first) * HDIM, count * HDIM)
        loads[h] = [copies.start(ref.at[:, src], buf.at[:, dst]) for ref, buf in zip(ins, bufs)]
    facts_in.wait()
    table = turned(facts_ref[...])
    row = lax.broadcasted_iota(jnp.int32, (rows, rows), 0)
    keep = row >= lax.broadcasted_iota(jnp.int32, (rows, rows), 1)
    shift = -0.5 * math.log2(HDIM)
    turn = math.log2(math.e)
    q_ref, k_ref, v_ref, do_ref = bufs
    for h in range(first, last):
        for copy in loads.get(h, ()):
            copy.wait()
        cols = slice((h - first) * HDIM, (h - first + 1) * HDIM)
        later = column(table, h) * turn + shift
        sooner = facts_ref[h : h + 1, :] * turn
        gap = jnp.concatenate([later] * (rows // LANES), axis=1) - sooner
        decays = jnp.exp2(jnp.where(keep, gap, -1e30))
        query, grad = q_ref[:, cols], do_ref[:, cols]
        scaled = scaled_keys(table, hp, h, k_ref[:, cols])
        wdv = (decays * dot(grad, v_ref[:, cols], NT)).astype(BF16)
        wkq = (decays * dot(query, scaled, NT)).astype(BF16)
        sides[0][:, cols] = dot(wdv, scaled, NN).astype(BF16)
        sides[1][:, cols] = dot(query, wdv, TN).T.astype(BF16)
        sides[2][:, cols] = dot(grad, wkq, TN).T.astype(BF16)
        if h + 1 == last or h + 1 in loads:
            from_head = h if h in loads else h - 1
            done = slice((from_head - first) * HDIM, (h + 1 - first) * HDIM)
            for side, out in zip(sides, outs):
                copies.store(side.at[:, done], out.at[:, done])
    copies.finish()


def inner(first, last, query, keys, values, d_out, facts, hp):
    rows = query.shape[0]
    width = (last - first) * HDIM
    pairs = -(-(last - first) // 2)
    return kernel_call(
        functools.partial(inner_kernel, first, last, hp),
        (query, keys, values, d_out, facts),
        [HB] * 5,
        [((rows, width), BF16)] * 3,
        (HB,) * 3,
        [
            *[pltpu.VMEM((rows, width), BF16)] * 4,
            pltpu.VMEM(facts.shape, F32),
            *[pltpu.VMEM((rows, width), BF16)] * 3,
            pltpu.SemaphoreType.DMA((1 + 7 * pairs,)),
        ],
        24,
        "inner",
        1,
    )


def whole_head(upper, h, mine_ref, theirs_ref):
    half = HDIM // 2
    at = slice(h * half, (h + 1) * half)
    mine, theirs = mine_ref[at, :], theirs_ref[at, :]
    return jnp.concatenate([jnp.where(upper, theirs, mine), jnp.where(upper, mine, theirs)], axis=0)


def rows_of(w_hbm, shift, count, feat):
    owner = lax.rem(lax.axis_index("head") + shift, count)
    return w_hbm.at[pl.ds(pl.multiple_of(owner * feat, feat), feat), :]


def fetch_kernel(heads, count, w_hbm, do_hbm, facts_hbm, *refs):
    inner_hbm, refs = refs[: len(spans_of(heads))], refs[len(spans_of(heads)) :]
    do_ref, local_ref, table_ref, outs, (facts_ref, sems) = refs[0], refs[1], refs[2], refs[3:-2], refs[-2:]
    copies = Copies(sems)
    facts_in = copies.start(facts_hbm, facts_ref)
    for index, out in enumerate(outs):
        copies.store(rows_of(w_hbm, index + 1, count, out.shape[0]), out)
    copies.store(do_hbm, do_ref)
    for (first, last), src in zip(spans_of(heads), inner_hbm):
        copies.store(src, local_ref.at[:, pl.ds(first * HDIM, (last - first) * HDIM)])
    facts_in.wait()
    table_ref[...] = turned(facts_ref[...])
    copies.finish()


def fetch(count, w_query, d_out, facts, inner_dq, feat, heads):
    rows, width = d_out.shape
    return kernel_call(
        functools.partial(fetch_kernel, heads, count),
        (w_query, d_out, facts, *inner_dq),
        [HB] * (3 + len(inner_dq)),
        [((rows, width), BF16)] * 2 + [((rows, LANES), F32)] + [((feat, width), BF16)] * (count - 1),
        (VM,) * (count + 2),
        [pltpu.VMEM(facts.shape, F32), pltpu.SemaphoreType.DMA((count + 1 + len(inner_dq),))],
        4,
        "fetch",
        4,
    )


def query_kernel(heads, hp, count, *refs):
    mine_ref, theirs_ref, w_ref, do_ref, local_ref, table_ref, k_hbm, v_hbm, w_hbm = refs[:9]
    parts = len(spans_of(heads))
    dks, dvs, refs = refs[9 : 9 + parts], refs[9 + parts : 9 + 2 * parts], refs[9 + 2 * parts :]
    held, out_ref, k_ref, v_ref, dk_ref, dv_ref, next_table, *owns, sems = refs
    upper = lax.axis_index("ctx") % 2 == 1
    copies = Copies(sems)
    copies.store(k_hbm, k_ref)
    copies.store(v_hbm, v_ref)
    for (first, last), dk, dv in zip(spans_of(heads), dks, dvs):
        wide = pl.ds(first * HDIM, (last - first) * HDIM)
        copies.store(dk, dk_ref.at[:, wide])
        copies.store(dv, dv_ref.at[:, wide])
    at, rows = 0, rows_of(w_hbm, 0, count, w_ref.shape[0])
    for own in owns:
        size = own.shape[0]
        copies.store(rows.at[pl.ds(at, size), :], own)
        at += size
    table = table_ref[...]
    next_table[...] = table
    for h in range(heads):
        cols = slice(h * HDIM, (h + 1) * HDIM)
        state = whole_head(upper, h, mine_ref, theirs_ref)
        carry = dot(do_ref[:, cols], state, NT)
        held[:, cols] = (local_ref[:, cols].astype(F32) + column(table, 3 * hp + h) * carry).astype(BF16)
    put_terms(held, w_ref, out_ref)
    copies.finish()


def put_terms(dq_ref, w_ref, out_ref, first=0):
    block = min(512, w_ref.shape[0])
    for at in range(0, w_ref.shape[0], block):
        out_ref[:, first + at : first + at + block] = dot(dq_ref[...], w_ref[at : at + block, :], NT).astype(BF16)


def query_term(halves, weight, fetched, keys, values, w_query, dks, dvs, count, heads, hp):
    rows, width = keys.shape
    feat = weight.shape[0]
    vm_args, hbm_args = (*halves, weight, *fetched), (keys, values, w_query, *dks, *dvs)
    return kernel_call(
        functools.partial(query_kernel, heads, hp, count),
        (*vm_args, *hbm_args),
        [VM] * len(vm_args) + [HB] * len(hbm_args),
        [((rows, width), BF16), ((rows, feat), BF16)]
        + [((rows, width), BF16)] * 4
        + [((rows, LANES), F32)]
        + [((size, width), BF16) for size in (feat // 2, feat // 2)],
        (VM,) * 9,
        [pltpu.SemaphoreType.DMA((4 + 2 * len(dks),))],
        8,
        "query_term",
        6,
    )


def plain_term(d_query, weight):
    return kernel_call(
        put_terms,
        (d_query, weight),
        [VM, VM],
        [((d_query.shape[0], weight.shape[0]), BF16)],
        (VM,),
        [],
        12,
        "term",
        4,
    )[0]


def finish_kernel(*refs):
    terms, (out_hbm, sent, sems) = refs[:-3], refs[-3:]
    feat = sent.shape[1]
    copies = Copies(sems)
    block = min(512, feat)
    for at in range(0, feat, block):
        wide = slice(at, at + block)
        total = terms[0][:, wide].astype(F32)
        for other in terms[1:]:
            total = total + other[:, wide].astype(F32)
        sent[:, wide] = total.astype(BF16)
        copies.store(sent.at[:, wide], out_hbm.at[:, wide])
    copies.finish()


def finish(terms):
    rows, feat = terms[0].shape
    return kernel_call(
        finish_kernel,
        terms,
        [VM] * len(terms),
        [((rows, feat), BF16)],
        (HB,),
        [
            pltpu.VMEM((rows, feat), BF16),
            pltpu.SemaphoreType.DMA((feat // min(512, feat),)),
        ],
        12,
        "finish",
        6,
    )[0]


def close_kernel(
    heads, hp, mine_ref, theirs_ref, k_ref, v_ref, dk_ref, dv_ref, table_ref, dq_ref, own_ref, second_ref, *refs
):
    dk_hbm, dv_hbm, term_ref, kside, vside, sems = refs
    upper = lax.axis_index("ctx") % 2 == 1
    pair = min(2, heads)
    copies = Copies(sems)
    table = table_ref[...]
    for h in range(heads):
        cols = slice(h * HDIM, (h + 1) * HDIM)
        adjoint = whole_head(upper, h, mine_ref, theirs_ref)
        tail, gain = column(table, 2 * hp + h), column(table, hp + h)
        carry_k = dot(v_ref[:, cols], adjoint, NT)
        kside[:, cols] = (gain * (dk_ref[:, cols].astype(F32) + tail * carry_k)).astype(BF16)
        carry_v = dot(scaled_keys(table, hp, h, k_ref[:, cols]), adjoint, NN)
        vside[:, cols] = (dv_ref[:, cols].astype(F32) + tail * carry_v).astype(BF16)
        if (h + 1) % pair == 0:
            wide = slice((h + 1 - pair) * HDIM, (h + 1) * HDIM)
            copies.store(kside.at[:, wide], dk_hbm.at[:, wide])
            copies.store(vside.at[:, wide], dv_hbm.at[:, wide])
    put_terms(dq_ref, own_ref, term_ref)
    put_terms(dq_ref, second_ref, term_ref, own_ref.shape[0])
    copies.finish()


def close(halves, held, d_query, owns, heads, hp):
    rows, width = d_query.shape
    args = (*halves, *held, d_query, *owns)
    buf = pltpu.VMEM((rows, width), BF16)
    return kernel_call(
        functools.partial(close_kernel, heads, hp),
        args,
        [VM] * len(args),
        [((rows, width), BF16)] * 2 + [((rows, sum(own.shape[0] for own in owns)), BF16)],
        (HB, HB, VM),
        [buf, buf, pltpu.SemaphoreType.DMA((2 * (heads // min(2, heads)),))],
        12,
        "close",
        100,
    )


def body(ctx_size, head_size, hidden, w_query, keys, values, d_out, log_decay):
    rows, feat = hidden.shape
    heads = log_decay.shape[1]
    width = w_query.shape[1]
    hp = sublanes(heads)
    scaling = HDIM ** (-0.5)
    me = lax.axis_index("ctx")

    parts = [hidden]
    for shift in range(1, head_size):
        ring = [(i, (i + shift) % head_size) for i in range(head_size)]
        parts.append(lax.ppermute(hidden, "head", ring))

    facts, kept, sent, share = prepare(log_decay.T, keys, values, heads, hp, scaling)
    query, akept, asent = project(parts, w_query, d_out, facts, hp)

    size = width // 2
    wide = lambda factor: factor[:heads, None, :]
    cube = lambda flat: flat[:size].reshape(heads, HDIM // 2, HDIM).astype(F32)
    flat = lambda cubes: cubes.astype(BF16).reshape(size, HDIM)
    split = lambda f: (f.astype(BF16), (f - f.astype(BF16).astype(F32)).astype(BF16))
    joined = lambda rows: rows[size : size + hp].astype(F32) + rows[size + hp :].astype(F32)
    stages = (ctx_size - 1).bit_length()
    uppers = [(me & (1 << stage)) != 0 for stage in range(stages)]

    def send(array, stage):
        dist = 1 << (stage % stages)
        return lax.ppermute(array, "ctx", [(i, i ^ dist) for i in range(ctx_size)])

    shares, others = [share], []
    before, after = [jnp.ones_like(share)], [jnp.ones_like(share)]

    def fold(stage, total, carried, arrived, up):
        upper = uppers[stage]
        first = upper if up else ~upper
        arrived = cube(arrived)
        if stage > 0:
            weight = jnp.where(first, before[stage] if up else after[stage], 0.0)
            carried = carried + wide(weight) * arrived
        if stage == stages - 1:
            lead = uppers[0] if up else ~uppers[0]
            block, other = total
            mine = jnp.where(lead, cube(other) + wide(others[0]) * carried, carried)
            theirs = jnp.where(lead, carried, cube(block) + wide(shares[0]) * carried)
            return flat(theirs), flat(mine), None
        own, other = jnp.where(first, 1.0, others[stage]), jnp.where(first, shares[stage], 1.0)
        total = wide(own) * total + wide(other) * arrived
        return flat(total), total, carried

    def fold_factors(stage, arrived):
        theirs = joined(arrived)
        others.append(theirs)
        shares.append(shares[stage] * theirs)
        upper = uppers[stage]
        pair = stage == 0
        before.append(before[stage] if pair else jnp.where(upper, before[stage] * theirs, before[stage]))
        after.append(after[stage] if pair else jnp.where(upper, after[stage], after[stage] * theirs))

    class Chain:
        def __init__(self, kept, sent, up):
            self.kept, self.sent, self.up = kept, sent, up
            self.total, self.carried, self.stage, self.arrived = cube(kept), jnp.zeros_like(cube(kept)), 0, None

        def go(self):
            self.arrived = send(self.sent, self.stage)

        def take(self):
            stage, self.stage = self.stage, self.stage + 1
            if stage == 0:
                self.first = self.arrived
            total = self.total if stage < stages - 1 else (self.kept, self.first)
            if self.up and stage < stages - 1:
                fold_factors(stage, self.arrived)
            self.sent, self.total, self.carried = fold(stage, total, self.carried, self.arrived, self.up)
            if self.up and stage + 2 < stages:
                self.sent = jnp.concatenate([self.sent, *split(shares[-1])], axis=0)

    states, adjoints = Chain(kept, sent, True), Chain(akept, asent, False)
    spans = spans_of(heads)
    pending = list(spans)
    inner_parts = []
    barrier = lax.optimization_barrier
    for stage in range(stages + 1):
        if stage == stages:
            weight, _ = barrier((w_query, adjoints.sent))
            dqs, dks, dvs = zip(*inner_parts)
            *fetched, = fetch(head_size, weight, d_out, facts, dqs, feat, heads)
            fetched, weights = fetched[:3], fetched[3:]
        states.go()
        if stage == 0:
            states.arrived, query, adjoints.kept, adjoints.sent = barrier(
                (states.arrived, query, adjoints.kept, adjoints.sent)
            )
            adjoints.total = cube(adjoints.kept)
        else:
            adjoints.go()
            if pending and stage <= len(spans):
                query, _ = barrier((query, adjoints.sent))
                part = inner(*pending.pop(0), query, keys, values, d_out, facts, hp)
                states.arrived, *part = barrier((states.arrived, *part))
                inner_parts.append(part)
        if stage == stages - 1:
            adjoints.take()
            states.arrived, _ = barrier((states.arrived, adjoints.sent))
            states.take()
            continue
        if stage < stages:
            states.take()
        if stage >= 1:
            adjoints.arrived, _ = barrier((adjoints.arrived, states.sent if stage < stages else states.total))
            adjoints.take()
    adjoints.go()
    states.arrived, _ = barrier((states.arrived, adjoints.sent))
    state_halves = (states.total, states.arrived)
    adjoint_halves = (adjoints.total, adjoints.arrived)
    arrived = []
    for shift in range(1, head_size):
        ring = [(i, (i + shift) % head_size) for i in range(head_size)]
        if shift == 1:
            d_query, term, *held, first, second = query_term(
                state_halves, weights[0], fetched, keys, values, w_query, dks, dvs, head_size, heads, hp
            )
        else:
            term = plain_term(d_query, weights[shift - 1])
        arrived.append(lax.ppermute(term, "head", ring))
    d_keys, d_values, own = close(adjoint_halves, held, d_query, (first, second), heads, hp)
    d_hidden = finish((own, *arrived))
    return (d_hidden, d_keys, d_values)


def solution(mesh):
    return jax.shard_map(
        functools.partial(body, mesh.shape["ctx"], mesh.shape["head"]),
        mesh=mesh,
        in_specs=(
            P("ctx", "head"),
            P(None, "head"),
            P("ctx", "head"),
            P("ctx", "head"),
            P("ctx", "head"),
            P("ctx", "head"),
        ),
        out_specs=(P("ctx", "head"), P("ctx", "head"), P("ctx", "head")),
        check_vma=False,
    )
```

```python
import functools
import math

import jax
import jax.numpy as jnp
from jax import lax
from jax.experimental import pallas as pl
from jax.experimental.pallas import tpu as pltpu
from jax.sharding import PartitionSpec as P

HDIM = 128
LANES = 128
F32, BF16 = jnp.float32, jnp.bfloat16
MIB = 1 << 20
VM = pl.BlockSpec(memory_space=pltpu.VMEM)
SM = pl.BlockSpec(memory_space=pltpu.SMEM)
HB = pl.BlockSpec(memory_space=pltpu.HBM)
AN = pl.BlockSpec(memory_space=pl.ANY)

NN = (((1,), (0,)), ((), ()))
NT = (((1,), (1,)), ((), ()))
TN = (((0,), (0,)), ((), ()))


def dot(a, b, dims):
    return lax.dot_general(a, b, dims, preferred_element_type=F32)


def kernel_call(kernel, args, specs, outs, out_specs, scratch, mib, name, micros):
    pinned = [pltpu.with_memory_space_constraint(a, pltpu.HBM) if s is HB else a for a, s in zip(args, specs)]
    placed = tuple(
        (pltpu.HBM if s is HB else jax.ShapeDtypeStruct)(shape, dtype) for (shape, dtype), s in zip(outs, out_specs)
    )
    return pl.pallas_call(
        kernel,
        in_specs=specs,
        out_specs=tuple(out_specs),
        out_shape=placed,
        scratch_shapes=scratch,
        compiler_params=pltpu.CompilerParams(vmem_limit_bytes=mib * MIB),
        cost_estimate=pl.CostEstimate(flops=int(micros * 1e9), bytes_accessed=1, transcendentals=0),
        name=name,
    )(*pinned)


def sublanes(count):
    return -(-count // 8) * 8


def expm1_negative(z):
    series = jnp.full_like(z, 1.0)
    for order in range(10, 1, -1):
        series = 1.0 + z * series * (1.0 / order)
    return jnp.where(z > -0.5, z * series, jnp.exp(z) - 1.0)


def column(table, lane, width=LANES):
    return jnp.broadcast_to(table[:, lane : lane + 1], (table.shape[0], width))


class Copies:
    def __init__(self, sems):
        self.sems, self.count, self.out = sems, 0, []

    def start(self, src, dst):
        copy = pltpu.make_async_copy(src, dst, self.sems.at[self.count])
        self.count += 1
        copy.start()
        return copy

    def store(self, src, dst):
        self.out.append(self.start(src, dst))

    def finish(self):
        for copy in self.out:
            copy.wait()


def spans_of(heads):
    edges = sorted({0, heads // 4, heads // 2, heads})
    return list(zip(edges, edges[1:]))


def groups(heads):
    size = min(4, heads)
    return [(f, f + size, slice(f * HDIM, (f + size) * HDIM)) for f in range(0, heads, size)]


def turned(facts):
    spare = jnp.zeros((LANES - facts.shape[0], facts.shape[1]), F32)
    return jnp.concatenate([facts, spare], axis=0).T


def put_halves(upper, h, local, kept_ref, sent_ref):
    half = HDIM // 2
    at = slice(h * half, (h + 1) * half)
    kept_ref[at, :] = jnp.where(upper, local[half:], local[:half]).astype(BF16)
    sent_ref[at, :] = jnp.where(upper, local[:half], local[half:]).astype(BF16)


def put_pairs(upper, first, last, left_ref, right_ref, kept_ref, sent_ref):
    for h in range(first, last, 2):
        count = min(2, last - h)
        cols = slice(h * HDIM, (h + count) * HDIM)
        both = dot(left_ref[:, cols], right_ref[:, cols], TN)
        for own in range(count):
            at = slice(own * HDIM, (own + 1) * HDIM)
            put_halves(upper, h + own, both[at, at], kept_ref, sent_ref)


def prepare_kernel(
    heads, hp, scaling, ld_hbm, k_hbm, v_hbm, facts_hbm, kept_ref, sent_ref, share_ref, *scratch
):
    ld, facts_ref, kbuf, vbuf, sems = scratch
    upper = lax.axis_index("ctx") % 2 == 1
    rows = kbuf.shape[0]
    copies = Copies(sems)
    ld_in = copies.start(ld_hbm, ld)
    loads = []
    for _, _, wide in groups(heads):
        loads.append([copies.start(src.at[:, wide], dst.at[:, wide]) for src, dst in ((k_hbm, kbuf), (v_hbm, vbuf))])
    ld_in.wait()
    logs = ld[...]
    if heads < hp:
        logs = jnp.concatenate([logs, jnp.zeros((hp - heads, rows), F32)], axis=0)
    lane = lax.broadcasted_iota(jnp.int32, logs.shape, 1)
    cumulative = logs
    step = 1
    while step < rows:
        moved = pltpu.roll(cumulative, step, 1)
        cumulative = cumulative + jnp.where(lane >= step, moved, 0.0)
        step *= 2
    total = cumulative[:, rows - 1 :]
    gain = jnp.sqrt(-expm1_negative(2.0 * logs))
    tail = jnp.exp(total - cumulative)
    lead = scaling * jnp.exp(cumulative)
    facts = jnp.concatenate([cumulative, gain, tail, lead], axis=0)
    facts_ref[...] = facts
    copies.store(facts_ref, facts_hbm)
    table = turned(facts)
    share = jnp.broadcast_to(jnp.exp(total), (hp, LANES))
    high = share.astype(BF16)
    low = (share - high.astype(F32)).astype(BF16)
    share_ref[...] = share
    base = heads * HDIM // 2
    sent_ref[base:, :] = jnp.concatenate([high.astype(F32), low.astype(F32)], axis=0).astype(BF16)
    for (first, last, _), load in zip(groups(heads), loads):
        for copy in load:
            copy.wait()
        for h in range(first, last):
            cols = slice(h * HDIM, (h + 1) * HDIM)
            scaled = scaled_keys(table, hp, h, kbuf[:, cols])
            kbuf[:, cols] = (column(table, 2 * hp + h) * scaled.astype(F32)).astype(BF16)
        put_pairs(upper, first, last, kbuf, vbuf, kept_ref, sent_ref)
    copies.finish()


def scaled_keys(table, hp, h, keys):
    return (column(table, hp + h) * keys.astype(F32)).astype(BF16)


def prepare(logs, keys, values, heads, hp, scaling):
    rows, width = keys.shape
    buf = pltpu.VMEM((rows, width), BF16)
    return kernel_call(
        functools.partial(prepare_kernel, heads, hp, scaling),
        (logs, keys, values),
        [HB] * 3,
        [
            ((4 * hp, rows), F32),
            ((width // 2, HDIM), BF16),
            ((width // 2 + 2 * hp, HDIM), BF16),
            ((hp, LANES), F32),
        ],
        (HB, VM, VM, VM),
        [
            pltpu.VMEM((heads, rows), F32),
            pltpu.VMEM((4 * hp, rows), F32),
            buf,
            buf,
            pltpu.SemaphoreType.DMA((2 + 2 * len(groups(heads)),)),
        ],
        12,
        "prepare",
        4,
    )


def project_kernel(hp, nparts, chunk, *refs):
    parts, (w_hbm, do_hbm, facts_hbm, q_hbm, kept_ref, sent_ref) = refs[:nparts], refs[nparts : nparts + 6]
    hbuf, wbuf, dobuf, facts_ref, qbuf, decayed, total, sems = refs[nparts + 6 :]
    rows, feat = parts[0].shape
    width = wbuf.shape[1]
    heads = width // HDIM
    upper = lax.axis_index("ctx") % 2 == 1
    copies = Copies(sems)
    loads = []
    for part, ref in enumerate(parts):
        for first in range(0, feat, chunk):
            here = pl.ds(part * feat + first, chunk)
            owner = lax.rem(lax.axis_index("head") + nparts - part, nparts)
            start = pl.multiple_of(owner * feat + first, chunk)
            loads.append(
                (
                    slice(part * feat + first, part * feat + first + chunk),
                    copies.start(ref.at[:, pl.ds(first, chunk)], hbuf.at[:, here]),
                    copies.start(w_hbm.at[pl.ds(start, chunk), :], wbuf.at[here, :]),
                )
            )
    late = [copies.start(facts_hbm, facts_ref), copies.start(do_hbm, dobuf)]
    block = min(256, width)
    for order, (here, h_in, w_in) in enumerate(loads):
        h_in.wait()
        w_in.wait()
        for first in range(0, width, block):
            wide = slice(first, first + block)
            term = dot(hbuf[:, here], wbuf[here, wide], NN)
            if order == 0:
                total[:, wide] = term
            elif order < len(loads) - 1:
                total[:, wide] += term
            else:
                qbuf[:, wide] = (total[:, wide] + term).astype(BF16)
    for copy in late:
        copy.wait()
    copies.store(qbuf, q_hbm)
    table = turned(facts_ref[...])
    for h in range(heads):
        cols = slice(h * HDIM, (h + 1) * HDIM)
        decayed[:, cols] = (column(table, 3 * hp + h) * qbuf[:, cols].astype(F32)).astype(BF16)
    put_pairs(upper, 0, heads, decayed, dobuf, kept_ref, sent_ref)
    copies.finish()


def project(parts, w_query, d_out, facts, hp):
    rows, feat = parts[0].shape
    depth, width = w_query.shape
    chunk = min(512, feat)
    return kernel_call(
        functools.partial(project_kernel, hp, len(parts), chunk),
        (*parts, w_query, d_out, facts),
        [HB] + [AN] * (len(parts) - 1) + [HB] * 3,
        [((rows, width), BF16), ((width // 2, HDIM), BF16), ((width // 2, HDIM), BF16)],
        (HB, VM, VM),
        [
            pltpu.VMEM((rows, depth), BF16),
            pltpu.VMEM((depth, width), BF16),
            pltpu.VMEM((rows, width), BF16),
            pltpu.VMEM(facts.shape, F32),
            pltpu.VMEM((rows, width), BF16),
            pltpu.VMEM((rows, width), BF16),
            pltpu.VMEM((rows, width), F32),
            pltpu.SemaphoreType.DMA((2 * len(parts) * (feat // chunk) + 3,)),
        ],
        28,
        "project",
        8,
    )


def inner_kernel(first, last, hp, *refs):
    ins, facts_hbm, outs = refs[:4], refs[4], refs[5:8]
    bufs, facts_ref, sides, sems = refs[8:12], refs[12], refs[13:16], refs[16]
    rows = ins[0].shape[0]
    copies = Copies(sems)
    facts_in = copies.start(facts_hbm, facts_ref)
    loads = {}
    for h in range(first, last, 2):
        count = min(2, last - h)
        src, dst = pl.ds(h * HDIM, count * HDIM), pl.ds((h - first) * HDIM, count * HDIM)
        loads[h] = [copies.start(ref.at[:, src], buf.at[:, dst]) for ref, buf in zip(ins, bufs)]
    facts_in.wait()
    table = turned(facts_ref[...])
    row = lax.broadcasted_iota(jnp.int32, (rows, rows), 0)
    keep = row >= lax.broadcasted_iota(jnp.int32, (rows, rows), 1)
    shift = -0.5 * math.log2(HDIM)
    turn = math.log2(math.e)
    q_ref, k_ref, v_ref, do_ref = bufs
    for h in range(first, last):
        for copy in loads.get(h, ()):
            copy.wait()
        cols = slice((h - first) * HDIM, (h - first + 1) * HDIM)
        later = column(table, h) * turn + shift
        sooner = facts_ref[h : h + 1, :] * turn
        gap = jnp.concatenate([later] * (rows // LANES), axis=1) - sooner
        decays = jnp.exp2(jnp.where(keep, gap, -1e30))
        query, grad = q_ref[:, cols], do_ref[:, cols]
        scaled = scaled_keys(table, hp, h, k_ref[:, cols])
        wdv = (decays * dot(grad, v_ref[:, cols], NT)).astype(BF16)
        wkq = (decays * dot(query, scaled, NT)).astype(BF16)
        sides[0][:, cols] = dot(wdv, scaled, NN).astype(BF16)
        sides[1][:, cols] = dot(query, wdv, TN).T.astype(BF16)
        sides[2][:, cols] = dot(grad, wkq, TN).T.astype(BF16)
        if h + 1 == last or h + 1 in loads:
            from_head = h if h in loads else h - 1
            done = slice((from_head - first) * HDIM, (h + 1 - first) * HDIM)
            for side, out in zip(sides, outs):
                copies.store(side.at[:, done], out.at[:, done])
    copies.finish()


def inner(first, last, query, keys, values, d_out, facts, hp):
    rows = query.shape[0]
    width = (last - first) * HDIM
    pairs = -(-(last - first) // 2)
    return kernel_call(
        functools.partial(inner_kernel, first, last, hp),
        (query, keys, values, d_out, facts),
        [HB] * 5,
        [((rows, width), BF16)] * 3,
        (HB,) * 3,
        [
            *[pltpu.VMEM((rows, width), BF16)] * 4,
            pltpu.VMEM(facts.shape, F32),
            *[pltpu.VMEM((rows, width), BF16)] * 3,
            pltpu.SemaphoreType.DMA((1 + 7 * pairs,)),
        ],
        24,
        "inner",
        1,
    )


def whole_head(upper, h, mine_ref, theirs_ref):
    half = HDIM // 2
    at = slice(h * half, (h + 1) * half)
    mine, theirs = mine_ref[at, :], theirs_ref[at, :]
    return jnp.concatenate([jnp.where(upper, theirs, mine), jnp.where(upper, mine, theirs)], axis=0)


def rows_of(w_hbm, shift, count, feat):
    owner = lax.rem(lax.axis_index("head") + shift, count)
    return w_hbm.at[pl.ds(pl.multiple_of(owner * feat, feat), feat), :]


def fetch_kernel(heads, count, w_hbm, do_hbm, facts_hbm, *refs):
    inner_hbm, refs = refs[: len(spans_of(heads))], refs[len(spans_of(heads)) :]
    do_ref, local_ref, table_ref, own_ref, outs, (facts_ref, sems) = *refs[:4], refs[4:-2], refs[-2:]
    copies = Copies(sems)
    facts_in = copies.start(facts_hbm, facts_ref)
    for index, out in enumerate(outs):
        copies.store(rows_of(w_hbm, index + 1, count, out.shape[0]), out)
    copies.store(do_hbm, do_ref)
    for (first, last), src in zip(spans_of(heads), inner_hbm):
        copies.store(src, local_ref.at[:, pl.ds(first * HDIM, (last - first) * HDIM)])
    copies.store(rows_of(w_hbm, 0, count, own_ref.shape[0]), own_ref)
    facts_in.wait()
    table_ref[...] = turned(facts_ref[...])
    copies.finish()


def fetch(count, w_query, d_out, facts, inner_dq, feat, heads):
    rows, width = d_out.shape
    return kernel_call(
        functools.partial(fetch_kernel, heads, count),
        (w_query, d_out, facts, *inner_dq),
        [HB] * (3 + len(inner_dq)),
        [((rows, width), BF16)] * 2
        + [((rows, LANES), F32), ((feat, width), BF16)]
        + [((feat, width), BF16)] * (count - 1),
        (VM,) * (count + 3),
        [pltpu.VMEM(facts.shape, F32), pltpu.SemaphoreType.DMA((count + 2 + len(inner_dq),))],
        4,
        "fetch",
        4,
    )


def query_kernel(heads, hp, *refs):
    mine_ref, theirs_ref, w_ref, do_ref, local_ref, table_ref, k_hbm, v_hbm = refs[:8]
    parts = len(spans_of(heads))
    dks, dvs, refs = refs[8 : 8 + parts], refs[8 + parts : 8 + 2 * parts], refs[8 + 2 * parts :]
    held, out_ref, k_ref, v_ref, dk_ref, dv_ref, next_table, sems = refs
    upper = lax.axis_index("ctx") % 2 == 1
    copies = Copies(sems)
    copies.store(k_hbm, k_ref)
    copies.store(v_hbm, v_ref)
    for (first, last), dk, dv in zip(spans_of(heads), dks, dvs):
        wide = pl.ds(first * HDIM, (last - first) * HDIM)
        copies.store(dk, dk_ref.at[:, wide])
        copies.store(dv, dv_ref.at[:, wide])
    table = table_ref[...]
    next_table[...] = table
    for h in range(heads):
        cols = slice(h * HDIM, (h + 1) * HDIM)
        state = whole_head(upper, h, mine_ref, theirs_ref)
        carry = dot(do_ref[:, cols], state, NT)
        held[:, cols] = (local_ref[:, cols].astype(F32) + column(table, 3 * hp + h) * carry).astype(BF16)
    put_terms(held, w_ref, out_ref)
    copies.finish()


def put_terms(dq_ref, w_ref, out_ref):
    block = min(512, w_ref.shape[0])
    for at in range(0, w_ref.shape[0], block):
        out_ref[:, at : at + block] = dot(dq_ref[...], w_ref[at : at + block, :], NT).astype(BF16)


def query_term(halves, weight, fetched, keys, values, dks, dvs, heads, hp):
    rows, width = keys.shape
    feat = weight.shape[0]
    vm_args, hbm_args = (*halves, weight, *fetched), (keys, values, *dks, *dvs)
    return kernel_call(
        functools.partial(query_kernel, heads, hp),
        (*vm_args, *hbm_args),
        [VM] * len(vm_args) + [HB] * len(hbm_args),
        [((rows, width), BF16), ((rows, feat), BF16)]
        + [((rows, width), BF16)] * 4
        + [((rows, LANES), F32)],
        (VM,) * 7,
        [pltpu.SemaphoreType.DMA((2 + 2 * len(dks),))],
        8,
        "query_term",
        6,
    )


def plain_term(d_query, weight):
    return kernel_call(
        put_terms,
        (d_query, weight),
        [VM, VM],
        [((d_query.shape[0], weight.shape[0]), BF16)],
        (VM,),
        [],
        12,
        "term",
        4,
    )[0]


def finish_kernel(*refs):
    terms, (out_hbm, sent, sems) = refs[:-3], refs[-3:]
    feat = sent.shape[1]
    copies = Copies(sems)
    block = min(512, feat)
    for at in range(0, feat, block):
        wide = slice(at, at + block)
        total = terms[0][:, wide].astype(F32)
        for other in terms[1:]:
            total = total + other[:, wide].astype(F32)
        sent[:, wide] = total.astype(BF16)
        copies.store(sent.at[:, wide], out_hbm.at[:, wide])
    copies.finish()


def finish(terms):
    rows, feat = terms[0].shape
    return kernel_call(
        finish_kernel,
        terms,
        [VM] * len(terms),
        [((rows, feat), BF16)],
        (HB,),
        [
            pltpu.VMEM((rows, feat), BF16),
            pltpu.SemaphoreType.DMA((feat // min(512, feat),)),
        ],
        12,
        "finish",
        6,
    )[0]


def close_kernel(
    heads, hp, mine_ref, theirs_ref, k_ref, v_ref, dk_ref, dv_ref, table_ref, dq_ref, own_ref, *refs
):
    dk_hbm, dv_hbm, term_ref, kside, vside, sems = refs
    upper = lax.axis_index("ctx") % 2 == 1
    pair = min(2, heads)
    copies = Copies(sems)
    table = table_ref[...]
    for h in range(heads):
        cols = slice(h * HDIM, (h + 1) * HDIM)
        adjoint = whole_head(upper, h, mine_ref, theirs_ref)
        tail, gain = column(table, 2 * hp + h), column(table, hp + h)
        carry_k = dot(v_ref[:, cols], adjoint, NT)
        kside[:, cols] = (gain * (dk_ref[:, cols].astype(F32) + tail * carry_k)).astype(BF16)
        carry_v = dot(scaled_keys(table, hp, h, k_ref[:, cols]), adjoint, NN)
        vside[:, cols] = (dv_ref[:, cols].astype(F32) + tail * carry_v).astype(BF16)
        if (h + 1) % pair == 0:
            wide = slice((h + 1 - pair) * HDIM, (h + 1) * HDIM)
            copies.store(kside.at[:, wide], dk_hbm.at[:, wide])
            copies.store(vside.at[:, wide], dv_hbm.at[:, wide])
    put_terms(dq_ref, own_ref, term_ref)
    copies.finish()


def close(halves, held, d_query, own, heads, hp):
    rows, width = d_query.shape
    args = (*halves, *held, d_query, own)
    buf = pltpu.VMEM((rows, width), BF16)
    return kernel_call(
        functools.partial(close_kernel, heads, hp),
        args,
        [VM] * len(args),
        [((rows, width), BF16)] * 2 + [((rows, own.shape[0]), BF16)],
        (HB, HB, VM),
        [buf, buf, pltpu.SemaphoreType.DMA((2 * (heads // min(2, heads)),))],
        12,
        "close",
        100,
    )


def body(ctx_size, head_size, hidden, w_query, keys, values, d_out, log_decay):
    rows, feat = hidden.shape
    heads = log_decay.shape[1]
    width = w_query.shape[1]
    hp = sublanes(heads)
    scaling = HDIM ** (-0.5)
    me = lax.axis_index("ctx")

    parts = [hidden]
    for shift in range(1, head_size):
        ring = [(i, (i + shift) % head_size) for i in range(head_size)]
        parts.append(lax.ppermute(hidden, "head", ring))

    facts, kept, sent, share = prepare(log_decay.T, keys, values, heads, hp, scaling)
    query, akept, asent = project(parts, w_query, d_out, facts, hp)

    size = width // 2
    wide = lambda factor: factor[:heads, None, :]
    cube = lambda flat: flat[:size].reshape(heads, HDIM // 2, HDIM).astype(F32)
    flat = lambda cubes: cubes.astype(BF16).reshape(size, HDIM)
    split = lambda f: (f.astype(BF16), (f - f.astype(BF16).astype(F32)).astype(BF16))
    joined = lambda rows: rows[size : size + hp].astype(F32) + rows[size + hp :].astype(F32)
    stages = (ctx_size - 1).bit_length()
    uppers = [(me & (1 << stage)) != 0 for stage in range(stages)]

    def send(array, stage):
        dist = 1 << (stage % stages)
        return lax.ppermute(array, "ctx", [(i, i ^ dist) for i in range(ctx_size)])

    shares, others = [share], []
    before, after = [jnp.ones_like(share)], [jnp.ones_like(share)]

    def fold(stage, total, carried, arrived, up):
        upper = uppers[stage]
        first = upper if up else ~upper
        arrived = cube(arrived)
        if stage > 0:
            weight = jnp.where(first, before[stage] if up else after[stage], 0.0)
            carried = carried + wide(weight) * arrived
        if stage == stages - 1:
            lead = uppers[0] if up else ~uppers[0]
            block, other = total
            mine = jnp.where(lead, cube(other) + wide(others[0]) * carried, carried)
            theirs = jnp.where(lead, carried, cube(block) + wide(shares[0]) * carried)
            return flat(theirs), flat(mine), None
        own, other = jnp.where(first, 1.0, others[stage]), jnp.where(first, shares[stage], 1.0)
        total = wide(own) * total + wide(other) * arrived
        return flat(total), total, carried

    def fold_factors(stage, arrived):
        theirs = joined(arrived)
        others.append(theirs)
        shares.append(shares[stage] * theirs)
        upper = uppers[stage]
        pair = stage == 0
        before.append(before[stage] if pair else jnp.where(upper, before[stage] * theirs, before[stage]))
        after.append(after[stage] if pair else jnp.where(upper, after[stage], after[stage] * theirs))

    class Chain:
        def __init__(self, kept, sent, up):
            self.kept, self.sent, self.up = kept, sent, up
            self.total, self.carried, self.stage, self.arrived = cube(kept), jnp.zeros_like(cube(kept)), 0, None

        def go(self):
            self.arrived = send(self.sent, self.stage)

        def take(self):
            stage, self.stage = self.stage, self.stage + 1
            if stage == 0:
                self.first = self.arrived
            total = self.total if stage < stages - 1 else (self.kept, self.first)
            if self.up and stage < stages - 1:
                fold_factors(stage, self.arrived)
            self.sent, self.total, self.carried = fold(stage, total, self.carried, self.arrived, self.up)
            if self.up and stage + 2 < stages:
                self.sent = jnp.concatenate([self.sent, *split(shares[-1])], axis=0)

    states, adjoints = Chain(kept, sent, True), Chain(akept, asent, False)
    spans = spans_of(heads)
    pending = list(spans)
    inner_parts = []
    barrier = lax.optimization_barrier
    for stage in range(stages + 1):
        if stage == stages:
            weight, _ = barrier((w_query, adjoints.sent))
            dqs, dks, dvs = zip(*inner_parts)
            *fetched, = fetch(head_size, weight, d_out, facts, dqs, feat, heads)
            fetched, own, weights = fetched[:3], fetched[3], fetched[4:]
        states.go()
        if stage == 0:
            states.arrived, query, adjoints.kept, adjoints.sent = barrier(
                (states.arrived, query, adjoints.kept, adjoints.sent)
            )
            adjoints.total = cube(adjoints.kept)
        else:
            adjoints.go()
            if pending and stage <= len(spans):
                query, _ = barrier((query, adjoints.sent))
                part = inner(*pending.pop(0), query, keys, values, d_out, facts, hp)
                states.arrived, *part = barrier((states.arrived, *part))
                inner_parts.append(part)
        if stage == stages - 1:
            adjoints.take()
            states.arrived, _ = barrier((states.arrived, adjoints.sent))
            states.take()
            continue
        if stage < stages:
            states.take()
        if stage >= 1:
            adjoints.arrived, _ = barrier((adjoints.arrived, states.sent if stage < stages else states.total))
            adjoints.take()
    adjoints.go()
    states.arrived, _ = barrier((states.arrived, adjoints.sent))
    state_halves = (states.total, states.arrived)
    adjoint_halves = (adjoints.total, adjoints.arrived)
    arrived = []
    for shift in range(1, head_size):
        ring = [(i, (i + shift) % head_size) for i in range(head_size)]
        if shift == 1:
            d_query, term, *held = query_term(
                state_halves, weights[0], fetched, keys, values, dks, dvs, heads, hp
            )
        else:
            term = plain_term(d_query, weights[shift - 1])
        arrived.append(lax.ppermute(term, "head", ring))
    d_keys, d_values, own = close(adjoint_halves, held, d_query, own, heads, hp)
    d_hidden = finish((own, *arrived))
    return (d_hidden, d_keys, d_values)


def solution(mesh):
    return jax.shard_map(
        functools.partial(body, mesh.shape["ctx"], mesh.shape["head"]),
        mesh=mesh,
        in_specs=(
            P("ctx", "head"),
            P(None, "head"),
            P("ctx", "head"),
            P("ctx", "head"),
            P("ctx", "head"),
            P("ctx", "head"),
        ),
        out_specs=(P("ctx", "head"), P("ctx", "head"), P("ctx", "head")),
        check_vma=False,
    )
```

```python
import functools
import math

import jax
import jax.numpy as jnp
from jax import lax
from jax.experimental import pallas as pl
from jax.experimental.pallas import tpu as pltpu
from jax.sharding import PartitionSpec as P

HDIM = 128
LANES = 128
F32, BF16 = jnp.float32, jnp.bfloat16
MIB = 1 << 20
VM = pl.BlockSpec(memory_space=pltpu.VMEM)
SM = pl.BlockSpec(memory_space=pltpu.SMEM)
HB = pl.BlockSpec(memory_space=pltpu.HBM)
AN = pl.BlockSpec(memory_space=pl.ANY)

NN = (((1,), (0,)), ((), ()))
NT = (((1,), (1,)), ((), ()))
TN = (((0,), (0,)), ((), ()))


def dot(a, b, dims):
    return lax.dot_general(a, b, dims, preferred_element_type=F32)


def kernel_call(kernel, args, specs, outs, out_specs, scratch, mib, name, micros):
    pinned = [pltpu.with_memory_space_constraint(a, pltpu.HBM) if s is HB else a for a, s in zip(args, specs)]
    placed = tuple(
        (pltpu.HBM if s is HB else jax.ShapeDtypeStruct)(shape, dtype) for (shape, dtype), s in zip(outs, out_specs)
    )
    return pl.pallas_call(
        kernel,
        in_specs=specs,
        out_specs=tuple(out_specs),
        out_shape=placed,
        scratch_shapes=scratch,
        compiler_params=pltpu.CompilerParams(vmem_limit_bytes=mib * MIB),
        cost_estimate=pl.CostEstimate(flops=int(micros * 1e9), bytes_accessed=1, transcendentals=0),
        name=name,
    )(*pinned)


def sublanes(count):
    return -(-count // 8) * 8


def expm1_negative(z):
    series = jnp.full_like(z, 1.0)
    for order in range(10, 1, -1):
        series = 1.0 + z * series * (1.0 / order)
    return jnp.where(z > -0.5, z * series, jnp.exp(z) - 1.0)


def column(table, lane, width=LANES):
    return jnp.broadcast_to(table[:, lane : lane + 1], (table.shape[0], width))


class Copies:
    def __init__(self, sems):
        self.sems, self.count, self.out = sems, 0, []

    def start(self, src, dst):
        copy = pltpu.make_async_copy(src, dst, self.sems.at[self.count])
        self.count += 1
        copy.start()
        return copy

    def store(self, src, dst):
        self.out.append(self.start(src, dst))

    def finish(self):
        for copy in self.out:
            copy.wait()


def spans_of(heads):
    edges = sorted({0, heads // 4, heads // 2, heads})
    return list(zip(edges, edges[1:]))


def groups(heads):
    size = min(8, heads)
    return [(f, f + size, slice(f * HDIM, (f + size) * HDIM)) for f in range(0, heads, size)]


def turned(facts):
    spare = jnp.zeros((LANES - facts.shape[0], facts.shape[1]), F32)
    return jnp.concatenate([facts, spare], axis=0).T


def put_halves(upper, h, local, kept_ref, sent_ref):
    half = HDIM // 2
    at = slice(h * half, (h + 1) * half)
    kept_ref[at, :] = jnp.where(upper, local[half:], local[:half]).astype(BF16)
    sent_ref[at, :] = jnp.where(upper, local[:half], local[half:]).astype(BF16)


def put_pairs(upper, first, last, left_ref, right_ref, kept_ref, sent_ref):
    for h in range(first, last, 2):
        count = min(2, last - h)
        cols = slice(h * HDIM, (h + count) * HDIM)
        both = dot(left_ref[:, cols], right_ref[:, cols], TN)
        for own in range(count):
            at = slice(own * HDIM, (own + 1) * HDIM)
            put_halves(upper, h + own, both[at, at], kept_ref, sent_ref)


def prepare_kernel(
    heads, hp, scaling, ld_hbm, k_hbm, v_hbm, facts_hbm, kept_ref, sent_ref, share_ref, *scratch
):
    ld, facts_ref, kbuf, vbuf, sems = scratch
    upper = lax.axis_index("ctx") % 2 == 1
    rows = kbuf.shape[0]
    copies = Copies(sems)
    ld_in = copies.start(ld_hbm, ld)
    loads = []
    for _, _, wide in groups(heads):
        loads.append([copies.start(src.at[:, wide], dst.at[:, wide]) for src, dst in ((k_hbm, kbuf), (v_hbm, vbuf))])
    ld_in.wait()
    logs = ld[...]
    if heads < hp:
        logs = jnp.concatenate([logs, jnp.zeros((hp - heads, rows), F32)], axis=0)
    lane = lax.broadcasted_iota(jnp.int32, logs.shape, 1)
    cumulative = logs
    step = 1
    while step < rows:
        moved = pltpu.roll(cumulative, step, 1)
        cumulative = cumulative + jnp.where(lane >= step, moved, 0.0)
        step *= 2
    total = cumulative[:, rows - 1 :]
    gain = jnp.sqrt(-expm1_negative(2.0 * logs))
    tail = jnp.exp(total - cumulative)
    lead = scaling * jnp.exp(cumulative)
    facts = jnp.concatenate([cumulative, gain, tail, lead], axis=0)
    facts_ref[...] = facts
    copies.store(facts_ref, facts_hbm)
    table = turned(facts)
    share = jnp.broadcast_to(jnp.exp(total), (hp, LANES))
    high = share.astype(BF16)
    low = (share - high.astype(F32)).astype(BF16)
    share_ref[...] = share
    base = heads * HDIM // 2
    sent_ref[base:, :] = jnp.concatenate([high.astype(F32), low.astype(F32)], axis=0).astype(BF16)
    for (first, last, _), load in zip(groups(heads), loads):
        for copy in load:
            copy.wait()
        for h in range(first, last):
            cols = slice(h * HDIM, (h + 1) * HDIM)
            scaled = scaled_keys(table, hp, h, kbuf[:, cols])
            kbuf[:, cols] = (column(table, 2 * hp + h) * scaled.astype(F32)).astype(BF16)
        put_pairs(upper, first, last, kbuf, vbuf, kept_ref, sent_ref)
    copies.finish()


def scaled_keys(table, hp, h, keys):
    return (column(table, hp + h) * keys.astype(F32)).astype(BF16)


def prepare(logs, keys, values, heads, hp, scaling):
    rows, width = keys.shape
    buf = pltpu.VMEM((rows, width), BF16)
    return kernel_call(
        functools.partial(prepare_kernel, heads, hp, scaling),
        (logs, keys, values),
        [HB] * 3,
        [
            ((4 * hp, rows), F32),
            ((width // 2, HDIM), BF16),
            ((width // 2 + 2 * hp, HDIM), BF16),
            ((hp, LANES), F32),
        ],
        (HB, VM, VM, VM),
        [
            pltpu.VMEM((heads, rows), F32),
            pltpu.VMEM((4 * hp, rows), F32),
            buf,
            buf,
            pltpu.SemaphoreType.DMA((2 + 2 * len(groups(heads)),)),
        ],
        12,
        "prepare",
        4,
    )


def project_kernel(hp, nparts, chunk, *refs):
    parts, (w_hbm, do_hbm, facts_hbm, q_hbm, kept_ref, sent_ref) = refs[:nparts], refs[nparts : nparts + 6]
    hbuf, wbuf, dobuf, facts_ref, qbuf, decayed, total, sems = refs[nparts + 6 :]
    rows, feat = parts[0].shape
    width = wbuf.shape[1]
    heads = width // HDIM
    upper = lax.axis_index("ctx") % 2 == 1
    copies = Copies(sems)
    loads = []
    for part, ref in enumerate(parts):
        for first in range(0, feat, chunk):
            here = pl.ds(part * feat + first, chunk)
            owner = lax.rem(lax.axis_index("head") + nparts - part, nparts)
            start = pl.multiple_of(owner * feat + first, chunk)
            loads.append(
                (
                    slice(part * feat + first, part * feat + first + chunk),
                    copies.start(ref.at[:, pl.ds(first, chunk)], hbuf.at[:, here]),
                    copies.start(w_hbm.at[pl.ds(start, chunk), :], wbuf.at[here, :]),
                )
            )
    late = [copies.start(facts_hbm, facts_ref), copies.start(do_hbm, dobuf)]
    block = min(256, width)
    for order, (here, h_in, w_in) in enumerate(loads):
        h_in.wait()
        w_in.wait()
        for first in range(0, width, block):
            wide = slice(first, first + block)
            term = dot(hbuf[:, here], wbuf[here, wide], NN)
            if order == 0:
                total[:, wide] = term
            elif order < len(loads) - 1:
                total[:, wide] += term
            else:
                qbuf[:, wide] = (total[:, wide] + term).astype(BF16)
    for copy in late:
        copy.wait()
    copies.store(qbuf, q_hbm)
    table = turned(facts_ref[...])
    for h in range(heads):
        cols = slice(h * HDIM, (h + 1) * HDIM)
        decayed[:, cols] = (column(table, 3 * hp + h) * qbuf[:, cols].astype(F32)).astype(BF16)
    put_pairs(upper, 0, heads, decayed, dobuf, kept_ref, sent_ref)
    copies.finish()


def project(parts, w_query, d_out, facts, hp):
    rows, feat = parts[0].shape
    depth, width = w_query.shape
    chunk = min(512, feat)
    return kernel_call(
        functools.partial(project_kernel, hp, len(parts), chunk),
        (*parts, w_query, d_out, facts),
        [HB] + [AN] * (len(parts) - 1) + [HB] * 3,
        [((rows, width), BF16), ((width // 2, HDIM), BF16), ((width // 2, HDIM), BF16)],
        (HB, VM, VM),
        [
            pltpu.VMEM((rows, depth), BF16),
            pltpu.VMEM((depth, width), BF16),
            pltpu.VMEM((rows, width), BF16),
            pltpu.VMEM(facts.shape, F32),
            pltpu.VMEM((rows, width), BF16),
            pltpu.VMEM((rows, width), BF16),
            pltpu.VMEM((rows, width), F32),
            pltpu.SemaphoreType.DMA((2 * len(parts) * (feat // chunk) + 3,)),
        ],
        28,
        "project",
        8,
    )


def inner_kernel(first, last, hp, *refs):
    ins, facts_hbm, outs = refs[:4], refs[4], refs[5:8]
    bufs, facts_ref, sides, sems = refs[8:12], refs[12], refs[13:16], refs[16]
    rows = ins[0].shape[0]
    copies = Copies(sems)
    facts_in = copies.start(facts_hbm, facts_ref)
    loads = {}
    for h in range(first, last, 2):
        count = min(2, last - h)
        src, dst = pl.ds(h * HDIM, count * HDIM), pl.ds((h - first) * HDIM, count * HDIM)
        loads[h] = [copies.start(ref.at[:, src], buf.at[:, dst]) for ref, buf in zip(ins, bufs)]
    facts_in.wait()
    table = turned(facts_ref[...])
    row = lax.broadcasted_iota(jnp.int32, (rows, rows), 0)
    keep = row >= lax.broadcasted_iota(jnp.int32, (rows, rows), 1)
    shift = -0.5 * math.log2(HDIM)
    turn = math.log2(math.e)
    q_ref, k_ref, v_ref, do_ref = bufs
    for h in range(first, last):
        for copy in loads.get(h, ()):
            copy.wait()
        cols = slice((h - first) * HDIM, (h - first + 1) * HDIM)
        later = column(table, h) * turn + shift
        sooner = facts_ref[h : h + 1, :] * turn
        gap = jnp.concatenate([later] * (rows // LANES), axis=1) - sooner
        decays = jnp.exp2(jnp.where(keep, gap, -1e30))
        query, grad = q_ref[:, cols], do_ref[:, cols]
        scaled = scaled_keys(table, hp, h, k_ref[:, cols])
        wdv = (decays * dot(grad, v_ref[:, cols], NT)).astype(BF16)
        wkq = (decays * dot(query, scaled, NT)).astype(BF16)
        sides[0][:, cols] = dot(wdv, scaled, NN).astype(BF16)
        sides[1][:, cols] = dot(query, wdv, TN).T.astype(BF16)
        sides[2][:, cols] = dot(grad, wkq, TN).T.astype(BF16)
        if h + 1 == last or h + 1 in loads:
            from_head = h if h in loads else h - 1
            done = slice((from_head - first) * HDIM, (h + 1 - first) * HDIM)
            for side, out in zip(sides, outs):
                copies.store(side.at[:, done], out.at[:, done])
    copies.finish()


def inner(first, last, query, keys, values, d_out, facts, hp):
    rows = query.shape[0]
    width = (last - first) * HDIM
    pairs = -(-(last - first) // 2)
    return kernel_call(
        functools.partial(inner_kernel, first, last, hp),
        (query, keys, values, d_out, facts),
        [HB] * 5,
        [((rows, width), BF16)] * 3,
        (HB,) * 3,
        [
            *[pltpu.VMEM((rows, width), BF16)] * 4,
            pltpu.VMEM(facts.shape, F32),
            *[pltpu.VMEM((rows, width), BF16)] * 3,
            pltpu.SemaphoreType.DMA((1 + 7 * pairs,)),
        ],
        24,
        "inner",
        1,
    )


def whole_head(upper, h, mine_ref, theirs_ref):
    half = HDIM // 2
    at = slice(h * half, (h + 1) * half)
    mine, theirs = mine_ref[at, :], theirs_ref[at, :]
    return jnp.concatenate([jnp.where(upper, theirs, mine), jnp.where(upper, mine, theirs)], axis=0)


def rows_of(w_hbm, shift, count, feat):
    owner = lax.rem(lax.axis_index("head") + shift, count)
    return w_hbm.at[pl.ds(pl.multiple_of(owner * feat, feat), feat), :]


def fetch_kernel(heads, count, w_hbm, do_hbm, facts_hbm, *refs):
    inner_hbm, refs = refs[: len(spans_of(heads))], refs[len(spans_of(heads)) :]
    do_ref, local_ref, table_ref, own_ref, outs, (facts_ref, sems) = *refs[:4], refs[4:-2], refs[-2:]
    copies = Copies(sems)
    facts_in = copies.start(facts_hbm, facts_ref)
    for index, out in enumerate(outs):
        copies.store(rows_of(w_hbm, index + 1, count, out.shape[0]), out)
    copies.store(do_hbm, do_ref)
    for (first, last), src in zip(spans_of(heads), inner_hbm):
        copies.store(src, local_ref.at[:, pl.ds(first * HDIM, (last - first) * HDIM)])
    copies.store(rows_of(w_hbm, 0, count, own_ref.shape[0]), own_ref)
    facts_in.wait()
    table_ref[...] = turned(facts_ref[...])
    copies.finish()


def fetch(count, w_query, d_out, facts, inner_dq, feat, heads):
    rows, width = d_out.shape
    return kernel_call(
        functools.partial(fetch_kernel, heads, count),
        (w_query, d_out, facts, *inner_dq),
        [HB] * (3 + len(inner_dq)),
        [((rows, width), BF16)] * 2
        + [((rows, LANES), F32), ((feat, width), BF16)]
        + [((feat, width), BF16)] * (count - 1),
        (VM,) * (count + 3),
        [pltpu.VMEM(facts.shape, F32), pltpu.SemaphoreType.DMA((count + 2 + len(inner_dq),))],
        4,
        "fetch",
        4,
    )


def query_kernel(heads, hp, *refs):
    mine_ref, theirs_ref, w_ref, do_ref, local_ref, table_ref, k_hbm, v_hbm = refs[:8]
    parts = len(spans_of(heads))
    dks, dvs, refs = refs[8 : 8 + parts], refs[8 + parts : 8 + 2 * parts], refs[8 + 2 * parts :]
    held, out_ref, k_ref, v_ref, dk_ref, dv_ref, next_table, sems = refs
    upper = lax.axis_index("ctx") % 2 == 1
    copies = Copies(sems)
    copies.store(k_hbm, k_ref)
    copies.store(v_hbm, v_ref)
    for (first, last), dk, dv in zip(spans_of(heads), dks, dvs):
        wide = pl.ds(first * HDIM, (last - first) * HDIM)
        copies.store(dk, dk_ref.at[:, wide])
        copies.store(dv, dv_ref.at[:, wide])
    table = table_ref[...]
    next_table[...] = table
    for h in range(heads):
        cols = slice(h * HDIM, (h + 1) * HDIM)
        state = whole_head(upper, h, mine_ref, theirs_ref)
        carry = dot(do_ref[:, cols], state, NT)
        held[:, cols] = (local_ref[:, cols].astype(F32) + column(table, 3 * hp + h) * carry).astype(BF16)
    put_terms(held, w_ref, out_ref)
    copies.finish()


def put_terms(dq_ref, w_ref, out_ref):
    block = min(512, w_ref.shape[0])
    for at in range(0, w_ref.shape[0], block):
        out_ref[:, at : at + block] = dot(dq_ref[...], w_ref[at : at + block, :], NT).astype(BF16)


def query_term(halves, weight, fetched, keys, values, dks, dvs, heads, hp):
    rows, width = keys.shape
    feat = weight.shape[0]
    vm_args, hbm_args = (*halves, weight, *fetched), (keys, values, *dks, *dvs)
    return kernel_call(
        functools.partial(query_kernel, heads, hp),
        (*vm_args, *hbm_args),
        [VM] * len(vm_args) + [HB] * len(hbm_args),
        [((rows, width), BF16), ((rows, feat), BF16)]
        + [((rows, width), BF16)] * 4
        + [((rows, LANES), F32)],
        (VM,) * 7,
        [pltpu.SemaphoreType.DMA((2 + 2 * len(dks),))],
        8,
        "query_term",
        6,
    )


def plain_term(d_query, weight):
    return kernel_call(
        put_terms,
        (d_query, weight),
        [VM, VM],
        [((d_query.shape[0], weight.shape[0]), BF16)],
        (VM,),
        [],
        12,
        "term",
        4,
    )[0]


def finish_kernel(*refs):
    terms, (out_hbm, sent, sems) = refs[:-3], refs[-3:]
    feat = sent.shape[1]
    copies = Copies(sems)
    block = min(512, feat)
    for at in range(0, feat, block):
        wide = slice(at, at + block)
        total = terms[0][:, wide].astype(F32)
        for other in terms[1:]:
            total = total + other[:, wide].astype(F32)
        sent[:, wide] = total.astype(BF16)
        copies.store(sent.at[:, wide], out_hbm.at[:, wide])
    copies.finish()


def finish(terms):
    rows, feat = terms[0].shape
    return kernel_call(
        finish_kernel,
        terms,
        [VM] * len(terms),
        [((rows, feat), BF16)],
        (HB,),
        [
            pltpu.VMEM((rows, feat), BF16),
            pltpu.SemaphoreType.DMA((feat // min(512, feat),)),
        ],
        12,
        "finish",
        6,
    )[0]


def close_kernel(
    heads, hp, mine_ref, theirs_ref, k_ref, v_ref, dk_ref, dv_ref, table_ref, dq_ref, own_ref, *refs
):
    dk_hbm, dv_hbm, term_ref, kside, vside, sems = refs
    upper = lax.axis_index("ctx") % 2 == 1
    pair = min(2, heads)
    copies = Copies(sems)
    table = table_ref[...]
    for h in range(heads):
        cols = slice(h * HDIM, (h + 1) * HDIM)
        adjoint = whole_head(upper, h, mine_ref, theirs_ref)
        tail, gain = column(table, 2 * hp + h), column(table, hp + h)
        carry_k = dot(v_ref[:, cols], adjoint, NT)
        kside[:, cols] = (gain * (dk_ref[:, cols].astype(F32) + tail * carry_k)).astype(BF16)
        carry_v = dot(scaled_keys(table, hp, h, k_ref[:, cols]), adjoint, NN)
        vside[:, cols] = (dv_ref[:, cols].astype(F32) + tail * carry_v).astype(BF16)
        if (h + 1) % pair == 0:
            wide = slice((h + 1 - pair) * HDIM, (h + 1) * HDIM)
            copies.store(kside.at[:, wide], dk_hbm.at[:, wide])
            copies.store(vside.at[:, wide], dv_hbm.at[:, wide])
    put_terms(dq_ref, own_ref, term_ref)
    copies.finish()


def close(halves, held, d_query, own, heads, hp):
    rows, width = d_query.shape
    args = (*halves, *held, d_query, own)
    buf = pltpu.VMEM((rows, width), BF16)
    return kernel_call(
        functools.partial(close_kernel, heads, hp),
        args,
        [VM] * len(args),
        [((rows, width), BF16)] * 2 + [((rows, own.shape[0]), BF16)],
        (HB, HB, VM),
        [buf, buf, pltpu.SemaphoreType.DMA((2 * (heads // min(2, heads)),))],
        12,
        "close",
        100,
    )


def body(ctx_size, head_size, hidden, w_query, keys, values, d_out, log_decay):
    rows, feat = hidden.shape
    heads = log_decay.shape[1]
    width = w_query.shape[1]
    hp = sublanes(heads)
    scaling = HDIM ** (-0.5)
    me = lax.axis_index("ctx")

    parts = [hidden]
    for shift in range(1, head_size):
        ring = [(i, (i + shift) % head_size) for i in range(head_size)]
        parts.append(lax.ppermute(hidden, "head", ring))

    facts, kept, sent, share = prepare(log_decay.T, keys, values, heads, hp, scaling)
    query, akept, asent = project(parts, w_query, d_out, facts, hp)

    size = width // 2
    wide = lambda factor: factor[:heads, None, :]
    cube = lambda flat: flat[:size].reshape(heads, HDIM // 2, HDIM).astype(F32)
    flat = lambda cubes: cubes.astype(BF16).reshape(size, HDIM)
    split = lambda f: (f.astype(BF16), (f - f.astype(BF16).astype(F32)).astype(BF16))
    joined = lambda rows: rows[size : size + hp].astype(F32) + rows[size + hp :].astype(F32)
    stages = (ctx_size - 1).bit_length()
    uppers = [(me & (1 << stage)) != 0 for stage in range(stages)]

    def send(array, stage):
        dist = 1 << (stage % stages)
        return lax.ppermute(array, "ctx", [(i, i ^ dist) for i in range(ctx_size)])

    shares, others = [share], []
    before, after = [jnp.ones_like(share)], [jnp.ones_like(share)]

    def fold(stage, total, carried, arrived, up):
        upper = uppers[stage]
        first = upper if up else ~upper
        arrived = cube(arrived)
        if stage > 0:
            weight = jnp.where(first, before[stage] if up else after[stage], 0.0)
            carried = carried + wide(weight) * arrived
        if stage == stages - 1:
            lead = uppers[0] if up else ~uppers[0]
            block, other = total
            mine = jnp.where(lead, cube(other) + wide(others[0]) * carried, carried)
            theirs = jnp.where(lead, carried, cube(block) + wide(shares[0]) * carried)
            return flat(theirs), flat(mine), None
        own, other = jnp.where(first, 1.0, others[stage]), jnp.where(first, shares[stage], 1.0)
        total = wide(own) * total + wide(other) * arrived
        return flat(total), total, carried

    def fold_factors(stage, arrived):
        theirs = joined(arrived)
        others.append(theirs)
        shares.append(shares[stage] * theirs)
        upper = uppers[stage]
        pair = stage == 0
        before.append(before[stage] if pair else jnp.where(upper, before[stage] * theirs, before[stage]))
        after.append(after[stage] if pair else jnp.where(upper, after[stage], after[stage] * theirs))

    class Chain:
        def __init__(self, kept, sent, up):
            self.kept, self.sent, self.up = kept, sent, up
            self.total, self.carried, self.stage, self.arrived = cube(kept), jnp.zeros_like(cube(kept)), 0, None

        def go(self):
            self.arrived = send(self.sent, self.stage)

        def take(self):
            stage, self.stage = self.stage, self.stage + 1
            if stage == 0:
                self.first = self.arrived
            total = self.total if stage < stages - 1 else (self.kept, self.first)
            if self.up and stage < stages - 1:
                fold_factors(stage, self.arrived)
            self.sent, self.total, self.carried = fold(stage, total, self.carried, self.arrived, self.up)
            if self.up and stage + 2 < stages:
                self.sent = jnp.concatenate([self.sent, *split(shares[-1])], axis=0)

    states, adjoints = Chain(kept, sent, True), Chain(akept, asent, False)
    spans = spans_of(heads)
    pending = list(spans)
    inner_parts = []
    barrier = lax.optimization_barrier
    for stage in range(stages + 1):
        if stage == stages:
            weight, _ = barrier((w_query, adjoints.sent))
            dqs, dks, dvs = zip(*inner_parts)
            *fetched, = fetch(head_size, weight, d_out, facts, dqs, feat, heads)
            fetched, own, weights = fetched[:3], fetched[3], fetched[4:]
        states.go()
        if stage == 0:
            states.arrived, query, adjoints.kept, adjoints.sent = barrier(
                (states.arrived, query, adjoints.kept, adjoints.sent)
            )
            adjoints.total = cube(adjoints.kept)
        else:
            adjoints.go()
            if pending and stage <= len(spans):
                query, _ = barrier((query, adjoints.sent))
                part = inner(*pending.pop(0), query, keys, values, d_out, facts, hp)
                states.arrived, *part = barrier((states.arrived, *part))
                inner_parts.append(part)
        if stage == stages - 1:
            adjoints.take()
            states.arrived, _ = barrier((states.arrived, adjoints.sent))
            states.take()
            continue
        if stage < stages:
            states.take()
        if stage >= 1:
            adjoints.arrived, _ = barrier((adjoints.arrived, states.sent if stage < stages else states.total))
            adjoints.take()
    adjoints.go()
    states.arrived, _ = barrier((states.arrived, adjoints.sent))
    state_halves = (states.total, states.arrived)
    adjoint_halves = (adjoints.total, adjoints.arrived)
    arrived = []
    for shift in range(1, head_size):
        ring = [(i, (i + shift) % head_size) for i in range(head_size)]
        if shift == 1:
            d_query, term, *held = query_term(
                state_halves, weights[0], fetched, keys, values, dks, dvs, heads, hp
            )
        else:
            term = plain_term(d_query, weights[shift - 1])
        arrived.append(lax.ppermute(term, "head", ring))
    d_keys, d_values, own = close(adjoint_halves, held, d_query, own, heads, hp)
    d_hidden = finish((own, *arrived))
    return (d_hidden, d_keys, d_values)


def solution(mesh):
    return jax.shard_map(
        functools.partial(body, mesh.shape["ctx"], mesh.shape["head"]),
        mesh=mesh,
        in_specs=(
            P("ctx", "head"),
            P(None, "head"),
            P("ctx", "head"),
            P("ctx", "head"),
            P("ctx", "head"),
            P("ctx", "head"),
        ),
        out_specs=(P("ctx", "head"), P("ctx", "head"), P("ctx", "head")),
        check_vma=False,
    )
```

```python
import functools
import math

import jax
import jax.numpy as jnp
from jax import lax
from jax.experimental import pallas as pl
from jax.experimental.pallas import tpu as pltpu
from jax.sharding import PartitionSpec as P

HDIM = 128
LANES = 128
F32, BF16 = jnp.float32, jnp.bfloat16
MIB = 1 << 20
VM = pl.BlockSpec(memory_space=pltpu.VMEM)
SM = pl.BlockSpec(memory_space=pltpu.SMEM)
HB = pl.BlockSpec(memory_space=pltpu.HBM)
AN = pl.BlockSpec(memory_space=pl.ANY)

NN = (((1,), (0,)), ((), ()))
NT = (((1,), (1,)), ((), ()))
TN = (((0,), (0,)), ((), ()))


def dot(a, b, dims):
    return lax.dot_general(a, b, dims, preferred_element_type=F32)


def kernel_call(kernel, args, specs, outs, out_specs, scratch, mib, name, micros):
    pinned = [pltpu.with_memory_space_constraint(a, pltpu.HBM) if s is HB else a for a, s in zip(args, specs)]
    placed = tuple(
        (pltpu.HBM if s is HB else jax.ShapeDtypeStruct)(shape, dtype) for (shape, dtype), s in zip(outs, out_specs)
    )
    return pl.pallas_call(
        kernel,
        in_specs=specs,
        out_specs=tuple(out_specs),
        out_shape=placed,
        scratch_shapes=scratch,
        compiler_params=pltpu.CompilerParams(vmem_limit_bytes=mib * MIB),
        cost_estimate=pl.CostEstimate(flops=int(micros * 1e9), bytes_accessed=1, transcendentals=0),
        name=name,
    )(*pinned)


def sublanes(count):
    return -(-count // 8) * 8


def expm1_negative(z):
    series = jnp.full_like(z, 1.0)
    for order in range(10, 1, -1):
        series = 1.0 + z * series * (1.0 / order)
    return jnp.where(z > -0.5, z * series, jnp.exp(z) - 1.0)


def column(table, lane, width=LANES):
    return jnp.broadcast_to(table[:, lane : lane + 1], (table.shape[0], width))


class Copies:
    def __init__(self, sems):
        self.sems, self.count, self.out = sems, 0, []

    def start(self, src, dst):
        copy = pltpu.make_async_copy(src, dst, self.sems.at[self.count])
        self.count += 1
        copy.start()
        return copy

    def store(self, src, dst):
        self.out.append(self.start(src, dst))

    def finish(self):
        for copy in self.out:
            copy.wait()


def spans_of(heads):
    edges = sorted({0, heads // 4, heads // 2, heads})
    return list(zip(edges, edges[1:]))


def groups(heads):
    size = min(8, heads)
    return [(f, f + size, slice(f * HDIM, (f + size) * HDIM)) for f in range(0, heads, size)]


def turned(facts):
    spare = jnp.zeros((LANES - facts.shape[0], facts.shape[1]), F32)
    return jnp.concatenate([facts, spare], axis=0).T


def put_halves(upper, h, local, kept_ref, sent_ref):
    half = HDIM // 2
    at = slice(h * half, (h + 1) * half)
    kept_ref[at, :] = jnp.where(upper, local[half:], local[:half]).astype(BF16)
    sent_ref[at, :] = jnp.where(upper, local[:half], local[half:]).astype(BF16)


def put_pairs(upper, first, last, left_ref, right_ref, kept_ref, sent_ref):
    for h in range(first, last, 2):
        count = min(2, last - h)
        cols = slice(h * HDIM, (h + count) * HDIM)
        both = dot(left_ref[:, cols], right_ref[:, cols], TN)
        for own in range(count):
            at = slice(own * HDIM, (own + 1) * HDIM)
            put_halves(upper, h + own, both[at, at], kept_ref, sent_ref)


def prepare_kernel(
    heads, hp, scaling, ld_hbm, k_hbm, v_hbm, facts_hbm, kept_ref, sent_ref, share_ref, *scratch
):
    ld, facts_ref, kbuf, vbuf, sems = scratch
    upper = lax.axis_index("ctx") % 2 == 1
    rows = kbuf.shape[0]
    copies = Copies(sems)
    ld_in = copies.start(ld_hbm, ld)
    loads = []
    for _, _, wide in groups(heads):
        loads.append([copies.start(src.at[:, wide], dst.at[:, wide]) for src, dst in ((k_hbm, kbuf), (v_hbm, vbuf))])
    ld_in.wait()
    logs = ld[...]
    if heads < hp:
        logs = jnp.concatenate([logs, jnp.zeros((hp - heads, rows), F32)], axis=0)
    lane = lax.broadcasted_iota(jnp.int32, logs.shape, 1)
    cumulative = logs
    step = 1
    while step < rows:
        moved = pltpu.roll(cumulative, step, 1)
        cumulative = cumulative + jnp.where(lane >= step, moved, 0.0)
        step *= 2
    total = cumulative[:, rows - 1 :]
    gain = jnp.sqrt(-expm1_negative(2.0 * logs))
    tail = jnp.exp(total - cumulative)
    lead = scaling * jnp.exp(cumulative)
    facts = jnp.concatenate([cumulative, gain, tail, lead], axis=0)
    facts_ref[...] = facts
    copies.store(facts_ref, facts_hbm)
    table = turned(facts)
    share = jnp.broadcast_to(jnp.exp(total), (hp, LANES))
    high = share.astype(BF16)
    low = (share - high.astype(F32)).astype(BF16)
    share_ref[...] = share
    base = heads * HDIM // 2
    sent_ref[base:, :] = jnp.concatenate([high.astype(F32), low.astype(F32)], axis=0).astype(BF16)
    for (first, last, _), load in zip(groups(heads), loads):
        for copy in load:
            copy.wait()
        for h in range(first, last):
            cols = slice(h * HDIM, (h + 1) * HDIM)
            scaled = scaled_keys(table, hp, h, kbuf[:, cols])
            kbuf[:, cols] = (column(table, 2 * hp + h) * scaled.astype(F32)).astype(BF16)
        put_pairs(upper, first, last, kbuf, vbuf, kept_ref, sent_ref)
    copies.finish()


def scaled_keys(table, hp, h, keys):
    return (column(table, hp + h) * keys.astype(F32)).astype(BF16)


def prepare(logs, keys, values, heads, hp, scaling):
    rows, width = keys.shape
    buf = pltpu.VMEM((rows, width), BF16)
    return kernel_call(
        functools.partial(prepare_kernel, heads, hp, scaling),
        (logs, keys, values),
        [HB] * 3,
        [
            ((4 * hp, rows), F32),
            ((width // 2, HDIM), BF16),
            ((width // 2 + 2 * hp, HDIM), BF16),
            ((hp, LANES), F32),
        ],
        (HB, VM, VM, VM),
        [
            pltpu.VMEM((heads, rows), F32),
            pltpu.VMEM((4 * hp, rows), F32),
            buf,
            buf,
            pltpu.SemaphoreType.DMA((2 + 2 * len(groups(heads)),)),
        ],
        12,
        "prepare",
        4,
    )


def project_kernel(hp, nparts, chunk, *refs):
    parts, (w_hbm, do_hbm, facts_hbm, q_hbm, kept_ref, sent_ref) = refs[:nparts], refs[nparts : nparts + 6]
    hbuf, wbuf, dobuf, facts_ref, qbuf, decayed, total, sems = refs[nparts + 6 :]
    rows, feat = parts[0].shape
    width = wbuf.shape[1]
    heads = width // HDIM
    upper = lax.axis_index("ctx") % 2 == 1
    copies = Copies(sems)
    loads = []
    for part, ref in enumerate(parts):
        for first in range(0, feat, chunk):
            here = pl.ds(part * feat + first, chunk)
            owner = lax.rem(lax.axis_index("head") + nparts - part, nparts)
            start = pl.multiple_of(owner * feat + first, chunk)
            loads.append(
                (
                    slice(part * feat + first, part * feat + first + chunk),
                    copies.start(ref.at[:, pl.ds(first, chunk)], hbuf.at[:, here]),
                    copies.start(w_hbm.at[pl.ds(start, chunk), :], wbuf.at[here, :]),
                )
            )
    late = [copies.start(facts_hbm, facts_ref), copies.start(do_hbm, dobuf)]
    block = min(256, width)
    for order, (here, h_in, w_in) in enumerate(loads):
        h_in.wait()
        w_in.wait()
        for first in range(0, width, block):
            wide = slice(first, first + block)
            term = dot(hbuf[:, here], wbuf[here, wide], NN)
            if order == 0:
                total[:, wide] = term
            elif order < len(loads) - 1:
                total[:, wide] += term
            else:
                qbuf[:, wide] = (total[:, wide] + term).astype(BF16)
    for copy in late:
        copy.wait()
    copies.store(qbuf, q_hbm)
    table = turned(facts_ref[...])
    for h in range(heads):
        cols = slice(h * HDIM, (h + 1) * HDIM)
        decayed[:, cols] = (column(table, 3 * hp + h) * qbuf[:, cols].astype(F32)).astype(BF16)
    put_pairs(upper, 0, heads, decayed, dobuf, kept_ref, sent_ref)
    copies.finish()


def project(parts, w_query, d_out, facts, hp):
    rows, feat = parts[0].shape
    depth, width = w_query.shape
    chunk = min(512, feat)
    return kernel_call(
        functools.partial(project_kernel, hp, len(parts), chunk),
        (*parts, w_query, d_out, facts),
        [HB] + [AN] * (len(parts) - 1) + [HB] * 3,
        [((rows, width), BF16), ((width // 2, HDIM), BF16), ((width // 2, HDIM), BF16)],
        (HB, VM, VM),
        [
            pltpu.VMEM((rows, depth), BF16),
            pltpu.VMEM((depth, width), BF16),
            pltpu.VMEM((rows, width), BF16),
            pltpu.VMEM(facts.shape, F32),
            pltpu.VMEM((rows, width), BF16),
            pltpu.VMEM((rows, width), BF16),
            pltpu.VMEM((rows, width), F32),
            pltpu.SemaphoreType.DMA((2 * len(parts) * (feat // chunk) + 3,)),
        ],
        28,
        "project",
        8,
    )


def inner_kernel(first, last, hp, *refs):
    ins, facts_hbm, outs = refs[:4], refs[4], refs[5:8]
    bufs, facts_ref, sides, sems = refs[8:12], refs[12], refs[13:16], refs[16]
    rows = ins[0].shape[0]
    copies = Copies(sems)
    facts_in = copies.start(facts_hbm, facts_ref)
    loads = {}
    for h in range(first, last, 2):
        count = min(2, last - h)
        src, dst = pl.ds(h * HDIM, count * HDIM), pl.ds((h - first) * HDIM, count * HDIM)
        loads[h] = [copies.start(ref.at[:, src], buf.at[:, dst]) for ref, buf in zip(ins, bufs)]
    facts_in.wait()
    table = turned(facts_ref[...])
    row = lax.broadcasted_iota(jnp.int32, (rows, rows), 0)
    keep = row >= lax.broadcasted_iota(jnp.int32, (rows, rows), 1)
    shift = -0.5 * math.log2(HDIM)
    turn = math.log2(math.e)
    q_ref, k_ref, v_ref, do_ref = bufs
    for h in range(first, last):
        for copy in loads.get(h, ()):
            copy.wait()
        cols = slice((h - first) * HDIM, (h - first + 1) * HDIM)
        later = column(table, h) * turn + shift
        sooner = facts_ref[h : h + 1, :] * turn
        gap = jnp.concatenate([later] * (rows // LANES), axis=1) - sooner
        decays = jnp.exp2(jnp.where(keep, gap, -1e30))
        query, grad = q_ref[:, cols], do_ref[:, cols]
        scaled = scaled_keys(table, hp, h, k_ref[:, cols])
        wdv = (decays * dot(grad, v_ref[:, cols], NT)).astype(BF16)
        wkq = (decays * dot(query, scaled, NT)).astype(BF16)
        sides[0][:, cols] = dot(wdv, scaled, NN).astype(BF16)
        sides[1][:, cols] = dot(query, wdv, TN).T.astype(BF16)
        sides[2][:, cols] = dot(grad, wkq, TN).T.astype(BF16)
        if h + 1 == last or h + 1 in loads:
            from_head = h if h in loads else h - 1
            done = slice((from_head - first) * HDIM, (h + 1 - first) * HDIM)
            for side, out in zip(sides, outs):
                copies.store(side.at[:, done], out.at[:, done])
    copies.finish()


def inner(first, last, query, keys, values, d_out, facts, hp):
    rows = query.shape[0]
    width = (last - first) * HDIM
    pairs = -(-(last - first) // 2)
    return kernel_call(
        functools.partial(inner_kernel, first, last, hp),
        (query, keys, values, d_out, facts),
        [HB] * 5,
        [((rows, width), BF16)] * 3,
        (HB,) * 3,
        [
            *[pltpu.VMEM((rows, width), BF16)] * 4,
            pltpu.VMEM(facts.shape, F32),
            *[pltpu.VMEM((rows, width), BF16)] * 3,
            pltpu.SemaphoreType.DMA((1 + 7 * pairs,)),
        ],
        24,
        "inner",
        1,
    )


def whole_head(upper, h, mine_ref, theirs_ref):
    half = HDIM // 2
    at = slice(h * half, (h + 1) * half)
    mine, theirs = mine_ref[at, :], theirs_ref[at, :]
    return jnp.concatenate([jnp.where(upper, theirs, mine), jnp.where(upper, mine, theirs)], axis=0)


def rows_of(w_hbm, shift, count, feat):
    owner = lax.rem(lax.axis_index("head") + shift, count)
    return w_hbm.at[pl.ds(pl.multiple_of(owner * feat, feat), feat), :]


def fetch_kernel(heads, count, w_hbm, do_hbm, facts_hbm, *refs):
    inner_hbm, refs = refs[: len(spans_of(heads))], refs[len(spans_of(heads)) :]
    do_ref, local_ref, table_ref, own_ref, outs, (facts_ref, sems) = *refs[:4], refs[4:-2], refs[-2:]
    copies = Copies(sems)
    facts_in = copies.start(facts_hbm, facts_ref)
    for index, out in enumerate(outs):
        copies.store(rows_of(w_hbm, index + 1, count, out.shape[0]), out)
    copies.store(do_hbm, do_ref)
    for (first, last), src in zip(spans_of(heads), inner_hbm):
        copies.store(src, local_ref.at[:, pl.ds(first * HDIM, (last - first) * HDIM)])
    copies.store(rows_of(w_hbm, 0, count, own_ref.shape[0]), own_ref)
    facts_in.wait()
    table_ref[...] = turned(facts_ref[...])
    copies.finish()


def fetch(count, w_query, d_out, facts, inner_dq, feat, heads):
    rows, width = d_out.shape
    return kernel_call(
        functools.partial(fetch_kernel, heads, count),
        (w_query, d_out, facts, *inner_dq),
        [HB] * (3 + len(inner_dq)),
        [((rows, width), BF16)] * 2
        + [((rows, LANES), F32), ((feat, width), BF16)]
        + [((feat, width), BF16)] * (count - 1),
        (VM,) * (count + 3),
        [pltpu.VMEM(facts.shape, F32), pltpu.SemaphoreType.DMA((count + 2 + len(inner_dq),))],
        4,
        "fetch",
        4,
    )


def query_kernel(heads, hp, *refs):
    mine_ref, theirs_ref, w_ref, do_ref, local_ref, table_ref, k_hbm, v_hbm = refs[:8]
    parts = len(spans_of(heads))
    dks, dvs, refs = refs[8 : 8 + parts], refs[8 + parts : 8 + 2 * parts], refs[8 + 2 * parts :]
    held, out_ref, k_ref, v_ref, dk_ref, dv_ref, next_table, sems = refs
    upper = lax.axis_index("ctx") % 2 == 1
    copies = Copies(sems)
    copies.store(k_hbm, k_ref)
    copies.store(v_hbm, v_ref)
    for (first, last), dk, dv in zip(spans_of(heads), dks, dvs):
        wide = pl.ds(first * HDIM, (last - first) * HDIM)
        copies.store(dk, dk_ref.at[:, wide])
        copies.store(dv, dv_ref.at[:, wide])
    table = table_ref[...]
    next_table[...] = table
    for h in range(heads):
        cols = slice(h * HDIM, (h + 1) * HDIM)
        state = whole_head(upper, h, mine_ref, theirs_ref)
        carry = dot(do_ref[:, cols], state, NT)
        held[:, cols] = (local_ref[:, cols].astype(F32) + column(table, 3 * hp + h) * carry).astype(BF16)
    put_terms(held, w_ref, out_ref)
    copies.finish()


def put_terms(dq_ref, w_ref, out_ref):
    block = min(512, w_ref.shape[0])
    for at in range(0, w_ref.shape[0], block):
        out_ref[:, at : at + block] = dot(dq_ref[...], w_ref[at : at + block, :], NT).astype(BF16)


def query_term(halves, weight, fetched, keys, values, dks, dvs, heads, hp):
    rows, width = keys.shape
    feat = weight.shape[0]
    vm_args, hbm_args = (*halves, weight, *fetched), (keys, values, *dks, *dvs)
    return kernel_call(
        functools.partial(query_kernel, heads, hp),
        (*vm_args, *hbm_args),
        [VM] * len(vm_args) + [HB] * len(hbm_args),
        [((rows, width), BF16), ((rows, feat), BF16)]
        + [((rows, width), BF16)] * 4
        + [((rows, LANES), F32)],
        (VM,) * 7,
        [pltpu.SemaphoreType.DMA((2 + 2 * len(dks),))],
        8,
        "query_term",
        6,
    )


def plain_term(d_query, weight):
    return kernel_call(
        put_terms,
        (d_query, weight),
        [VM, VM],
        [((d_query.shape[0], weight.shape[0]), BF16)],
        (VM,),
        [],
        12,
        "term",
        4,
    )[0]


def early_kernel(dq_ref, w_ref, out_ref):
    put_terms(dq_ref, w_ref.at[: out_ref.shape[1]], out_ref)


def early_term(d_query, own):
    return kernel_call(
        early_kernel,
        (d_query, own),
        [VM, VM],
        [((d_query.shape[0], own.shape[0] // 4), BF16)],
        (VM,),
        [],
        8,
        "early",
        1,
    )[0]


def finish_kernel(early_ref, rest_ref, *refs):
    terms, (out_hbm, sent, sems) = refs[:-3], refs[-3:]
    feat = sent.shape[1]
    copies = Copies(sems)
    block = early_ref.shape[1]
    for at in range(0, feat, block):
        wide = slice(at, at + block)
        total = (rest_ref[:, at - block : at] if at else early_ref[...]).astype(F32)
        for other in terms:
            total = total + other[:, wide].astype(F32)
        sent[:, wide] = total.astype(BF16)
        copies.store(sent.at[:, wide], out_hbm.at[:, wide])
    copies.finish()


def finish(terms):
    rows, feat = terms[-1].shape
    return kernel_call(
        finish_kernel,
        terms,
        [VM] * len(terms),
        [((rows, feat), BF16)],
        (HB,),
        [
            pltpu.VMEM((rows, feat), BF16),
            pltpu.SemaphoreType.DMA((feat // terms[0].shape[1],)),
        ],
        12,
        "finish",
        6,
    )[0]


def close_kernel(
    heads, hp, mine_ref, theirs_ref, k_ref, v_ref, dk_ref, dv_ref, table_ref, dq_ref, own_ref, *refs
):
    dk_hbm, dv_hbm, term_ref, kside, vside, sems = refs
    upper = lax.axis_index("ctx") % 2 == 1
    pair = min(2, heads)
    copies = Copies(sems)
    table = table_ref[...]
    for h in range(heads):
        cols = slice(h * HDIM, (h + 1) * HDIM)
        adjoint = whole_head(upper, h, mine_ref, theirs_ref)
        tail, gain = column(table, 2 * hp + h), column(table, hp + h)
        carry_k = dot(v_ref[:, cols], adjoint, NT)
        kside[:, cols] = (gain * (dk_ref[:, cols].astype(F32) + tail * carry_k)).astype(BF16)
        carry_v = dot(scaled_keys(table, hp, h, k_ref[:, cols]), adjoint, NN)
        vside[:, cols] = (dv_ref[:, cols].astype(F32) + tail * carry_v).astype(BF16)
        if (h + 1) % pair == 0:
            wide = slice((h + 1 - pair) * HDIM, (h + 1) * HDIM)
            copies.store(kside.at[:, wide], dk_hbm.at[:, wide])
            copies.store(vside.at[:, wide], dv_hbm.at[:, wide])
    put_terms(dq_ref, own_ref.at[own_ref.shape[0] - term_ref.shape[1] :], term_ref)
    copies.finish()


def close(halves, held, d_query, own, heads, hp):
    rows, width = d_query.shape
    args = (*halves, *held, d_query, own)
    buf = pltpu.VMEM((rows, width), BF16)
    return kernel_call(
        functools.partial(close_kernel, heads, hp),
        args,
        [VM] * len(args),
        [((rows, width), BF16)] * 2 + [((rows, own.shape[0] * 3 // 4), BF16)],
        (HB, HB, VM),
        [buf, buf, pltpu.SemaphoreType.DMA((2 * (heads // min(2, heads)),))],
        12,
        "close",
        100,
    )


def body(ctx_size, head_size, hidden, w_query, keys, values, d_out, log_decay):
    rows, feat = hidden.shape
    heads = log_decay.shape[1]
    width = w_query.shape[1]
    hp = sublanes(heads)
    scaling = HDIM ** (-0.5)
    me = lax.axis_index("ctx")

    parts = [hidden]
    for shift in range(1, head_size):
        ring = [(i, (i + shift) % head_size) for i in range(head_size)]
        parts.append(lax.ppermute(hidden, "head", ring))

    facts, kept, sent, share = prepare(log_decay.T, keys, values, heads, hp, scaling)
    query, akept, asent = project(parts, w_query, d_out, facts, hp)

    size = width // 2
    wide = lambda factor: factor[:heads, None, :]
    cube = lambda flat: flat[:size].reshape(heads, HDIM // 2, HDIM).astype(F32)
    flat = lambda cubes: cubes.astype(BF16).reshape(size, HDIM)
    split = lambda f: (f.astype(BF16), (f - f.astype(BF16).astype(F32)).astype(BF16))
    joined = lambda rows: rows[size : size + hp].astype(F32) + rows[size + hp :].astype(F32)
    stages = (ctx_size - 1).bit_length()
    uppers = [(me & (1 << stage)) != 0 for stage in range(stages)]

    def send(array, stage):
        dist = 1 << (stage % stages)
        return lax.ppermute(array, "ctx", [(i, i ^ dist) for i in range(ctx_size)])

    shares, others = [share], []
    before, after = [jnp.ones_like(share)], [jnp.ones_like(share)]

    def fold(stage, total, carried, arrived, up):
        upper = uppers[stage]
        first = upper if up else ~upper
        arrived = cube(arrived)
        if stage > 0:
            weight = jnp.where(first, before[stage] if up else after[stage], 0.0)
            carried = carried + wide(weight) * arrived
        if stage == stages - 1:
            lead = uppers[0] if up else ~uppers[0]
            block, other = total
            mine = jnp.where(lead, cube(other) + wide(others[0]) * carried, carried)
            theirs = jnp.where(lead, carried, cube(block) + wide(shares[0]) * carried)
            return flat(theirs), flat(mine), None
        own, other = jnp.where(first, 1.0, others[stage]), jnp.where(first, shares[stage], 1.0)
        total = wide(own) * total + wide(other) * arrived
        return flat(total), total, carried

    def fold_factors(stage, arrived):
        theirs = joined(arrived)
        others.append(theirs)
        shares.append(shares[stage] * theirs)
        upper = uppers[stage]
        pair = stage == 0
        before.append(before[stage] if pair else jnp.where(upper, before[stage] * theirs, before[stage]))
        after.append(after[stage] if pair else jnp.where(upper, after[stage], after[stage] * theirs))

    class Chain:
        def __init__(self, kept, sent, up):
            self.kept, self.sent, self.up = kept, sent, up
            self.total, self.carried, self.stage, self.arrived = cube(kept), jnp.zeros_like(cube(kept)), 0, None

        def go(self):
            self.arrived = send(self.sent, self.stage)

        def take(self):
            stage, self.stage = self.stage, self.stage + 1
            if stage == 0:
                self.first = self.arrived
            total = self.total if stage < stages - 1 else (self.kept, self.first)
            if self.up and stage < stages - 1:
                fold_factors(stage, self.arrived)
            self.sent, self.total, self.carried = fold(stage, total, self.carried, self.arrived, self.up)
            if self.up and stage + 2 < stages:
                self.sent = jnp.concatenate([self.sent, *split(shares[-1])], axis=0)

    states, adjoints = Chain(kept, sent, True), Chain(akept, asent, False)
    spans = spans_of(heads)
    pending = list(spans)
    inner_parts = []
    barrier = lax.optimization_barrier
    for stage in range(stages + 1):
        if stage == stages:
            weight, _ = barrier((w_query, adjoints.sent))
            dqs, dks, dvs = zip(*inner_parts)
            *fetched, = fetch(head_size, weight, d_out, facts, dqs, feat, heads)
            fetched, own, weights = fetched[:3], fetched[3], fetched[4:]
        states.go()
        if stage == 0:
            states.arrived, query, adjoints.kept, adjoints.sent = barrier(
                (states.arrived, query, adjoints.kept, adjoints.sent)
            )
            adjoints.total = cube(adjoints.kept)
        else:
            adjoints.go()
            if pending and stage <= len(spans):
                query, _ = barrier((query, adjoints.sent))
                part = inner(*pending.pop(0), query, keys, values, d_out, facts, hp)
                states.arrived, *part = barrier((states.arrived, *part))
                inner_parts.append(part)
        if stage == stages - 1:
            adjoints.take()
            states.arrived, _ = barrier((states.arrived, adjoints.sent))
            states.take()
            continue
        if stage < stages:
            states.take()
        if stage >= 1:
            adjoints.arrived, _ = barrier((adjoints.arrived, states.sent if stage < stages else states.total))
            adjoints.take()
    adjoints.go()
    states.arrived, _ = barrier((states.arrived, adjoints.sent))
    state_halves = (states.total, states.arrived)
    adjoint_halves = (adjoints.total, adjoints.arrived)
    arrived = []
    for shift in range(1, head_size):
        ring = [(i, (i + shift) % head_size) for i in range(head_size)]
        if shift == 1:
            d_query, term, *held = query_term(
                state_halves, weights[0], fetched, keys, values, dks, dvs, heads, hp
            )
        else:
            term = plain_term(d_query, weights[shift - 1])
        arrived.append(lax.ppermute(term, "head", ring))
    early = early_term(d_query, own)
    d_keys, d_values, rest = close(adjoint_halves, held, d_query, own, heads, hp)
    d_hidden = finish((early, rest, *arrived))
    return (d_hidden, d_keys, d_values)


def solution(mesh):
    return jax.shard_map(
        functools.partial(body, mesh.shape["ctx"], mesh.shape["head"]),
        mesh=mesh,
        in_specs=(
            P("ctx", "head"),
            P(None, "head"),
            P("ctx", "head"),
            P("ctx", "head"),
            P("ctx", "head"),
            P("ctx", "head"),
        ),
        out_specs=(P("ctx", "head"), P("ctx", "head"), P("ctx", "head")),
        check_vma=False,
    )
```
